32 devices in a mesh: section: 2 (over x), shard: 16 (over z, y, core).
Axes of the slice: x: 2, y: 2, z: 4, core: 2. Of those that a mesh axis runs over, the one named last changes fastest.
Arguments:
- embedded: bfloat16 [2, 2048, 2048], P(None, 'shard'), may hold values from -6 to 6
- cotangent: bfloat16 [2, 2048, 2048], P(None, 'shard'), may hold values from -6 to 6
- segments: int32 [2, 2048], replicated, may hold values from 0 to 3, as said below
- first_gain: bfloat16 [2, 2048], P('section', 'shard'), may hold values from 0.25 to 1.75
- first_shift: bfloat16 [2, 2048], P('section', 'shard'), may hold values from -1 to 1
- mixer_weight: bfloat16 [2, 2048, 2304], P('section', 'shard'), may hold values from -0.1875 to 0.1875
- mixer_bias: bfloat16 [2, 2176], P('section', 'shard'), may hold values from -1 to 1
- output_weight: bfloat16 [2, 2048, 2048], P('section', 'shard'), may hold values from -0.5 to 0.5
- output_bias: bfloat16 [2, 2048], P('section', 'shard'), may hold values from -1 to 1
- second_gain: bfloat16 [2, 2048], P('section', 'shard'), may hold values from 0.25 to 1.75
- second_shift: bfloat16 [2, 2048], P('section', 'shard'), may hold values from -1 to 1
- expand_weight: bfloat16 [2, 2048, 8192], P('section', 'shard'), may hold values from -0.125 to 0.125
- expand_bias: bfloat16 [2, 8192], P('section', 'shard'), may hold values from -1 to 1
- contract_weight: bfloat16 [2, 8192, 2048], P('section', 'shard'), may hold values from -0.125 to 0.125
- contract_bias: bfloat16 [2, 2048], P('section', 'shard'), may hold values from -1 to 1
Outputs:
- section_outputs: bfloat16 [2, 2, 2048, 2048], P('section', None, 'shard')
- input_grads: float32 [2, 2, 2048, 2048], P('section', None, 'shard')
- first_gain_grad: float32 [2, 2048], P('section', 'shard')
- first_shift_grad: float32 [2, 2048], P('section', 'shard')
- mixer_weight_grad: float32 [2, 2048, 2304], P('section', 'shard')
- mixer_bias_grad: float32 [2, 2176], P('section', 'shard')
- output_weight_grad: float32 [2, 2048, 2048], P('section', 'shard')
- output_bias_grad: float32 [2, 2048], P('section', 'shard')
- second_gain_grad: float32 [2, 2048], P('section', 'shard')
- second_shift_grad: float32 [2, 2048], P('section', 'shard')
- expand_weight_grad: float32 [2, 2048, 8192], P('section', 'shard')
- expand_bias_grad: float32 [2, 8192], P('section', 'shard')
- contract_weight_grad: float32 [2, 8192, 2048], P('section', 'shard')
- contract_bias_grad: float32 [2, 2048], P('section', 'shard')
The draws below stay inside these ranges and needn't reach their ends.
Inputs may be any that keep to these rules, and one draw needn't show every extreme that they name: `segments`: in each row, segment numbers start at 0 at position 0, never fall, rise by at most one from one position to the next, and end at 3; in one row, drawn from the seed, no document begins between position 128 and position 1920.
All inputs are finite; a program needn't handle non-finite values.
Results may differ from the reference program's by a relative error of at most 0.03.
Values may be sent and summed in bfloat16 or wider, within the bound.
A program may use at most 384 MiB of HBM per device.

```python
import jax
import jax.numpy as jnp
from jax import lax

D = 2048
HEADS = 16
HD = 128
FF = 8192
WINDOW = 1024
MICRO = 2
TOK_DEV = 128
QKV = 2304
SEQ = 2048
N_SECTION = 2


def draw_segments(key, part):
    key = jax.random.fold_in(key, 7)
    rank_key, row_key = jax.random.split(key, 2)
    start_count = 2 * SEQ // WINDOW - 1
    row_keys = jax.random.split(rank_key, MICRO)
    ranks = jax.vmap(lambda one_key: jax.random.permutation(one_key, SEQ - 1))(row_keys).astype(jnp.int32)
    spanning = jax.random.randint(row_key, (), 0, MICRO)
    position = jnp.arange(1, SEQ)
    interior = (position >= TOK_DEV) & (position < SEQ - TOK_DEV)
    row_ids = jnp.arange(MICRO)
    ranks = jnp.where((row_ids[:, None] == spanning) & interior[None, :], ranks - SEQ, ranks)
    top_values, picked = lax.top_k(ranks, start_count)
    marks = jnp.sum((picked[:, :, None] == jnp.arange(SEQ - 1)[None, None, :]).astype(jnp.int32), axis=1)
    starts = jnp.concatenate([jnp.zeros((MICRO, 1), jnp.int32), marks], axis=1)
    return jnp.cumsum(starts, axis=1).astype(jnp.int32)


def block_scale(rng, extent, shards, least, top_value):
    factor_of, own = 1.0, jax.random.fold_in(rng, 6)
    for dim, shards_of in shards:
        steps = jnp.exp(jax.random.uniform(jax.random.fold_in(own, dim), (shards_of,), jnp.float32, least / len(shards), top_value / len(shards)))
        factor_of = factor_of * jnp.repeat(steps, extent[dim] // shards_of).reshape([-1 if axis == dim else 1 for axis in range(len(extent))])
    return factor_of


def noise(key, extent, scale, reach, cuts=(), dtype=jnp.bfloat16):
    level = block_scale(key, extent, cuts, -0.22, 0.18) if cuts else 1.0
    array = jax.random.normal(key, extent, jnp.float32) * scale * level
    return jnp.minimum(jnp.maximum(array, -reach), reach).astype(dtype)


def setup_inputs(seed: int = 0) -> dict:
    splits = jax.random.split(jax.random.key(seed), 16)
    return {
        "embedded": noise(splits[0], (MICRO, SEQ, D), 1.0, 6.0, ((1, 16),)),
        "cotangent": noise(splits[1], (MICRO, SEQ, D), 1.0, 6.0, ((1, 16),)),
        "segments": draw_segments(jax.random.fold_in(splits[15], 71), 0),
        "first_gain": jnp.clip(1.0 + 0.15 * jax.random.normal(splits[3], (N_SECTION, D), jnp.float32), 0.25, 1.75).astype(jnp.bfloat16),
        "first_shift": noise(splits[4], (N_SECTION, D), 0.2, 1.0, ((0, 2), (1, 16))),
        "mixer_weight": noise(splits[5], (N_SECTION, D, QKV), (D // 2) ** -0.5, 0.1875, ((0, 2), (1, 16))),
        "mixer_bias": noise(splits[6], (N_SECTION, D + HD), 0.2, 1.0, ((0, 2), (1, 16))),
        "output_weight": noise(splits[7], (N_SECTION, D, D), (D // 16) ** -0.5, 0.5, ((0, 2), (1, 16))),
        "output_bias": noise(splits[8], (N_SECTION, D), 0.2, 1.0, ((0, 2), (1, 16))),
        "second_gain": jnp.clip(1.0 + 0.15 * jax.random.normal(splits[9], (N_SECTION, D), jnp.float32), 0.25, 1.75).astype(jnp.bfloat16),
        "second_shift": noise(splits[10], (N_SECTION, D), 0.2, 1.0, ((0, 2), (1, 16))),
        "expand_weight": noise(splits[11], (N_SECTION, D, FF), D ** -0.5, 0.125, ((0, 2), (1, 16))),
        "expand_bias": noise(splits[12], (N_SECTION, FF), 0.2, 1.0, ((0, 2), (1, 16))),
        "contract_weight": noise(splits[13], (N_SECTION, FF, D), (FF // 4) ** -0.5, 0.125, ((0, 2), (1, 16))),
        "contract_bias": noise(splits[14], (N_SECTION, D), 0.2, 1.0, ((0, 2), (1, 16))),
    }


@jax.custom_vjp
def low(v):
    return lax.optimization_barrier(v.astype(jnp.bfloat16)).astype(jnp.float32)

@jax.custom_vjp
def low_back(v):
    return v

def low_keep(v):
    return (low(v), None)

def low_pass(kept, grad):
    return (grad,)

def back_keep(v):
    return (v, None)

def back_low(kept, grad):
    return (low(grad),)
low.defvjp(low_keep, low_pass)
low_back.defvjp(back_keep, back_low)

def product(left_side, right_side):
    return jnp.dot(left_side, right_side, precision=lax.Precision.HIGHEST)

def layer_norm(values, gain_row, shift_row):
    center = values - lax.optimization_barrier(jnp.mean(values, axis=-1, keepdims=True))
    spread = lax.optimization_barrier(jnp.mean(center * center, axis=-1, keepdims=True))
    return center * lax.rsqrt(spread + 1e-05) * gain_row + shift_row

def attend(queries, key_value, seg_row):
    length = queries.shape[0]
    block_rows = min(512, length)
    score_scale = HD ** (-0.5)
    padded_pairs = jnp.concatenate([jnp.zeros((WINDOW, 2 * HD), jnp.float32), key_value], axis=0)
    padded_segments = jnp.concatenate([jnp.full((WINDOW,), -1, jnp.int32), seg_row.astype(jnp.int32)])

    def one_block(start_row):
        block_queries = lax.dynamic_slice_in_dim(queries, start_row, block_rows, 0)
        block_pairs = lax.dynamic_slice_in_dim(padded_pairs, start_row, WINDOW + block_rows, 0)
        query_segments = lax.dynamic_slice_in_dim(seg_row.astype(jnp.int32), start_row, block_rows)
        key_segments = lax.dynamic_slice_in_dim(padded_segments, start_row, WINDOW + block_rows)
        distance = jnp.arange(block_rows)[:, None] + WINDOW - jnp.arange(WINDOW + block_rows)[None, :]
        allowed = (distance >= 0) & (distance < WINDOW) & (query_segments[:, None] == key_segments[None, :])
        scores = low_back(jnp.einsum('thd,kd->htk', block_queries, block_pairs[:, :HD], precision=lax.Precision.HIGHEST) * score_scale)
        masked = jnp.where(allowed[None], scores, -1e+30)
        top_score = lax.optimization_barrier(jnp.max(masked, axis=2, keepdims=True))
        exponent = jnp.exp(masked - top_score)
        prob_low = low(exponent / lax.optimization_barrier(jnp.sum(exponent, axis=2, keepdims=True)))
        return jnp.einsum('htk,kd->thd', prob_low, block_pairs[:, HD:], precision=lax.Precision.HIGHEST)
    starts = (jnp.arange(length // block_rows) * block_rows).astype(jnp.int32)
    blocks = lax.map(jax.checkpoint(one_block), starts)
    return blocks.reshape(length, HEADS * HD)

def run_layer(hidden, weights, seg_row):
    first_gain, first_shift, mixer_weight, mixer_bias, output_weight, output_bias, second_gain, second_shift, expand_weight, expand_bias, contract_weight, contract_bias = weights
    normed_one = low(layer_norm(hidden, first_gain, first_shift))
    full_bias = jnp.concatenate([mixer_bias[:D], jnp.zeros((HD,), jnp.float32), mixer_bias[D:]])
    projected = low(low_back(product(normed_one, mixer_weight) + full_bias))
    queries = projected[:, :D].reshape(-1, HEADS, HD)
    mixed_rows = low(low_back(attend(queries, projected[:, D:], seg_row)))
    middle = hidden + low_back(product(mixed_rows, output_weight) + output_bias)
    normed_two = low(layer_norm(middle, second_gain, second_shift))
    pre_gelu = low_back(product(normed_two, expand_weight) + expand_bias)
    activated = low(jax.nn.gelu(pre_gelu, approximate=True))
    return middle + low_back(product(activated, contract_weight) + contract_bias)

def reference(embedded, cotangent, segments, first_gain, first_shift, mixer_weight, mixer_bias, output_weight, output_bias, second_gain, second_shift, expand_weight, expand_bias, contract_weight, contract_bias):
    params = [member.astype(jnp.float32) for member in (first_gain, first_shift, mixer_weight, mixer_bias, output_weight, output_bias, second_gain, second_shift, expand_weight, expand_bias, contract_weight, contract_bias)]
    inputs = embedded.astype(jnp.float32)
    boundary = jnp.zeros(inputs.shape, jnp.float32)

    def forward(inputs, boundary, params):
        sent_list = []
        final_list = []
        for micro_index in range(MICRO):
            first_out = run_layer(inputs[micro_index], [member[0] for member in params], segments[micro_index])
            sent_rows = low_back(low(first_out))
            final_rows = run_layer(sent_rows + boundary[micro_index], [member[1] for member in params], segments[micro_index])
            sent_list.append(sent_rows)
            final_list.append(final_rows)
        return (jnp.stack(sent_list), jnp.stack(final_list))
    (sent_all, final_all), pullback = jax.vjp(forward, inputs, boundary, params)
    grad_inputs, grad_boundary, grad_params = pullback((jnp.zeros_like(sent_all), cotangent.astype(jnp.float32)))
    section_outputs = jnp.stack([sent_all, final_all]).astype(jnp.bfloat16)
    input_grads = jnp.stack([grad_inputs, grad_boundary])
    return (section_outputs, input_grads, grad_params[0], grad_params[1], grad_params[2], grad_params[3], grad_params[4], grad_params[5], grad_params[6], grad_params[7], grad_params[8], grad_params[9], grad_params[10], grad_params[11])
```

```python
import functools

import jax
import jax.numpy as jnp
from jax import lax
from jax.experimental import pallas as pl
from jax.experimental.pallas import tpu as pltpu
from jax.sharding import PartitionSpec as P

D = 2048
HEADS = 16
HD = 128
WINDOW = 1024


epsilon = 1e-05


def passed_along(block, axis, distance):
    devices = range(lax.axis_size(axis))
    route = [(i - distance, i) for i in devices if i - distance in devices]
    return lax.ppermute(block, axis, route)


def layer_norm(values, gain_row, shift_row):
    center = values - jnp.mean(values, axis=-1, keepdims=True)
    spread = jnp.mean(center * center, axis=-1, keepdims=True)
    return center * lax.rsqrt(spread + epsilon) * gain_row + shift_row


def gelu_tanh(values):
    return jax.nn.gelu(values, approximate=True)


def window_mask(segments, micro_index, device, row_count, reach_blocks):
    seg_row = lax.dynamic_index_in_dim(segments, micro_index, 0, keepdims=False)
    padded = jnp.concatenate([jnp.full((reach_blocks * row_count,), -1, jnp.int32), seg_row])
    key_segments = lax.dynamic_slice_in_dim(
        padded, device * row_count, (reach_blocks + 1) * row_count
    )
    query_segments = lax.dynamic_slice_in_dim(seg_row, device * row_count, row_count)
    distance = (
        jnp.arange(row_count)[:, None]
        + reach_blocks * row_count
        - jnp.arange((reach_blocks + 1) * row_count)[None, :]
    )
    return (
        (distance >= 0) & (distance < WINDOW) & (query_segments[:, None] == key_segments[None, :])
    )


def fetch_window(key_value, reach_blocks):
    earlier = [passed_along(key_value, "shard", offset) for offset in range(reach_blocks, 0, -1)]
    return jnp.concatenate(earlier + [key_value], axis=0)


def return_window(window_grad, reach_blocks, row_count):
    own_rows = window_grad[reach_blocks * row_count :]
    for offset in range(1, reach_blocks + 1):
        start_row = (reach_blocks - offset) * row_count
        own_rows = own_rows + passed_along(
            window_grad[start_row : start_row + row_count].astype(jnp.bfloat16), "shard", -offset
        ).astype(jnp.float32)
    return own_rows


def forward_layer(hidden, weights, key_mask, reach_blocks):
    (
        first_gain,
        first_shift,
        mixer_weight,
        mixer_bias,
        output_weight,
        output_bias,
        second_gain,
        second_shift,
        expand_weight,
        expand_bias,
        contract_weight,
        contract_bias,
    ) = weights
    row_count = hidden.shape[0]
    score_scale = HD ** (-0.5)
    normed_one = layer_norm(
        hidden, first_gain.astype(jnp.float32), first_shift.astype(jnp.float32)
    ).astype(jnp.bfloat16)
    full_bias = jnp.concatenate(
        [mixer_bias[:D], jnp.zeros((HD,), mixer_bias.dtype), mixer_bias[D:]]
    ).astype(jnp.float32)
    projected = (
        jnp.dot(normed_one, mixer_weight, preferred_element_type=jnp.float32) + full_bias
    ).astype(jnp.bfloat16)
    queries = projected[:, :D].reshape(row_count, HEADS, HD)
    window_pairs = fetch_window(projected[:, D:], reach_blocks)
    scores = (
        jnp.einsum("thd,kd->htk", queries, window_pairs[:, :HD], preferred_element_type=jnp.float32)
        * score_scale
    )
    masked = jnp.where(key_mask[None], scores, -1e30)
    top_score = jnp.max(masked, axis=2, keepdims=True)
    exponent = jnp.exp(masked - top_score)
    totals = jnp.sum(exponent, axis=2, keepdims=True)
    prob_low = (exponent / totals).astype(jnp.bfloat16)
    log_total = top_score + jnp.log(totals)
    mixed_rows = (
        jnp.einsum(
            "htk,kd->thd", prob_low, window_pairs[:, HD:], preferred_element_type=jnp.float32
        )
        .reshape(row_count, D)
        .astype(jnp.bfloat16)
    )
    middle = (
        hidden
        + jnp.dot(mixed_rows, output_weight, preferred_element_type=jnp.float32)
        + output_bias.astype(jnp.float32)
    )
    normed_two = layer_norm(
        middle, second_gain.astype(jnp.float32), second_shift.astype(jnp.float32)
    ).astype(jnp.bfloat16)
    pre_gelu = jnp.dot(
        normed_two, expand_weight, preferred_element_type=jnp.float32
    ) + expand_bias.astype(jnp.float32)
    activated = gelu_tanh(pre_gelu).astype(jnp.bfloat16)
    result = (
        middle
        + jnp.dot(activated, contract_weight, preferred_element_type=jnp.float32)
        + contract_bias.astype(jnp.float32)
    )
    return (
        result,
        (
            hidden,
            normed_one,
            projected,
            window_pairs,
            log_total,
            mixed_rows,
            middle,
            normed_two,
            pre_gelu,
            activated,
        ),
    )


def backward_layer(grad_result, weights, saved_state, key_mask, reach_blocks):
    (
        first_gain,
        first_shift,
        mixer_weight,
        mixer_bias,
        output_weight,
        output_bias,
        second_gain,
        second_shift,
        expand_weight,
        expand_bias,
        contract_weight,
        contract_bias,
    ) = weights
    (
        hidden,
        normed_one,
        projected,
        window_pairs,
        log_total,
        mixed_rows,
        middle,
        normed_two,
        pre_gelu,
        activated,
    ) = saved_state
    row_count = hidden.shape[0]
    score_scale = HD ** (-0.5)
    grad_out_low = grad_result.astype(jnp.bfloat16)
    grad_act = jnp.einsum(
        "rd,fd->rf", grad_out_low, contract_weight, preferred_element_type=jnp.float32
    )
    gelu_value, gelu_back = jax.vjp(gelu_tanh, pre_gelu)
    grad_pre = gelu_back(grad_act)[0].astype(jnp.bfloat16)
    grad_normed_two = jnp.einsum(
        "rf,df->rd", grad_pre, expand_weight, preferred_element_type=jnp.float32
    )
    norm_value_two, norm_back_two = jax.vjp(
        layer_norm, middle, second_gain.astype(jnp.float32), second_shift.astype(jnp.float32)
    )
    grad_middle_part, grad_gain_two, grad_shift_two = norm_back_two(grad_normed_two)
    grad_middle = grad_result + grad_middle_part
    grad_attended = grad_middle.astype(jnp.bfloat16)
    grad_mixed = (
        jnp.einsum("re,de->rd", grad_attended, output_weight, preferred_element_type=jnp.float32)
        .astype(jnp.bfloat16)
        .reshape(row_count, HEADS, HD)
    )
    queries = projected[:, :D].reshape(row_count, HEADS, HD)
    key_part = window_pairs[:, :HD]
    value_part = window_pairs[:, HD:]
    scores = (
        jnp.einsum("thd,kd->htk", queries, key_part, preferred_element_type=jnp.float32)
        * score_scale
    )
    prob_full = jnp.where(key_mask[None], jnp.exp(scores - log_total), 0.0)
    prob_low = prob_full.astype(jnp.bfloat16)
    grad_probs = jnp.einsum(
        "thd,kd->htk", grad_mixed, value_part, preferred_element_type=jnp.float32
    )
    row_dot = jnp.sum(prob_full * grad_probs, axis=2, keepdims=True)
    grad_scores = (prob_full * (grad_probs - row_dot)).astype(jnp.bfloat16)
    grad_queries = (
        jnp.einsum("htk,kd->thd", grad_scores, key_part, preferred_element_type=jnp.float32)
        * score_scale
    ).reshape(row_count, D)
    grad_keys = (
        jnp.einsum("htk,thd->kd", grad_scores, queries, preferred_element_type=jnp.float32)
        * score_scale
    )
    grad_values = jnp.einsum(
        "htk,thd->kd", prob_low, grad_mixed, preferred_element_type=jnp.float32
    )
    grad_window = jnp.concatenate([grad_keys, grad_values], axis=1)
    grad_own_pairs = return_window(grad_window, reach_blocks, row_count)
    grad_projected = jnp.concatenate([grad_queries, grad_own_pairs], axis=1).astype(jnp.bfloat16)
    grad_normed_one = jnp.einsum(
        "rq,dq->rd", grad_projected, mixer_weight, preferred_element_type=jnp.float32
    )
    norm_value_one, norm_back_one = jax.vjp(
        layer_norm, hidden, first_gain.astype(jnp.float32), first_shift.astype(jnp.float32)
    )
    grad_hidden_part, grad_gain_one, grad_shift_one = norm_back_one(grad_normed_one)
    grad_hidden = grad_middle + grad_hidden_part
    return (
        grad_hidden,
        (
            grad_projected,
            grad_attended,
            grad_pre,
            grad_out_low,
            grad_gain_one,
            grad_shift_one,
            grad_gain_two,
            grad_shift_two,
            normed_one,
            mixed_rows,
            normed_two,
            activated,
        ),
    )


def flatten_rows(stacked):
    return stacked.reshape((-1, stacked.shape[-1]))


def weight_terms(row_items, norm_items):
    (
        grad_projected_rows,
        grad_attended_rows,
        grad_pre_rows,
        grad_out_rows,
        normed_one_rows,
        mixed_all,
        normed_two_rows,
        activated_rows,
    ) = row_items
    first_gain_term, first_shift_term, second_gain_term, second_shift_term = norm_items
    mixer_weight_term = jnp.einsum(
        "rd,rq->dq", normed_one_rows, grad_projected_rows, preferred_element_type=jnp.float32
    )
    column_totals = jnp.sum(grad_projected_rows.astype(jnp.float32), axis=0)
    mixer_bias_term = jnp.concatenate([column_totals[:D], column_totals[D + HD :]])
    output_weight_term = jnp.einsum(
        "rd,re->de", mixed_all, grad_attended_rows, preferred_element_type=jnp.float32
    )
    output_bias_term = jnp.sum(grad_attended_rows.astype(jnp.float32), axis=0)
    expand_weight_term = jnp.einsum(
        "rd,rf->df", normed_two_rows, grad_pre_rows, preferred_element_type=jnp.float32
    )
    expand_bias_term = jnp.sum(grad_pre_rows.astype(jnp.float32), axis=0)
    contract_weight_term = jnp.einsum(
        "rf,rd->fd", activated_rows, grad_out_rows, preferred_element_type=jnp.float32
    )
    contract_bias_term = jnp.sum(grad_out_rows.astype(jnp.float32), axis=0)
    return (
        first_gain_term[None],
        first_shift_term[None],
        mixer_weight_term[None],
        mixer_bias_term[None],
        output_weight_term[None],
        output_bias_term[None],
        second_gain_term[None],
        second_shift_term[None],
        expand_weight_term[None],
        expand_bias_term[None],
        contract_weight_term[None],
        contract_bias_term[None],
    )


def on_device_general(
    embedded,
    cotangent,
    segments,
    first_gain,
    first_shift,
    mixer_weight,
    mixer_bias,
    output_weight,
    output_bias,
    second_gain,
    second_shift,
    expand_weight,
    expand_bias,
    contract_weight,
    contract_bias,
):
    section_index = lax.axis_index("section")
    device = lax.axis_index("shard")
    micro_count = embedded.shape[0]
    row_count = embedded.shape[1]
    reach_blocks = WINDOW // row_count
    own_params = (
        first_gain[0],
        first_shift[0],
        mixer_weight[0],
        mixer_bias[0],
        output_weight[0],
        output_bias[0],
        second_gain[0],
        second_shift[0],
        expand_weight[0],
        expand_bias[0],
        contract_weight[0],
        contract_bias[0],
    )
    forward_weights = (
        lax.all_gather(own_params[0], "shard", axis=0, tiled=True),
        lax.all_gather(own_params[1], "shard", axis=0, tiled=True),
        lax.all_gather(own_params[2], "shard", axis=0, tiled=True),
        lax.all_gather(own_params[3], "shard", axis=0, tiled=True),
        lax.all_gather(own_params[4], "shard", axis=0, tiled=True),
        lax.all_gather(own_params[5], "shard", axis=0, tiled=True),
        lax.all_gather(own_params[6], "shard", axis=0, tiled=True),
        lax.all_gather(own_params[7], "shard", axis=0, tiled=True),
        lax.all_gather(own_params[8], "shard", axis=0, tiled=True),
        lax.all_gather(own_params[9], "shard", axis=0, tiled=True),
        lax.all_gather(own_params[10], "shard", axis=0, tiled=True),
        lax.all_gather(own_params[11], "shard", axis=0, tiled=True),
    )
    zero_rows = jnp.zeros((row_count, D), jnp.float32)
    arrived = zero_rows
    sent_list = []
    kept_states = []
    for step_index in range(micro_count + 1):
        own_input = (
            embedded[step_index].astype(jnp.float32) if step_index < micro_count else zero_rows
        )
        hidden = jnp.where(section_index == 0, own_input, arrived)
        micro_index = jnp.clip(step_index - section_index, 0, micro_count - 1)
        key_mask = window_mask(segments, micro_index, device, row_count, reach_blocks)
        result, saved_state = forward_layer(hidden, forward_weights, key_mask, reach_blocks)
        result_low = result.astype(jnp.bfloat16)
        sent_list.append(result_low)
        kept_states.append(saved_state)
        if step_index < micro_count:
            arrived = passed_along(result_low, "section", 1).astype(jnp.float32)
    section_outputs = lax.dynamic_slice_in_dim(jnp.stack(sent_list), section_index, micro_count, 0)[
        None
    ]
    stacked_states = [
        jnp.stack([state_item[item_index] for state_item in kept_states])
        for item_index in range(10)
    ]
    valid_start = 1 - section_index
    arrived_grad = zero_rows
    grad_records = []
    hidden_grads = []
    for step_index in range(micro_count + 1):
        own_grad = (
            cotangent[step_index].astype(jnp.float32) if step_index < micro_count else zero_rows
        )
        grad_result = jnp.where(section_index == 1, own_grad, arrived_grad)
        forward_index = jnp.clip(step_index - 1 + 2 * section_index, 0, micro_count)
        micro_index = jnp.clip(step_index - 1 + section_index, 0, micro_count - 1)
        saved_state = [
            lax.dynamic_index_in_dim(stacked, forward_index, 0, keepdims=False)
            for stacked in stacked_states
        ]
        key_mask = window_mask(segments, micro_index, device, row_count, reach_blocks)
        grad_hidden, record = backward_layer(
            grad_result, forward_weights, saved_state, key_mask, reach_blocks
        )
        hidden_grads.append(grad_hidden)
        if step_index < micro_count:
            arrived_grad = passed_along(grad_hidden.astype(jnp.bfloat16), "section", -1).astype(
                jnp.float32
            )
        grad_records.append(record)
    input_grads = lax.dynamic_slice_in_dim(jnp.stack(hidden_grads), valid_start, micro_count, 0)[
        None
    ]
    chosen = [
        lax.dynamic_slice_in_dim(
            jnp.stack([record[item_index] for record in grad_records]), valid_start, micro_count, 0
        )
        for item_index in range(12)
    ]
    row_items = (
        flatten_rows(chosen[0]),
        flatten_rows(chosen[1]),
        flatten_rows(chosen[2]),
        flatten_rows(chosen[3]),
        flatten_rows(chosen[8]),
        flatten_rows(chosen[9]),
        flatten_rows(chosen[10]),
        flatten_rows(chosen[11]),
    )
    norm_items = (
        jnp.sum(chosen[4], axis=0),
        jnp.sum(chosen[5], axis=0),
        jnp.sum(chosen[6], axis=0),
        jnp.sum(chosen[7], axis=0),
    )
    all_terms = weight_terms(row_items, norm_items)
    summed = (
        lax.psum_scatter(all_terms[0], "shard", scatter_dimension=1, tiled=True),
        lax.psum_scatter(all_terms[1], "shard", scatter_dimension=1, tiled=True),
        lax.psum_scatter(all_terms[2], "shard", scatter_dimension=1, tiled=True),
        lax.psum_scatter(all_terms[3], "shard", scatter_dimension=1, tiled=True),
        lax.psum_scatter(all_terms[4], "shard", scatter_dimension=1, tiled=True),
        lax.psum_scatter(all_terms[5], "shard", scatter_dimension=1, tiled=True),
        lax.psum_scatter(all_terms[6], "shard", scatter_dimension=1, tiled=True),
        lax.psum_scatter(all_terms[7], "shard", scatter_dimension=1, tiled=True),
        lax.psum_scatter(all_terms[8], "shard", scatter_dimension=1, tiled=True),
        lax.psum_scatter(all_terms[9], "shard", scatter_dimension=1, tiled=True),
        lax.psum_scatter(all_terms[10], "shard", scatter_dimension=1, tiled=True),
        lax.psum_scatter(all_terms[11], "shard", scatter_dimension=1, tiled=True),
    )
    return (
        section_outputs,
        input_grads,
        summed[0],
        summed[1],
        summed[2],
        summed[3],
        summed[4],
        summed[5],
        summed[6],
        summed[7],
        summed[8],
        summed[9],
        summed[10],
        summed[11],
    )


MESH = pl.DeviceIdType.MESH
LIMIT = 60 << 20
CUBE = ("x", 4, 2, 1)
ALL = ("x", 8, 4, 2, 1)


class Hyper:
    def __init__(self, dims):
        sec = lax.axis_index("section")
        shd = lax.axis_index("shard")
        self.dims = dims
        self.partner, self.delta, self.pos = {}, {}, 0
        for n, d in enumerate(dims):
            weight = 1 << (len(dims) - 1 - n)
            if d == "x":
                bit = sec
                self.partner[d] = (1 - sec, shd)
            else:
                bit = lax.rem(shd // d, 2)
                self.partner[d] = (sec, shd + d * (1 - 2 * bit))
            self.pos = self.pos + bit * weight
            self.delta[d] = weight * (1 - 2 * bit)

    def at(self, order, offset):
        place = self.pos
        for j, d in enumerate(order):
            if offset >> j & 1:
                place = place + self.delta[d]
        return place

    def barrier(self, more=()):
        sem = pltpu.get_barrier_semaphore()
        partners = [self.partner[d] for d in self.dims] + list(more)
        for partner in partners:
            pl.semaphore_signal(sem, inc=1, device_id=partner, device_id_type=MESH)
        pl.semaphore_wait(sem, len(partners))


def cube_parts(rows, widths, col0=0):
    orders = (("x", 4, 2, 1), (4, 2, "x", 1), (2, "x", 4, 1))
    parts = []
    for width, order in zip(widths, orders):
        parts.append((0, rows, col0, width, order))
        col0 += width
    return tuple(parts)


class Gather:
    def __init__(self, h, parts, src, dst, send_sem, recv_sem):
        self.h, self.parts, self.src, self.dst = h, parts, src, dst
        self.send_sem, self.recv_sem = send_sem, recv_sem

    def copy(self, p, offset, j):
        r0, rn, c0, cn, order = self.parts[p]
        rows, cols = pl.ds(r0, rn), pl.ds(c0, cn)
        there = self.dst.at[self.h.at(order, offset), rows, cols]
        here = self.src.at[rows, cols] if offset == 0 else there
        n = offset | 1 << j
        return pltpu.make_async_remote_copy(
            src_ref=here,
            dst_ref=there,
            send_sem=self.send_sem.at[p, n],
            recv_sem=self.recv_sem.at[p, n],
            device_id=self.h.partner[order[j]],
            device_id_type=MESH,
        )

    def start(self, chosen):
        for j in range(len(self.h.dims)):
            for p in chosen:
                self.copy(p, 0, j).start()

    def forward(self, chosen):
        k = len(self.h.dims)
        for j in range(k):
            for low in range(1 << j):
                for p in chosen:
                    self.copy(p, low, j).wait_recv()
                    for later in range(j + 1, k):
                        self.copy(p, low | 1 << j, later).start()

    def finish(self):
        for p in range(len(self.parts)):
            for j in range(len(self.h.dims)):
                for low in range(1 << j):
                    self.copy(p, low, j).wait_send()


def gather_kernel(dims, parts, x_ref, o_ref, send_sem, recv_sem, local_sem):
    h = Hyper(dims)
    h.barrier()
    own = pltpu.make_async_copy(x_ref, o_ref.at[h.pos], local_sem)
    own.start()
    g = Gather(h, parts, x_ref, o_ref, send_sem, recv_sem)
    chosen = range(len(parts))
    g.start(chosen)
    g.forward(chosen)
    g.finish()
    own.wait()


def gather(x, dims, parts, collective_id, name):
    n = 1 << len(dims)
    return pl.pallas_call(
        functools.partial(gather_kernel, dims, parts),
        out_shape=jax.ShapeDtypeStruct((n,) + x.shape, x.dtype),
        in_specs=[pl.BlockSpec(memory_space=pl.ANY)],
        out_specs=pl.BlockSpec(memory_space=pl.ANY),
        scratch_shapes=[
            pltpu.SemaphoreType.DMA((len(parts), n)),
            pltpu.SemaphoreType.DMA((len(parts), n)),
            pltpu.SemaphoreType.DMA,
        ],
        compiler_params=pltpu.CompilerParams(
            collective_id=collective_id, has_side_effects=True, vmem_limit_bytes=LIMIT
        ),
        name=name,
    )(x)


def gather_window_kernel(parts, x_ref, kv_ref, o_ref, okv_ref, far, *sems):
    send_sem, recv_sem, kv_send, kv_recv, own_sem, swap_send, swap_recv = sems
    h = Hyper(CUBE)
    sec, shd = lax.axis_index("section"), lax.axis_index("shard")
    other = (sec, shd + 8 * (1 - 2 * lax.rem(shd // 8, 2)))
    h.barrier((other,))
    swap = pltpu.make_async_remote_copy(
        src_ref=kv_ref,
        dst_ref=far,
        send_sem=swap_send,
        recv_sem=swap_recv,
        device_id=other,
        device_id_type=MESH,
    )
    swap.start()
    own = pltpu.make_async_copy(x_ref, o_ref.at[h.pos], own_sem.at[0])
    own.start()
    g = Gather(h, parts, x_ref, o_ref, send_sem, recv_sem)
    g.start(range(3))
    swap.wait_recv()
    own_kv = pltpu.make_async_copy(far, okv_ref.at[h.pos], own_sem.at[1])
    own_kv.start()
    kv_parts = tuple((0, kv_ref.shape[0], 0, kv_ref.shape[1], order) for order in (CUBE,))
    gkv = Gather(h, kv_parts, far, okv_ref, kv_send, kv_recv)
    gkv.start(range(1))
    k = len(CUBE)
    for j in range(k):
        for low in range(1 << j):
            for one, chosen in ((g, range(3)), (gkv, range(1))):
                for p in chosen:
                    one.copy(p, low, j).wait_recv()
                    for later in range(j + 1, k):
                        one.copy(p, low | 1 << j, later).start()
    g.finish()
    gkv.finish()
    swap.wait_send()
    own.wait()
    own_kv.wait()


def gather_window(x, kv, collective_id):
    parts = cube_parts(x.shape[0], (768, 640, 640))
    n = 16
    return pl.pallas_call(
        functools.partial(gather_window_kernel, parts),
        out_shape=(
            jax.ShapeDtypeStruct((n,) + x.shape, x.dtype),
            jax.ShapeDtypeStruct((n,) + kv.shape, kv.dtype),
        ),
        in_specs=[pl.BlockSpec(memory_space=pl.ANY)] * 2,
        out_specs=[pl.BlockSpec(memory_space=pl.ANY)] * 2,
        scratch_shapes=[
            pltpu.VMEM(kv.shape, kv.dtype),
            pltpu.SemaphoreType.DMA((3, n)),
            pltpu.SemaphoreType.DMA((3, n)),
            pltpu.SemaphoreType.DMA((1, n)),
            pltpu.SemaphoreType.DMA((1, n)),
            pltpu.SemaphoreType.DMA((2,)),
            pltpu.SemaphoreType.DMA,
            pltpu.SemaphoreType.DMA,
        ],
        compiler_params=pltpu.CompilerParams(
            collective_id=collective_id, has_side_effects=True, vmem_limit_bytes=LIMIT
        ),
        name="gather_window",
    )(x, kv)


def reduce_kernel(dims, parts, swap_cols, x_ref, o_ref, *scratch):
    if swap_cols:
        buf, send_sem, recv_sem, swapped, swap_send, swap_recv = scratch
    else:
        buf, send_sem, recv_sem = scratch
    h = Hyper(dims)
    k = len(dims)
    sec, shd = lax.axis_index("section"), lax.axis_index("shard")
    other = (sec, shd + 8 * (1 - 2 * lax.rem(shd // 8, 2)))
    h.barrier((other,) if swap_cols else ())

    def window(p):
        r0, rn, c0, cn, order = parts[p]
        return pl.ds(r0, rn), pl.ds(c0, cn)

    def held(p, j, offset):
        if j == k - 1:
            return x_ref.at[(h.at(parts[p][4], offset),) + window(p)]
        return buf.at[((1 << (j + 1)) | offset,) + window(p)]

    def copy(p, j, low):
        n = (1 << j) | low
        return pltpu.make_async_remote_copy(
            src_ref=held(p, j, low | 1 << j),
            dst_ref=buf.at[(n,) + window(p)],
            send_sem=send_sem.at[p, n],
            recv_sem=recv_sem.at[p, n],
            device_id=h.partner[parts[p][4][j]],
            device_id_type=MESH,
        )

    for low in reversed(range(1 << (k - 1))):
        for p in range(len(parts)):
            copy(p, k - 1, low).start()
    step = 16
    for j in reversed(range(k)):
        for low in reversed(range(1 << j)):
            for p in range(len(parts)):
                r0, rn, c0, cn, order = parts[p]
                copy(p, j, low).wait_recv()
                mine = held(p, j, low)
                came = buf.at[((1 << j) | low,) + window(p)]

                @pl.loop(0, rn // step)
                def _(i):
                    rows = pl.ds(pl.multiple_of(i * step, step), step)
                    total = mine[rows, :].astype(jnp.float32) + came[rows, :].astype(jnp.float32)
                    if j > 0:
                        came[rows, :] = total.astype(came.dtype)
                    else:
                        out_rows = pl.ds(pl.multiple_of(r0 + i * step, step), step)
                        o_ref[out_rows, pl.ds(c0, cn)] = total

                if j > 0 and low >> (j - 1) & 1:
                    copy(p, j - 1, low ^ (1 << (j - 1))).start()
    if swap_cols:
        c0, cn = swap_cols
        rows = x_ref.shape[1]
        swapped[0] = o_ref[:, c0 : c0 + cn].astype(swapped.dtype)
        swap = pltpu.make_async_remote_copy(
            src_ref=swapped.at[0],
            dst_ref=swapped.at[1],
            send_sem=swap_send,
            recv_sem=swap_recv,
            device_id=other,
            device_id_type=MESH,
        )
        swap.start()
        swap.wait()
        o_ref[:, c0 : c0 + cn] = swapped[1].astype(jnp.float32)
    for p in range(len(parts)):
        for j in range(k):
            for low in range(1 << j):
                copy(p, j, low).wait_send()


def reduce(x, dims, parts, collective_id, name, swap_cols=None):
    n = 1 << len(dims)
    block = x.shape[1:]
    scratch = [
        pltpu.VMEM((n,) + block, x.dtype),
        pltpu.SemaphoreType.DMA((len(parts), n)),
        pltpu.SemaphoreType.DMA((len(parts), n)),
    ]
    if swap_cols:
        scratch += [
            pltpu.VMEM((2, block[0], swap_cols[1]), x.dtype),
            pltpu.SemaphoreType.DMA,
            pltpu.SemaphoreType.DMA,
        ]
    return pl.pallas_call(
        functools.partial(reduce_kernel, dims, parts, swap_cols),
        out_shape=jax.ShapeDtypeStruct(block, jnp.float32),
        in_specs=[pl.BlockSpec(memory_space=pltpu.VMEM)],
        out_specs=pl.BlockSpec(memory_space=pltpu.VMEM),
        scratch_shapes=scratch,
        compiler_params=pltpu.CompilerParams(
            collective_id=collective_id, has_side_effects=True, vmem_limit_bytes=LIMIT
        ),
        name=name,
    )(x)


def block_of(sec, shd):
    return 8 * lax.rem(sec + lax.rem(shd, 2), 2) + lax.rem(shd, 8)


def everyone_barrier(me):
    sem = pltpu.get_barrier_semaphore()

    @pl.loop(1, 32)
    def _(d):
        there = lax.rem(me + d, 32)
        pl.semaphore_signal(
            sem, inc=1, device_id=(there // 16, lax.rem(there, 16)), device_id_type=MESH
        )

    pl.semaphore_wait(sem, 31)


def fetch_kernel(mix, exp, out, con, wq, we, wo, wc, *sems):
    q_send, q_recv, e_send, e_recv, row_send, row_recv, own_sem = sems
    sec, shd = lax.axis_index("section"), lax.axis_index("shard")
    me = sec * 16 + shd
    everyone_barrier(me)
    f = block_of(sec, shd)

    def column_copies(d):
        there = lax.rem(me + d, 32)
        ts, tj = there // 16, lax.rem(there, 16)
        tf = block_of(ts, tj)
        result = []
        for src, dst, send, recv, wide in ((mix, wq, q_send, q_recv, HD), (exp, we, e_send, e_recv, 512)):
            result.append(
                pltpu.make_async_remote_copy(
                    src_ref=src.at[:, pl.ds(pl.multiple_of(tf * wide, wide), wide)],
                    dst_ref=dst.at[sec, shd],
                    send_sem=send.at[d],
                    recv_sem=recv.at[d],
                    device_id=(ts, tj),
                    device_id_type=MESH,
                )
            )
        return result

    own = [
        pltpu.make_async_copy(
            mix.at[:, pl.ds(pl.multiple_of(f * HD, HD), HD)], wq.at[sec, shd], own_sem.at[0]
        ),
        pltpu.make_async_copy(
            exp.at[:, pl.ds(pl.multiple_of(f * 512, 512), 512)], we.at[sec, shd], own_sem.at[1]
        ),
    ]
    for one in own:
        one.start()

    @pl.loop(1, 32)
    def _(d):
        for one in column_copies(d):
            one.start()

    low = lax.rem(shd, 8)
    half = shd // 8
    to_x = lax.rem(half + lax.rem(shd, 2), 2)
    from_half = lax.rem(sec + lax.rem(shd, 2), 2)

    def row_copies(z):
        return [
            pltpu.make_async_remote_copy(
                src_ref=src,
                dst_ref=dst.at[sec],
                send_sem=row_send.at[n, z],
                recv_sem=row_recv.at[n, sec],
                device_id=(to_x, 8 * z + low),
                device_id_type=MESH,
            )
            for n, (src, dst) in enumerate(((out, wo), (con, wc)))
        ]

    def arrivals(s):
        return [
            pltpu.make_async_remote_copy(
                src_ref=src,
                dst_ref=dst.at[s],
                send_sem=row_send.at[n, 0],
                recv_sem=row_recv.at[n, s],
                device_id=(to_x, low),
                device_id_type=MESH,
            )
            for n, (src, dst) in enumerate(((out, wo), (con, wc)))
        ]

    def own_rows():
        return [
            pltpu.make_async_copy(src, dst.at[sec], own_sem.at[2 + n])
            for n, (src, dst) in enumerate(((out, wo), (con, wc)))
        ]

    for z in range(2):
        mine = jnp.logical_and(to_x == sec, half == z)

        @pl.when(mine)
        def _():
            for one in own_rows():
                one.start()

        @pl.when(jnp.logical_not(mine))
        def _():
            for one in row_copies(z):
                one.start()

    @pl.loop(1, 32)
    def _(d):
        for one in column_copies(d):
            one.wait_recv()

    for s in range(2):
        mine = jnp.logical_and(sec == s, from_half == half)

        @pl.when(jnp.logical_not(mine))
        def _():
            for one in arrivals(s):
                one.wait_recv()

    @pl.loop(1, 32)
    def _(d):
        for one in column_copies(d):
            one.wait_send()

    for z in range(2):
        mine = jnp.logical_and(to_x == sec, half == z)

        @pl.when(mine)
        def _():
            for one in own_rows():
                one.wait()

        @pl.when(jnp.logical_not(mine))
        def _():
            for one in row_copies(z):
                one.wait_send()

    for one in own:
        one.wait()


def fetch_weights(mix, exp, out, con):
    bf16 = jnp.bfloat16
    dma = pltpu.SemaphoreType.DMA
    return pl.pallas_call(
        fetch_kernel,
        out_shape=(
            jax.ShapeDtypeStruct((2, 16, 128, HD), bf16),
            jax.ShapeDtypeStruct((2, 16, 128, 512), bf16),
            jax.ShapeDtypeStruct((2, 128, D), bf16),
            jax.ShapeDtypeStruct((2, 512, D), bf16),
        ),
        in_specs=[pl.BlockSpec(memory_space=pl.ANY)] * 4,
        out_specs=[pl.BlockSpec(memory_space=pl.ANY)] * 4,
        scratch_shapes=[dma((32,)), dma((32,)), dma((32,)), dma((32,)), dma((2, 2)), dma((2, 2)), dma((4,))],
        compiler_params=pltpu.CompilerParams(
            collective_id=1, has_side_effects=True, vmem_limit_bytes=LIMIT
        ),
        name="fetch_weights",
    )(mix, exp, out, con)


def return_kernel(gq, ge, go, gc, rq, re, ro, rc, *sems):
    q_send, q_recv, e_send, e_recv, row_send, row_recv, own_sem = sems
    sec, shd = lax.axis_index("section"), lax.axis_index("shard")
    me = sec * 16 + shd
    everyone_barrier(me)
    f = block_of(sec, shd)
    low = lax.rem(shd, 8)
    half = shd // 8

    def column_copies(d):
        there = lax.rem(me + d, 32)
        ts, tj = there // 16, lax.rem(there, 16)
        result = []
        for src, dst, send, recv, wide in ((gq, rq, q_send, q_recv, HD), (ge, re, e_send, e_recv, 512)):
            result.append(
                pltpu.make_async_remote_copy(
                    src_ref=src.at[ts, tj],
                    dst_ref=dst.at[half, :, pl.ds(pl.multiple_of(f * wide, wide), wide)],
                    send_sem=send.at[d],
                    recv_sem=recv.at[d],
                    device_id=(ts, tj),
                    device_id_type=MESH,
                )
            )
        return result

    own = [
        pltpu.make_async_copy(
            gq.at[sec, shd], rq.at[half, :, pl.ds(pl.multiple_of(f * HD, HD), HD)], own_sem.at[0]
        ),
        pltpu.make_async_copy(
            ge.at[sec, shd], re.at[half, :, pl.ds(pl.multiple_of(f * 512, 512), 512)], own_sem.at[1]
        ),
    ]
    for one in own:
        one.start()

    def row_copies(s):
        return [
            pltpu.make_async_remote_copy(
                src_ref=src.at[s],
                dst_ref=dst.at[half],
                send_sem=row_send.at[n, s],
                recv_sem=row_recv.at[n, half],
                device_id=(s, f),
                device_id_type=MESH,
            )
            for n, (src, dst) in enumerate(((go, ro), (gc, rc)))
        ]

    def arrivals(z):
        return [
            pltpu.make_async_remote_copy(
                src_ref=src.at[0],
                dst_ref=dst.at[z],
                send_sem=row_send.at[n, 0],
                recv_sem=row_recv.at[n, z],
                device_id=(sec, f),
                device_id_type=MESH,
            )
            for n, (src, dst) in enumerate(((go, ro), (gc, rc)))
        ]

    def own_rows():
        return [
            pltpu.make_async_copy(src.at[sec], dst.at[half], own_sem.at[2 + n])
            for n, (src, dst) in enumerate(((go, ro), (gc, rc)))
        ]

    for s in range(2):
        mine = jnp.logical_and(sec == s, f == shd)

        @pl.when(mine)
        def _():
            for one in own_rows():
                one.start()

        @pl.when(jnp.logical_not(mine))
        def _():
            for one in row_copies(s):
                one.start()

    @pl.loop(1, 32)
    def _(d):
        for one in column_copies(d):
            one.start()

    @pl.loop(1, 32)
    def _(d):
        for one in column_copies(d):
            one.wait_recv()

    for z in range(2):
        mine = jnp.logical_and(f == shd, half == z)

        @pl.when(jnp.logical_not(mine))
        def _():
            for one in arrivals(z):
                one.wait_recv()

    @pl.loop(1, 32)
    def _(d):
        for one in column_copies(d):
            one.wait_send()

    for s in range(2):
        mine = jnp.logical_and(sec == s, f == shd)

        @pl.when(mine)
        def _():
            for one in own_rows():
                one.wait()

        @pl.when(jnp.logical_not(mine))
        def _():
            for one in row_copies(s):
                one.wait_send()

    for one in own:
        one.wait()


def return_grads(gq, ge, go, gc):
    bf16 = jnp.bfloat16
    dma = pltpu.SemaphoreType.DMA
    return pl.pallas_call(
        return_kernel,
        out_shape=(
            jax.ShapeDtypeStruct((2, 128, D), bf16),
            jax.ShapeDtypeStruct((2, 128, 8192), bf16),
            jax.ShapeDtypeStruct((2, 128, D), bf16),
            jax.ShapeDtypeStruct((2, 512, D), bf16),
        ),
        in_specs=[pl.BlockSpec(memory_space=pl.ANY)] * 4,
        out_specs=[pl.BlockSpec(memory_space=pl.ANY)] * 4,
        scratch_shapes=[dma((32,)), dma((32,)), dma((32,)), dma((32,)), dma((2, 2)), dma((2, 2)), dma((4,))],
        compiler_params=pltpu.CompilerParams(
            collective_id=2, has_side_effects=True, vmem_limit_bytes=LIMIT
        ),
        name="return_grads",
    )(gq, ge, go, gc)


QB = 256
KB = WINDOW + QB
SCALE = HD ** (-0.5)
NT = (((1,), (1,)), ((), ()))
TN = (((0,), (0,)), ((), ()))


def kept_pairs(lo_ref, a):
    key = a + lax.broadcasted_iota(jnp.int32, (KB, QB), 0)
    last = a + WINDOW + lax.broadcasted_iota(jnp.int32, (KB, QB), 1)
    return (key >= lo_ref[0]) & (key <= last)


def attend_kernel(lo_ref, q_ref, k_ref, v_ref, o_ref, lse_ref):
    a = pl.multiple_of(lax.rem(pl.program_id(0), 4) * QB, QB)
    keys = pl.ds(a, KB)
    s = lax.dot_general(k_ref[0, keys], q_ref[0], NT, preferred_element_type=jnp.float32) * SCALE
    s = jnp.where(kept_pairs(lo_ref, a), s, -1e30)
    top = jnp.max(s, axis=0, keepdims=True)
    e = jnp.exp(s - top)
    total = jnp.sum(e, axis=0, keepdims=True)
    probs = (e * (1.0 / total)).astype(jnp.bfloat16)
    o_ref[0] = lax.dot_general(probs, v_ref[0, keys], TN, preferred_element_type=jnp.float32).astype(
        o_ref.dtype
    )
    lse_ref[0] = top + jnp.log(total)


def attend(lo, q, k, v):
    per_q = pl.BlockSpec((1, QB, HD), lambda n: (n, 0, 0))
    per_row = pl.BlockSpec((1, 1, QB), lambda n: (n, 0, 0))
    per_micro = pl.BlockSpec((1, 2 * WINDOW, HD), lambda n: (n // 4, 0, 0))
    return pl.pallas_call(
        attend_kernel,
        grid=(8,),
        out_shape=(
            jax.ShapeDtypeStruct((8, QB, HD), jnp.bfloat16),
            jax.ShapeDtypeStruct((8, 1, QB), jnp.float32),
        ),
        in_specs=[per_row, per_q, per_micro, per_micro],
        out_specs=[per_q, per_row],
        compiler_params=pltpu.CompilerParams(vmem_limit_bytes=LIMIT),
        name="attend",
    )(lo, q, k, v)


def attend_back_kernel(lo_ref, lse_ref, q_ref, k_ref, v_ref, g_ref, dq_ref, dk_ref, dv_ref):
    n = lax.rem(pl.program_id(0), 4)
    a = pl.multiple_of(n * QB, QB)
    keys = pl.ds(a, KB)

    @pl.when(n == 0)
    def _():
        dk_ref[...] = jnp.zeros_like(dk_ref)
        dv_ref[...] = jnp.zeros_like(dv_ref)

    q, g, k = q_ref[0], g_ref[0], k_ref[0, keys]
    s = lax.dot_general(k, q, NT, preferred_element_type=jnp.float32) * SCALE
    probs = jnp.where(kept_pairs(lo_ref, a), jnp.exp(s - lse_ref[0]), 0.0)
    gp = lax.dot_general(v_ref[0, keys], g, NT, preferred_element_type=jnp.float32)
    dot = jnp.sum(probs * gp, axis=0, keepdims=True)
    gs = (probs * (gp - dot)).astype(jnp.bfloat16)
    dq = lax.dot_general(gs, k, TN, preferred_element_type=jnp.float32) * SCALE
    dq_ref[0] = dq.astype(dq_ref.dtype)
    dk_ref[0, keys] += jnp.dot(gs, q, preferred_element_type=jnp.float32) * SCALE
    dv_ref[0, keys] += jnp.dot(probs.astype(jnp.bfloat16), g, preferred_element_type=jnp.float32)


def attend_back(lo, lse, q, k, v, g):
    per_q = pl.BlockSpec((1, QB, HD), lambda n: (n, 0, 0))
    per_row = pl.BlockSpec((1, 1, QB), lambda n: (n, 0, 0))
    per_micro = pl.BlockSpec((1, 2 * WINDOW, HD), lambda n: (n // 4, 0, 0))
    return pl.pallas_call(
        attend_back_kernel,
        grid=(8,),
        out_shape=(
            jax.ShapeDtypeStruct((8, QB, HD), jnp.bfloat16),
            jax.ShapeDtypeStruct((2, 2 * WINDOW, HD), jnp.float32),
            jax.ShapeDtypeStruct((2, 2 * WINDOW, HD), jnp.float32),
        ),
        in_specs=[per_row, per_row, per_q, per_micro, per_micro, per_q],
        out_specs=[per_q, per_micro, per_micro],
        compiler_params=pltpu.CompilerParams(vmem_limit_bytes=LIMIT),
        name="attend_back",
    )(lo, lse, q, k, v, g)


def dot32(a, b):
    return jnp.dot(a, b, preferred_element_type=jnp.float32)


def dot_nt(a, b):
    return lax.dot_general(a, b, NT, preferred_element_type=jnp.float32)


def dot_tn(a, b):
    return lax.dot_general(a, b, TN, preferred_element_type=jnp.float32)


PLAIN = cube_parts(128, (768, 640, 640))
WIDE = cube_parts(128, (896, 896, 768))
SMALL = tuple(
    (48 * n, 48, 0, 256, order)
    for n, order in enumerate(((8, "x", 4, 2, 1), (8, 4, 2, "x", 1), (8, 2, "x", 4, 1)))
)
BIAS = D + HD


def on_device_fast(
    embedded,
    cotangent,
    segments,
    first_gain,
    first_shift,
    mixer_weight,
    mixer_bias,
    output_weight,
    output_bias,
    second_gain,
    second_shift,
    expand_weight,
    expand_bias,
    contract_weight,
    contract_bias,
):
    bf16, f32 = jnp.bfloat16, jnp.float32
    sec, shd = lax.axis_index("section"), lax.axis_index("shard")
    half = shd // 8
    f = block_of(sec, shd)

    small = jnp.concatenate(
        [
            first_gain[0],
            first_shift[0],
            second_gain[0],
            second_shift[0],
            output_bias[0],
            contract_bias[0],
            expand_bias[0],
            mixer_bias[0],
        ]
    )
    small = jnp.concatenate([small, jnp.zeros((16 * 256 - small.shape[0],), bf16)]).reshape(16, 256)
    shared = gather(
        jnp.concatenate([mixer_weight[0][:, D:], small], axis=0), ALL, SMALL, 3, "gather_shared"
    ).reshape(2, 16, 144, 256)
    wkv = shared[:, :, :128].reshape(2, D, 256)
    vectors = shared[:, :, 128:].reshape(2, 16, 4096)

    def vector(n):
        return vectors[:, :, 128 * n : 128 * (n + 1)].reshape(2, D).astype(f32)

    gain_one, shift_one, gain_two, shift_two, bias_out, bias_con = [vector(n) for n in range(6)]
    bias_exp = vectors[:, :, 768:1280].reshape(2, 8192).astype(f32)
    bias_exp = lax.dynamic_slice_in_dim(bias_exp, f * 512, 512, 1)
    bias_mix = vectors[:, :, 1280 : 1280 + 136].reshape(2, BIAS).astype(f32)
    bias_q = lax.dynamic_slice_in_dim(bias_mix, f * HD, HD, 1)
    bias_kv = jnp.concatenate([jnp.zeros((2, HD), f32), bias_mix[:, D:]], axis=1)

    wq, we, wo, wc = fetch_weights(
        mixer_weight[0][:, :D], expand_weight[0], output_weight[0], contract_weight[0]
    )
    wq = wq.reshape(2, D, HD)
    we = we.reshape(2, D, 512)

    starts = jnp.sum(
        (segments[:, None, :] < lax.dynamic_slice_in_dim(segments, half * WINDOW, WINDOW, 1)[:, :, None]),
        axis=2,
        dtype=jnp.int32,
    )
    lo = jnp.maximum(jnp.arange(1, WINDOW + 1)[None], starts - half * WINDOW + WINDOW)
    lo = lo.reshape(8, 1, QB)

    hidden = lax.dynamic_index_in_dim(embedded, sec, 0, keepdims=False).astype(f32)
    results, kept = [], []
    for s in range(2):
        n1 = layer_norm(hidden, gain_one[s], shift_one[s]).astype(bf16)
        kv_rows = (dot32(n1, wkv[s]) + bias_kv[s]).astype(bf16)
        all_n1, far_kv = gather_window(n1, kv_rows, 4)
        all_n1 = all_n1.reshape(2048, D)
        q = (dot32(all_n1, wq[s]) + bias_q[s]).astype(bf16).reshape(8, QB, HD)
        kv = (dot32(all_n1, wkv[s]) + bias_kv[s]).astype(bf16).reshape(2, WINDOW, 256)
        kv = jnp.concatenate([far_kv.reshape(2, WINDOW, 256), kv], axis=1)
        k, v = kv[:, :, :HD], kv[:, :, HD:]
        mixed, lse = attend(lo, q, k, v)
        mixed = mixed.reshape(2048, HD)
        part = dot32(mixed, wo[s]).astype(bf16).reshape(16, 128, D)
        middle = hidden + reduce(part, CUBE, PLAIN, 5, "reduce_rows") + bias_out[s]
        n2 = layer_norm(middle, gain_two[s], shift_two[s]).astype(bf16)
        all_n2 = gather(n2, CUBE, PLAIN, 6, "gather_rows").reshape(2048, D)
        pre = dot32(all_n2, we[s]) + bias_exp[s]
        act = gelu_tanh(pre).astype(bf16)
        part = dot32(act, wc[s]).astype(bf16).reshape(16, 128, D)
        result = middle + reduce(part, CUBE, PLAIN, 5, "reduce_rows") + bias_con[s]
        results.append(result.astype(bf16))
        kept.append((hidden, n1, all_n1, q, k, v, lse, mixed, middle, all_n2, pre, act))
        hidden = results[-1].astype(f32)

    grad = lax.dynamic_index_in_dim(cotangent, sec, 0, keepdims=False).astype(f32)
    input_grads = [None, None]
    weight_grads = [None, None]
    small_grads = [None, None]
    for s in (1, 0):
        hidden, n1, all_n1, q, k, v, lse, mixed, middle, all_n2, pre, act = kept[s]
        go = grad.astype(bf16)
        all_go = gather(go, CUBE, PLAIN, 6, "gather_rows").reshape(2048, D)
        _, gelu_back = jax.vjp(gelu_tanh, pre)
        g_pre = gelu_back(dot_nt(all_go, wc[s]))[0].astype(bf16)
        part = dot_nt(g_pre, we[s]).astype(bf16).reshape(16, 128, D)
        g_n2 = reduce(part, CUBE, PLAIN, 5, "reduce_rows")
        d_wc = dot_tn(act, all_go).astype(bf16)
        d_we = dot_tn(all_n2, g_pre).astype(bf16)
        d_be = jnp.sum(g_pre.astype(f32), axis=0)
        _, back = jax.vjp(layer_norm, middle, gain_two[s], shift_two[s])
        g_mid, d_gain_two, d_shift_two = back(g_n2)
        g_mid = grad + g_mid
        ga = g_mid.astype(bf16)
        all_ga = gather(ga, CUBE, PLAIN, 6, "gather_rows").reshape(2048, D)
        g_mixed = dot_nt(all_ga, wo[s]).astype(bf16).reshape(8, QB, HD)
        d_wo = dot_tn(mixed, all_ga).astype(bf16)
        dq, dk, dv = attend_back(lo, lse, q, k, v, g_mixed)
        dq = dq.reshape(2048, HD)
        d_kv = jnp.concatenate([dk, dv], axis=2).astype(bf16)
        part = jnp.concatenate(
            [
                dot_nt(dq, wq[s]).astype(bf16).reshape(16, 128, D),
                d_kv[:, WINDOW:].reshape(16, 128, 256),
                d_kv[:, :WINDOW].reshape(16, 128, 256),
            ],
            axis=2,
        )
        rows = reduce(part, CUBE, WIDE, 7, "reduce_window", (D + 256, 256))
        dkv_rows = (rows[:, D : D + 256] + jnp.where(half == 0, rows[:, D + 256 :], 0.0)).astype(bf16)
        g_n1 = rows[:, :D] + dot_nt(dkv_rows, wkv[s])
        _, back = jax.vjp(layer_norm, hidden, gain_one[s], shift_one[s])
        g_in, d_gain_one, d_shift_one = back(g_n1)
        g_in = g_mid + g_in
        input_grads[s] = g_in
        d_wq = dot_tn(all_n1, dq).astype(bf16)
        d_wkv = dot_tn(n1, dkv_rows)
        d_bq = jnp.sum(dq.astype(f32), axis=0)
        d_bv = jnp.sum(dkv_rows[:, HD:].astype(f32), axis=0)
        weight_grads[s] = (d_wq.reshape(16, 128, HD), d_we.reshape(16, 128, 512), d_wo, d_wc)
        spread = [
            d_gain_one,
            d_shift_one,
            d_gain_two,
            d_shift_two,
            jnp.sum(ga.astype(f32), axis=0),
            jnp.sum(go.astype(f32), axis=0),
        ]
        d_be = lax.dynamic_update_slice_in_dim(jnp.zeros((8192,), f32), d_be, f * 512, 0)
        d_bm = lax.dynamic_update_slice_in_dim(jnp.zeros((D,), f32), d_bq, f * HD, 0)
        vec = jnp.concatenate(
            [one.reshape(16, 128) for one in spread]
            + [d_be.reshape(16, 512), jnp.concatenate([d_bm, d_bv]).reshape(16, 136)],
            axis=1,
        )
        vec = jnp.pad(vec, ((0, 0), (0, 4096 - vec.shape[1]))).reshape(16, 16, 256)
        small_grads[s] = jnp.concatenate([d_wkv.reshape(16, 128, 256), vec], axis=1)
        grad = g_in.astype(bf16).astype(f32)

    mine = reduce(
        jnp.concatenate(small_grads, axis=0).astype(bf16), ALL, SMALL, 8, "reduce_shared"
    )
    vec = mine[128:].reshape(4096)
    rq, re, ro, rc = return_grads(
        *[jnp.stack([weight_grads[0][n], weight_grads[1][n]]) for n in range(4)]
    )

    def both(r):
        return r[0].astype(f32) + r[1].astype(f32)

    def swap(pair):
        theirs = jnp.where(sec == 0, pair[1].astype(bf16), pair[0].astype(bf16))
        own = jnp.where(sec == 0, pair[0], pair[1])
        came = lax.ppermute(theirs, "section", [(0, 1), (1, 0)]).astype(own.dtype)
        first = jnp.where(sec == 0, own, came)
        second = jnp.where(sec == 0, came, own)
        return jnp.stack([first, second])[None]

    return (
        swap(results),
        swap(input_grads),
        vec[0:128][None],
        vec[128:256][None],
        jnp.concatenate([both(rq), mine[:128]], axis=1)[None],
        vec[1280 : 1280 + 136][None],
        both(ro)[None],
        vec[512:640][None],
        vec[256:384][None],
        vec[384:512][None],
        both(re)[None],
        vec[768:1280][None],
        both(rc)[None],
        vec[640:768][None],
    )


def solution(mesh):
    in_specs = (
        P(None, "shard", None),
        P(None, "shard", None),
        P(),
        P("section", "shard"),
        P("section", "shard"),
        P("section", "shard", None),
        P("section", "shard"),
        P("section", "shard", None),
        P("section", "shard"),
        P("section", "shard"),
        P("section", "shard"),
        P("section", "shard", None),
        P("section", "shard"),
        P("section", "shard", None),
        P("section", "shard"),
    )
    out_specs = (
        P("section", None, "shard", None),
        P("section", None, "shard", None),
        P("section", "shard"),
        P("section", "shard"),
        P("section", "shard", None),
        P("section", "shard"),
        P("section", "shard", None),
        P("section", "shard"),
        P("section", "shard"),
        P("section", "shard"),
        P("section", "shard", None),
        P("section", "shard"),
        P("section", "shard", None),
        P("section", "shard"),
    )
    fits = mesh.shape["section"] == 2 and mesh.shape["shard"] == HEADS
    on_device = on_device_fast if fits else on_device_general
    return jax.shard_map(
        on_device, mesh=mesh, in_specs=in_specs, out_specs=out_specs, check_vma=False
    )
```

```python
import functools

import jax
import jax.numpy as jnp
from jax import lax
from jax.experimental import pallas as pl
from jax.experimental.pallas import tpu as pltpu
from jax.sharding import PartitionSpec as P

D = 2048
HEADS = 16
HD = 128
WINDOW = 1024


epsilon = 1e-05


def passed_along(block, axis, distance):
    devices = range(lax.axis_size(axis))
    route = [(i - distance, i) for i in devices if i - distance in devices]
    return lax.ppermute(block, axis, route)


def layer_norm(values, gain_row, shift_row):
    center = values - jnp.mean(values, axis=-1, keepdims=True)
    spread = jnp.mean(center * center, axis=-1, keepdims=True)
    return center * lax.rsqrt(spread + epsilon) * gain_row + shift_row


def gelu_tanh(values):
    return jax.nn.gelu(values, approximate=True)


def window_mask(segments, micro_index, device, row_count, reach_blocks):
    seg_row = lax.dynamic_index_in_dim(segments, micro_index, 0, keepdims=False)
    padded = jnp.concatenate([jnp.full((reach_blocks * row_count,), -1, jnp.int32), seg_row])
    key_segments = lax.dynamic_slice_in_dim(
        padded, device * row_count, (reach_blocks + 1) * row_count
    )
    query_segments = lax.dynamic_slice_in_dim(seg_row, device * row_count, row_count)
    distance = (
        jnp.arange(row_count)[:, None]
        + reach_blocks * row_count
        - jnp.arange((reach_blocks + 1) * row_count)[None, :]
    )
    return (
        (distance >= 0) & (distance < WINDOW) & (query_segments[:, None] == key_segments[None, :])
    )


def fetch_window(key_value, reach_blocks):
    earlier = [passed_along(key_value, "shard", offset) for offset in range(reach_blocks, 0, -1)]
    return jnp.concatenate(earlier + [key_value], axis=0)


def return_window(window_grad, reach_blocks, row_count):
    own_rows = window_grad[reach_blocks * row_count :]
    for offset in range(1, reach_blocks + 1):
        start_row = (reach_blocks - offset) * row_count
        own_rows = own_rows + passed_along(
            window_grad[start_row : start_row + row_count].astype(jnp.bfloat16), "shard", -offset
        ).astype(jnp.float32)
    return own_rows


def forward_layer(hidden, weights, key_mask, reach_blocks):
    (
        first_gain,
        first_shift,
        mixer_weight,
        mixer_bias,
        output_weight,
        output_bias,
        second_gain,
        second_shift,
        expand_weight,
        expand_bias,
        contract_weight,
        contract_bias,
    ) = weights
    row_count = hidden.shape[0]
    score_scale = HD ** (-0.5)
    normed_one = layer_norm(
        hidden, first_gain.astype(jnp.float32), first_shift.astype(jnp.float32)
    ).astype(jnp.bfloat16)
    full_bias = jnp.concatenate(
        [mixer_bias[:D], jnp.zeros((HD,), mixer_bias.dtype), mixer_bias[D:]]
    ).astype(jnp.float32)
    projected = (
        jnp.dot(normed_one, mixer_weight, preferred_element_type=jnp.float32) + full_bias
    ).astype(jnp.bfloat16)
    queries = projected[:, :D].reshape(row_count, HEADS, HD)
    window_pairs = fetch_window(projected[:, D:], reach_blocks)
    scores = (
        jnp.einsum("thd,kd->htk", queries, window_pairs[:, :HD], preferred_element_type=jnp.float32)
        * score_scale
    )
    masked = jnp.where(key_mask[None], scores, -1e30)
    top_score = jnp.max(masked, axis=2, keepdims=True)
    exponent = jnp.exp(masked - top_score)
    totals = jnp.sum(exponent, axis=2, keepdims=True)
    prob_low = (exponent / totals).astype(jnp.bfloat16)
    log_total = top_score + jnp.log(totals)
    mixed_rows = (
        jnp.einsum(
            "htk,kd->thd", prob_low, window_pairs[:, HD:], preferred_element_type=jnp.float32
        )
        .reshape(row_count, D)
        .astype(jnp.bfloat16)
    )
    middle = (
        hidden
        + jnp.dot(mixed_rows, output_weight, preferred_element_type=jnp.float32)
        + output_bias.astype(jnp.float32)
    )
    normed_two = layer_norm(
        middle, second_gain.astype(jnp.float32), second_shift.astype(jnp.float32)
    ).astype(jnp.bfloat16)
    pre_gelu = jnp.dot(
        normed_two, expand_weight, preferred_element_type=jnp.float32
    ) + expand_bias.astype(jnp.float32)
    activated = gelu_tanh(pre_gelu).astype(jnp.bfloat16)
    result = (
        middle
        + jnp.dot(activated, contract_weight, preferred_element_type=jnp.float32)
        + contract_bias.astype(jnp.float32)
    )
    return (
        result,
        (
            hidden,
            normed_one,
            projected,
            window_pairs,
            log_total,
            mixed_rows,
            middle,
            normed_two,
            pre_gelu,
            activated,
        ),
    )


def backward_layer(grad_result, weights, saved_state, key_mask, reach_blocks):
    (
        first_gain,
        first_shift,
        mixer_weight,
        mixer_bias,
        output_weight,
        output_bias,
        second_gain,
        second_shift,
        expand_weight,
        expand_bias,
        contract_weight,
        contract_bias,
    ) = weights
    (
        hidden,
        normed_one,
        projected,
        window_pairs,
        log_total,
        mixed_rows,
        middle,
        normed_two,
        pre_gelu,
        activated,
    ) = saved_state
    row_count = hidden.shape[0]
    score_scale = HD ** (-0.5)
    grad_out_low = grad_result.astype(jnp.bfloat16)
    grad_act = jnp.einsum(
        "rd,fd->rf", grad_out_low, contract_weight, preferred_element_type=jnp.float32
    )
    gelu_value, gelu_back = jax.vjp(gelu_tanh, pre_gelu)
    grad_pre = gelu_back(grad_act)[0].astype(jnp.bfloat16)
    grad_normed_two = jnp.einsum(
        "rf,df->rd", grad_pre, expand_weight, preferred_element_type=jnp.float32
    )
    norm_value_two, norm_back_two = jax.vjp(
        layer_norm, middle, second_gain.astype(jnp.float32), second_shift.astype(jnp.float32)
    )
    grad_middle_part, grad_gain_two, grad_shift_two = norm_back_two(grad_normed_two)
    grad_middle = grad_result + grad_middle_part
    grad_attended = grad_middle.astype(jnp.bfloat16)
    grad_mixed = (
        jnp.einsum("re,de->rd", grad_attended, output_weight, preferred_element_type=jnp.float32)
        .astype(jnp.bfloat16)
        .reshape(row_count, HEADS, HD)
    )
    queries = projected[:, :D].reshape(row_count, HEADS, HD)
    key_part = window_pairs[:, :HD]
    value_part = window_pairs[:, HD:]
    scores = (
        jnp.einsum("thd,kd->htk", queries, key_part, preferred_element_type=jnp.float32)
        * score_scale
    )
    prob_full = jnp.where(key_mask[None], jnp.exp(scores - log_total), 0.0)
    prob_low = prob_full.astype(jnp.bfloat16)
    grad_probs = jnp.einsum(
        "thd,kd->htk", grad_mixed, value_part, preferred_element_type=jnp.float32
    )
    row_dot = jnp.sum(prob_full * grad_probs, axis=2, keepdims=True)
    grad_scores = (prob_full * (grad_probs - row_dot)).astype(jnp.bfloat16)
    grad_queries = (
        jnp.einsum("htk,kd->thd", grad_scores, key_part, preferred_element_type=jnp.float32)
        * score_scale
    ).reshape(row_count, D)
    grad_keys = (
        jnp.einsum("htk,thd->kd", grad_scores, queries, preferred_element_type=jnp.float32)
        * score_scale
    )
    grad_values = jnp.einsum(
        "htk,thd->kd", prob_low, grad_mixed, preferred_element_type=jnp.float32
    )
    grad_window = jnp.concatenate([grad_keys, grad_values], axis=1)
    grad_own_pairs = return_window(grad_window, reach_blocks, row_count)
    grad_projected = jnp.concatenate([grad_queries, grad_own_pairs], axis=1).astype(jnp.bfloat16)
    grad_normed_one = jnp.einsum(
        "rq,dq->rd", grad_projected, mixer_weight, preferred_element_type=jnp.float32
    )
    norm_value_one, norm_back_one = jax.vjp(
        layer_norm, hidden, first_gain.astype(jnp.float32), first_shift.astype(jnp.float32)
    )
    grad_hidden_part, grad_gain_one, grad_shift_one = norm_back_one(grad_normed_one)
    grad_hidden = grad_middle + grad_hidden_part
    return (
        grad_hidden,
        (
            grad_projected,
            grad_attended,
            grad_pre,
            grad_out_low,
            grad_gain_one,
            grad_shift_one,
            grad_gain_two,
            grad_shift_two,
            normed_one,
            mixed_rows,
            normed_two,
            activated,
        ),
    )


def flatten_rows(stacked):
    return stacked.reshape((-1, stacked.shape[-1]))


def weight_terms(row_items, norm_items):
    (
        grad_projected_rows,
        grad_attended_rows,
        grad_pre_rows,
        grad_out_rows,
        normed_one_rows,
        mixed_all,
        normed_two_rows,
        activated_rows,
    ) = row_items
    first_gain_term, first_shift_term, second_gain_term, second_shift_term = norm_items
    mixer_weight_term = jnp.einsum(
        "rd,rq->dq", normed_one_rows, grad_projected_rows, preferred_element_type=jnp.float32
    )
    column_totals = jnp.sum(grad_projected_rows.astype(jnp.float32), axis=0)
    mixer_bias_term = jnp.concatenate([column_totals[:D], column_totals[D + HD :]])
    output_weight_term = jnp.einsum(
        "rd,re->de", mixed_all, grad_attended_rows, preferred_element_type=jnp.float32
    )
    output_bias_term = jnp.sum(grad_attended_rows.astype(jnp.float32), axis=0)
    expand_weight_term = jnp.einsum(
        "rd,rf->df", normed_two_rows, grad_pre_rows, preferred_element_type=jnp.float32
    )
    expand_bias_term = jnp.sum(grad_pre_rows.astype(jnp.float32), axis=0)
    contract_weight_term = jnp.einsum(
        "rf,rd->fd", activated_rows, grad_out_rows, preferred_element_type=jnp.float32
    )
    contract_bias_term = jnp.sum(grad_out_rows.astype(jnp.float32), axis=0)
    return (
        first_gain_term[None],
        first_shift_term[None],
        mixer_weight_term[None],
        mixer_bias_term[None],
        output_weight_term[None],
        output_bias_term[None],
        second_gain_term[None],
        second_shift_term[None],
        expand_weight_term[None],
        expand_bias_term[None],
        contract_weight_term[None],
        contract_bias_term[None],
    )


def on_device_general(
    embedded,
    cotangent,
    segments,
    first_gain,
    first_shift,
    mixer_weight,
    mixer_bias,
    output_weight,
    output_bias,
    second_gain,
    second_shift,
    expand_weight,
    expand_bias,
    contract_weight,
    contract_bias,
):
    section_index = lax.axis_index("section")
    device = lax.axis_index("shard")
    micro_count = embedded.shape[0]
    row_count = embedded.shape[1]
    reach_blocks = WINDOW // row_count
    own_params = (
        first_gain[0],
        first_shift[0],
        mixer_weight[0],
        mixer_bias[0],
        output_weight[0],
        output_bias[0],
        second_gain[0],
        second_shift[0],
        expand_weight[0],
        expand_bias[0],
        contract_weight[0],
        contract_bias[0],
    )
    forward_weights = (
        lax.all_gather(own_params[0], "shard", axis=0, tiled=True),
        lax.all_gather(own_params[1], "shard", axis=0, tiled=True),
        lax.all_gather(own_params[2], "shard", axis=0, tiled=True),
        lax.all_gather(own_params[3], "shard", axis=0, tiled=True),
        lax.all_gather(own_params[4], "shard", axis=0, tiled=True),
        lax.all_gather(own_params[5], "shard", axis=0, tiled=True),
        lax.all_gather(own_params[6], "shard", axis=0, tiled=True),
        lax.all_gather(own_params[7], "shard", axis=0, tiled=True),
        lax.all_gather(own_params[8], "shard", axis=0, tiled=True),
        lax.all_gather(own_params[9], "shard", axis=0, tiled=True),
        lax.all_gather(own_params[10], "shard", axis=0, tiled=True),
        lax.all_gather(own_params[11], "shard", axis=0, tiled=True),
    )
    zero_rows = jnp.zeros((row_count, D), jnp.float32)
    arrived = zero_rows
    sent_list = []
    kept_states = []
    for step_index in range(micro_count + 1):
        own_input = (
            embedded[step_index].astype(jnp.float32) if step_index < micro_count else zero_rows
        )
        hidden = jnp.where(section_index == 0, own_input, arrived)
        micro_index = jnp.clip(step_index - section_index, 0, micro_count - 1)
        key_mask = window_mask(segments, micro_index, device, row_count, reach_blocks)
        result, saved_state = forward_layer(hidden, forward_weights, key_mask, reach_blocks)
        result_low = result.astype(jnp.bfloat16)
        sent_list.append(result_low)
        kept_states.append(saved_state)
        if step_index < micro_count:
            arrived = passed_along(result_low, "section", 1).astype(jnp.float32)
    section_outputs = lax.dynamic_slice_in_dim(jnp.stack(sent_list), section_index, micro_count, 0)[
        None
    ]
    stacked_states = [
        jnp.stack([state_item[item_index] for state_item in kept_states])
        for item_index in range(10)
    ]
    valid_start = 1 - section_index
    arrived_grad = zero_rows
    grad_records = []
    hidden_grads = []
    for step_index in range(micro_count + 1):
        own_grad = (
            cotangent[step_index].astype(jnp.float32) if step_index < micro_count else zero_rows
        )
        grad_result = jnp.where(section_index == 1, own_grad, arrived_grad)
        forward_index = jnp.clip(step_index - 1 + 2 * section_index, 0, micro_count)
        micro_index = jnp.clip(step_index - 1 + section_index, 0, micro_count - 1)
        saved_state = [
            lax.dynamic_index_in_dim(stacked, forward_index, 0, keepdims=False)
            for stacked in stacked_states
        ]
        key_mask = window_mask(segments, micro_index, device, row_count, reach_blocks)
        grad_hidden, record = backward_layer(
            grad_result, forward_weights, saved_state, key_mask, reach_blocks
        )
        hidden_grads.append(grad_hidden)
        if step_index < micro_count:
            arrived_grad = passed_along(grad_hidden.astype(jnp.bfloat16), "section", -1).astype(
                jnp.float32
            )
        grad_records.append(record)
    input_grads = lax.dynamic_slice_in_dim(jnp.stack(hidden_grads), valid_start, micro_count, 0)[
        None
    ]
    chosen = [
        lax.dynamic_slice_in_dim(
            jnp.stack([record[item_index] for record in grad_records]), valid_start, micro_count, 0
        )
        for item_index in range(12)
    ]
    row_items = (
        flatten_rows(chosen[0]),
        flatten_rows(chosen[1]),
        flatten_rows(chosen[2]),
        flatten_rows(chosen[3]),
        flatten_rows(chosen[8]),
        flatten_rows(chosen[9]),
        flatten_rows(chosen[10]),
        flatten_rows(chosen[11]),
    )
    norm_items = (
        jnp.sum(chosen[4], axis=0),
        jnp.sum(chosen[5], axis=0),
        jnp.sum(chosen[6], axis=0),
        jnp.sum(chosen[7], axis=0),
    )
    all_terms = weight_terms(row_items, norm_items)
    summed = (
        lax.psum_scatter(all_terms[0], "shard", scatter_dimension=1, tiled=True),
        lax.psum_scatter(all_terms[1], "shard", scatter_dimension=1, tiled=True),
        lax.psum_scatter(all_terms[2], "shard", scatter_dimension=1, tiled=True),
        lax.psum_scatter(all_terms[3], "shard", scatter_dimension=1, tiled=True),
        lax.psum_scatter(all_terms[4], "shard", scatter_dimension=1, tiled=True),
        lax.psum_scatter(all_terms[5], "shard", scatter_dimension=1, tiled=True),
        lax.psum_scatter(all_terms[6], "shard", scatter_dimension=1, tiled=True),
        lax.psum_scatter(all_terms[7], "shard", scatter_dimension=1, tiled=True),
        lax.psum_scatter(all_terms[8], "shard", scatter_dimension=1, tiled=True),
        lax.psum_scatter(all_terms[9], "shard", scatter_dimension=1, tiled=True),
        lax.psum_scatter(all_terms[10], "shard", scatter_dimension=1, tiled=True),
        lax.psum_scatter(all_terms[11], "shard", scatter_dimension=1, tiled=True),
    )
    return (
        section_outputs,
        input_grads,
        summed[0],
        summed[1],
        summed[2],
        summed[3],
        summed[4],
        summed[5],
        summed[6],
        summed[7],
        summed[8],
        summed[9],
        summed[10],
        summed[11],
    )


MESH = pl.DeviceIdType.MESH
LIMIT = 60 << 20
CUBE = ("x", 4, 2, 1)
ALL = ("x", 8, 4, 2, 1)


def columns(n, wide):
    return pl.ds(pl.multiple_of(n * wide, wide), wide)


def remote(src, dst, send, recv, there):
    return pltpu.make_async_remote_copy(
        src_ref=src, dst_ref=dst, send_sem=send, recv_sem=recv, device_id=there, device_id_type=MESH
    )


class Hyper:
    def __init__(self, dims):
        sec = lax.axis_index("section")
        shd = lax.axis_index("shard")
        self.dims = dims
        self.partner, self.delta, self.pos = {}, {}, 0
        for n, d in enumerate(dims):
            weight = 1 << (len(dims) - 1 - n)
            if d == "x":
                bit = sec
                self.partner[d] = (1 - sec, shd)
            else:
                bit = lax.rem(shd // d, 2)
                self.partner[d] = (sec, shd + d * (1 - 2 * bit))
            self.pos = self.pos + bit * weight
            self.delta[d] = weight * (1 - 2 * bit)

    def at(self, order, offset):
        place = self.pos
        for j, d in enumerate(order):
            if offset >> j & 1:
                place = place + self.delta[d]
        return place

    def barrier(self, more=()):
        sem = pltpu.get_barrier_semaphore()
        partners = [self.partner[d] for d in self.dims] + list(more)
        for partner in partners:
            pl.semaphore_signal(sem, inc=1, device_id=partner, device_id_type=MESH)
        pl.semaphore_wait(sem, len(partners))


def cube_parts(rows, widths, col0=0):
    orders = (("x", 4, 2, 1), (4, 2, "x", 1), (2, "x", 4, 1))
    parts = []
    for width, order in zip(widths, orders):
        parts.append((0, rows, col0, width, order))
        col0 += width
    return tuple(parts)


class Gather:
    def __init__(self, h, parts, src, dst, send_sem, recv_sem):
        self.h, self.parts, self.src, self.dst = h, parts, src, dst
        self.send_sem, self.recv_sem = send_sem, recv_sem

    def copy(self, p, offset, j):
        r0, rn, c0, cn, order = self.parts[p]
        rows, cols = pl.ds(r0, rn), pl.ds(c0, cn)
        there = self.dst.at[self.h.at(order, offset), rows, cols]
        here = self.src.at[rows, cols] if offset == 0 else there
        n = offset | 1 << j
        return pltpu.make_async_remote_copy(
            src_ref=here,
            dst_ref=there,
            send_sem=self.send_sem.at[p, n],
            recv_sem=self.recv_sem.at[p, n],
            device_id=self.h.partner[order[j]],
            device_id_type=MESH,
        )

    def start(self, chosen):
        for j in range(len(self.h.dims)):
            for p in chosen:
                self.copy(p, 0, j).start()

    def forward(self, chosen):
        k = len(self.h.dims)
        for j in range(k):
            for low in range(1 << j):
                for p in chosen:
                    self.copy(p, low, j).wait_recv()
                    for later in range(j + 1, k):
                        self.copy(p, low | 1 << j, later).start()

    def finish(self):
        for p in range(len(self.parts)):
            for j in range(len(self.h.dims)):
                for low in range(1 << j):
                    self.copy(p, low, j).wait_send()


def gather_kernel(dims, parts, x_ref, o_ref, send_sem, recv_sem, local_sem):
    h = Hyper(dims)
    h.barrier()
    own = pltpu.make_async_copy(x_ref, o_ref.at[h.pos], local_sem)
    own.start()
    g = Gather(h, parts, x_ref, o_ref, send_sem, recv_sem)
    chosen = range(len(parts))
    g.start(chosen)
    g.forward(chosen)
    g.finish()
    own.wait()


def gather(x, dims, parts, collective_id, name):
    n = 1 << len(dims)
    return pl.pallas_call(
        functools.partial(gather_kernel, dims, parts),
        out_shape=jax.ShapeDtypeStruct((n,) + x.shape, x.dtype),
        in_specs=[pl.BlockSpec(memory_space=pl.ANY)],
        out_specs=pl.BlockSpec(memory_space=pl.ANY),
        scratch_shapes=[
            pltpu.SemaphoreType.DMA((len(parts), n)),
            pltpu.SemaphoreType.DMA((len(parts), n)),
            pltpu.SemaphoreType.DMA,
        ],
        compiler_params=pltpu.CompilerParams(
            collective_id=collective_id, has_side_effects=True, vmem_limit_bytes=LIMIT
        ),
        name=name,
    )(x)


def gather_window_kernel(parts, weights, *refs):
    if weights:
        x_ref, kv_ref, exp, con, o_ref, okv_ref, we, wc, far = refs[:9]
        sems = refs[9:]
        spread_sems = sems[7:]
    else:
        x_ref, kv_ref, o_ref, okv_ref, far = refs[:5]
        sems = refs[5:]
    send_sem, recv_sem, kv_send, kv_recv, own_sem, swap_send, swap_recv = sems[:7]
    h = Hyper(CUBE)
    sec, shd = lax.axis_index("section"), lax.axis_index("shard")
    low = lax.rem(shd, 8)
    other = (sec, shd + 8 * (1 - 2 * lax.rem(shd // 8, 2)))
    if weights:
        w_send, w_recv, con_send, con_recv, w_own = spread_sems

        def pieces(ts, tj):
            for n in range(2):
                yield (
                    exp.at[:, columns(2 * (8 * n + lax.rem(tj, 8)) + ts, 256)],
                    we.at[sec, low, :, pl.ds(256 * n, 256)],
                )

        spread = Spread(pieces, w_own, w_send, w_recv)
        spread.barrier()
    else:
        h.barrier((other,))
    swap = remote(kv_ref, far, swap_send, swap_recv, other)
    swap.start()
    own = pltpu.make_async_copy(x_ref, o_ref.at[h.pos], own_sem.at[0])
    own.start()
    g = Gather(h, parts, x_ref, o_ref, send_sem, recv_sem)
    g.start(range(3))
    if weights:
        spread.start()
        own_rows = pltpu.make_async_copy(con.at[pl.ds(256 * sec, 256)], wc.at[sec], w_own.at[2])
        own_rows.start()
        rows = remote(
            con.at[pl.ds(256 * (1 - sec), 256)], wc.at[sec], con_send, con_recv, (1 - sec, shd)
        )
        rows.start()
    swap.wait_recv()
    own_kv = pltpu.make_async_copy(far, okv_ref.at[h.pos], own_sem.at[1])
    own_kv.start()
    kv_parts = tuple((0, kv_ref.shape[0], 0, kv_ref.shape[1], order) for order in (CUBE,))
    gkv = Gather(h, kv_parts, far, okv_ref, kv_send, kv_recv)
    gkv.start(range(1))
    k = len(CUBE)
    for j in range(k):
        for n in range(1 << j):
            for one, chosen in ((g, range(3)), (gkv, range(1))):
                for p in chosen:
                    one.copy(p, n, j).wait_recv()
                    for later in range(j + 1, k):
                        one.copy(p, n | 1 << j, later).start()
    if weights:
        spread.wait()
        remote(
            con.at[pl.ds(0, 256)], wc.at[1 - sec], con_send, con_recv, (1 - sec, shd)
        ).wait_recv()
        rows.wait_send()
        own_rows.wait()
    g.finish()
    gkv.finish()
    swap.wait_send()
    own.wait()
    own_kv.wait()


def gather_window(x, kv, collective_id, weights=()):
    parts = cube_parts(x.shape[0], (768, 640, 640))
    n = 16
    dma = pltpu.SemaphoreType.DMA
    out = [
        jax.ShapeDtypeStruct((n,) + x.shape, x.dtype),
        jax.ShapeDtypeStruct((n,) + kv.shape, kv.dtype),
    ]
    sems = [dma((3, n)), dma((3, n)), dma((1, n)), dma((1, n)), dma((2,)), dma, dma]
    if weights:
        out += [
            jax.ShapeDtypeStruct((2, 8, 128, 512), kv.dtype),
            jax.ShapeDtypeStruct((2, 256, D), kv.dtype),
        ]
        sems += [dma((2, 16)), dma((2, 16)), dma, dma, dma((3,))]
    return pl.pallas_call(
        functools.partial(gather_window_kernel, parts, bool(weights)),
        out_shape=out,
        in_specs=[pl.BlockSpec(memory_space=pl.ANY)] * (2 + len(weights)),
        out_specs=[pl.BlockSpec(memory_space=pl.ANY)] * len(out),
        scratch_shapes=[pltpu.VMEM(kv.shape, kv.dtype)] + sems,
        compiler_params=pltpu.CompilerParams(
            collective_id=collective_id, has_side_effects=True, vmem_limit_bytes=LIMIT
        ),
        name="gather_window",
    )(x, kv, *weights)


class Reduce:
    def __init__(self, h, parts, src, buf, send_sem, recv_sem):
        self.h, self.parts, self.src, self.buf = h, parts, src, buf
        self.send_sem, self.recv_sem = send_sem, recv_sem

    def window(self, p):
        r0, rn, c0, cn, order = self.parts[p]
        return pl.ds(r0, rn), pl.ds(c0, cn)

    def held(self, p, j, offset):
        if j == len(self.h.dims) - 1:
            return self.src.at[(self.h.at(self.parts[p][4], offset),) + self.window(p)]
        return self.buf.at[((1 << (j + 1)) | offset,) + self.window(p)]

    def copy(self, p, j, low):
        n = (1 << j) | low
        return remote(
            self.held(p, j, low | 1 << j),
            self.buf.at[(n,) + self.window(p)],
            self.send_sem.at[p, n],
            self.recv_sem.at[p, n],
            self.h.partner[self.parts[p][4][j]],
        )

    def add(self, p, j, low, out=None):
        self.copy(p, j, low).wait_recv()
        r0, rn, c0, cn, order = self.parts[p]
        mine = self.held(p, j, low)
        came = self.buf.at[((1 << j) | low,) + self.window(p)]
        step = 16

        @pl.loop(0, rn // step)
        def _(i):
            rows = pl.ds(pl.multiple_of(i * step, step), step)
            total = mine[rows, :].astype(jnp.float32) + came[rows, :].astype(jnp.float32)
            if j > 0:
                came[rows, :] = total.astype(came.dtype)
            else:
                out[pl.ds(pl.multiple_of(r0 + i * step, step), step), pl.ds(c0, cn)] = total

        if j > 0 and low >> (j - 1) & 1:
            self.copy(p, j - 1, low ^ (1 << (j - 1))).start()

    def finish(self):
        for p in range(len(self.parts)):
            for j in range(len(self.h.dims)):
                for low in range(1 << j):
                    self.copy(p, j, low).wait_send()


def reduce_kernel(dims, all_parts, swapped, *refs):
    count = len(all_parts)
    xs, outs, bufs = refs[:count], refs[count : 2 * count], refs[2 * count : 3 * count]
    sems = refs[3 * count :]
    h = Hyper(dims)
    k = len(dims)
    sec, shd = lax.axis_index("section"), lax.axis_index("shard")
    other = (sec, shd + 8 * (1 - 2 * lax.rem(shd // 8, 2)))
    h.barrier((other,) if swapped else ())
    sums = [
        Reduce(h, parts, xs[n], bufs[n], sems[2 * n], sems[2 * n + 1])
        for n, parts in enumerate(all_parts)
    ]
    every = [(r, p, outs[n]) for n, r in enumerate(sums) for p in range(len(all_parts[n]))]
    for low in reversed(range(1 << (k - 1))):
        for r, p, _ in every:
            r.copy(p, k - 1, low).start()
    for j in reversed(range(k)):
        for low in reversed(range(1 << j)):
            for r, p, out in every:
                r.add(p, j, low, out)
    if swapped:
        sent, swap_send, swap_recv = sems[2 * count :]
        out = outs[-1]
        sent[0] = out[...].astype(sent.dtype)
        swap = remote(sent.at[0], sent.at[1], swap_send, swap_recv, other)
        swap.start()
        swap.wait()
        out[...] = sent[1].astype(jnp.float32)
    for r in sums:
        r.finish()


def reduce(xs, dims, all_parts, collective_id, name, swapped=False):
    n = 1 << len(dims)
    dma = pltpu.SemaphoreType.DMA
    vmem = pl.BlockSpec(memory_space=pltpu.VMEM)
    scratch = [pltpu.VMEM(x.shape, x.dtype) for x in xs]
    for parts in all_parts:
        scratch += [dma((len(parts), n))] * 2
    if swapped:
        scratch += [pltpu.VMEM((2,) + xs[-1].shape[1:], xs[-1].dtype), dma, dma]
    return pl.pallas_call(
        functools.partial(reduce_kernel, dims, all_parts, swapped),
        out_shape=[jax.ShapeDtypeStruct(x.shape[1:], jnp.float32) for x in xs],
        in_specs=[vmem] * len(xs),
        out_specs=[vmem] * len(xs),
        scratch_shapes=scratch,
        compiler_params=pltpu.CompilerParams(
            collective_id=collective_id, has_side_effects=True, vmem_limit_bytes=LIMIT
        ),
        name=name,
    )(*xs)


def block_of(sec, shd):
    return 8 * lax.rem(sec + lax.rem(shd, 2), 2) + lax.rem(shd, 8)


def half_group(sec, shd):
    first = 8 * (shd // 8)
    return 8 * sec + lax.rem(shd, 8), lambda n: (n // 8, first + lax.rem(n, 8))


def half_barrier(me, place, sec, shd):
    sem = pltpu.get_barrier_semaphore()

    @pl.loop(1, 16)
    def _(d):
        pl.semaphore_signal(
            sem, inc=1, device_id=place(lax.rem(me + d, 16)), device_id_type=MESH
        )

    across = shd + 8 * (1 - 2 * (shd // 8))
    for s in range(2):
        pl.semaphore_signal(sem, inc=1, device_id=(s, across), device_id_type=MESH)
    pl.semaphore_wait(sem, 17)


class Spread:
    def __init__(self, pieces, own_sem, send, recv):
        self.sec, self.shd = lax.axis_index("section"), lax.axis_index("shard")
        self.me, self.place = half_group(self.sec, self.shd)
        self.pieces, self.own_sem, self.send, self.recv = pieces, own_sem, send, recv

    def barrier(self):
        half_barrier(self.me, self.place, self.sec, self.shd)

    def copies(self, d):
        there = self.place(lax.rem(self.me + d, 16))
        return [
            remote(src, dst, self.send.at[n, d], self.recv.at[n, d], there)
            for n, (src, dst) in enumerate(self.pieces(*there))
        ]

    def own(self):
        return [
            pltpu.make_async_copy(src, dst, self.own_sem.at[n])
            for n, (src, dst) in enumerate(self.pieces(self.sec, self.shd))
        ]

    def start(self):
        @pl.loop(1, 16)
        def _(d):
            for one in self.copies(d):
                one.start()

        for one in self.own():
            one.start()

    def wait(self):
        @pl.loop(1, 16)
        def _(d):
            for one in self.copies(d):
                one.wait_recv()

        @pl.loop(1, 16)
        def _(d):
            for one in self.copies(d):
                one.wait_send()

        for one in self.own():
            one.wait()


def first_kernel(block, mix, out, shared, wq, wo, *sems):
    send, recv, out_send, out_recv, own_sem, sh_send, sh_recv = sems
    sec, shd = lax.axis_index("section"), lax.axis_index("shard")
    low, half = lax.rem(shd, 8), shd // 8

    def pieces(ts, tj):
        yield mix.at[:, columns(block_of(ts, tj), HD)], wq.at[sec, low]

    spread = Spread(pieces, own_sem, send, recv)
    spread.barrier()
    h = Hyper(ALL)
    own_block = pltpu.make_async_copy(block, shared.at[h.pos], own_sem.at[1])
    own_block.start()
    g = Gather(h, SMALL, block, shared, sh_send, sh_recv)
    g.start(range(3))
    spread.start()

    to_x = lax.rem(half + lax.rem(shd, 2), 2)
    from_half = lax.rem(sec + lax.rem(shd, 2), 2)
    own_out = pltpu.make_async_copy(out, wo.at[sec], own_sem.at[2])
    for z in range(2):
        mine = jnp.logical_and(to_x == sec, half == z)
        there = remote(out, wo.at[sec], out_send.at[z], out_recv.at[sec], (to_x, 8 * z + low))

        @pl.when(mine)
        def _():
            own_out.start()

        @pl.when(jnp.logical_not(mine))
        def _():
            there.start()

    g.forward(range(3))
    spread.wait()
    for s in range(2):
        mine = jnp.logical_and(sec == s, from_half == half)

        @pl.when(jnp.logical_not(mine))
        def _():
            remote(out, wo.at[s], out_send.at[0], out_recv.at[s], (1 - sec, shd)).wait_recv()

    for z in range(2):
        mine = jnp.logical_and(to_x == sec, half == z)
        there = remote(out, wo.at[sec], out_send.at[z], out_recv.at[sec], (to_x, 8 * z + low))

        @pl.when(mine)
        def _():
            own_out.wait()

        @pl.when(jnp.logical_not(mine))
        def _():
            there.wait_send()

    g.finish()
    own_block.wait()


def fetch_first(block, mix, out):
    bf16 = jnp.bfloat16
    dma = pltpu.SemaphoreType.DMA
    return pl.pallas_call(
        first_kernel,
        out_shape=(
            jax.ShapeDtypeStruct((32,) + block.shape, bf16),
            jax.ShapeDtypeStruct((2, 8, 128, HD), bf16),
            jax.ShapeDtypeStruct((2, 128, D), bf16),
        ),
        in_specs=[pl.BlockSpec(memory_space=pl.ANY)] * 3,
        out_specs=[pl.BlockSpec(memory_space=pl.ANY)] * 3,
        scratch_shapes=[dma((1, 16)), dma((1, 16)), dma((2,)), dma((2,)), dma((3,)), dma((3, 32)), dma((3, 32))],
        compiler_params=pltpu.CompilerParams(
            collective_id=1, has_side_effects=True, vmem_limit_bytes=LIMIT
        ),
        name="fetch_first",
    )(block, mix, out)


def return_kernel(gq, ge, go, gc, rq, re, ro, rc, *sems):
    send, recv, con_send, con_recv, out_send, out_recv, own_sem = sems
    sec, shd = lax.axis_index("section"), lax.axis_index("shard")
    me, place = half_group(sec, shd)
    half_barrier(me, place, sec, shd)
    low, half = lax.rem(shd, 8), shd // 8
    f = block_of(sec, shd)

    def pieces(ts, tj):
        tlow = lax.rem(tj, 8)
        yield gq.at[ts, tlow], rq.at[:, columns(f, HD)]
        for h in range(2):
            yield (
                ge.at[ts, tlow, :, pl.ds(256 * h, 256)],
                re.at[:, columns(2 * (8 * h + low) + sec, 256)],
            )

    def spread(d):
        there = place(lax.rem(me + d, 16))
        return [
            remote(src, dst, send.at[n, d], recv.at[n, d], there)
            for n, (src, dst) in enumerate(pieces(*there))
        ]

    @pl.loop(1, 16)
    def _(d):
        for one in spread(d):
            one.start()

    own = [
        pltpu.make_async_copy(src, dst, own_sem.at[n])
        for n, (src, dst) in enumerate(pieces(sec, shd))
    ]
    own.append(pltpu.make_async_copy(gc.at[sec], rc.at[pl.ds(256 * sec, 256)], own_sem.at[3]))
    for one in own:
        one.start()
    rows = remote(gc.at[1 - sec], rc.at[pl.ds(256 * sec, 256)], con_send, con_recv, (1 - sec, shd))
    rows.start()

    own_out = pltpu.make_async_copy(go.at[sec], ro.at[half], own_sem.at[4])
    for s in range(2):
        mine = jnp.logical_and(sec == s, f == shd)
        there = remote(go.at[s], ro.at[half], out_send.at[s], out_recv.at[half], (s, f))

        @pl.when(mine)
        def _():
            own_out.start()

        @pl.when(jnp.logical_not(mine))
        def _():
            there.start()

    @pl.loop(1, 16)
    def _(d):
        for one in spread(d):
            one.wait_recv()

    remote(gc.at[0], rc.at[pl.ds(256 * (1 - sec), 256)], con_send, con_recv, (1 - sec, shd)).wait_recv()
    for z in range(2):
        mine = jnp.logical_and(f == shd, half == z)

        @pl.when(jnp.logical_not(mine))
        def _():
            remote(go.at[0], ro.at[z], out_send.at[0], out_recv.at[z], (1 - sec, shd)).wait_recv()

    @pl.loop(1, 16)
    def _(d):
        for one in spread(d):
            one.wait_send()

    rows.wait_send()
    for s in range(2):
        mine = jnp.logical_and(sec == s, f == shd)
        there = remote(go.at[s], ro.at[half], out_send.at[s], out_recv.at[half], (s, f))

        @pl.when(mine)
        def _():
            own_out.wait()

        @pl.when(jnp.logical_not(mine))
        def _():
            there.wait_send()

    for one in own:
        one.wait()


def return_grads(gq, ge, go, gc):
    bf16 = jnp.bfloat16
    dma = pltpu.SemaphoreType.DMA
    return pl.pallas_call(
        return_kernel,
        out_shape=(
            jax.ShapeDtypeStruct((128, D), bf16),
            jax.ShapeDtypeStruct((128, 8192), bf16),
            jax.ShapeDtypeStruct((2, 128, D), bf16),
            jax.ShapeDtypeStruct((512, D), bf16),
        ),
        in_specs=[pl.BlockSpec(memory_space=pl.ANY)] * 4,
        out_specs=[pl.BlockSpec(memory_space=pl.ANY)] * 4,
        scratch_shapes=[dma((3, 16)), dma((3, 16)), dma, dma, dma((2,)), dma((2,)), dma((5,))],
        compiler_params=pltpu.CompilerParams(
            collective_id=2, has_side_effects=True, vmem_limit_bytes=LIMIT
        ),
        name="return_grads",
    )(gq, ge, go, gc)


HALVES = [[n, n + 8] for n in range(8)]


def from_halves(x):
    return lax.all_gather(x, "shard", axis=0, tiled=True, axis_index_groups=HALVES)


def to_halves(x):
    return lax.psum_scatter(x, "shard", scatter_dimension=0, tiled=True, axis_index_groups=HALVES)


NT = (((1,), (1,)), ((), ()))
TN = (((0,), (0,)), ((), ()))


def dot32(a, b):
    return jnp.dot(a, b, preferred_element_type=jnp.float32)


def dot_nt(a, b):
    return lax.dot_general(a, b, NT, preferred_element_type=jnp.float32)


def dot_tn(a, b):
    return lax.dot_general(a, b, TN, preferred_element_type=jnp.float32)


PLAIN = cube_parts(128, (768, 640, 640))
TRIO = ("x", 4, 2)
CHUNK = 64


def spaced(many, few):
    result = []
    for n, step in enumerate(many):
        result.append(step)
        done = len(few) * (n + 1) // len(many)
        result.extend(few[len(few) * n // len(many) : done])
    return result


def chunk_gather_steps(g, count):
    k = len(g.h.dims)

    def step(j, low):
        for p in range(count):
            g.copy(p, low, j).wait_recv()
            for later in range(j + 1, k):
                g.copy(p, low | 1 << j, later).start()

    return [functools.partial(step, j, low) for j in range(k) for low in range(1 << j)]


def chunk_reduce_steps(r, out):
    k = len(r.h.dims)
    return [
        functools.partial(r.add, p, j, low, out)
        for j in reversed(range(k))
        for low in reversed(range(1 << j))
        for p in range(len(r.parts))
    ]


GELU_K = (2.0 / 3.141592653589793) ** 0.5


def gelu_pair(u):
    square = u * u
    t = jnp.tanh(GELU_K * (u + 0.044715 * u * square))
    half = 0.5 * (1.0 + t)
    slope = half + 0.5 * u * (1.0 - t * t) * (GELU_K * (1.0 + 3 * 0.044715 * square))
    return u * half, slope


def hidden_kernel(back, *refs):
    if back:
        x_ref, we_hbm, wc_hbm, slope_hbm, o_ref, x_out, h_out = refs[:7]
        scratch = refs[7:]
    else:
        x_ref, we_hbm, wc_hbm, be_ref, o_ref, x_out, h_out, slope_out = refs[:8]
        scratch = refs[8:]
    x_all, we, wc, h_all, slope, part, came, buf = scratch[:8]
    g_send, g_recv, c_send, c_recv, r_send, r_recv, own_sem, load_sem, out_sem = scratch[8:]
    h = Hyper(CUBE)
    trio = Hyper(TRIO)
    h.barrier()
    loads = [pltpu.make_async_copy(we_hbm, we, load_sem.at[0]), pltpu.make_async_copy(wc_hbm, wc, load_sem.at[1])]
    if back:
        loads.append(pltpu.make_async_copy(slope_hbm, slope, load_sem.at[2]))
    parts = tuple((0, CHUNK, c0, cn, order) for _, _, c0, cn, order in PLAIN)
    gathers, sums = [], []
    for n in range(2):
        mine = x_ref.at[pl.ds(CHUNK * n, CHUNK)]
        own = pltpu.make_async_copy(mine, x_all.at[n, h.pos], own_sem.at[n])
        own.start()
        loads.append(own)
        gathers.append(Gather(h, parts, mine, x_all.at[n], g_send.at[n], g_recv.at[n]))
        sums.append(
            Reduce(
                trio,
                tuple((0, CHUNK, c0, cn, order[:3]) for _, _, c0, cn, order in PLAIN),
                came.at[n],
                buf.at[n],
                r_send.at[n],
                r_recv.at[n],
            )
        )
        gathers[n].start(range(3))
    for one in loads[:-2]:
        one.start()
    core = 1 - lax.rem(lax.axis_index("shard"), 2)

    def quad(r):
        return 4 * (h.pos // 4) + (h.delta["x"] if r & 2 else 0) + (h.delta[4] if r & 1 else 0)

    def pair(r, y):
        return quad(r) + 2 * (lax.rem(h.pos, 4) // 2) + (h.delta[2] if y else 0)

    def compute(n, r):
        four = pl.ds(quad(r), 4)
        x = x_all[n, four].reshape(4 * CHUNK, D)
        if back:
            inner = dot_nt(x, wc[...]).reshape(4, CHUNK, 512)
            mid = (inner * slope[n, four].astype(jnp.float32)).astype(jnp.bfloat16)
        else:
            inner = dot32(x, we[...]) + be_ref[...]
            act, grad = gelu_pair(inner)
            mid = act.astype(jnp.bfloat16).reshape(4, CHUNK, 512)
            slope[n, four] = grad.astype(jnp.bfloat16).reshape(4, CHUNK, 512)
        h_all[n, four] = mid
        mid = mid.reshape(4 * CHUNK, 512)
        for c in range(4):
            cols = pl.ds(512 * c, 512)
            tile = dot_nt(mid, we[cols, :]) if back else dot32(mid, wc[:, cols])
            part[n, four, :, cols] = tile.astype(jnp.bfloat16).reshape(4, CHUNK, 512)
        for y in reversed(range(2)):
            core_copy(n, r, y).start()

    def core_copy(n, r, y):
        at = pair(r, y)
        return remote(
            part.at[n, at + core],
            came.at[n, at // 2],
            c_send.at[n, 2 * r + y],
            c_recv.at[n, 2 * r + y],
            h.partner[1],
        )

    def core_add(n, r):
        for y in reversed(range(2)):
            core_copy(n, r, y).wait_recv()
            at = pair(r, y)

            @pl.loop(0, CHUNK // 16)
            def _(i):
                rows = pl.ds(pl.multiple_of(i * 16, 16), 16)
                total = part[n, at + 1 - core, rows, :].astype(jnp.float32) + came[
                    n, at // 2, rows, :
                ].astype(jnp.float32)
                came[n, at // 2, rows, :] = total.astype(jnp.bfloat16)

            offset = ((r >> 1) & 1, r & 1, y)
            for p, (_, _, _, _, order) in enumerate(sums[n].parts):
                bits = [offset[TRIO.index(d)] for d in order]
                if bits[2]:
                    sums[n].copy(p, 2, bits[0] | bits[1] << 1).start()

    def compute_steps(n):
        steps = []
        for r in (3, 2, 1, 0):
            steps.append(functools.partial(compute, n, r))
            if r < 3:
                steps.append(functools.partial(core_add, n, r + 1))
        return steps + [functools.partial(core_add, n, 0)]

    for step in chunk_gather_steps(gathers[0], 3):
        step()
    for one in loads:
        one.wait()
    for step in spaced(chunk_gather_steps(gathers[1], 3), compute_steps(0)):
        step()
    outs = [pltpu.make_async_copy(x_all, x_out, out_sem.at[0])]
    outs[0].start()
    out_rows = [o_ref.at[pl.ds(CHUNK * n, CHUNK)] for n in range(2)]
    first = chunk_reduce_steps(sums[0], out_rows[0])
    for step in spaced(first, compute_steps(1)):
        step()
    outs.append(pltpu.make_async_copy(h_all, h_out, out_sem.at[1]))
    if not back:
        outs.append(pltpu.make_async_copy(slope, slope_out, out_sem.at[2]))
    for one in outs[1:]:
        one.start()
    for step in chunk_reduce_steps(sums[1], out_rows[1]):
        step()
    for n in range(2):
        gathers[n].finish()
        sums[n].finish()
        for r in range(4):
            for y in range(2):
                core_copy(n, r, y).wait_send()
    for one in outs:
        one.wait()


def hidden_layer(back, x, we, wc, last, collective_id, name):
    bf16, f32 = jnp.bfloat16, jnp.float32
    dma = pltpu.SemaphoreType.DMA
    hbm, vmem = pl.BlockSpec(memory_space=pl.ANY), pl.BlockSpec(memory_space=pltpu.VMEM)
    wide, narrow = (2, 16, CHUNK, D), (2, 16, CHUNK, 512)
    out = [
        jax.ShapeDtypeStruct((128, D), f32),
        jax.ShapeDtypeStruct(wide, bf16),
        jax.ShapeDtypeStruct(narrow, bf16),
    ]
    if not back:
        out.append(jax.ShapeDtypeStruct(narrow, bf16))
    return pl.pallas_call(
        functools.partial(hidden_kernel, back),
        out_shape=out,
        in_specs=[hbm, hbm, hbm, hbm if back else vmem],
        out_specs=[vmem] + [hbm] * (len(out) - 1),
        scratch_shapes=[
            pltpu.VMEM(wide, bf16),
            pltpu.VMEM((D, 512), bf16),
            pltpu.VMEM((512, D), bf16),
            pltpu.VMEM(narrow, bf16),
            pltpu.VMEM(narrow, bf16),
            pltpu.VMEM(wide, bf16),
            pltpu.VMEM((2, 8, CHUNK, D), bf16),
            pltpu.VMEM((2, 8, CHUNK, D), bf16),
            dma((2, 3, 16)),
            dma((2, 3, 16)),
            dma((2, 8)),
            dma((2, 8)),
            dma((2, 3, 8)),
            dma((2, 3, 8)),
            dma((2,)),
            dma((3,)),
            dma((3,)),
        ],
        compiler_params=pltpu.CompilerParams(
            collective_id=collective_id, has_side_effects=True, vmem_limit_bytes=LIMIT
        ),
        name=name,
    )(x, we, wc, last)


QB = 256
KB = WINDOW + QB
SCALE = HD ** (-0.5)


def kept_pairs(lo_ref, a):
    key = a + lax.broadcasted_iota(jnp.int32, (KB, QB), 0)
    last = a + WINDOW + lax.broadcasted_iota(jnp.int32, (KB, QB), 1)
    return (key >= lo_ref[0]) & (key <= last)


def attend_kernel(lo_ref, q_ref, k_ref, v_ref, o_ref, lse_ref):
    a = pl.multiple_of(lax.rem(pl.program_id(0), 4) * QB, QB)
    keys = pl.ds(a, KB)
    s = lax.dot_general(k_ref[0, keys], q_ref[0], NT, preferred_element_type=jnp.float32) * SCALE
    s = jnp.where(kept_pairs(lo_ref, a), s, -1e30)
    top = jnp.max(s, axis=0, keepdims=True)
    e = jnp.exp(s - top)
    total = jnp.sum(e, axis=0, keepdims=True)
    probs = (e * (1.0 / total)).astype(jnp.bfloat16)
    o_ref[0] = lax.dot_general(probs, v_ref[0, keys], TN, preferred_element_type=jnp.float32).astype(
        o_ref.dtype
    )
    lse_ref[0] = top + jnp.log(total)


def attend(lo, q, k, v):
    per_q = pl.BlockSpec((1, QB, HD), lambda n: (n, 0, 0))
    per_row = pl.BlockSpec((1, 1, QB), lambda n: (n, 0, 0))
    per_micro = pl.BlockSpec((1, 2 * WINDOW, HD), lambda n: (n // 4, 0, 0))
    return pl.pallas_call(
        attend_kernel,
        grid=(8,),
        out_shape=(
            jax.ShapeDtypeStruct((8, QB, HD), jnp.bfloat16),
            jax.ShapeDtypeStruct((8, 1, QB), jnp.float32),
        ),
        in_specs=[per_row, per_q, per_micro, per_micro],
        out_specs=[per_q, per_row],
        compiler_params=pltpu.CompilerParams(vmem_limit_bytes=LIMIT),
        name="attend",
    )(lo, q, k, v)


def attend_back_kernel(lo_ref, lse_ref, q_ref, k_ref, v_ref, g_ref, dq_ref, far_ref, own_ref, dk_ref, dv_ref):
    n = lax.rem(pl.program_id(0), 4)
    a = pl.multiple_of(n * QB, QB)
    keys = pl.ds(a, KB)

    @pl.when(n == 0)
    def _():
        dk_ref[...] = jnp.zeros_like(dk_ref)
        dv_ref[...] = jnp.zeros_like(dv_ref)

    q, g, k = q_ref[0], g_ref[0], k_ref[0, keys]
    s = lax.dot_general(k, q, NT, preferred_element_type=jnp.float32) * SCALE
    probs = jnp.where(kept_pairs(lo_ref, a), jnp.exp(s - lse_ref[0]), 0.0)
    gp = lax.dot_general(v_ref[0, keys], g, NT, preferred_element_type=jnp.float32)
    dot = jnp.sum(probs * gp, axis=0, keepdims=True)
    gs = (probs * (gp - dot)).astype(jnp.bfloat16)
    dq = lax.dot_general(gs, k, TN, preferred_element_type=jnp.float32) * SCALE
    dq_ref[0] = dq.astype(dq_ref.dtype)
    dk_ref[keys] += jnp.dot(gs, q, preferred_element_type=jnp.float32) * SCALE
    dv_ref[keys] += jnp.dot(probs.astype(jnp.bfloat16), g, preferred_element_type=jnp.float32)

    @pl.when(n == 3)
    def _():
        for out, first in ((far_ref, 0), (own_ref, WINDOW)):
            rows = pl.ds(first, WINDOW)
            out[0, :, :HD] = dk_ref[rows].astype(out.dtype)
            out[0, :, HD:] = dv_ref[rows].astype(out.dtype)


def attend_back(lo, lse, q, k, v, g):
    per_q = pl.BlockSpec((1, QB, HD), lambda n: (n, 0, 0))
    per_row = pl.BlockSpec((1, 1, QB), lambda n: (n, 0, 0))
    per_micro = pl.BlockSpec((1, 2 * WINDOW, HD), lambda n: (n // 4, 0, 0))
    per_half = pl.BlockSpec((1, WINDOW, 2 * HD), lambda n: (n // 4, 0, 0))
    return pl.pallas_call(
        attend_back_kernel,
        grid=(8,),
        out_shape=(
            jax.ShapeDtypeStruct((8, QB, HD), jnp.bfloat16),
            jax.ShapeDtypeStruct((2, WINDOW, 2 * HD), jnp.bfloat16),
            jax.ShapeDtypeStruct((2, WINDOW, 2 * HD), jnp.bfloat16),
        ),
        in_specs=[per_row, per_row, per_q, per_micro, per_micro, per_q],
        out_specs=[per_q, per_half, per_half],
        scratch_shapes=[pltpu.VMEM((2 * WINDOW, HD), jnp.float32)] * 2,
        compiler_params=pltpu.CompilerParams(vmem_limit_bytes=LIMIT),
        name="attend_back",
    )(lo, lse, q, k, v, g)


BESIDE = ((0, 128, 0, 256, (4, 2, "x", 1)),), ((0, 128, 0, 256, (2, "x", 4, 1)),)
SMALL = tuple(
    (48 * n, 48, 0, 256, order)
    for n, order in enumerate(((8, "x", 4, 2, 1), (8, 4, 2, "x", 1), (8, 2, "x", 4, 1)))
)
BIAS = D + HD


def on_device_fast(
    embedded,
    cotangent,
    segments,
    first_gain,
    first_shift,
    mixer_weight,
    mixer_bias,
    output_weight,
    output_bias,
    second_gain,
    second_shift,
    expand_weight,
    expand_bias,
    contract_weight,
    contract_bias,
):
    bf16, f32 = jnp.bfloat16, jnp.float32
    sec, shd = lax.axis_index("section"), lax.axis_index("shard")
    half = shd // 8
    f = block_of(sec, shd)

    small = jnp.concatenate(
        [
            first_gain[0],
            first_shift[0],
            second_gain[0],
            second_shift[0],
            output_bias[0],
            contract_bias[0],
            expand_bias[0],
            mixer_bias[0],
        ]
    )
    small = jnp.concatenate([small, jnp.zeros((16 * 256 - small.shape[0],), bf16)]).reshape(16, 256)
    shared, wq, wo = fetch_first(
        jnp.concatenate([mixer_weight[0][:, D:], small], axis=0), mixer_weight[0], output_weight[0]
    )
    shared = shared.reshape(2, 16, 144, 256)
    wq = from_halves(wq.reshape(2, 8 * 128, HD).transpose(1, 0, 2)).transpose(1, 0, 2)
    wkv = shared[:, :, :128].reshape(2, D, 256)
    vectors = shared[:, :, 128:].reshape(2, 16, 4096)

    def vector(n):
        return vectors[:, :, 128 * n : 128 * (n + 1)].reshape(2, D).astype(f32)

    gain_one, shift_one, gain_two, shift_two, bias_out, bias_con = [vector(n) for n in range(6)]
    bias_exp = vectors[:, :, 768:1280].reshape(2, 8192).astype(f32)
    hidden_units = [512 * (8 * h + lax.rem(shd, 8)) + 256 * sec for h in range(2)]
    bias_exp = jnp.concatenate(
        [lax.dynamic_slice_in_dim(bias_exp, first, 256, 1) for first in hidden_units], axis=1
    )
    bias_mix = vectors[:, :, 1280 : 1280 + 136].reshape(2, BIAS).astype(f32)
    bias_q = lax.dynamic_slice_in_dim(bias_mix, f * HD, HD, 1)
    bias_kv = jnp.concatenate([jnp.zeros((2, HD), f32), bias_mix[:, D:]], axis=1)

    starts = jnp.sum(
        (segments[:, None, :] < lax.dynamic_slice_in_dim(segments, half * WINDOW, WINDOW, 1)[:, :, None]),
        axis=2,
        dtype=jnp.int32,
    )
    lo = jnp.maximum(jnp.arange(1, WINDOW + 1)[None], starts - half * WINDOW + WINDOW)
    lo = lo.reshape(8, 1, QB)

    hidden = lax.dynamic_index_in_dim(embedded, sec, 0, keepdims=False).astype(f32)
    results, kept = [], []
    for s in range(2):
        n1 = layer_norm(hidden, gain_one[s], shift_one[s]).astype(bf16)
        kv_rows = (dot32(n1, wkv[s]) + bias_kv[s]).astype(bf16)
        if s == 0:
            all_n1, far_kv, we, wc = gather_window(
                n1, kv_rows, 3, (expand_weight[0], contract_weight[0])
            )
            we = [from_halves(we[n].reshape(8 * 128, 512)) for n in range(2)]
            wc = [from_halves(wc[n]) for n in range(2)]
        else:
            all_n1, far_kv = gather_window(n1, kv_rows, 4)
        all_n1 = all_n1.reshape(2048, D)
        q = (dot32(all_n1, wq[s]) + bias_q[s]).astype(bf16).reshape(8, QB, HD)
        kv = (dot32(all_n1, wkv[s]) + bias_kv[s]).astype(bf16).reshape(2, WINDOW, 256)
        kv = jnp.concatenate([far_kv.reshape(2, WINDOW, 256), kv], axis=1)
        k, v = kv[:, :, :HD], kv[:, :, HD:]
        mixed, lse = attend(lo, q, k, v)
        mixed = mixed.reshape(2048, HD)
        part = dot32(mixed, wo[s]).astype(bf16).reshape(16, 128, D)
        middle = hidden + reduce([part], CUBE, [PLAIN], 5, "reduce_rows")[0] + bias_out[s]
        n2 = layer_norm(middle, gain_two[s], shift_two[s]).astype(bf16)
        rows, all_n2, act, slope = hidden_layer(False, n2, we[s], wc[s], bias_exp[s][None], 9, "hidden")
        result = middle + rows + bias_con[s]
        results.append(result.astype(bf16))
        kept.append((hidden, n1, all_n1, q, k, v, lse, mixed, middle, all_n2, act, slope))
        hidden = results[-1].astype(f32)

    grad = lax.dynamic_index_in_dim(cotangent, sec, 0, keepdims=False).astype(f32)
    input_grads = [None, None]
    weight_grads = [None, None]
    small_grads = [None, None]
    for s in (1, 0):
        hidden, n1, all_n1, q, k, v, lse, mixed, middle, all_n2, act, slope = kept[s]
        go = grad.astype(bf16)
        g_n2, all_go, g_pre = hidden_layer(True, go, we[s], wc[s], slope, 10, "hidden_back")
        all_go, all_n2 = all_go.reshape(2048, D), all_n2.reshape(2048, D)
        act, g_pre = act.reshape(2048, 512), g_pre.reshape(2048, 512)
        d_wc = to_halves(dot_tn(act, all_go).astype(bf16))
        d_we = to_halves(dot_tn(all_n2, g_pre).astype(bf16))
        d_be = jnp.sum(g_pre.astype(f32), axis=0)
        _, back = jax.vjp(layer_norm, middle, gain_two[s], shift_two[s])
        g_mid, d_gain_two, d_shift_two = back(g_n2)
        g_mid = grad + g_mid
        ga = g_mid.astype(bf16)
        all_ga = gather(ga, CUBE, PLAIN, 6, "gather_rows").reshape(2048, D)
        g_mixed = dot_nt(all_ga, wo[s]).astype(bf16).reshape(8, QB, HD)
        d_wo = dot_tn(mixed, all_ga).astype(bf16)
        dq, d_far, d_own = attend_back(lo, lse, q, k, v, g_mixed)
        dq = dq.reshape(2048, HD)
        d_wq = to_halves(dot_tn(all_n1, dq).astype(bf16))
        part = dot_nt(dq, wq[s]).astype(bf16).reshape(16, 128, D)
        rows, kv_own, kv_far = reduce(
            [part, d_own.reshape(16, 128, 256), d_far.reshape(16, 128, 256)],
            CUBE,
            (PLAIN,) + BESIDE,
            7,
            "reduce_window",
            True,
        )
        dkv_rows = (kv_own + jnp.where(half == 0, kv_far, 0.0)).astype(bf16)
        g_n1 = rows + dot_nt(dkv_rows, wkv[s])
        _, back = jax.vjp(layer_norm, hidden, gain_one[s], shift_one[s])
        g_in, d_gain_one, d_shift_one = back(g_n1)
        g_in = g_mid + g_in
        input_grads[s] = g_in
        d_wkv = dot_tn(n1, dkv_rows)
        d_bq = jnp.sum(dq.astype(f32), axis=0)
        d_bv = jnp.sum(dkv_rows[:, HD:].astype(f32), axis=0)
        weight_grads[s] = (
            d_wq.reshape(8, 128, HD),
            d_we.reshape(8, 128, 512),
            d_wo,
            d_wc,
        )
        spread = [
            d_gain_one,
            d_shift_one,
            d_gain_two,
            d_shift_two,
            jnp.sum(ga.astype(f32), axis=0),
            jnp.sum(go.astype(f32), axis=0),
        ]
        placed = jnp.zeros((8192,), f32)
        for h, first in enumerate(hidden_units):
            placed = lax.dynamic_update_slice_in_dim(placed, d_be[256 * h : 256 * (h + 1)], first, 0)
        d_bm = lax.dynamic_update_slice_in_dim(jnp.zeros((D,), f32), d_bq, f * HD, 0)
        vec = jnp.concatenate(
            [one.reshape(16, 128) for one in spread]
            + [placed.reshape(16, 512), jnp.concatenate([d_bm, d_bv]).reshape(16, 136)],
            axis=1,
        )
        vec = jnp.pad(vec, ((0, 0), (0, 4096 - vec.shape[1]))).reshape(16, 16, 256)
        small_grads[s] = jnp.concatenate([d_wkv.reshape(16, 128, 256), vec], axis=1)
        grad = g_in.astype(bf16).astype(f32)

    mine = reduce(
        [jnp.concatenate(small_grads, axis=0).astype(bf16)], ALL, [SMALL], 8, "reduce_shared"
    )[0]
    vec = mine[128:].reshape(4096)
    rq, re, ro, rc = return_grads(
        *[jnp.stack([weight_grads[0][n], weight_grads[1][n]]) for n in range(4)]
    )

    def both(r):
        return r[0].astype(f32) + r[1].astype(f32)

    def swap(pair):
        theirs = jnp.where(sec == 0, pair[1].astype(bf16), pair[0].astype(bf16))
        own = jnp.where(sec == 0, pair[0], pair[1])
        came = lax.ppermute(theirs, "section", [(0, 1), (1, 0)]).astype(own.dtype)
        first = jnp.where(sec == 0, own, came)
        second = jnp.where(sec == 0, came, own)
        return jnp.stack([first, second])[None]

    return (
        swap(results),
        swap(input_grads),
        vec[0:128][None],
        vec[128:256][None],
        jnp.concatenate([rq.astype(f32), mine[:128]], axis=1)[None],
        vec[1280 : 1280 + 136][None],
        both(ro)[None],
        vec[512:640][None],
        vec[256:384][None],
        vec[384:512][None],
        re.astype(f32)[None],
        vec[768:1280][None],
        rc.astype(f32)[None],
        vec[640:768][None],
    )


def solution(mesh):
    in_specs = (
        P(None, "shard", None),
        P(None, "shard", None),
        P(),
        P("section", "shard"),
        P("section", "shard"),
        P("section", "shard", None),
        P("section", "shard"),
        P("section", "shard", None),
        P("section", "shard"),
        P("section", "shard"),
        P("section", "shard"),
        P("section", "shard", None),
        P("section", "shard"),
        P("section", "shard", None),
        P("section", "shard"),
    )
    out_specs = (
        P("section", None, "shard", None),
        P("section", None, "shard", None),
        P("section", "shard"),
        P("section", "shard"),
        P("section", "shard", None),
        P("section", "shard"),
        P("section", "shard", None),
        P("section", "shard"),
        P("section", "shard"),
        P("section", "shard"),
        P("section", "shard", None),
        P("section", "shard"),
        P("section", "shard", None),
        P("section", "shard"),
    )
    fits = mesh.shape["section"] == 2 and mesh.shape["shard"] == HEADS
    on_device = on_device_fast if fits else on_device_general
    return jax.shard_map(
        on_device, mesh=mesh, in_specs=in_specs, out_specs=out_specs, check_vma=False
    )
```

```python
import functools

import jax
import jax.numpy as jnp
from jax import lax
from jax.experimental import pallas as pl
from jax.experimental.pallas import tpu as pltpu
from jax.sharding import PartitionSpec as P

D = 2048
HEADS = 16
HD = 128
WINDOW = 1024


epsilon = 1e-05


def passed_along(block, axis, distance):
    devices = range(lax.axis_size(axis))
    route = [(i - distance, i) for i in devices if i - distance in devices]
    return lax.ppermute(block, axis, route)


def layer_norm(values, gain_row, shift_row):
    center = values - jnp.mean(values, axis=-1, keepdims=True)
    spread = jnp.mean(center * center, axis=-1, keepdims=True)
    return center * lax.rsqrt(spread + epsilon) * gain_row + shift_row


def gelu_tanh(values):
    return jax.nn.gelu(values, approximate=True)


def window_mask(segments, micro_index, device, row_count, reach_blocks):
    seg_row = lax.dynamic_index_in_dim(segments, micro_index, 0, keepdims=False)
    padded = jnp.concatenate([jnp.full((reach_blocks * row_count,), -1, jnp.int32), seg_row])
    key_segments = lax.dynamic_slice_in_dim(
        padded, device * row_count, (reach_blocks + 1) * row_count
    )
    query_segments = lax.dynamic_slice_in_dim(seg_row, device * row_count, row_count)
    distance = (
        jnp.arange(row_count)[:, None]
        + reach_blocks * row_count
        - jnp.arange((reach_blocks + 1) * row_count)[None, :]
    )
    return (
        (distance >= 0) & (distance < WINDOW) & (query_segments[:, None] == key_segments[None, :])
    )


def fetch_window(key_value, reach_blocks):
    earlier = [passed_along(key_value, "shard", offset) for offset in range(reach_blocks, 0, -1)]
    return jnp.concatenate(earlier + [key_value], axis=0)


def return_window(window_grad, reach_blocks, row_count):
    own_rows = window_grad[reach_blocks * row_count :]
    for offset in range(1, reach_blocks + 1):
        start_row = (reach_blocks - offset) * row_count
        own_rows = own_rows + passed_along(
            window_grad[start_row : start_row + row_count].astype(jnp.bfloat16), "shard", -offset
        ).astype(jnp.float32)
    return own_rows


def forward_layer(hidden, weights, key_mask, reach_blocks):
    (
        first_gain,
        first_shift,
        mixer_weight,
        mixer_bias,
        output_weight,
        output_bias,
        second_gain,
        second_shift,
        expand_weight,
        expand_bias,
        contract_weight,
        contract_bias,
    ) = weights
    row_count = hidden.shape[0]
    score_scale = HD ** (-0.5)
    normed_one = layer_norm(
        hidden, first_gain.astype(jnp.float32), first_shift.astype(jnp.float32)
    ).astype(jnp.bfloat16)
    full_bias = jnp.concatenate(
        [mixer_bias[:D], jnp.zeros((HD,), mixer_bias.dtype), mixer_bias[D:]]
    ).astype(jnp.float32)
    projected = (
        jnp.dot(normed_one, mixer_weight, preferred_element_type=jnp.float32) + full_bias
    ).astype(jnp.bfloat16)
    queries = projected[:, :D].reshape(row_count, HEADS, HD)
    window_pairs = fetch_window(projected[:, D:], reach_blocks)
    scores = (
        jnp.einsum("thd,kd->htk", queries, window_pairs[:, :HD], preferred_element_type=jnp.float32)
        * score_scale
    )
    masked = jnp.where(key_mask[None], scores, -1e30)
    top_score = jnp.max(masked, axis=2, keepdims=True)
    exponent = jnp.exp(masked - top_score)
    totals = jnp.sum(exponent, axis=2, keepdims=True)
    prob_low = (exponent / totals).astype(jnp.bfloat16)
    log_total = top_score + jnp.log(totals)
    mixed_rows = (
        jnp.einsum(
            "htk,kd->thd", prob_low, window_pairs[:, HD:], preferred_element_type=jnp.float32
        )
        .reshape(row_count, D)
        .astype(jnp.bfloat16)
    )
    middle = (
        hidden
        + jnp.dot(mixed_rows, output_weight, preferred_element_type=jnp.float32)
        + output_bias.astype(jnp.float32)
    )
    normed_two = layer_norm(
        middle, second_gain.astype(jnp.float32), second_shift.astype(jnp.float32)
    ).astype(jnp.bfloat16)
    pre_gelu = jnp.dot(
        normed_two, expand_weight, preferred_element_type=jnp.float32
    ) + expand_bias.astype(jnp.float32)
    activated = gelu_tanh(pre_gelu).astype(jnp.bfloat16)
    result = (
        middle
        + jnp.dot(activated, contract_weight, preferred_element_type=jnp.float32)
        + contract_bias.astype(jnp.float32)
    )
    return (
        result,
        (
            hidden,
            normed_one,
            projected,
            window_pairs,
            log_total,
            mixed_rows,
            middle,
            normed_two,
            pre_gelu,
            activated,
        ),
    )


def backward_layer(grad_result, weights, saved_state, key_mask, reach_blocks):
    (
        first_gain,
        first_shift,
        mixer_weight,
        mixer_bias,
        output_weight,
        output_bias,
        second_gain,
        second_shift,
        expand_weight,
        expand_bias,
        contract_weight,
        contract_bias,
    ) = weights
    (
        hidden,
        normed_one,
        projected,
        window_pairs,
        log_total,
        mixed_rows,
        middle,
        normed_two,
        pre_gelu,
        activated,
    ) = saved_state
    row_count = hidden.shape[0]
    score_scale = HD ** (-0.5)
    grad_out_low = grad_result.astype(jnp.bfloat16)
    grad_act = jnp.einsum(
        "rd,fd->rf", grad_out_low, contract_weight, preferred_element_type=jnp.float32
    )
    gelu_value, gelu_back = jax.vjp(gelu_tanh, pre_gelu)
    grad_pre = gelu_back(grad_act)[0].astype(jnp.bfloat16)
    grad_normed_two = jnp.einsum(
        "rf,df->rd", grad_pre, expand_weight, preferred_element_type=jnp.float32
    )
    norm_value_two, norm_back_two = jax.vjp(
        layer_norm, middle, second_gain.astype(jnp.float32), second_shift.astype(jnp.float32)
    )
    grad_middle_part, grad_gain_two, grad_shift_two = norm_back_two(grad_normed_two)
    grad_middle = grad_result + grad_middle_part
    grad_attended = grad_middle.astype(jnp.bfloat16)
    grad_mixed = (
        jnp.einsum("re,de->rd", grad_attended, output_weight, preferred_element_type=jnp.float32)
        .astype(jnp.bfloat16)
        .reshape(row_count, HEADS, HD)
    )
    queries = projected[:, :D].reshape(row_count, HEADS, HD)
    key_part = window_pairs[:, :HD]
    value_part = window_pairs[:, HD:]
    scores = (
        jnp.einsum("thd,kd->htk", queries, key_part, preferred_element_type=jnp.float32)
        * score_scale
    )
    prob_full = jnp.where(key_mask[None], jnp.exp(scores - log_total), 0.0)
    prob_low = prob_full.astype(jnp.bfloat16)
    grad_probs = jnp.einsum(
        "thd,kd->htk", grad_mixed, value_part, preferred_element_type=jnp.float32
    )
    row_dot = jnp.sum(prob_full * grad_probs, axis=2, keepdims=True)
    grad_scores = (prob_full * (grad_probs - row_dot)).astype(jnp.bfloat16)
    grad_queries = (
        jnp.einsum("htk,kd->thd", grad_scores, key_part, preferred_element_type=jnp.float32)
        * score_scale
    ).reshape(row_count, D)
    grad_keys = (
        jnp.einsum("htk,thd->kd", grad_scores, queries, preferred_element_type=jnp.float32)
        * score_scale
    )
    grad_values = jnp.einsum(
        "htk,thd->kd", prob_low, grad_mixed, preferred_element_type=jnp.float32
    )
    grad_window = jnp.concatenate([grad_keys, grad_values], axis=1)
    grad_own_pairs = return_window(grad_window, reach_blocks, row_count)
    grad_projected = jnp.concatenate([grad_queries, grad_own_pairs], axis=1).astype(jnp.bfloat16)
    grad_normed_one = jnp.einsum(
        "rq,dq->rd", grad_projected, mixer_weight, preferred_element_type=jnp.float32
    )
    norm_value_one, norm_back_one = jax.vjp(
        layer_norm, hidden, first_gain.astype(jnp.float32), first_shift.astype(jnp.float32)
    )
    grad_hidden_part, grad_gain_one, grad_shift_one = norm_back_one(grad_normed_one)
    grad_hidden = grad_middle + grad_hidden_part
    return (
        grad_hidden,
        (
            grad_projected,
            grad_attended,
            grad_pre,
            grad_out_low,
            grad_gain_one,
            grad_shift_one,
            grad_gain_two,
            grad_shift_two,
            normed_one,
            mixed_rows,
            normed_two,
            activated,
        ),
    )


def flatten_rows(stacked):
    return stacked.reshape((-1, stacked.shape[-1]))


def weight_terms(row_items, norm_items):
    (
        grad_projected_rows,
        grad_attended_rows,
        grad_pre_rows,
        grad_out_rows,
        normed_one_rows,
        mixed_all,
        normed_two_rows,
        activated_rows,
    ) = row_items
    first_gain_term, first_shift_term, second_gain_term, second_shift_term = norm_items
    mixer_weight_term = jnp.einsum(
        "rd,rq->dq", normed_one_rows, grad_projected_rows, preferred_element_type=jnp.float32
    )
    column_totals = jnp.sum(grad_projected_rows.astype(jnp.float32), axis=0)
    mixer_bias_term = jnp.concatenate([column_totals[:D], column_totals[D + HD :]])
    output_weight_term = jnp.einsum(
        "rd,re->de", mixed_all, grad_attended_rows, preferred_element_type=jnp.float32
    )
    output_bias_term = jnp.sum(grad_attended_rows.astype(jnp.float32), axis=0)
    expand_weight_term = jnp.einsum(
        "rd,rf->df", normed_two_rows, grad_pre_rows, preferred_element_type=jnp.float32
    )
    expand_bias_term = jnp.sum(grad_pre_rows.astype(jnp.float32), axis=0)
    contract_weight_term = jnp.einsum(
        "rf,rd->fd", activated_rows, grad_out_rows, preferred_element_type=jnp.float32
    )
    contract_bias_term = jnp.sum(grad_out_rows.astype(jnp.float32), axis=0)
    return (
        first_gain_term[None],
        first_shift_term[None],
        mixer_weight_term[None],
        mixer_bias_term[None],
        output_weight_term[None],
        output_bias_term[None],
        second_gain_term[None],
        second_shift_term[None],
        expand_weight_term[None],
        expand_bias_term[None],
        contract_weight_term[None],
        contract_bias_term[None],
    )


def on_device_general(
    embedded,
    cotangent,
    segments,
    first_gain,
    first_shift,
    mixer_weight,
    mixer_bias,
    output_weight,
    output_bias,
    second_gain,
    second_shift,
    expand_weight,
    expand_bias,
    contract_weight,
    contract_bias,
):
    section_index = lax.axis_index("section")
    device = lax.axis_index("shard")
    micro_count = embedded.shape[0]
    row_count = embedded.shape[1]
    reach_blocks = WINDOW // row_count
    own_params = (
        first_gain[0],
        first_shift[0],
        mixer_weight[0],
        mixer_bias[0],
        output_weight[0],
        output_bias[0],
        second_gain[0],
        second_shift[0],
        expand_weight[0],
        expand_bias[0],
        contract_weight[0],
        contract_bias[0],
    )
    forward_weights = (
        lax.all_gather(own_params[0], "shard", axis=0, tiled=True),
        lax.all_gather(own_params[1], "shard", axis=0, tiled=True),
        lax.all_gather(own_params[2], "shard", axis=0, tiled=True),
        lax.all_gather(own_params[3], "shard", axis=0, tiled=True),
        lax.all_gather(own_params[4], "shard", axis=0, tiled=True),
        lax.all_gather(own_params[5], "shard", axis=0, tiled=True),
        lax.all_gather(own_params[6], "shard", axis=0, tiled=True),
        lax.all_gather(own_params[7], "shard", axis=0, tiled=True),
        lax.all_gather(own_params[8], "shard", axis=0, tiled=True),
        lax.all_gather(own_params[9], "shard", axis=0, tiled=True),
        lax.all_gather(own_params[10], "shard", axis=0, tiled=True),
        lax.all_gather(own_params[11], "shard", axis=0, tiled=True),
    )
    zero_rows = jnp.zeros((row_count, D), jnp.float32)
    arrived = zero_rows
    sent_list = []
    kept_states = []
    for step_index in range(micro_count + 1):
        own_input = (
            embedded[step_index].astype(jnp.float32) if step_index < micro_count else zero_rows
        )
        hidden = jnp.where(section_index == 0, own_input, arrived)
        micro_index = jnp.clip(step_index - section_index, 0, micro_count - 1)
        key_mask = window_mask(segments, micro_index, device, row_count, reach_blocks)
        result, saved_state = forward_layer(hidden, forward_weights, key_mask, reach_blocks)
        result_low = result.astype(jnp.bfloat16)
        sent_list.append(result_low)
        kept_states.append(saved_state)
        if step_index < micro_count:
            arrived = passed_along(result_low, "section", 1).astype(jnp.float32)
    section_outputs = lax.dynamic_slice_in_dim(jnp.stack(sent_list), section_index, micro_count, 0)[
        None
    ]
    stacked_states = [
        jnp.stack([state_item[item_index] for state_item in kept_states])
        for item_index in range(10)
    ]
    valid_start = 1 - section_index
    arrived_grad = zero_rows
    grad_records = []
    hidden_grads = []
    for step_index in range(micro_count + 1):
        own_grad = (
            cotangent[step_index].astype(jnp.float32) if step_index < micro_count else zero_rows
        )
        grad_result = jnp.where(section_index == 1, own_grad, arrived_grad)
        forward_index = jnp.clip(step_index - 1 + 2 * section_index, 0, micro_count)
        micro_index = jnp.clip(step_index - 1 + section_index, 0, micro_count - 1)
        saved_state = [
            lax.dynamic_index_in_dim(stacked, forward_index, 0, keepdims=False)
            for stacked in stacked_states
        ]
        key_mask = window_mask(segments, micro_index, device, row_count, reach_blocks)
        grad_hidden, record = backward_layer(
            grad_result, forward_weights, saved_state, key_mask, reach_blocks
        )
        hidden_grads.append(grad_hidden)
        if step_index < micro_count:
            arrived_grad = passed_along(grad_hidden.astype(jnp.bfloat16), "section", -1).astype(
                jnp.float32
            )
        grad_records.append(record)
    input_grads = lax.dynamic_slice_in_dim(jnp.stack(hidden_grads), valid_start, micro_count, 0)[
        None
    ]
    chosen = [
        lax.dynamic_slice_in_dim(
            jnp.stack([record[item_index] for record in grad_records]), valid_start, micro_count, 0
        )
        for item_index in range(12)
    ]
    row_items = (
        flatten_rows(chosen[0]),
        flatten_rows(chosen[1]),
        flatten_rows(chosen[2]),
        flatten_rows(chosen[3]),
        flatten_rows(chosen[8]),
        flatten_rows(chosen[9]),
        flatten_rows(chosen[10]),
        flatten_rows(chosen[11]),
    )
    norm_items = (
        jnp.sum(chosen[4], axis=0),
        jnp.sum(chosen[5], axis=0),
        jnp.sum(chosen[6], axis=0),
        jnp.sum(chosen[7], axis=0),
    )
    all_terms = weight_terms(row_items, norm_items)
    summed = (
        lax.psum_scatter(all_terms[0], "shard", scatter_dimension=1, tiled=True),
        lax.psum_scatter(all_terms[1], "shard", scatter_dimension=1, tiled=True),
        lax.psum_scatter(all_terms[2], "shard", scatter_dimension=1, tiled=True),
        lax.psum_scatter(all_terms[3], "shard", scatter_dimension=1, tiled=True),
        lax.psum_scatter(all_terms[4], "shard", scatter_dimension=1, tiled=True),
        lax.psum_scatter(all_terms[5], "shard", scatter_dimension=1, tiled=True),
        lax.psum_scatter(all_terms[6], "shard", scatter_dimension=1, tiled=True),
        lax.psum_scatter(all_terms[7], "shard", scatter_dimension=1, tiled=True),
        lax.psum_scatter(all_terms[8], "shard", scatter_dimension=1, tiled=True),
        lax.psum_scatter(all_terms[9], "shard", scatter_dimension=1, tiled=True),
        lax.psum_scatter(all_terms[10], "shard", scatter_dimension=1, tiled=True),
        lax.psum_scatter(all_terms[11], "shard", scatter_dimension=1, tiled=True),
    )
    return (
        section_outputs,
        input_grads,
        summed[0],
        summed[1],
        summed[2],
        summed[3],
        summed[4],
        summed[5],
        summed[6],
        summed[7],
        summed[8],
        summed[9],
        summed[10],
        summed[11],
    )


MESH = pl.DeviceIdType.MESH
LIMIT = 60 << 20
CUBE = ("x", 4, 2, 1)
ALL = ("x", 8, 4, 2, 1)


def columns(n, wide):
    return pl.ds(pl.multiple_of(n * wide, wide), wide)


def remote(src, dst, send, recv, there):
    return pltpu.make_async_remote_copy(
        src_ref=src, dst_ref=dst, send_sem=send, recv_sem=recv, device_id=there, device_id_type=MESH
    )


class Hyper:
    def __init__(self, dims):
        sec = lax.axis_index("section")
        shd = lax.axis_index("shard")
        self.dims = dims
        self.partner, self.delta, self.pos = {}, {}, 0
        for n, d in enumerate(dims):
            weight = 1 << (len(dims) - 1 - n)
            if d == "x":
                bit = sec
                self.partner[d] = (1 - sec, shd)
            else:
                bit = lax.rem(shd // d, 2)
                self.partner[d] = (sec, shd + d * (1 - 2 * bit))
            self.pos = self.pos + bit * weight
            self.delta[d] = weight * (1 - 2 * bit)

    def at(self, order, offset):
        place = self.pos
        for j, d in enumerate(order):
            if offset >> j & 1:
                place = place + self.delta[d]
        return place

    def barrier(self, more=()):
        sem = pltpu.get_barrier_semaphore()
        partners = [self.partner[d] for d in self.dims] + list(more)
        for partner in partners:
            pl.semaphore_signal(sem, inc=1, device_id=partner, device_id_type=MESH)
        pl.semaphore_wait(sem, len(partners))


def cube_parts(rows, widths, col0=0):
    orders = (("x", 4, 2, 1), (4, 2, "x", 1), (2, "x", 4, 1))
    parts = []
    for width, order in zip(widths, orders):
        parts.append((0, rows, col0, width, order))
        col0 += width
    return tuple(parts)


class Gather:
    def __init__(self, h, parts, src, dst, send_sem, recv_sem):
        self.h, self.parts, self.src, self.dst = h, parts, src, dst
        self.send_sem, self.recv_sem = send_sem, recv_sem

    def copy(self, p, offset, j):
        r0, rn, c0, cn, order = self.parts[p]
        rows, cols = pl.ds(r0, rn), pl.ds(c0, cn)
        there = self.dst.at[self.h.at(order, offset), rows, cols]
        here = self.src.at[rows, cols] if offset == 0 else there
        n = offset | 1 << j
        return pltpu.make_async_remote_copy(
            src_ref=here,
            dst_ref=there,
            send_sem=self.send_sem.at[p, n],
            recv_sem=self.recv_sem.at[p, n],
            device_id=self.h.partner[order[j]],
            device_id_type=MESH,
        )

    def start(self, chosen):
        for j in range(len(self.h.dims)):
            for p in chosen:
                self.copy(p, 0, j).start()

    def forward(self, chosen):
        k = len(self.h.dims)
        for j in range(k):
            for low in range(1 << j):
                for p in chosen:
                    self.copy(p, low, j).wait_recv()
                    for later in range(j + 1, k):
                        self.copy(p, low | 1 << j, later).start()

    def finish(self):
        for p in range(len(self.parts)):
            for j in range(len(self.h.dims)):
                for low in range(1 << j):
                    self.copy(p, low, j).wait_send()


def gather_kernel(dims, parts, x_ref, o_ref, send_sem, recv_sem, local_sem):
    h = Hyper(dims)
    h.barrier()
    own = pltpu.make_async_copy(x_ref, o_ref.at[h.pos], local_sem)
    own.start()
    g = Gather(h, parts, x_ref, o_ref, send_sem, recv_sem)
    chosen = range(len(parts))
    g.start(chosen)
    g.forward(chosen)
    g.finish()
    own.wait()


def gather(x, dims, parts, collective_id, name):
    n = 1 << len(dims)
    return pl.pallas_call(
        functools.partial(gather_kernel, dims, parts),
        out_shape=jax.ShapeDtypeStruct((n,) + x.shape, x.dtype),
        in_specs=[pl.BlockSpec(memory_space=pl.ANY)],
        out_specs=pl.BlockSpec(memory_space=pl.ANY),
        scratch_shapes=[
            pltpu.SemaphoreType.DMA((len(parts), n)),
            pltpu.SemaphoreType.DMA((len(parts), n)),
            pltpu.SemaphoreType.DMA,
        ],
        compiler_params=pltpu.CompilerParams(
            collective_id=collective_id, has_side_effects=True, vmem_limit_bytes=LIMIT
        ),
        name=name,
    )(x)


class Reduce:
    def __init__(self, h, parts, src, buf, send_sem, recv_sem):
        self.h, self.parts, self.src, self.buf = h, parts, src, buf
        self.send_sem, self.recv_sem = send_sem, recv_sem

    def window(self, p):
        r0, rn, c0, cn, order = self.parts[p]
        return pl.ds(r0, rn), pl.ds(c0, cn)

    def held(self, p, j, offset):
        if j == len(self.h.dims) - 1:
            return self.src.at[(self.h.at(self.parts[p][4], offset),) + self.window(p)]
        return self.buf.at[((1 << (j + 1)) | offset,) + self.window(p)]

    def copy(self, p, j, low):
        n = (1 << j) | low
        return remote(
            self.held(p, j, low | 1 << j),
            self.buf.at[(n,) + self.window(p)],
            self.send_sem.at[p, n],
            self.recv_sem.at[p, n],
            self.h.partner[self.parts[p][4][j]],
        )

    def add(self, p, j, low, out=None):
        self.copy(p, j, low).wait_recv()
        r0, rn, c0, cn, order = self.parts[p]
        mine = self.held(p, j, low)
        came = self.buf.at[((1 << j) | low,) + self.window(p)]
        step = 16

        @pl.loop(0, rn // step)
        def _(i):
            rows = pl.ds(pl.multiple_of(i * step, step), step)
            total = mine[rows, :].astype(jnp.float32) + came[rows, :].astype(jnp.float32)
            if j > 0:
                came[rows, :] = total.astype(came.dtype)
            else:
                out[pl.ds(pl.multiple_of(r0 + i * step, step), step), pl.ds(c0, cn)] = total

        if j > 0 and low >> (j - 1) & 1:
            self.copy(p, j - 1, low ^ (1 << (j - 1))).start()

    def finish(self):
        for p in range(len(self.parts)):
            for j in range(len(self.h.dims)):
                for low in range(1 << j):
                    self.copy(p, j, low).wait_send()


def reduce_kernel(dims, all_parts, swapped, *refs):
    count = len(all_parts)
    xs, outs, bufs = refs[:count], refs[count : 2 * count], refs[2 * count : 3 * count]
    sems = refs[3 * count :]
    h = Hyper(dims)
    k = len(dims)
    sec, shd = lax.axis_index("section"), lax.axis_index("shard")
    other = (sec, shd + 8 * (1 - 2 * lax.rem(shd // 8, 2)))
    h.barrier((other,) if swapped else ())
    sums = [
        Reduce(h, parts, xs[n], bufs[n], sems[2 * n], sems[2 * n + 1])
        for n, parts in enumerate(all_parts)
    ]
    every = [(r, p, outs[n]) for n, r in enumerate(sums) for p in range(len(all_parts[n]))]
    for low in reversed(range(1 << (k - 1))):
        for r, p, _ in every:
            r.copy(p, k - 1, low).start()
    for j in reversed(range(k)):
        for low in reversed(range(1 << j)):
            for r, p, out in every:
                r.add(p, j, low, out)
    if swapped:
        sent, swap_send, swap_recv = sems[2 * count :]
        out = outs[-1]
        sent[0] = out[...].astype(sent.dtype)
        swap = remote(sent.at[0], sent.at[1], swap_send, swap_recv, other)
        swap.start()
        swap.wait()
        out[...] = sent[1].astype(jnp.float32)
    for r in sums:
        r.finish()


def reduce(xs, dims, all_parts, collective_id, name, swapped=False):
    n = 1 << len(dims)
    dma = pltpu.SemaphoreType.DMA
    vmem = pl.BlockSpec(memory_space=pltpu.VMEM)
    scratch = [pltpu.VMEM(x.shape, x.dtype) for x in xs]
    for parts in all_parts:
        scratch += [dma((len(parts), n))] * 2
    if swapped:
        scratch += [pltpu.VMEM((2,) + xs[-1].shape[1:], xs[-1].dtype), dma, dma]
    return pl.pallas_call(
        functools.partial(reduce_kernel, dims, all_parts, swapped),
        out_shape=[jax.ShapeDtypeStruct(x.shape[1:], jnp.float32) for x in xs],
        in_specs=[vmem] * len(xs),
        out_specs=[vmem] * len(xs),
        scratch_shapes=scratch,
        compiler_params=pltpu.CompilerParams(
            collective_id=collective_id, has_side_effects=True, vmem_limit_bytes=LIMIT
        ),
        name=name,
    )(*xs)


def block_of(sec, shd):
    return 8 * lax.rem(sec + lax.rem(shd, 2), 2) + lax.rem(shd, 8)


def half_group(sec, shd):
    first = 8 * (shd // 8)
    return 8 * sec + lax.rem(shd, 8), lambda n: (n // 8, first + lax.rem(n, 8))


def half_barrier(me, place, sec, shd):
    sem = pltpu.get_barrier_semaphore()

    @pl.loop(1, 16)
    def _(d):
        pl.semaphore_signal(
            sem, inc=1, device_id=place(lax.rem(me + d, 16)), device_id_type=MESH
        )

    across = shd + 8 * (1 - 2 * (shd // 8))
    for s in range(2):
        pl.semaphore_signal(sem, inc=1, device_id=(s, across), device_id_type=MESH)
    pl.semaphore_wait(sem, 17)


class Spread:
    def __init__(self, pieces, own_sem, send, recv):
        self.sec, self.shd = lax.axis_index("section"), lax.axis_index("shard")
        self.me, self.place = half_group(self.sec, self.shd)
        self.pieces, self.own_sem, self.send, self.recv = pieces, own_sem, send, recv

    def barrier(self):
        half_barrier(self.me, self.place, self.sec, self.shd)

    def copies(self, d):
        there = self.place(lax.rem(self.me + d, 16))
        return [
            remote(src, dst, self.send.at[n, d], self.recv.at[n, d], there)
            for n, (src, dst) in enumerate(self.pieces(*there))
        ]

    def own(self):
        return [
            pltpu.make_async_copy(src, dst, self.own_sem.at[n])
            for n, (src, dst) in enumerate(self.pieces(self.sec, self.shd))
        ]

    def start(self):
        @pl.loop(1, 16)
        def _(d):
            for one in self.copies(d):
                one.start()

        for one in self.own():
            one.start()

    def wait(self):
        @pl.loop(1, 16)
        def _(d):
            for one in self.copies(d):
                one.wait_recv()

        @pl.loop(1, 16)
        def _(d):
            for one in self.copies(d):
                one.wait_send()

        for one in self.own():
            one.wait()


def everyone_barrier(me):
    sem = pltpu.get_barrier_semaphore()

    @pl.loop(1, 32)
    def _(d):
        there = lax.rem(me + d, 32)
        pl.semaphore_signal(
            sem, inc=1, device_id=(there // 16, lax.rem(there, 16)), device_id_type=MESH
        )

    pl.semaphore_wait(sem, 31)


def fetch_kernel(block, mix, out, exp, con, shared, wq, wo, we, wc, *sems):
    q_send, q_recv, send, recv, con_send, con_recv, out_send, out_recv, own_sem, sh_send, sh_recv = sems
    sec, shd = lax.axis_index("section"), lax.axis_index("shard")
    low, half = lax.rem(shd, 8), shd // 8
    me = 16 * sec + shd
    everyone_barrier(me)
    h = Hyper(ALL)
    g = Gather(h, SMALL, block, shared, sh_send, sh_recv)
    g.start(range(3))

    def query(d):
        there = lax.rem(me + d, 32)
        ts, tj = there // 16, lax.rem(there, 16)
        return remote(
            mix.at[:, columns(block_of(ts, tj), HD)], wq.at[sec, shd], q_send.at[d], q_recv.at[d], (ts, tj)
        )

    @pl.loop(1, 32)
    def _(d):
        query(d).start()

    to_x = lax.rem(half + lax.rem(shd, 2), 2)
    from_half = lax.rem(sec + lax.rem(shd, 2), 2)
    own_out = pltpu.make_async_copy(out, wo.at[sec], own_sem.at[5])
    for z in range(2):
        mine = jnp.logical_and(to_x == sec, half == z)
        there = remote(out, wo.at[sec], out_send.at[z], out_recv.at[sec], (to_x, 8 * z + low))

        @pl.when(mine)
        def _():
            own_out.start()

        @pl.when(jnp.logical_not(mine))
        def _():
            there.start()

    own = [
        pltpu.make_async_copy(block, shared.at[h.pos], own_sem.at[2]),
        pltpu.make_async_copy(mix.at[:, columns(block_of(sec, shd), HD)], wq.at[sec, shd], own_sem.at[3]),
        pltpu.make_async_copy(con.at[pl.ds(256 * sec, 256)], wc.at[sec], own_sem.at[4]),
    ]
    for one in own:
        one.start()

    def pieces(ts, tj):
        for n in range(2):
            yield (
                exp.at[:, columns(2 * (8 * n + lax.rem(tj, 8)) + ts, 256)],
                we.at[sec, low, :, pl.ds(256 * n, 256)],
            )

    spread = Spread(pieces, own_sem, send, recv)
    spread.start()
    rows = remote(con.at[pl.ds(256 * (1 - sec), 256)], wc.at[sec], con_send, con_recv, (1 - sec, shd))
    rows.start()
    g.forward(range(3))

    @pl.loop(1, 32)
    def _(d):
        query(d).wait_recv()

    for s in range(2):
        mine = jnp.logical_and(sec == s, from_half == half)

        @pl.when(jnp.logical_not(mine))
        def _():
            remote(out, wo.at[s], out_send.at[0], out_recv.at[s], (1 - sec, shd)).wait_recv()

    spread.wait()
    remote(con.at[pl.ds(0, 256)], wc.at[1 - sec], con_send, con_recv, (1 - sec, shd)).wait_recv()
    rows.wait_send()

    @pl.loop(1, 32)
    def _(d):
        query(d).wait_send()

    for z in range(2):
        mine = jnp.logical_and(to_x == sec, half == z)
        there = remote(out, wo.at[sec], out_send.at[z], out_recv.at[sec], (to_x, 8 * z + low))

        @pl.when(mine)
        def _():
            own_out.wait()

        @pl.when(jnp.logical_not(mine))
        def _():
            there.wait_send()

    g.finish()
    for one in own:
        one.wait()


def fetch_weights(block, mix, out, exp, con):
    bf16 = jnp.bfloat16
    dma = pltpu.SemaphoreType.DMA
    return pl.pallas_call(
        fetch_kernel,
        out_shape=(
            jax.ShapeDtypeStruct((32,) + block.shape, bf16),
            jax.ShapeDtypeStruct((2, 16, 128, HD), bf16),
            jax.ShapeDtypeStruct((2, 128, D), bf16),
            jax.ShapeDtypeStruct((2, 8, 128, 512), bf16),
            jax.ShapeDtypeStruct((2, 256, D), bf16),
        ),
        in_specs=[pl.BlockSpec(memory_space=pl.ANY)] * 5,
        out_specs=[pl.BlockSpec(memory_space=pl.ANY)] * 5,
        scratch_shapes=[
            dma((32,)),
            dma((32,)),
            dma((2, 16)),
            dma((2, 16)),
            dma,
            dma,
            dma((2,)),
            dma((2,)),
            dma((6,)),
            dma((3, 32)),
            dma((3, 32)),
        ],
        compiler_params=pltpu.CompilerParams(
            collective_id=1, has_side_effects=True, vmem_limit_bytes=LIMIT
        ),
        name="fetch_weights",
    )(block, mix, out, exp, con)


def return_kernel(gq, ge, go, gc, rq, re, ro, rc, *sems):
    send, recv, con_send, con_recv, out_send, out_recv, own_sem = sems
    sec, shd = lax.axis_index("section"), lax.axis_index("shard")
    me, place = half_group(sec, shd)
    half_barrier(me, place, sec, shd)
    low, half = lax.rem(shd, 8), shd // 8
    f = block_of(sec, shd)

    def pieces(ts, tj):
        tlow = lax.rem(tj, 8)
        yield gq.at[ts, tlow], rq.at[:, columns(f, HD)]
        for h in range(2):
            yield (
                ge.at[ts, tlow, :, pl.ds(256 * h, 256)],
                re.at[:, columns(2 * (8 * h + low) + sec, 256)],
            )

    def spread(d):
        there = place(lax.rem(me + d, 16))
        return [
            remote(src, dst, send.at[n, d], recv.at[n, d], there)
            for n, (src, dst) in enumerate(pieces(*there))
        ]

    @pl.loop(1, 16)
    def _(d):
        for one in spread(d):
            one.start()

    own = [
        pltpu.make_async_copy(src, dst, own_sem.at[n])
        for n, (src, dst) in enumerate(pieces(sec, shd))
    ]
    own.append(pltpu.make_async_copy(gc.at[sec], rc.at[pl.ds(256 * sec, 256)], own_sem.at[3]))
    for one in own:
        one.start()
    rows = remote(gc.at[1 - sec], rc.at[pl.ds(256 * sec, 256)], con_send, con_recv, (1 - sec, shd))
    rows.start()

    own_out = pltpu.make_async_copy(go.at[sec], ro.at[half], own_sem.at[4])
    for s in range(2):
        mine = jnp.logical_and(sec == s, f == shd)
        there = remote(go.at[s], ro.at[half], out_send.at[s], out_recv.at[half], (s, f))

        @pl.when(mine)
        def _():
            own_out.start()

        @pl.when(jnp.logical_not(mine))
        def _():
            there.start()

    @pl.loop(1, 16)
    def _(d):
        for one in spread(d):
            one.wait_recv()

    remote(gc.at[0], rc.at[pl.ds(256 * (1 - sec), 256)], con_send, con_recv, (1 - sec, shd)).wait_recv()
    for z in range(2):
        mine = jnp.logical_and(f == shd, half == z)

        @pl.when(jnp.logical_not(mine))
        def _():
            remote(go.at[0], ro.at[z], out_send.at[0], out_recv.at[z], (1 - sec, shd)).wait_recv()

    @pl.loop(1, 16)
    def _(d):
        for one in spread(d):
            one.wait_send()

    rows.wait_send()
    for s in range(2):
        mine = jnp.logical_and(sec == s, f == shd)
        there = remote(go.at[s], ro.at[half], out_send.at[s], out_recv.at[half], (s, f))

        @pl.when(mine)
        def _():
            own_out.wait()

        @pl.when(jnp.logical_not(mine))
        def _():
            there.wait_send()

    for one in own:
        one.wait()


def return_grads(gq, ge, go, gc):
    bf16 = jnp.bfloat16
    dma = pltpu.SemaphoreType.DMA
    return pl.pallas_call(
        return_kernel,
        out_shape=(
            jax.ShapeDtypeStruct((128, D), bf16),
            jax.ShapeDtypeStruct((128, 8192), bf16),
            jax.ShapeDtypeStruct((2, 128, D), bf16),
            jax.ShapeDtypeStruct((512, D), bf16),
        ),
        in_specs=[pl.BlockSpec(memory_space=pl.ANY)] * 4,
        out_specs=[pl.BlockSpec(memory_space=pl.ANY)] * 4,
        scratch_shapes=[dma((3, 16)), dma((3, 16)), dma, dma, dma((2,)), dma((2,)), dma((5,))],
        compiler_params=pltpu.CompilerParams(
            collective_id=2, has_side_effects=True, vmem_limit_bytes=LIMIT
        ),
        name="return_grads",
    )(gq, ge, go, gc)


HALVES = [[n, n + 8] for n in range(8)]


def from_halves(x):
    return lax.all_gather(x, "shard", axis=0, tiled=True, axis_index_groups=HALVES)


def with_other(x, came):
    mine = lax.dynamic_index_in_dim(x, lax.axis_index("shard") // 8, 0, keepdims=False)
    return (mine.astype(jnp.float32) + came.astype(jnp.float32)).astype(x.dtype)


def to_halves(x):
    return lax.psum_scatter(x, "shard", scatter_dimension=0, tiled=True, axis_index_groups=HALVES)


NT = (((1,), (1,)), ((), ()))
TN = (((0,), (0,)), ((), ()))


def dot32(a, b):
    return jnp.dot(a, b, preferred_element_type=jnp.float32)


def dot_nt(a, b):
    return lax.dot_general(a, b, NT, preferred_element_type=jnp.float32)


def dot_tn(a, b):
    return lax.dot_general(a, b, TN, preferred_element_type=jnp.float32)


EVEN = cube_parts(128, (768, 640, 640))
LIGHT = cube_parts(128, (896, 896, 256))
TRIO = ("x", 4, 2)
CHUNK = 64


def spaced(many, few):
    result = []
    for n, step in enumerate(many):
        result.append(step)
        done = len(few) * (n + 1) // len(many)
        result.extend(few[len(few) * n // len(many) : done])
    return result


def chunk_gather_steps(g, count):
    k = len(g.h.dims)

    def step(j, low):
        for p in range(count):
            g.copy(p, low, j).wait_recv()
            for later in range(j + 1, k):
                g.copy(p, low | 1 << j, later).start()

    return [functools.partial(step, j, low) for j in range(k) for low in range(1 << j)]


def chunk_reduce_steps(r, out):
    k = len(r.h.dims)
    return [
        functools.partial(r.add, p, j, low, out)
        for j in reversed(range(k))
        for low in reversed(range(1 << j))
        for p in range(len(r.parts))
    ]


GELU_K = (2.0 / 3.141592653589793) ** 0.5


def gelu_pair(u):
    square = u * u
    t = jnp.tanh(GELU_K * (u + 0.044715 * u * square))
    half = 0.5 * (1.0 + t)
    slope = half + 0.5 * u * (1.0 - t * t) * (GELU_K * (1.0 + 3 * 0.044715 * square))
    return u * half, slope


def hidden_kernel(back, plan, *refs):
    if back:
        x_ref, we_hbm, wc_hbm, slope_hbm, act_hbm, n2_hbm, o_ref, dc_out, de_out, be_ref = refs[:10]
        act_all, n2_all, d_tile = refs[10:13]
        scratch = refs[13:]
    else:
        x_ref, we_hbm, wc_hbm, be_ref, o_ref, x_out, h_out, slope_out = refs[:8]
        scratch = refs[8:]
    x_all, we, wc, h_all, slope, part, came, buf = scratch[:8]
    g_send, g_recv, c_send, c_recv, r_send, r_recv, own_sem, load_sem, out_sem = scratch[8:]
    h = Hyper(CUBE)
    trio = Hyper(TRIO)
    h.barrier()
    loads = [pltpu.make_async_copy(we_hbm, we, load_sem.at[0]), pltpu.make_async_copy(wc_hbm, wc, load_sem.at[1])]
    if back:
        loads.append(pltpu.make_async_copy(slope_hbm, slope, load_sem.at[2]))
        late = [
            pltpu.make_async_copy(act_hbm, act_all, load_sem.at[3]),
            pltpu.make_async_copy(n2_hbm, n2_all, load_sem.at[4]),
        ]
    parts = tuple((0, CHUNK, c0, cn, order) for _, _, c0, cn, order in plan)
    gathers, sums = [], []
    for n in range(2):
        mine = x_ref.at[pl.ds(CHUNK * n, CHUNK)]
        own = pltpu.make_async_copy(mine, x_all.at[n, h.pos], own_sem.at[n])
        own.start()
        loads.append(own)
        gathers.append(Gather(h, parts, mine, x_all.at[n], g_send.at[n], g_recv.at[n]))
        sums.append(
            Reduce(
                trio,
                tuple((0, CHUNK, c0, cn, order[:3]) for _, _, c0, cn, order in plan),
                came.at[n],
                buf.at[n],
                r_send.at[n],
                r_recv.at[n],
            )
        )
        gathers[n].start(range(len(plan)))
    for one in loads[:-2]:
        one.start()
    core = 1 - lax.rem(lax.axis_index("shard"), 2)

    def quad(r):
        return 4 * (h.pos // 4) + (h.delta["x"] if r & 2 else 0) + (h.delta[4] if r & 1 else 0)

    def pair(r, y):
        return quad(r) + 2 * (lax.rem(h.pos, 4) // 2) + (h.delta[2] if y else 0)

    def compute(n, r):
        four = pl.ds(quad(r), 4)
        x = x_all[n, four].reshape(4 * CHUNK, D)
        if back:
            inner = dot_nt(x, wc[...]).reshape(4, CHUNK, 512)
            mid = (inner * slope[n, four].astype(jnp.float32)).astype(jnp.bfloat16)
        else:
            inner = dot32(x, we[...]) + be_ref[...]
            act, grad = gelu_pair(inner)
            mid = act.astype(jnp.bfloat16).reshape(4, CHUNK, 512)
            slope[n, four] = grad.astype(jnp.bfloat16).reshape(4, CHUNK, 512)
        h_all[n, four] = mid
        mid = mid.reshape(4 * CHUNK, 512)
        if back:
            be_ref[...] += jnp.sum(mid.astype(jnp.float32), axis=0, keepdims=True)
        for c in range(4):
            cols = pl.ds(512 * c, 512)
            tile = dot_nt(mid, we[cols, :]) if back else dot32(mid, wc[:, cols])
            part[n, four, :, cols] = tile.astype(jnp.bfloat16).reshape(4, CHUNK, 512)
        for y in reversed(range(2)):
            core_copy(n, r, y).start()

    def core_copy(n, r, y):
        at = pair(r, y)
        return remote(
            part.at[n, at + core],
            came.at[n, at // 2],
            c_send.at[n, 2 * r + y],
            c_recv.at[n, 2 * r + y],
            h.partner[1],
        )

    def core_add(n, r):
        for y in reversed(range(2)):
            core_copy(n, r, y).wait_recv()
            at = pair(r, y)

            @pl.loop(0, CHUNK // 16)
            def _(i):
                rows = pl.ds(pl.multiple_of(i * 16, 16), 16)
                total = part[n, at + 1 - core, rows, :].astype(jnp.float32) + came[
                    n, at // 2, rows, :
                ].astype(jnp.float32)
                came[n, at // 2, rows, :] = total.astype(jnp.bfloat16)

            offset = ((r >> 1) & 1, r & 1, y)
            for p, (_, _, _, _, order) in enumerate(sums[n].parts):
                bits = [offset[TRIO.index(d)] for d in order]
                if bits[2]:
                    sums[n].copy(p, 2, bits[0] | bits[1] << 1).start()

    def compute_steps(n):
        steps = []
        for r in (3, 2, 1, 0):
            steps.append(functools.partial(compute, n, r))
            if r < 3:
                steps.append(functools.partial(core_add, n, r + 1))
        return steps + [functools.partial(core_add, n, 0)]

    for step in chunk_gather_steps(gathers[0], len(plan)):
        step()
    for one in loads:
        one.wait()
    if back:
        for one in late:
            one.start()
        be_ref[...] = jnp.zeros_like(be_ref)

    tiles = []

    def product(left, right, c, n, dst, slot):
        if len(tiles) >= 2:
            tiles[-2].wait()
        if left is act_all:
            x = right[:, :, :, pl.ds(512 * c, 512)].reshape(D, 512)
            d_tile[slot] = dot_tn(left[...].reshape(D, 512), x).astype(jnp.bfloat16)
        else:
            x = left[:, :, :, pl.ds(512 * c, 512)].reshape(D, 512)
            d_tile[slot] = dot_tn(x, right[...].reshape(D, 512)).astype(jnp.bfloat16)
        tiles.append(pltpu.make_async_copy(d_tile.at[slot], dst, out_sem.at[slot]))
        tiles[-1].start()

    for step in spaced(chunk_gather_steps(gathers[1], len(plan)), compute_steps(0)):
        step()
    out_rows = [o_ref.at[pl.ds(CHUNK * n, CHUNK)] for n in range(2)]
    first = chunk_reduce_steps(sums[0], out_rows[0])
    outs = []
    if back:
        wait_late = [one.wait for one in late]
        of_wc = [
            functools.partial(product, act_all, x_all, c, n, dc_out.at[:, pl.ds(512 * c, 512)], c % 2)
            for n, c in enumerate(range(4))
        ]
        of_we = [
            functools.partial(product, n2_all, h_all, c, n, de_out.at[pl.ds(512 * c, 512)], c % 2)
            for n, c in enumerate(range(4))
        ]
    else:
        outs = [pltpu.make_async_copy(x_all, x_out, out_sem.at[0])]
        outs[0].start()
    for step in spaced(first, compute_steps(1)):
        step()
    last_steps = chunk_reduce_steps(sums[1], out_rows[1])
    if back:
        last_steps = spaced(last_steps, wait_late + of_wc + of_we)
    else:
        outs.append(pltpu.make_async_copy(h_all, h_out, out_sem.at[1]))
        outs.append(pltpu.make_async_copy(slope, slope_out, out_sem.at[2]))
        for one in outs[1:]:
            one.start()
    for step in last_steps:
        step()
    outs += tiles[-2:]
    for n in range(2):
        gathers[n].finish()
        sums[n].finish()
        for r in range(4):
            for y in range(2):
                core_copy(n, r, y).wait_send()
    for one in outs:
        one.wait()


def hidden_layer(back, x, we, wc, rest, plan, collective_id, name):
    bf16, f32 = jnp.bfloat16, jnp.float32
    dma = pltpu.SemaphoreType.DMA
    hbm, vmem = pl.BlockSpec(memory_space=pl.ANY), pl.BlockSpec(memory_space=pltpu.VMEM)
    wide, narrow = (2, 16, CHUNK, D), (2, 16, CHUNK, 512)
    out = [jax.ShapeDtypeStruct((128, D), f32)]
    more = []
    if back:
        out += [
            jax.ShapeDtypeStruct((512, D), bf16),
            jax.ShapeDtypeStruct((D, 512), bf16),
            jax.ShapeDtypeStruct((1, 512), f32),
        ]
        out_specs = [vmem, hbm, hbm, vmem]
        more = [pltpu.VMEM(narrow, bf16), pltpu.VMEM(wide, bf16), pltpu.VMEM((2, 512, 512), bf16)]
    else:
        out += [
            jax.ShapeDtypeStruct(wide, bf16),
            jax.ShapeDtypeStruct(narrow, bf16),
            jax.ShapeDtypeStruct(narrow, bf16),
        ]
        out_specs = [vmem, hbm, hbm, hbm]
    return pl.pallas_call(
        functools.partial(hidden_kernel, back, plan),
        out_shape=out,
        in_specs=[hbm, hbm, hbm] + ([hbm] * 3 if back else [vmem]),
        out_specs=out_specs,
        scratch_shapes=more
        + [
            pltpu.VMEM(wide, bf16),
            pltpu.VMEM((D, 512), bf16),
            pltpu.VMEM((512, D), bf16),
            pltpu.VMEM(narrow, bf16),
            pltpu.VMEM(narrow, bf16),
            pltpu.VMEM(wide, bf16),
            pltpu.VMEM((2, 8, CHUNK, D), bf16),
            pltpu.VMEM((2, 8, CHUNK, D), bf16),
            dma((2, 3, 16)),
            dma((2, 3, 16)),
            dma((2, 8)),
            dma((2, 8)),
            dma((2, 3, 8)),
            dma((2, 3, 8)),
            dma((2,)),
            dma((5,)),
            dma((3,)),
        ],
        compiler_params=pltpu.CompilerParams(
            collective_id=collective_id, has_side_effects=True, vmem_limit_bytes=LIMIT
        ),
        name=name,
    )(x, we, wc, *rest)


QB = 256
KB = WINDOW + QB
SCALE = HD ** (-0.5)
NEAR = (2, 4, "x")


def kept_pairs(lo, a):
    key = a + lax.broadcasted_iota(jnp.int32, (KB, QB), 0)
    last = a + WINDOW + lax.broadcasted_iota(jnp.int32, (KB, QB), 1)
    return (key >= lo) & (key <= last)


class PairSum:
    def __init__(self, h, trio, plan, part, came, buf, sems):
        self.c_send, self.c_recv, r_send, r_recv = sems
        self.h, self.trio, self.part, self.came = h, trio, part, came
        parts = tuple((0, 128, c0, cn, order[:3]) for _, _, c0, cn, order in plan)
        self.sums = Reduce(trio, parts, came, buf, r_send, r_recv)
        self.core = lax.rem(lax.axis_index("shard"), 2)

    def pair(self, o):
        return self.trio.at(NEAR, o)

    def core_copy(self, o):
        n = self.pair(o)
        return remote(
            self.part.at[2 * n + 1 - self.core],
            self.came.at[n],
            self.c_send.at[o],
            self.c_recv.at[o],
            self.h.partner[1],
        )

    def core_add(self, o):
        self.core_copy(o).wait_recv()
        n = self.pair(o)

        @pl.loop(0, 8)
        def _(i):
            rows = pl.ds(pl.multiple_of(i * 16, 16), 16)
            total = self.part[2 * n + self.core, rows, :].astype(jnp.float32) + self.came[
                n, rows, :
            ].astype(jnp.float32)
            self.came[n, rows, :] = total.astype(jnp.bfloat16)

        for p, (_, _, _, _, order) in enumerate(self.sums.parts):
            bits = [o >> NEAR.index(d) & 1 for d in order]
            if bits[2]:
                self.sums.copy(p, 2, bits[0] | bits[1] << 1).start()

    def schedule(self, compute, out, lag=2):
        steps, waiting, made = [], [], []
        for n, o in enumerate(range(7, -1, -1)):
            steps.append(functools.partial(compute, o))
            if n:
                steps.append(functools.partial(self.core_add, o + 1))
                made.append(o + 1)
            for p, (_, _, _, _, order) in enumerate(self.sums.parts):
                for low in range(4):
                    own = sum((low >> b & 1) << NEAR.index(order[b]) for b in range(2))
                    if own in made and made.index(own) <= len(made) - 1 - lag and (p, low) not in waiting:
                        waiting.append((p, low))
                        steps.append(functools.partial(self.sums.add, p, 2, low, out))
        steps.append(functools.partial(self.core_add, 0))
        rest = [
            functools.partial(self.sums.add, p, j, low, out)
            for j in reversed(range(3))
            for low in reversed(range(1 << j))
            for p in range(len(self.sums.parts))
            if j < 2 or (p, low) not in waiting
        ]
        return steps, rest

    def finish(self):
        self.sums.finish()
        for o in range(8):
            self.core_copy(o).wait_send()


def pair_gather_steps(g, used):
    def number(o, order):
        return sum((o >> NEAR.index(d) & 1) << n for n, d in enumerate(order[:3]))

    def link(j, low):
        for p in range(len(g.parts)):
            g.copy(p, low, j).wait_recv()
            for later in range(j + 1, 4):
                g.copy(p, low | 1 << j, later).start()

    def pair(o):
        for p, part in enumerate(g.parts):
            g.copy(p, number(o, part[4]), 3).wait_recv()
        used(o)

    steps = []
    for j in range(3):
        for low in range(1 << j):
            steps.append(functools.partial(link, j, low))
            for o in range(8):
                if max(1, *[number(o, part[4]) for part in g.parts]) == low | 1 << j:
                    steps.append(functools.partial(pair, o))
    return steps


def attend_kernel(plan, *refs):
    ins, refs = refs[:8], refs[8:]
    x_ref, kv_ref, wq_hbm, wkv_hbm, wo_hbm, bq_ref, bkv_ref, lo_ref = ins
    o_ref, x_out, q_out, kv_out, mixed_out, lse_ref = refs[:6]
    refs = refs[6:]
    x_all, wq, wkv, wo, far, far_all, q_all, kv_all, mixed, part, came, buf = refs[:12]
    g_send, g_recv, k_send, k_recv, swap_send, swap_recv, own_sem, load_sem, out_sem = refs[12:21]
    pair_sems = refs[21:]
    h, trio = Hyper(CUBE), Hyper(TRIO)
    sec, shd = lax.axis_index("section"), lax.axis_index("shard")
    other = (sec, shd + 8 * (1 - 2 * (shd // 8)))
    h.barrier((other,))
    swap = remote(kv_ref, far, swap_send, swap_recv, other)
    swap.start()
    loads = [
        pltpu.make_async_copy(x_ref, x_all.at[h.pos], own_sem),
        pltpu.make_async_copy(wq_hbm, wq, load_sem.at[0]),
        pltpu.make_async_copy(wkv_hbm, wkv, load_sem.at[1]),
        pltpu.make_async_copy(wo_hbm, wo, load_sem.at[2]),
    ]
    for one in loads:
        one.start()
    g = Gather(h, plan, x_ref, x_all, g_send, g_recv)
    g.start(range(len(plan)))
    swap.wait_recv()
    far_all[h.pos] = far[...]
    gkv = Gather(h, ((0, 128, 0, 2 * HD, CUBE),), far, far_all, k_send, k_recv)
    gkv.start(range(1))
    for one in loads:
        one.wait()
    sums = PairSum(h, trio, plan, part, came, buf, pair_sems)

    def project(o):
        n = sums.pair(o)
        x = x_all[pl.ds(2 * n, 2)].reshape(QB, D)
        q_all[n] = (dot32(x, wq[...]) + bq_ref[...]).astype(jnp.bfloat16)
        at = pl.ds(pl.multiple_of(WINDOW + QB * lax.rem(n, 4), QB), QB)
        kv_all[n // 4, at] = (dot32(x, wkv[...]) + bkv_ref[...]).astype(jnp.bfloat16)

    far_steps = chunk_gather_steps(gkv, 1)
    for step in spaced(pair_gather_steps(g, project), far_steps):
        step()
    kv_all[:, :WINDOW] = far_all[...].reshape(2, WINDOW, 2 * HD)

    def compute(o):
        n = sums.pair(o)
        m, a = n // 4, pl.multiple_of(QB * lax.rem(n, 4), QB)
        keys = pl.ds(a, KB)
        s = dot_nt(kv_all[m, keys, :HD], q_all[n]) * SCALE
        s = jnp.where(kept_pairs(lo_ref[n], a), s, -1e30)
        top = jnp.max(s, axis=0, keepdims=True)
        e = jnp.exp(s - top)
        total = jnp.sum(e, axis=0, keepdims=True)
        probs = (e * (1.0 / total)).astype(jnp.bfloat16)
        mix = dot_tn(probs, kv_all[m, keys, HD:]).astype(jnp.bfloat16)
        mixed[n] = mix
        lse_ref[n] = top + jnp.log(total)
        for c in range(4):
            cols = pl.ds(512 * c, 512)
            part[pl.ds(2 * n, 2), :, cols] = (
                dot32(mix, wo[:, cols]).astype(jnp.bfloat16).reshape(2, 128, 512)
            )
        sums.core_copy(o).start()

    outs = [
        pltpu.make_async_copy(x_all, x_out, out_sem.at[0]),
        pltpu.make_async_copy(q_all, q_out, out_sem.at[1]),
        pltpu.make_async_copy(kv_all, kv_out, out_sem.at[2]),
    ]
    for one in outs:
        one.start()
    steps, rest = sums.schedule(compute, o_ref)
    for step in steps:
        step()
    outs.append(pltpu.make_async_copy(mixed, mixed_out, out_sem.at[3]))
    outs[-1].start()
    for step in rest:
        step()
    g.finish()
    gkv.finish()
    swap.wait_send()
    sums.finish()
    for one in outs:
        one.wait()


def attend_layer(x, kv, wq, wkv, wo, bq, bkv, lo, plan, collective_id):
    bf16, f32 = jnp.bfloat16, jnp.float32
    dma = pltpu.SemaphoreType.DMA
    hbm, vmem = pl.BlockSpec(memory_space=pl.ANY), pl.BlockSpec(memory_space=pltpu.VMEM)
    out = [
        jax.ShapeDtypeStruct((128, D), f32),
        jax.ShapeDtypeStruct((16, 128, D), bf16),
        jax.ShapeDtypeStruct((8, QB, HD), bf16),
        jax.ShapeDtypeStruct((2, 2 * WINDOW, 2 * HD), bf16),
        jax.ShapeDtypeStruct((8, QB, HD), bf16),
        jax.ShapeDtypeStruct((8, 1, QB), f32),
    ]
    out_specs = [vmem, hbm, hbm, hbm, hbm, vmem]
    return pl.pallas_call(
        functools.partial(attend_kernel, plan),
        out_shape=out,
        in_specs=[hbm] * 5 + [vmem] * 3,
        out_specs=out_specs,
        scratch_shapes=[
            pltpu.VMEM((16, 128, D), bf16),
            pltpu.VMEM((D, HD), bf16),
            pltpu.VMEM((D, 2 * HD), bf16),
            pltpu.VMEM((HD, D), bf16),
            pltpu.VMEM((128, 2 * HD), bf16),
            pltpu.VMEM((16, 128, 2 * HD), bf16),
            pltpu.VMEM((8, QB, HD), bf16),
            pltpu.VMEM((2, 2 * WINDOW, 2 * HD), bf16),
            pltpu.VMEM((8, QB, HD), bf16),
            pltpu.VMEM((16, 128, D), bf16),
            pltpu.VMEM((8, 128, D), bf16),
            pltpu.VMEM((8, 128, D), bf16),
            dma((3, 16)),
            dma((3, 16)),
            dma((1, 16)),
            dma((1, 16)),
            dma,
            dma,
            dma,
            dma((3,)),
            dma((4,)),
            dma((8,)),
            dma((8,)),
            dma((3, 8)),
            dma((3, 8)),
        ],
        compiler_params=pltpu.CompilerParams(
            collective_id=collective_id, has_side_effects=True, vmem_limit_bytes=LIMIT
        ),
        name="attend",
    )(x, kv, wq, wkv, wo, bq, bkv, lo)


def attend_back_kernel(plan, *refs):
    x_ref, n1_hbm, wq_hbm, wo_hbm, q_hbm, kv_hbm, mixed_hbm, lse_ref, lo_ref, gc, ge = refs[:11]
    o_ref, own_ref, far_ref, wo_ref, wq_ref, bq_ref, rc, re = refs[11:19]
    x_all, n1, wq, wo, q_all, kv_all, mixed, dq_all, g_all, dk, dv, part, came, buf = refs[19:33]
    kv_parts, kv_bufs, sent = refs[33:35], refs[35:37], refs[37]
    g_send, g_recv, swap_send, swap_recv, own_sem, load_sem, bg_send, bg_recv = refs[38:46]
    pair_sems, kv_sems = refs[46:50], refs[50:54]
    h, trio = Hyper(CUBE), Hyper(TRIO)
    sec, shd = lax.axis_index("section"), lax.axis_index("shard")
    half = shd // 8
    other = (sec, shd + 8 * (1 - 2 * half))
    h.barrier((other,))

    def beside(n):
        if n < 8:
            rows = pl.ds(32 * n, 32)
            src, dst = gc.at[1 - half, rows], rc.at[rows]
        else:
            rows = pl.ds(128 * (n - 8), 128)
            src, dst = ge.at[1 - half, rows], re.at[rows]
        return remote(src, dst, bg_send.at[n], bg_recv.at[n], other)

    pending = list(range(16))

    def feed(steps, every):
        for n, step in enumerate(steps):
            step()
            if pending and n % every == 0:
                beside(pending.pop(0)).start()

    own = pltpu.make_async_copy(x_ref, x_all.at[h.pos], own_sem)
    own.start()
    g = Gather(h, plan, x_ref, x_all, g_send, g_recv)
    g.start(range(len(plan)))
    pairs = ((wq_hbm, wq), (wo_hbm, wo), (q_hbm, q_all), (kv_hbm, kv_all), (mixed_hbm, mixed), (n1_hbm, n1))
    loads = [pltpu.make_async_copy(src, dst, load_sem.at[n]) for n, (src, dst) in enumerate(pairs)]
    for one in loads:
        one.start()
    own.wait()
    for one in loads[:5]:
        one.wait()
    sums = PairSum(h, trio, plan, part, came, buf, pair_sems)

    def project(o):
        n = sums.pair(o)
        g_all[n] = dot_nt(x_all[pl.ds(2 * n, 2)].reshape(QB, D), wo[...]).astype(jnp.bfloat16)

    feed(pair_gather_steps(g, project), 3)
    bq_ref[...] = jnp.zeros_like(bq_ref)

    def compute(o):
        n = sums.pair(o)
        m, a = n // 4, pl.multiple_of(QB * lax.rem(n, 4), QB)
        keys = pl.ds(a, KB)
        if o % 4 == 3:
            dk[...] = jnp.zeros_like(dk)
            dv[...] = jnp.zeros_like(dv)
        q, gm, k = q_all[n], g_all[n], kv_all[m, keys, :HD]
        s = dot_nt(k, q) * SCALE
        probs = jnp.where(kept_pairs(lo_ref[n], a), jnp.exp(s - lse_ref[n]), 0.0)
        gp = dot_nt(kv_all[m, keys, HD:], gm)
        row = jnp.sum(probs * gp, axis=0, keepdims=True)
        gs = (probs * (gp - row)).astype(jnp.bfloat16)
        dq = (dot_tn(gs, k) * SCALE).astype(jnp.bfloat16)
        dq_all[n] = dq
        bq_ref[...] += jnp.sum(dq.astype(jnp.float32), axis=0, keepdims=True)
        for c in range(4):
            rows = pl.ds(512 * c, 512)
            part[pl.ds(2 * n, 2), :, rows] = (
                dot_nt(dq, wq[rows, :]).astype(jnp.bfloat16).reshape(2, 128, 512)
            )
        sums.core_copy(o).start()
        dk[keys] += dot32(gs, q) * SCALE
        dv[keys] += dot32(probs.astype(jnp.bfloat16), gm)
        if o % 4 == 0:
            eight = pl.ds(8 * m, 8)
            for one, first in zip(kv_parts, (WINDOW, 0)):
                rows = pl.ds(first, WINDOW)
                one[eight, :, :HD] = dk[rows].astype(jnp.bfloat16).reshape(8, 128, HD)
                one[eight, :, HD:] = dv[rows].astype(jnp.bfloat16).reshape(8, 128, HD)

    steps, rest = sums.schedule(compute, o_ref)
    feed(steps, 3)
    kv_sums = [
        Reduce(h, BESIDE[n], kv_parts[n], kv_bufs[n], kv_sems[2 * n], kv_sems[2 * n + 1]) for n in range(2)
    ]
    for n in reversed(range(8)):
        for r in kv_sums:
            r.copy(0, 3, n).start()

    def product(out, left, right, c):
        cols = pl.ds(512 * c, 512)
        out[:, cols] = dot_tn(left[...].reshape(D, HD), right[:, :, cols].reshape(D, 512)).astype(out.dtype)

    products = [functools.partial(product, wo_ref, mixed, x_all, c) for c in range(4)]
    products += [loads[5].wait] + [functools.partial(product, wq_ref, dq_all, n1, c) for c in range(4)]
    kv_steps = [
        step
        for pair in zip(chunk_reduce_steps(kv_sums[0], own_ref), chunk_reduce_steps(kv_sums[1], far_ref))
        for step in pair
    ]
    feed(spaced(spaced(rest, kv_steps), products), 3)
    while pending:
        beside(pending.pop(0)).start()
    sent[0] = far_ref[...].astype(sent.dtype)
    swap = remote(sent.at[0], sent.at[1], swap_send, swap_recv, other)
    swap.start()
    g.finish()
    sums.finish()
    for r in kv_sums:
        r.finish()
    swap.wait()
    far_ref[...] = sent[1].astype(jnp.float32)
    for n in range(16):
        beside(n).wait()


def attend_back_layer(x, n1, wq, wo, q, kv, mixed, lse, lo, gc, ge, plan, collective_id):
    bf16, f32 = jnp.bfloat16, jnp.float32
    dma = pltpu.SemaphoreType.DMA
    hbm, vmem = pl.BlockSpec(memory_space=pl.ANY), pl.BlockSpec(memory_space=pltpu.VMEM)
    pair = pltpu.VMEM((16, 128, 2 * HD), bf16)
    return pl.pallas_call(
        functools.partial(attend_back_kernel, plan),
        out_shape=[
            jax.ShapeDtypeStruct((128, D), f32),
            jax.ShapeDtypeStruct((128, 2 * HD), f32),
            jax.ShapeDtypeStruct((128, 2 * HD), f32),
            jax.ShapeDtypeStruct((HD, D), bf16),
            jax.ShapeDtypeStruct((HD, D), bf16),
            jax.ShapeDtypeStruct((1, HD), f32),
            jax.ShapeDtypeStruct((256, D), bf16),
            jax.ShapeDtypeStruct((1024, 512), bf16),
        ],
        in_specs=[hbm] * 7 + [vmem] * 2 + [hbm] * 2,
        out_specs=[vmem] * 6 + [hbm] * 2,
        scratch_shapes=[
            pltpu.VMEM((16, 128, D), bf16),
            pltpu.VMEM((16, 128, D), bf16),
            pltpu.VMEM((D, HD), bf16),
            pltpu.VMEM((HD, D), bf16),
            pltpu.VMEM((8, QB, HD), bf16),
            pltpu.VMEM((2, 2 * WINDOW, 2 * HD), bf16),
            pltpu.VMEM((8, QB, HD), bf16),
            pltpu.VMEM((8, QB, HD), bf16),
            pltpu.VMEM((8, QB, HD), bf16),
            pltpu.VMEM((2 * WINDOW, HD), f32),
            pltpu.VMEM((2 * WINDOW, HD), f32),
            pltpu.VMEM((16, 128, D), bf16),
            pltpu.VMEM((8, 128, D), bf16),
            pltpu.VMEM((8, 128, D), bf16),
            pair,
            pair,
            pair,
            pair,
            pltpu.VMEM((2, 128, 2 * HD), bf16),
            dma((3, 16)),
            dma((3, 16)),
            dma,
            dma,
            dma,
            dma((6,)),
            dma((16,)),
            dma((16,)),
            dma((8,)),
            dma((8,)),
            dma((3, 8)),
            dma((3, 8)),
            dma((1, 16)),
            dma((1, 16)),
            dma((1, 16)),
            dma((1, 16)),
        ],
        compiler_params=pltpu.CompilerParams(
            collective_id=collective_id, has_side_effects=True, vmem_limit_bytes=LIMIT
        ),
        name="attend_back",
    )(x, n1, wq, wo, q, kv, mixed, lse, lo, gc, ge)


BESIDE = ((0, 128, 0, 256, (4, 2, "x", 1)),), ((0, 128, 0, 256, (2, "x", 4, 1)),)
SMALL = tuple(
    (48 * n, 48, 0, 256, order)
    for n, order in enumerate(((8, "x", 4, 2, 1), (8, 4, 2, "x", 1), (8, 2, "x", 4, 1)))
)
BIAS = D + HD


def on_device_fast(
    embedded,
    cotangent,
    segments,
    first_gain,
    first_shift,
    mixer_weight,
    mixer_bias,
    output_weight,
    output_bias,
    second_gain,
    second_shift,
    expand_weight,
    expand_bias,
    contract_weight,
    contract_bias,
):
    bf16, f32 = jnp.bfloat16, jnp.float32
    sec, shd = lax.axis_index("section"), lax.axis_index("shard")
    half = shd // 8
    f = block_of(sec, shd)

    small = jnp.concatenate(
        [
            first_gain[0],
            first_shift[0],
            second_gain[0],
            second_shift[0],
            output_bias[0],
            contract_bias[0],
            expand_bias[0],
            mixer_bias[0],
        ]
    )
    small = jnp.concatenate([small, jnp.zeros((16 * 256 - small.shape[0],), bf16)]).reshape(16, 256)
    shared, wq, wo, we, wc = fetch_weights(
        jnp.concatenate([mixer_weight[0][:, D:], small], axis=0),
        mixer_weight[0],
        output_weight[0],
        expand_weight[0],
        contract_weight[0],
    )
    we = [we[s].reshape(8 * 128, 512) for s in range(2)]
    for s in range(2):
        we[s] = from_halves(we[s])
    wc = [from_halves(wc[s]) for s in range(2)]
    wq = wq.reshape(2, D, HD)
    shared = shared.reshape(2, 16, 144, 256)
    wkv = shared[:, :, :128].reshape(2, D, 256)
    vectors = shared[:, :, 128:].reshape(2, 16, 4096)

    def vector(n):
        return vectors[:, :, 128 * n : 128 * (n + 1)].reshape(2, D).astype(f32)

    gain_one, shift_one, gain_two, shift_two, bias_out, bias_con = [vector(n) for n in range(6)]
    bias_exp = vectors[:, :, 768:1280].reshape(2, 8192).astype(f32)
    hidden_units = [512 * (8 * h + lax.rem(shd, 8)) + 256 * sec for h in range(2)]
    bias_exp = jnp.concatenate(
        [lax.dynamic_slice_in_dim(bias_exp, first, 256, 1) for first in hidden_units], axis=1
    )
    bias_mix = vectors[:, :, 1280 : 1280 + 136].reshape(2, BIAS).astype(f32)
    bias_q = lax.dynamic_slice_in_dim(bias_mix, f * HD, HD, 1)
    bias_kv = jnp.concatenate([jnp.zeros((2, HD), f32), bias_mix[:, D:]], axis=1)

    starts = jnp.sum(
        (segments[:, None, :] < lax.dynamic_slice_in_dim(segments, half * WINDOW, WINDOW, 1)[:, :, None]),
        axis=2,
        dtype=jnp.int32,
    )
    lo = jnp.maximum(jnp.arange(1, WINDOW + 1)[None], starts - half * WINDOW + WINDOW)
    lo = lo.reshape(8, 1, QB)

    hidden = lax.dynamic_index_in_dim(embedded, sec, 0, keepdims=False).astype(f32)
    results, kept = [], []
    for s in range(2):
        n1 = layer_norm(hidden, gain_one[s], shift_one[s]).astype(bf16)
        kv_rows = (dot32(n1, wkv[s]) + bias_kv[s]).astype(bf16)
        rows, all_n1, q, kv, mixed, lse = attend_layer(
            n1,
            kv_rows,
            wq[s],
            wkv[s],
            wo[s],
            bias_q[s][None],
            bias_kv[s][None],
            lo,
            LIGHT if s == 0 else EVEN,
            3 + s,
        )
        middle = hidden + rows + bias_out[s]
        n2 = layer_norm(middle, gain_two[s], shift_two[s]).astype(bf16)
        rows, all_n2, act, slope = hidden_layer(False, n2, we[s], wc[s], (bias_exp[s][None],), LIGHT if s == 0 else EVEN, 9 + 2 * s, "hidden")
        result = middle + rows + bias_con[s]
        results.append(result.astype(bf16))
        kept.append((hidden, n1, all_n1, q, kv, lse, mixed, middle, all_n2, act, slope))
        hidden = results[-1].astype(f32)

    grad = lax.dynamic_index_in_dim(cotangent, sec, 0, keepdims=False).astype(f32)
    input_grads = [None, None]
    weight_grads = [None, None]
    small_grads = [None, None]
    for s in (1, 0):
        hidden, n1, all_n1, q, kv, lse, mixed, middle, all_n2, act, slope = kept[s]
        go = grad.astype(bf16)
        g_n2, d_wc, d_we, d_be = hidden_layer(
            True, go, we[s], wc[s], (slope, act, all_n2), EVEN, 10, "hidden_back"
        )
        d_wc, d_we, d_be = d_wc.reshape(2, 256, D), d_we.reshape(2, 1024, 512), d_be[0]
        _, back = jax.vjp(layer_norm, middle, gain_two[s], shift_two[s])
        g_mid, d_gain_two, d_shift_two = back(g_n2)
        g_mid = grad + g_mid
        ga = g_mid.astype(bf16)
        rows, kv_own, kv_far, d_wo, d_wq, d_bq, came_wc, came_we = attend_back_layer(
            ga, all_n1, wq[s], wo[s], q, kv, mixed, lse, lo, d_wc, d_we, LIGHT, 5
        )
        d_wc, d_we = with_other(d_wc, came_wc), with_other(d_we, came_we)
        dkv_rows = (kv_own + jnp.where(half == 0, kv_far, 0.0)).astype(bf16)
        g_n1 = rows + dot_nt(dkv_rows, wkv[s])
        _, back = jax.vjp(layer_norm, hidden, gain_one[s], shift_one[s])
        g_in, d_gain_one, d_shift_one = back(g_n1)
        g_in = g_mid + g_in
        input_grads[s] = g_in
        d_wkv = dot_tn(n1, dkv_rows)
        d_bq = d_bq[0]
        d_bv = jnp.sum(dkv_rows[:, HD:].astype(f32), axis=0)
        weight_grads[s] = (
            to_halves(d_wq.reshape(HD, 16, 128).transpose(1, 2, 0)).reshape(8, 128, HD),
            d_we.reshape(8, 128, 512),
            d_wo,
            d_wc,
        )
        spread = [
            d_gain_one,
            d_shift_one,
            d_gain_two,
            d_shift_two,
            jnp.sum(ga.astype(f32), axis=0),
            jnp.sum(go.astype(f32), axis=0),
        ]
        placed = jnp.zeros((8192,), f32)
        for h, first in enumerate(hidden_units):
            placed = lax.dynamic_update_slice_in_dim(placed, d_be[256 * h : 256 * (h + 1)], first, 0)
        d_bm = lax.dynamic_update_slice_in_dim(jnp.zeros((D,), f32), d_bq, f * HD, 0)
        vec = jnp.concatenate(
            [one.reshape(16, 128) for one in spread]
            + [placed.reshape(16, 512), jnp.concatenate([d_bm, d_bv]).reshape(16, 136)],
            axis=1,
        )
        vec = jnp.pad(vec, ((0, 0), (0, 4096 - vec.shape[1]))).reshape(16, 16, 256)
        small_grads[s] = jnp.concatenate([d_wkv.reshape(16, 128, 256), vec], axis=1)
        grad = g_in.astype(bf16).astype(f32)

    mine = reduce(
        [jnp.concatenate(small_grads, axis=0).astype(bf16)], ALL, [SMALL], 8, "reduce_shared"
    )[0]
    vec = mine[128:].reshape(4096)
    rq, re, ro, rc = return_grads(
        *[jnp.stack([weight_grads[0][n], weight_grads[1][n]]) for n in range(4)]
    )

    def both(r):
        return r[0].astype(f32) + r[1].astype(f32)

    def swap(pair):
        theirs = jnp.where(sec == 0, pair[1].astype(bf16), pair[0].astype(bf16))
        own = jnp.where(sec == 0, pair[0], pair[1])
        came = lax.ppermute(theirs, "section", [(0, 1), (1, 0)]).astype(own.dtype)
        first = jnp.where(sec == 0, own, came)
        second = jnp.where(sec == 0, came, own)
        return jnp.stack([first, second])[None]

    return (
        swap(results),
        swap(input_grads),
        vec[0:128][None],
        vec[128:256][None],
        jnp.concatenate([rq.astype(f32), mine[:128]], axis=1)[None],
        vec[1280 : 1280 + 136][None],
        both(ro)[None],
        vec[512:640][None],
        vec[256:384][None],
        vec[384:512][None],
        re.astype(f32)[None],
        vec[768:1280][None],
        rc.astype(f32)[None],
        vec[640:768][None],
    )


def solution(mesh):
    in_specs = (
        P(None, "shard", None),
        P(None, "shard", None),
        P(),
        P("section", "shard"),
        P("section", "shard"),
        P("section", "shard", None),
        P("section", "shard"),
        P("section", "shard", None),
        P("section", "shard"),
        P("section", "shard"),
        P("section", "shard"),
        P("section", "shard", None),
        P("section", "shard"),
        P("section", "shard", None),
        P("section", "shard"),
    )
    out_specs = (
        P("section", None, "shard", None),
        P("section", None, "shard", None),
        P("section", "shard"),
        P("section", "shard"),
        P("section", "shard", None),
        P("section", "shard"),
        P("section", "shard", None),
        P("section", "shard"),
        P("section", "shard"),
        P("section", "shard"),
        P("section", "shard", None),
        P("section", "shard"),
        P("section", "shard", None),
        P("section", "shard"),
    )
    fits = mesh.shape["section"] == 2 and mesh.shape["shard"] == HEADS
    on_device = on_device_fast if fits else on_device_general
    return jax.shard_map(
        on_device, mesh=mesh, in_specs=in_specs, out_specs=out_specs, check_vma=False
    )
```

```python
import functools

import jax
import jax.numpy as jnp
from jax import lax
from jax.experimental import pallas as pl
from jax.experimental.pallas import tpu as pltpu
from jax.sharding import PartitionSpec as P

D = 2048
HEADS = 16
HD = 128
WINDOW = 1024


epsilon = 1e-05


def passed_along(block, axis, distance):
    devices = range(lax.axis_size(axis))
    route = [(i - distance, i) for i in devices if i - distance in devices]
    return lax.ppermute(block, axis, route)


def layer_norm(values, gain_row, shift_row):
    center = values - jnp.mean(values, axis=-1, keepdims=True)
    spread = jnp.mean(center * center, axis=-1, keepdims=True)
    return center * lax.rsqrt(spread + epsilon) * gain_row + shift_row


def gelu_tanh(values):
    return jax.nn.gelu(values, approximate=True)


def window_mask(segments, micro_index, device, row_count, reach_blocks):
    seg_row = lax.dynamic_index_in_dim(segments, micro_index, 0, keepdims=False)
    padded = jnp.concatenate([jnp.full((reach_blocks * row_count,), -1, jnp.int32), seg_row])
    key_segments = lax.dynamic_slice_in_dim(
        padded, device * row_count, (reach_blocks + 1) * row_count
    )
    query_segments = lax.dynamic_slice_in_dim(seg_row, device * row_count, row_count)
    distance = (
        jnp.arange(row_count)[:, None]
        + reach_blocks * row_count
        - jnp.arange((reach_blocks + 1) * row_count)[None, :]
    )
    return (
        (distance >= 0) & (distance < WINDOW) & (query_segments[:, None] == key_segments[None, :])
    )


def fetch_window(key_value, reach_blocks):
    earlier = [passed_along(key_value, "shard", offset) for offset in range(reach_blocks, 0, -1)]
    return jnp.concatenate(earlier + [key_value], axis=0)


def return_window(window_grad, reach_blocks, row_count):
    own_rows = window_grad[reach_blocks * row_count :]
    for offset in range(1, reach_blocks + 1):
        start_row = (reach_blocks - offset) * row_count
        own_rows = own_rows + passed_along(
            window_grad[start_row : start_row + row_count].astype(jnp.bfloat16), "shard", -offset
        ).astype(jnp.float32)
    return own_rows


def forward_layer(hidden, weights, key_mask, reach_blocks):
    (
        first_gain,
        first_shift,
        mixer_weight,
        mixer_bias,
        output_weight,
        output_bias,
        second_gain,
        second_shift,
        expand_weight,
        expand_bias,
        contract_weight,
        contract_bias,
    ) = weights
    row_count = hidden.shape[0]
    score_scale = HD ** (-0.5)
    normed_one = layer_norm(
        hidden, first_gain.astype(jnp.float32), first_shift.astype(jnp.float32)
    ).astype(jnp.bfloat16)
    full_bias = jnp.concatenate(
        [mixer_bias[:D], jnp.zeros((HD,), mixer_bias.dtype), mixer_bias[D:]]
    ).astype(jnp.float32)
    projected = (
        jnp.dot(normed_one, mixer_weight, preferred_element_type=jnp.float32) + full_bias
    ).astype(jnp.bfloat16)
    queries = projected[:, :D].reshape(row_count, HEADS, HD)
    window_pairs = fetch_window(projected[:, D:], reach_blocks)
    scores = (
        jnp.einsum("thd,kd->htk", queries, window_pairs[:, :HD], preferred_element_type=jnp.float32)
        * score_scale
    )
    masked = jnp.where(key_mask[None], scores, -1e30)
    top_score = jnp.max(masked, axis=2, keepdims=True)
    exponent = jnp.exp(masked - top_score)
    totals = jnp.sum(exponent, axis=2, keepdims=True)
    prob_low = (exponent / totals).astype(jnp.bfloat16)
    log_total = top_score + jnp.log(totals)
    mixed_rows = (
        jnp.einsum(
            "htk,kd->thd", prob_low, window_pairs[:, HD:], preferred_element_type=jnp.float32
        )
        .reshape(row_count, D)
        .astype(jnp.bfloat16)
    )
    middle = (
        hidden
        + jnp.dot(mixed_rows, output_weight, preferred_element_type=jnp.float32)
        + output_bias.astype(jnp.float32)
    )
    normed_two = layer_norm(
        middle, second_gain.astype(jnp.float32), second_shift.astype(jnp.float32)
    ).astype(jnp.bfloat16)
    pre_gelu = jnp.dot(
        normed_two, expand_weight, preferred_element_type=jnp.float32
    ) + expand_bias.astype(jnp.float32)
    activated = gelu_tanh(pre_gelu).astype(jnp.bfloat16)
    result = (
        middle
        + jnp.dot(activated, contract_weight, preferred_element_type=jnp.float32)
        + contract_bias.astype(jnp.float32)
    )
    return (
        result,
        (
            hidden,
            normed_one,
            projected,
            window_pairs,
            log_total,
            mixed_rows,
            middle,
            normed_two,
            pre_gelu,
            activated,
        ),
    )


def backward_layer(grad_result, weights, saved_state, key_mask, reach_blocks):
    (
        first_gain,
        first_shift,
        mixer_weight,
        mixer_bias,
        output_weight,
        output_bias,
        second_gain,
        second_shift,
        expand_weight,
        expand_bias,
        contract_weight,
        contract_bias,
    ) = weights
    (
        hidden,
        normed_one,
        projected,
        window_pairs,
        log_total,
        mixed_rows,
        middle,
        normed_two,
        pre_gelu,
        activated,
    ) = saved_state
    row_count = hidden.shape[0]
    score_scale = HD ** (-0.5)
    grad_out_low = grad_result.astype(jnp.bfloat16)
    grad_act = jnp.einsum(
        "rd,fd->rf", grad_out_low, contract_weight, preferred_element_type=jnp.float32
    )
    gelu_value, gelu_back = jax.vjp(gelu_tanh, pre_gelu)
    grad_pre = gelu_back(grad_act)[0].astype(jnp.bfloat16)
    grad_normed_two = jnp.einsum(
        "rf,df->rd", grad_pre, expand_weight, preferred_element_type=jnp.float32
    )
    norm_value_two, norm_back_two = jax.vjp(
        layer_norm, middle, second_gain.astype(jnp.float32), second_shift.astype(jnp.float32)
    )
    grad_middle_part, grad_gain_two, grad_shift_two = norm_back_two(grad_normed_two)
    grad_middle = grad_result + grad_middle_part
    grad_attended = grad_middle.astype(jnp.bfloat16)
    grad_mixed = (
        jnp.einsum("re,de->rd", grad_attended, output_weight, preferred_element_type=jnp.float32)
        .astype(jnp.bfloat16)
        .reshape(row_count, HEADS, HD)
    )
    queries = projected[:, :D].reshape(row_count, HEADS, HD)
    key_part = window_pairs[:, :HD]
    value_part = window_pairs[:, HD:]
    scores = (
        jnp.einsum("thd,kd->htk", queries, key_part, preferred_element_type=jnp.float32)
        * score_scale
    )
    prob_full = jnp.where(key_mask[None], jnp.exp(scores - log_total), 0.0)
    prob_low = prob_full.astype(jnp.bfloat16)
    grad_probs = jnp.einsum(
        "thd,kd->htk", grad_mixed, value_part, preferred_element_type=jnp.float32
    )
    row_dot = jnp.sum(prob_full * grad_probs, axis=2, keepdims=True)
    grad_scores = (prob_full * (grad_probs - row_dot)).astype(jnp.bfloat16)
    grad_queries = (
        jnp.einsum("htk,kd->thd", grad_scores, key_part, preferred_element_type=jnp.float32)
        * score_scale
    ).reshape(row_count, D)
    grad_keys = (
        jnp.einsum("htk,thd->kd", grad_scores, queries, preferred_element_type=jnp.float32)
        * score_scale
    )
    grad_values = jnp.einsum(
        "htk,thd->kd", prob_low, grad_mixed, preferred_element_type=jnp.float32
    )
    grad_window = jnp.concatenate([grad_keys, grad_values], axis=1)
    grad_own_pairs = return_window(grad_window, reach_blocks, row_count)
    grad_projected = jnp.concatenate([grad_queries, grad_own_pairs], axis=1).astype(jnp.bfloat16)
    grad_normed_one = jnp.einsum(
        "rq,dq->rd", grad_projected, mixer_weight, preferred_element_type=jnp.float32
    )
    norm_value_one, norm_back_one = jax.vjp(
        layer_norm, hidden, first_gain.astype(jnp.float32), first_shift.astype(jnp.float32)
    )
    grad_hidden_part, grad_gain_one, grad_shift_one = norm_back_one(grad_normed_one)
    grad_hidden = grad_middle + grad_hidden_part
    return (
        grad_hidden,
        (
            grad_projected,
            grad_attended,
            grad_pre,
            grad_out_low,
            grad_gain_one,
            grad_shift_one,
            grad_gain_two,
            grad_shift_two,
            normed_one,
            mixed_rows,
            normed_two,
            activated,
        ),
    )


def flatten_rows(stacked):
    return stacked.reshape((-1, stacked.shape[-1]))


def weight_terms(row_items, norm_items):
    (
        grad_projected_rows,
        grad_attended_rows,
        grad_pre_rows,
        grad_out_rows,
        normed_one_rows,
        mixed_all,
        normed_two_rows,
        activated_rows,
    ) = row_items
    first_gain_term, first_shift_term, second_gain_term, second_shift_term = norm_items
    mixer_weight_term = jnp.einsum(
        "rd,rq->dq", normed_one_rows, grad_projected_rows, preferred_element_type=jnp.float32
    )
    column_totals = jnp.sum(grad_projected_rows.astype(jnp.float32), axis=0)
    mixer_bias_term = jnp.concatenate([column_totals[:D], column_totals[D + HD :]])
    output_weight_term = jnp.einsum(
        "rd,re->de", mixed_all, grad_attended_rows, preferred_element_type=jnp.float32
    )
    output_bias_term = jnp.sum(grad_attended_rows.astype(jnp.float32), axis=0)
    expand_weight_term = jnp.einsum(
        "rd,rf->df", normed_two_rows, grad_pre_rows, preferred_element_type=jnp.float32
    )
    expand_bias_term = jnp.sum(grad_pre_rows.astype(jnp.float32), axis=0)
    contract_weight_term = jnp.einsum(
        "rf,rd->fd", activated_rows, grad_out_rows, preferred_element_type=jnp.float32
    )
    contract_bias_term = jnp.sum(grad_out_rows.astype(jnp.float32), axis=0)
    return (
        first_gain_term[None],
        first_shift_term[None],
        mixer_weight_term[None],
        mixer_bias_term[None],
        output_weight_term[None],
        output_bias_term[None],
        second_gain_term[None],
        second_shift_term[None],
        expand_weight_term[None],
        expand_bias_term[None],
        contract_weight_term[None],
        contract_bias_term[None],
    )


def on_device_general(
    embedded,
    cotangent,
    segments,
    first_gain,
    first_shift,
    mixer_weight,
    mixer_bias,
    output_weight,
    output_bias,
    second_gain,
    second_shift,
    expand_weight,
    expand_bias,
    contract_weight,
    contract_bias,
):
    section_index = lax.axis_index("section")
    device = lax.axis_index("shard")
    micro_count = embedded.shape[0]
    row_count = embedded.shape[1]
    reach_blocks = WINDOW // row_count
    own_params = (
        first_gain[0],
        first_shift[0],
        mixer_weight[0],
        mixer_bias[0],
        output_weight[0],
        output_bias[0],
        second_gain[0],
        second_shift[0],
        expand_weight[0],
        expand_bias[0],
        contract_weight[0],
        contract_bias[0],
    )
    forward_weights = (
        lax.all_gather(own_params[0], "shard", axis=0, tiled=True),
        lax.all_gather(own_params[1], "shard", axis=0, tiled=True),
        lax.all_gather(own_params[2], "shard", axis=0, tiled=True),
        lax.all_gather(own_params[3], "shard", axis=0, tiled=True),
        lax.all_gather(own_params[4], "shard", axis=0, tiled=True),
        lax.all_gather(own_params[5], "shard", axis=0, tiled=True),
        lax.all_gather(own_params[6], "shard", axis=0, tiled=True),
        lax.all_gather(own_params[7], "shard", axis=0, tiled=True),
        lax.all_gather(own_params[8], "shard", axis=0, tiled=True),
        lax.all_gather(own_params[9], "shard", axis=0, tiled=True),
        lax.all_gather(own_params[10], "shard", axis=0, tiled=True),
        lax.all_gather(own_params[11], "shard", axis=0, tiled=True),
    )
    zero_rows = jnp.zeros((row_count, D), jnp.float32)
    arrived = zero_rows
    sent_list = []
    kept_states = []
    for step_index in range(micro_count + 1):
        own_input = (
            embedded[step_index].astype(jnp.float32) if step_index < micro_count else zero_rows
        )
        hidden = jnp.where(section_index == 0, own_input, arrived)
        micro_index = jnp.clip(step_index - section_index, 0, micro_count - 1)
        key_mask = window_mask(segments, micro_index, device, row_count, reach_blocks)
        result, saved_state = forward_layer(hidden, forward_weights, key_mask, reach_blocks)
        result_low = result.astype(jnp.bfloat16)
        sent_list.append(result_low)
        kept_states.append(saved_state)
        if step_index < micro_count:
            arrived = passed_along(result_low, "section", 1).astype(jnp.float32)
    section_outputs = lax.dynamic_slice_in_dim(jnp.stack(sent_list), section_index, micro_count, 0)[
        None
    ]
    stacked_states = [
        jnp.stack([state_item[item_index] for state_item in kept_states])
        for item_index in range(10)
    ]
    valid_start = 1 - section_index
    arrived_grad = zero_rows
    grad_records = []
    hidden_grads = []
    for step_index in range(micro_count + 1):
        own_grad = (
            cotangent[step_index].astype(jnp.float32) if step_index < micro_count else zero_rows
        )
        grad_result = jnp.where(section_index == 1, own_grad, arrived_grad)
        forward_index = jnp.clip(step_index - 1 + 2 * section_index, 0, micro_count)
        micro_index = jnp.clip(step_index - 1 + section_index, 0, micro_count - 1)
        saved_state = [
            lax.dynamic_index_in_dim(stacked, forward_index, 0, keepdims=False)
            for stacked in stacked_states
        ]
        key_mask = window_mask(segments, micro_index, device, row_count, reach_blocks)
        grad_hidden, record = backward_layer(
            grad_result, forward_weights, saved_state, key_mask, reach_blocks
        )
        hidden_grads.append(grad_hidden)
        if step_index < micro_count:
            arrived_grad = passed_along(grad_hidden.astype(jnp.bfloat16), "section", -1).astype(
                jnp.float32
            )
        grad_records.append(record)
    input_grads = lax.dynamic_slice_in_dim(jnp.stack(hidden_grads), valid_start, micro_count, 0)[
        None
    ]
    chosen = [
        lax.dynamic_slice_in_dim(
            jnp.stack([record[item_index] for record in grad_records]), valid_start, micro_count, 0
        )
        for item_index in range(12)
    ]
    row_items = (
        flatten_rows(chosen[0]),
        flatten_rows(chosen[1]),
        flatten_rows(chosen[2]),
        flatten_rows(chosen[3]),
        flatten_rows(chosen[8]),
        flatten_rows(chosen[9]),
        flatten_rows(chosen[10]),
        flatten_rows(chosen[11]),
    )
    norm_items = (
        jnp.sum(chosen[4], axis=0),
        jnp.sum(chosen[5], axis=0),
        jnp.sum(chosen[6], axis=0),
        jnp.sum(chosen[7], axis=0),
    )
    all_terms = weight_terms(row_items, norm_items)
    summed = (
        lax.psum_scatter(all_terms[0], "shard", scatter_dimension=1, tiled=True),
        lax.psum_scatter(all_terms[1], "shard", scatter_dimension=1, tiled=True),
        lax.psum_scatter(all_terms[2], "shard", scatter_dimension=1, tiled=True),
        lax.psum_scatter(all_terms[3], "shard", scatter_dimension=1, tiled=True),
        lax.psum_scatter(all_terms[4], "shard", scatter_dimension=1, tiled=True),
        lax.psum_scatter(all_terms[5], "shard", scatter_dimension=1, tiled=True),
        lax.psum_scatter(all_terms[6], "shard", scatter_dimension=1, tiled=True),
        lax.psum_scatter(all_terms[7], "shard", scatter_dimension=1, tiled=True),
        lax.psum_scatter(all_terms[8], "shard", scatter_dimension=1, tiled=True),
        lax.psum_scatter(all_terms[9], "shard", scatter_dimension=1, tiled=True),
        lax.psum_scatter(all_terms[10], "shard", scatter_dimension=1, tiled=True),
        lax.psum_scatter(all_terms[11], "shard", scatter_dimension=1, tiled=True),
    )
    return (
        section_outputs,
        input_grads,
        summed[0],
        summed[1],
        summed[2],
        summed[3],
        summed[4],
        summed[5],
        summed[6],
        summed[7],
        summed[8],
        summed[9],
        summed[10],
        summed[11],
    )


MESH = pl.DeviceIdType.MESH
LIMIT = 60 << 20
CUBE = ("x", 4, 2, 1)
ALL = ("x", 8, 4, 2, 1)


def columns(n, wide):
    return pl.ds(pl.multiple_of(n * wide, wide), wide)


def remote(src, dst, send, recv, there):
    return pltpu.make_async_remote_copy(
        src_ref=src, dst_ref=dst, send_sem=send, recv_sem=recv, device_id=there, device_id_type=MESH
    )


class Hyper:
    def __init__(self, dims):
        sec = lax.axis_index("section")
        shd = lax.axis_index("shard")
        self.dims = dims
        self.partner, self.delta, self.pos = {}, {}, 0
        for n, d in enumerate(dims):
            weight = 1 << (len(dims) - 1 - n)
            if d == "x":
                bit = sec
                self.partner[d] = (1 - sec, shd)
            else:
                bit = lax.rem(shd // d, 2)
                self.partner[d] = (sec, shd + d * (1 - 2 * bit))
            self.pos = self.pos + bit * weight
            self.delta[d] = weight * (1 - 2 * bit)

    def at(self, order, offset):
        place = self.pos
        for j, d in enumerate(order):
            if offset >> j & 1:
                place = place + self.delta[d]
        return place

    def barrier(self, more=()):
        sem = pltpu.get_barrier_semaphore()
        partners = [self.partner[d] for d in self.dims] + list(more)
        for partner in partners:
            pl.semaphore_signal(sem, inc=1, device_id=partner, device_id_type=MESH)
        pl.semaphore_wait(sem, len(partners))


def cube_parts(rows, widths, col0=0):
    orders = (("x", 4, 2, 1), (4, 2, "x", 1), (2, "x", 4, 1))
    parts = []
    for width, order in zip(widths, orders):
        parts.append((0, rows, col0, width, order))
        col0 += width
    return tuple(parts)


class Gather:
    def __init__(self, h, parts, src, dst, send_sem, recv_sem):
        self.h, self.parts, self.src, self.dst = h, parts, src, dst
        self.send_sem, self.recv_sem = send_sem, recv_sem

    def copy(self, p, offset, j):
        r0, rn, c0, cn, order = self.parts[p]
        rows, cols = pl.ds(r0, rn), pl.ds(c0, cn)
        there = self.dst.at[self.h.at(order, offset), rows, cols]
        here = self.src.at[rows, cols] if offset == 0 else there
        n = offset | 1 << j
        return pltpu.make_async_remote_copy(
            src_ref=here,
            dst_ref=there,
            send_sem=self.send_sem.at[p, n],
            recv_sem=self.recv_sem.at[p, n],
            device_id=self.h.partner[order[j]],
            device_id_type=MESH,
        )

    def start(self, chosen):
        for j in range(len(self.h.dims)):
            for p in chosen:
                self.copy(p, 0, j).start()

    def forward(self, chosen):
        k = len(self.h.dims)
        for j in range(k):
            for low in range(1 << j):
                for p in chosen:
                    self.copy(p, low, j).wait_recv()
                    for later in range(j + 1, k):
                        self.copy(p, low | 1 << j, later).start()

    def finish(self):
        for p in range(len(self.parts)):
            for j in range(len(self.h.dims)):
                for low in range(1 << j):
                    self.copy(p, low, j).wait_send()


class Reduce:
    def __init__(self, h, parts, src, buf, send_sem, recv_sem):
        self.h, self.parts, self.src, self.buf = h, parts, src, buf
        self.send_sem, self.recv_sem = send_sem, recv_sem

    def window(self, p):
        r0, rn, c0, cn, order = self.parts[p]
        return pl.ds(r0, rn), pl.ds(c0, cn)

    def held(self, p, j, offset):
        if j == len(self.h.dims) - 1:
            return self.src.at[(self.h.at(self.parts[p][4], offset),) + self.window(p)]
        return self.buf.at[((1 << (j + 1)) | offset,) + self.window(p)]

    def copy(self, p, j, low):
        n = (1 << j) | low
        return remote(
            self.held(p, j, low | 1 << j),
            self.buf.at[(n,) + self.window(p)],
            self.send_sem.at[p, n],
            self.recv_sem.at[p, n],
            self.h.partner[self.parts[p][4][j]],
        )

    def add(self, p, j, low, out=None):
        self.copy(p, j, low).wait_recv()
        r0, rn, c0, cn, order = self.parts[p]
        mine = self.held(p, j, low)
        came = self.buf.at[((1 << j) | low,) + self.window(p)]
        step = 16

        @pl.loop(0, rn // step)
        def _(i):
            rows = pl.ds(pl.multiple_of(i * step, step), step)
            total = mine[rows, :].astype(jnp.float32) + came[rows, :].astype(jnp.float32)
            if j > 0:
                came[rows, :] = total.astype(came.dtype)
            else:
                out[pl.ds(pl.multiple_of(r0 + i * step, step), step), pl.ds(c0, cn)] = total

        if j > 0 and low >> (j - 1) & 1:
            self.copy(p, j - 1, low ^ (1 << (j - 1))).start()

    def finish(self):
        for p in range(len(self.parts)):
            for j in range(len(self.h.dims)):
                for low in range(1 << j):
                    self.copy(p, j, low).wait_send()


def block_of(sec, shd):
    return 8 * lax.rem(sec + lax.rem(shd, 2), 2) + lax.rem(shd, 8)


def half_group(sec, shd):
    first = 8 * (shd // 8)
    return 8 * sec + lax.rem(shd, 8), lambda n: (n // 8, first + lax.rem(n, 8))


def half_barrier(me, place, sec, shd):
    sem = pltpu.get_barrier_semaphore()

    @pl.loop(1, 16)
    def _(d):
        pl.semaphore_signal(
            sem, inc=1, device_id=place(lax.rem(me + d, 16)), device_id_type=MESH
        )

    across = shd + 8 * (1 - 2 * (shd // 8))
    for s in range(2):
        pl.semaphore_signal(sem, inc=1, device_id=(s, across), device_id_type=MESH)
    pl.semaphore_wait(sem, 17)


class Spread:
    def __init__(self, pieces, own_sem, send, recv):
        self.sec, self.shd = lax.axis_index("section"), lax.axis_index("shard")
        self.me, self.place = half_group(self.sec, self.shd)
        self.pieces, self.own_sem, self.send, self.recv = pieces, own_sem, send, recv

    def barrier(self):
        half_barrier(self.me, self.place, self.sec, self.shd)

    def copies(self, d):
        there = self.place(lax.rem(self.me + d, 16))
        return [
            remote(src, dst, self.send.at[n, d], self.recv.at[n, d], there)
            for n, (src, dst) in enumerate(self.pieces(*there))
        ]

    def own(self):
        return [
            pltpu.make_async_copy(src, dst, self.own_sem.at[n])
            for n, (src, dst) in enumerate(self.pieces(self.sec, self.shd))
        ]

    def start(self):
        @pl.loop(1, 16)
        def _(d):
            for one in self.copies(d):
                one.start()

        for one in self.own():
            one.start()

    def wait(self):
        @pl.loop(1, 16)
        def _(d):
            for one in self.copies(d):
                one.wait_recv()

        @pl.loop(1, 16)
        def _(d):
            for one in self.copies(d):
                one.wait_send()

        for one in self.own():
            one.wait()


def everyone_barrier(me):
    sem = pltpu.get_barrier_semaphore()

    @pl.loop(1, 32)
    def _(d):
        there = lax.rem(me + d, 32)
        pl.semaphore_signal(
            sem, inc=1, device_id=(there // 16, lax.rem(there, 16)), device_id_type=MESH
        )

    pl.semaphore_wait(sem, 31)


def fetch_kernel(block, mix, out, exp, con, shared, wq, wo, we, wc, *sems):
    q_send, q_recv, send, recv, con_send, con_recv, out_send, out_recv, own_sem, sh_send, sh_recv = sems
    sec, shd = lax.axis_index("section"), lax.axis_index("shard")
    low, half = lax.rem(shd, 8), shd // 8
    me = 16 * sec + shd
    everyone_barrier(me)
    h = Hyper(ALL)
    g = Gather(h, SMALL, block, shared, sh_send, sh_recv)
    g.start(range(3))

    def query(d):
        there = lax.rem(me + d, 32)
        ts, tj = there // 16, lax.rem(there, 16)
        return remote(
            mix.at[:, columns(block_of(ts, tj), HD)], wq.at[sec, shd], q_send.at[d], q_recv.at[d], (ts, tj)
        )

    @pl.loop(1, 32)
    def _(d):
        query(d).start()

    to_x = lax.rem(half + lax.rem(shd, 2), 2)
    from_half = lax.rem(sec + lax.rem(shd, 2), 2)
    own_out = pltpu.make_async_copy(out, wo.at[sec], own_sem.at[5])
    for z in range(2):
        mine = jnp.logical_and(to_x == sec, half == z)
        there = remote(out, wo.at[sec], out_send.at[z], out_recv.at[sec], (to_x, 8 * z + low))

        @pl.when(mine)
        def _():
            own_out.start()

        @pl.when(jnp.logical_not(mine))
        def _():
            there.start()

    own = [
        pltpu.make_async_copy(block, shared.at[h.pos], own_sem.at[2]),
        pltpu.make_async_copy(mix.at[:, columns(block_of(sec, shd), HD)], wq.at[sec, shd], own_sem.at[3]),
        pltpu.make_async_copy(con.at[pl.ds(256 * sec, 256)], wc.at[sec], own_sem.at[4]),
    ]
    for one in own:
        one.start()

    def pieces(ts, tj):
        for n in range(2):
            yield (
                exp.at[:, columns(2 * (8 * n + lax.rem(tj, 8)) + ts, 256)],
                we.at[sec, low, :, pl.ds(256 * n, 256)],
            )

    spread = Spread(pieces, own_sem, send, recv)
    spread.start()
    rows = remote(con.at[pl.ds(256 * (1 - sec), 256)], wc.at[sec], con_send, con_recv, (1 - sec, shd))
    rows.start()
    g.forward(range(3))

    @pl.loop(1, 32)
    def _(d):
        query(d).wait_recv()

    for s in range(2):
        mine = jnp.logical_and(sec == s, from_half == half)

        @pl.when(jnp.logical_not(mine))
        def _():
            remote(out, wo.at[s], out_send.at[0], out_recv.at[s], (1 - sec, shd)).wait_recv()

    spread.wait()
    remote(con.at[pl.ds(0, 256)], wc.at[1 - sec], con_send, con_recv, (1 - sec, shd)).wait_recv()
    rows.wait_send()

    @pl.loop(1, 32)
    def _(d):
        query(d).wait_send()

    for z in range(2):
        mine = jnp.logical_and(to_x == sec, half == z)
        there = remote(out, wo.at[sec], out_send.at[z], out_recv.at[sec], (to_x, 8 * z + low))

        @pl.when(mine)
        def _():
            own_out.wait()

        @pl.when(jnp.logical_not(mine))
        def _():
            there.wait_send()

    g.finish()
    for one in own:
        one.wait()


def fetch_weights(block, mix, out, exp, con):
    bf16 = jnp.bfloat16
    dma = pltpu.SemaphoreType.DMA
    return pl.pallas_call(
        fetch_kernel,
        out_shape=(
            jax.ShapeDtypeStruct((32,) + block.shape, bf16),
            jax.ShapeDtypeStruct((2, 16, 128, HD), bf16),
            jax.ShapeDtypeStruct((2, 128, D), bf16),
            jax.ShapeDtypeStruct((2, 8, 128, 512), bf16),
            jax.ShapeDtypeStruct((2, 256, D), bf16),
        ),
        in_specs=[pl.BlockSpec(memory_space=pl.ANY)] * 5,
        out_specs=[pl.BlockSpec(memory_space=pl.ANY)] * 5,
        scratch_shapes=[
            dma((32,)),
            dma((32,)),
            dma((2, 16)),
            dma((2, 16)),
            dma,
            dma,
            dma((2,)),
            dma((2,)),
            dma((6,)),
            dma((3, 32)),
            dma((3, 32)),
        ],
        compiler_params=pltpu.CompilerParams(
            collective_id=1, has_side_effects=True, vmem_limit_bytes=LIMIT
        ),
        name="fetch_weights",
    )(block, mix, out, exp, con)


def last_kernel(small, gq0, gq1, go0, go1, cross, total, rq, ro, crossed, *scratch):
    buf, s_send, s_recv, q_send, q_recv, out_send, out_recv, own_sem, x_send, x_recv = scratch
    sec, shd = lax.axis_index("section"), lax.axis_index("shard")
    half = shd // 8
    f = block_of(sec, shd)
    everyone_barrier(16 * sec + shd)
    h = Hyper(ALL)
    k = len(ALL)
    r = Reduce(h, SMALL, small, buf, s_send, s_recv)
    for low in reversed(range(1 << (k - 1))):
        for p in range(len(SMALL)):
            r.copy(p, k - 1, low).start()
    swap = remote(cross, crossed, x_send, x_recv, (1 - sec, shd))
    pl.when(sec == 1)(swap.start)

    def query(s, d):
        src = (gq0, gq1)[s].at[lax.rem(shd + d, 16)]
        dst = rq.at[half, :, columns(f, HD)]
        return src, dst, remote(src, dst, q_send.at[s, d], q_recv.at[sec, d], (s, lax.rem(shd + d, 16)))

    def rows(s):
        src, dst = (go0, go1)[s], ro.at[half]
        return src, dst, remote(src, dst, out_send.at[s], out_recv.at[half], (s, f))

    def either(local, n, copy, start):
        src, dst, there = copy
        here = pltpu.make_async_copy(src, dst, own_sem.at[n])

        @pl.when(local)
        def _():
            here.start() if start else here.wait()

        @pl.when(jnp.logical_not(local))
        def _():
            there.start() if start else there.wait_send()

    for s in range(2):
        either(sec == s, 0, query(s, 0), True)
        either(jnp.logical_and(sec == s, f == shd), 1, rows(s), True)

        @pl.loop(1, 16)
        def _(d):
            query(s, d)[2].start()

    for j in reversed(range(k)):
        for low in reversed(range(1 << j)):
            for p in range(len(SMALL)):
                r.add(p, j, low, total)
    pl.when(sec == 1)(swap.wait_send)
    pl.when(sec == 0)(swap.wait_recv)

    def arrival(s, d):
        return remote(gq0.at[0], rq.at[0, :, pl.ds(0, HD)], q_send.at[0, 0], q_recv.at[s, d], (1 - sec, shd))

    for s in range(2):

        @pl.when(sec != s)
        def _():
            arrival(s, 0).wait_recv()

        @pl.loop(1, 16)
        def _(d):
            arrival(s, d).wait_recv()

        @pl.when(jnp.logical_not(jnp.logical_and(f == shd, half == s)))
        def _():
            remote(go0, ro.at[s], out_send.at[0], out_recv.at[s], (1 - sec, shd)).wait_recv()

    for s in range(2):
        either(sec == s, 0, query(s, 0), False)
        either(jnp.logical_and(sec == s, f == shd), 1, rows(s), False)

        @pl.loop(1, 16)
        def _(d):
            query(s, d)[2].wait_send()

    r.finish()


def return_last(small, gq, go, cross):
    bf16, f32 = jnp.bfloat16, jnp.float32
    dma = pltpu.SemaphoreType.DMA
    hbm, vmem = pl.BlockSpec(memory_space=pl.ANY), pl.BlockSpec(memory_space=pltpu.VMEM)
    return pl.pallas_call(
        last_kernel,
        out_shape=(
            jax.ShapeDtypeStruct(small.shape[1:], f32),
            jax.ShapeDtypeStruct((2, 128, D), bf16),
            jax.ShapeDtypeStruct((2, 128, D), bf16),
            jax.ShapeDtypeStruct((128, D), bf16),
        ),
        in_specs=[vmem] + [hbm] * 5,
        out_specs=[vmem] + [hbm] * 3,
        scratch_shapes=[
            pltpu.VMEM(small.shape, bf16),
            dma((3, 32)),
            dma((3, 32)),
            dma((2, 16)),
            dma((2, 16)),
            dma((2,)),
            dma((2,)),
            dma((2,)),
            dma,
            dma,
        ],
        compiler_params=pltpu.CompilerParams(
            collective_id=2, has_side_effects=True, vmem_limit_bytes=LIMIT
        ),
        name="return_last",
    )(small, *gq, *go, cross)


HALVES = [[n, n + 8] for n in range(8)]


def from_halves(x):
    return lax.all_gather(x, "shard", axis=0, tiled=True, axis_index_groups=HALVES)


NT = (((1,), (1,)), ((), ()))
TN = (((0,), (0,)), ((), ()))


def dot32(a, b):
    return jnp.dot(a, b, preferred_element_type=jnp.float32)


def dot_nt(a, b):
    return lax.dot_general(a, b, NT, preferred_element_type=jnp.float32)


def dot_tn(a, b):
    return lax.dot_general(a, b, TN, preferred_element_type=jnp.float32)


EVEN = cube_parts(128, (768, 640, 640))
LIGHT = cube_parts(128, (896, 896, 256))
TRIO = ("x", 4, 2)
CHUNK = 64


def spaced(many, few):
    result = []
    for n, step in enumerate(many):
        result.append(step)
        done = len(few) * (n + 1) // len(many)
        result.extend(few[len(few) * n // len(many) : done])
    return result


def chunk_gather_steps(g, count):
    k = len(g.h.dims)

    def step(j, low):
        for p in range(count):
            g.copy(p, low, j).wait_recv()
            for later in range(j + 1, k):
                g.copy(p, low | 1 << j, later).start()

    return [functools.partial(step, j, low) for j in range(k) for low in range(1 << j)]


def chunk_reduce_steps(r, out):
    k = len(r.h.dims)
    return [
        functools.partial(r.add, p, j, low, out)
        for j in reversed(range(k))
        for low in reversed(range(1 << j))
        for p in range(len(r.parts))
    ]


GELU_K = (2.0 / 3.141592653589793) ** 0.5


def gelu_pair(u):
    square = u * u
    t = jnp.tanh(GELU_K * (u + 0.044715 * u * square))
    half = 0.5 * (1.0 + t)
    slope = half + 0.5 * u * (1.0 - t * t) * (GELU_K * (1.0 + 3 * 0.044715 * square))
    return u * half, slope


def hidden_kernel(back, plan, *refs):
    if back:
        x_ref, we_hbm, wc_hbm, slope_hbm, act_hbm, n2_hbm, o_ref, dc_out, de_out, be_ref = refs[:10]
        act_all, n2_all, d_tile = refs[10:13]
        scratch = refs[13:]
    else:
        x_ref, we_hbm, wc_hbm, be_ref, o_ref, x_out, h_out, slope_out = refs[:8]
        scratch = refs[8:]
    x_all, we, wc, h_all, slope, part, came, buf = scratch[:8]
    g_send, g_recv, c_send, c_recv, r_send, r_recv, own_sem, load_sem, out_sem = scratch[8:]
    h = Hyper(CUBE)
    trio = Hyper(TRIO)
    h.barrier()
    loads = [pltpu.make_async_copy(we_hbm, we, load_sem.at[0]), pltpu.make_async_copy(wc_hbm, wc, load_sem.at[1])]
    if back:
        loads.append(pltpu.make_async_copy(slope_hbm, slope, load_sem.at[2]))
        late = [
            pltpu.make_async_copy(act_hbm, act_all, load_sem.at[3]),
            pltpu.make_async_copy(n2_hbm, n2_all, load_sem.at[4]),
        ]
    parts = tuple((0, CHUNK, c0, cn, order) for _, _, c0, cn, order in plan)
    gathers, sums = [], []
    for n in range(2):
        mine = x_ref.at[pl.ds(CHUNK * n, CHUNK)]
        own = pltpu.make_async_copy(mine, x_all.at[n, h.pos], own_sem.at[n])
        own.start()
        loads.append(own)
        gathers.append(Gather(h, parts, mine, x_all.at[n], g_send.at[n], g_recv.at[n]))
        sums.append(
            Reduce(
                trio,
                tuple((0, CHUNK, c0, cn, order[:3]) for _, _, c0, cn, order in plan),
                came.at[n],
                buf.at[n],
                r_send.at[n],
                r_recv.at[n],
            )
        )
        gathers[n].start(range(len(plan)))
    for one in loads[:-2]:
        one.start()
    core = 1 - lax.rem(lax.axis_index("shard"), 2)

    def quad(r):
        return 4 * (h.pos // 4) + (h.delta["x"] if r & 2 else 0) + (h.delta[4] if r & 1 else 0)

    def pair(r, y):
        return quad(r) + 2 * (lax.rem(h.pos, 4) // 2) + (h.delta[2] if y else 0)

    def compute(n, r):
        four = pl.ds(quad(r), 4)
        x = x_all[n, four].reshape(4 * CHUNK, D)
        if back:
            inner = dot_nt(x, wc[...]).reshape(4, CHUNK, 512)
            mid = (inner * slope[n, four].astype(jnp.float32)).astype(jnp.bfloat16)
        else:
            inner = dot32(x, we[...]) + be_ref[...]
            act, grad = gelu_pair(inner)
            mid = act.astype(jnp.bfloat16).reshape(4, CHUNK, 512)
            slope[n, four] = grad.astype(jnp.bfloat16).reshape(4, CHUNK, 512)
        h_all[n, four] = mid
        mid = mid.reshape(4 * CHUNK, 512)
        if back:
            be_ref[...] += jnp.sum(mid.astype(jnp.float32), axis=0, keepdims=True)
        for c in range(4):
            cols = pl.ds(512 * c, 512)
            tile = dot_nt(mid, we[cols, :]) if back else dot32(mid, wc[:, cols])
            part[n, four, :, cols] = tile.astype(jnp.bfloat16).reshape(4, CHUNK, 512)
        for y in reversed(range(2)):
            core_copy(n, r, y).start()

    def core_copy(n, r, y):
        at = pair(r, y)
        return remote(
            part.at[n, at + core],
            came.at[n, at // 2],
            c_send.at[n, 2 * r + y],
            c_recv.at[n, 2 * r + y],
            h.partner[1],
        )

    def core_add(n, r):
        for y in reversed(range(2)):
            core_copy(n, r, y).wait_recv()
            at = pair(r, y)

            @pl.loop(0, CHUNK // 16)
            def _(i):
                rows = pl.ds(pl.multiple_of(i * 16, 16), 16)
                total = part[n, at + 1 - core, rows, :].astype(jnp.float32) + came[
                    n, at // 2, rows, :
                ].astype(jnp.float32)
                came[n, at // 2, rows, :] = total.astype(jnp.bfloat16)

            offset = ((r >> 1) & 1, r & 1, y)
            for p, (_, _, _, _, order) in enumerate(sums[n].parts):
                bits = [offset[TRIO.index(d)] for d in order]
                if bits[2]:
                    sums[n].copy(p, 2, bits[0] | bits[1] << 1).start()

    def compute_steps(n):
        steps = []
        for r in (3, 2, 1, 0):
            steps.append(functools.partial(compute, n, r))
            if r < 3:
                steps.append(functools.partial(core_add, n, r + 1))
        return steps + [functools.partial(core_add, n, 0)]

    for step in chunk_gather_steps(gathers[0], len(plan)):
        step()
    for one in loads:
        one.wait()
    if back:
        for one in late:
            one.start()
        be_ref[...] = jnp.zeros_like(be_ref)

    tiles = []

    def product(left, right, c, n, dst, slot):
        if len(tiles) >= 2:
            tiles[-2].wait()
        if left is act_all:
            x = right[:, :, :, pl.ds(512 * c, 512)].reshape(D, 512)
            d_tile[slot] = dot_tn(left[...].reshape(D, 512), x).astype(jnp.bfloat16)
        else:
            x = left[:, :, :, pl.ds(512 * c, 512)].reshape(D, 512)
            d_tile[slot] = dot_tn(x, right[...].reshape(D, 512)).astype(jnp.bfloat16)
        tiles.append(pltpu.make_async_copy(d_tile.at[slot], dst, out_sem.at[slot]))
        tiles[-1].start()

    for step in spaced(chunk_gather_steps(gathers[1], len(plan)), compute_steps(0)):
        step()
    out_rows = [o_ref.at[pl.ds(CHUNK * n, CHUNK)] for n in range(2)]
    first = chunk_reduce_steps(sums[0], out_rows[0])
    outs = []
    if back:
        wait_late = [one.wait for one in late]
        of_wc = [
            functools.partial(product, act_all, x_all, c, n, dc_out.at[:, pl.ds(512 * c, 512)], c % 2)
            for n, c in enumerate(range(4))
        ]
        of_we = [
            functools.partial(product, n2_all, h_all, c, n, de_out.at[pl.ds(512 * c, 512)], c % 2)
            for n, c in enumerate(range(4))
        ]
    else:
        outs = [pltpu.make_async_copy(x_all, x_out, out_sem.at[0])]
        outs[0].start()
    for step in spaced(first, compute_steps(1)):
        step()
    last_steps = chunk_reduce_steps(sums[1], out_rows[1])
    if back:
        last_steps = spaced(last_steps, wait_late + of_wc + of_we)
    else:
        outs.append(pltpu.make_async_copy(h_all, h_out, out_sem.at[1]))
        outs.append(pltpu.make_async_copy(slope, slope_out, out_sem.at[2]))
        for one in outs[1:]:
            one.start()
    for step in last_steps:
        step()
    outs += tiles[-2:]
    for n in range(2):
        gathers[n].finish()
        sums[n].finish()
        for r in range(4):
            for y in range(2):
                core_copy(n, r, y).wait_send()
    for one in outs:
        one.wait()


def hidden_layer(back, x, we, wc, rest, plan, collective_id, name):
    bf16, f32 = jnp.bfloat16, jnp.float32
    dma = pltpu.SemaphoreType.DMA
    hbm, vmem = pl.BlockSpec(memory_space=pl.ANY), pl.BlockSpec(memory_space=pltpu.VMEM)
    wide, narrow = (2, 16, CHUNK, D), (2, 16, CHUNK, 512)
    out = [jax.ShapeDtypeStruct((128, D), f32)]
    more = []
    if back:
        out += [
            jax.ShapeDtypeStruct((512, D), bf16),
            jax.ShapeDtypeStruct((D, 512), bf16),
            jax.ShapeDtypeStruct((1, 512), f32),
        ]
        out_specs = [vmem, hbm, hbm, vmem]
        more = [pltpu.VMEM(narrow, bf16), pltpu.VMEM(wide, bf16), pltpu.VMEM((2, 512, 512), bf16)]
    else:
        out += [
            jax.ShapeDtypeStruct(wide, bf16),
            jax.ShapeDtypeStruct(narrow, bf16),
            jax.ShapeDtypeStruct(narrow, bf16),
        ]
        out_specs = [vmem, hbm, hbm, hbm]
    return pl.pallas_call(
        functools.partial(hidden_kernel, back, plan),
        out_shape=out,
        in_specs=[hbm, hbm, hbm] + ([hbm] * 3 if back else [vmem]),
        out_specs=out_specs,
        scratch_shapes=more
        + [
            pltpu.VMEM(wide, bf16),
            pltpu.VMEM((D, 512), bf16),
            pltpu.VMEM((512, D), bf16),
            pltpu.VMEM(narrow, bf16),
            pltpu.VMEM(narrow, bf16),
            pltpu.VMEM(wide, bf16),
            pltpu.VMEM((2, 8, CHUNK, D), bf16),
            pltpu.VMEM((2, 8, CHUNK, D), bf16),
            dma((2, 3, 16)),
            dma((2, 3, 16)),
            dma((2, 8)),
            dma((2, 8)),
            dma((2, 3, 8)),
            dma((2, 3, 8)),
            dma((2,)),
            dma((5,)),
            dma((3,)),
        ],
        compiler_params=pltpu.CompilerParams(
            collective_id=collective_id, has_side_effects=True, vmem_limit_bytes=LIMIT
        ),
        name=name,
    )(x, we, wc, *rest)


QB = 256
KB = WINDOW + QB
SCALE = HD ** (-0.5)
NEAR = (2, 4, "x")


def kept_pairs(lo, a):
    key = a + lax.broadcasted_iota(jnp.int32, (KB, QB), 0)
    last = a + WINDOW + lax.broadcasted_iota(jnp.int32, (KB, QB), 1)
    return (key >= lo) & (key <= last)


class PairSum:
    def __init__(self, h, trio, plan, part, came, buf, sems):
        self.c_send, self.c_recv, r_send, r_recv = sems
        self.h, self.trio, self.part, self.came = h, trio, part, came
        parts = tuple((0, 128, c0, cn, order[:3]) for _, _, c0, cn, order in plan)
        self.sums = Reduce(trio, parts, came, buf, r_send, r_recv)
        self.core = lax.rem(lax.axis_index("shard"), 2)

    def pair(self, o):
        return self.trio.at(NEAR, o)

    def core_copy(self, o):
        n = self.pair(o)
        return remote(
            self.part.at[2 * n + 1 - self.core],
            self.came.at[n],
            self.c_send.at[o],
            self.c_recv.at[o],
            self.h.partner[1],
        )

    def core_add(self, o):
        self.core_copy(o).wait_recv()
        n = self.pair(o)

        @pl.loop(0, 8)
        def _(i):
            rows = pl.ds(pl.multiple_of(i * 16, 16), 16)
            total = self.part[2 * n + self.core, rows, :].astype(jnp.float32) + self.came[
                n, rows, :
            ].astype(jnp.float32)
            self.came[n, rows, :] = total.astype(jnp.bfloat16)

        for p, (_, _, _, _, order) in enumerate(self.sums.parts):
            bits = [o >> NEAR.index(d) & 1 for d in order]
            if bits[2]:
                self.sums.copy(p, 2, bits[0] | bits[1] << 1).start()

    def schedule(self, compute, out, lag=2):
        steps, waiting, made = [], [], []
        for n, o in enumerate(range(7, -1, -1)):
            steps.append(functools.partial(compute, o))
            if n:
                steps.append(functools.partial(self.core_add, o + 1))
                made.append(o + 1)
            for p, (_, _, _, _, order) in enumerate(self.sums.parts):
                for low in range(4):
                    own = sum((low >> b & 1) << NEAR.index(order[b]) for b in range(2))
                    if own in made and made.index(own) <= len(made) - 1 - lag and (p, low) not in waiting:
                        waiting.append((p, low))
                        steps.append(functools.partial(self.sums.add, p, 2, low, out))
        steps.append(functools.partial(self.core_add, 0))
        rest = [
            functools.partial(self.sums.add, p, j, low, out)
            for j in reversed(range(3))
            for low in reversed(range(1 << j))
            for p in range(len(self.sums.parts))
            if j < 2 or (p, low) not in waiting
        ]
        return steps, rest

    def following(self, compute):
        before = []

        def step(o):
            compute(o)
            if before:
                self.core_add(before.pop())
            before.append(o)

        return step, lambda: self.core_add(before.pop())

    def finish(self):
        self.sums.finish()
        for o in range(8):
            self.core_copy(o).wait_send()


def pair_gather_steps(g, used):
    def number(o, order):
        return sum((o >> NEAR.index(d) & 1) << n for n, d in enumerate(order[:3]))

    def link(j, low):
        for p in range(len(g.parts)):
            g.copy(p, low, j).wait_recv()
            for later in range(j + 1, 4):
                g.copy(p, low | 1 << j, later).start()

    def pair(o):
        for p, part in enumerate(g.parts):
            g.copy(p, number(o, part[4]), 3).wait_recv()
        used(o)

    steps = []
    for j in range(3):
        for low in range(1 << j):
            steps.append(functools.partial(link, j, low))
            for o in range(8):
                if max(1, *[number(o, part[4]) for part in g.parts]) == low | 1 << j:
                    steps.append(functools.partial(pair, o))
    return steps


def attend_kernel(plan, *refs):
    ins, refs = refs[:8], refs[8:]
    x_ref, kv_ref, wq_hbm, wkv_hbm, wo_hbm, bq_ref, bkv_ref, lo_ref = ins
    o_ref, x_out, q_out, kv_out, mixed_out, lse_ref = refs[:6]
    refs = refs[6:]
    x_all, wq, wkv, wo, far, far_all, q_all, kv_all, mixed, part, came, buf = refs[:12]
    g_send, g_recv, k_send, k_recv, swap_send, swap_recv, own_sem, load_sem, out_sem = refs[12:21]
    pair_sems = refs[21:]
    h, trio = Hyper(CUBE), Hyper(TRIO)
    sec, shd = lax.axis_index("section"), lax.axis_index("shard")
    other = (sec, shd + 8 * (1 - 2 * (shd // 8)))
    h.barrier((other,))
    swap = remote(kv_ref, far, swap_send, swap_recv, other)
    swap.start()
    loads = [
        pltpu.make_async_copy(x_ref, x_all.at[h.pos], own_sem),
        pltpu.make_async_copy(wq_hbm, wq, load_sem.at[0]),
        pltpu.make_async_copy(wkv_hbm, wkv, load_sem.at[1]),
        pltpu.make_async_copy(wo_hbm, wo, load_sem.at[2]),
    ]
    for one in loads:
        one.start()
    g = Gather(h, plan, x_ref, x_all, g_send, g_recv)
    g.start(range(len(plan)))
    swap.wait_recv()
    far_all[h.pos] = far[...]
    gkv = Gather(h, ((0, 128, 0, 2 * HD, CUBE),), far, far_all, k_send, k_recv)
    gkv.start(range(1))
    for one in loads:
        one.wait()
    sums = PairSum(h, trio, plan, part, came, buf, pair_sems)

    def project(o):
        n = sums.pair(o)
        x = x_all[pl.ds(2 * n, 2)].reshape(QB, D)
        q_all[n] = (dot32(x, wq[...]) + bq_ref[...]).astype(jnp.bfloat16)
        at = pl.ds(pl.multiple_of(WINDOW + QB * lax.rem(n, 4), QB), QB)
        kv_all[n // 4, at] = (dot32(x, wkv[...]) + bkv_ref[...]).astype(jnp.bfloat16)

    far_steps = chunk_gather_steps(gkv, 1)
    for step in spaced(pair_gather_steps(g, project), far_steps):
        step()
    kv_all[:, :WINDOW] = far_all[...].reshape(2, WINDOW, 2 * HD)

    def compute(o):
        n = sums.pair(o)
        m, a = n // 4, pl.multiple_of(QB * lax.rem(n, 4), QB)
        keys = pl.ds(a, KB)
        s = dot_nt(kv_all[m, keys, :HD], q_all[n]) * SCALE
        s = jnp.where(kept_pairs(lo_ref[n], a), s, -1e30)
        top = jnp.max(s, axis=0, keepdims=True)
        e = jnp.exp(s - top)
        total = jnp.sum(e, axis=0, keepdims=True)
        probs = (e * (1.0 / total)).astype(jnp.bfloat16)
        mix = dot_tn(probs, kv_all[m, keys, HD:]).astype(jnp.bfloat16)
        mixed[n] = mix
        lse_ref[n] = top + jnp.log(total)
        for c in range(4):
            cols = pl.ds(512 * c, 512)
            part[pl.ds(2 * n, 2), :, cols] = (
                dot32(mix, wo[:, cols]).astype(jnp.bfloat16).reshape(2, 128, 512)
            )
        sums.core_copy(o).start()

    outs = [
        pltpu.make_async_copy(x_all, x_out, out_sem.at[0]),
        pltpu.make_async_copy(q_all, q_out, out_sem.at[1]),
        pltpu.make_async_copy(kv_all, kv_out, out_sem.at[2]),
    ]
    for one in outs:
        one.start()
    steps, rest = sums.schedule(compute, o_ref)
    for step in steps:
        step()
    outs.append(pltpu.make_async_copy(mixed, mixed_out, out_sem.at[3]))
    outs[-1].start()
    for step in rest:
        step()
    g.finish()
    gkv.finish()
    swap.wait_send()
    sums.finish()
    for one in outs:
        one.wait()


def attend_layer(x, kv, wq, wkv, wo, bq, bkv, lo, plan, collective_id):
    bf16, f32 = jnp.bfloat16, jnp.float32
    dma = pltpu.SemaphoreType.DMA
    hbm, vmem = pl.BlockSpec(memory_space=pl.ANY), pl.BlockSpec(memory_space=pltpu.VMEM)
    out = [
        jax.ShapeDtypeStruct((128, D), f32),
        jax.ShapeDtypeStruct((16, 128, D), bf16),
        jax.ShapeDtypeStruct((8, QB, HD), bf16),
        jax.ShapeDtypeStruct((2, 2 * WINDOW, 2 * HD), bf16),
        jax.ShapeDtypeStruct((8, QB, HD), bf16),
        jax.ShapeDtypeStruct((8, 1, QB), f32),
    ]
    out_specs = [vmem, hbm, hbm, hbm, hbm, vmem]
    return pl.pallas_call(
        functools.partial(attend_kernel, plan),
        out_shape=out,
        in_specs=[hbm] * 5 + [vmem] * 3,
        out_specs=out_specs,
        scratch_shapes=[
            pltpu.VMEM((16, 128, D), bf16),
            pltpu.VMEM((D, HD), bf16),
            pltpu.VMEM((D, 2 * HD), bf16),
            pltpu.VMEM((HD, D), bf16),
            pltpu.VMEM((128, 2 * HD), bf16),
            pltpu.VMEM((16, 128, 2 * HD), bf16),
            pltpu.VMEM((8, QB, HD), bf16),
            pltpu.VMEM((2, 2 * WINDOW, 2 * HD), bf16),
            pltpu.VMEM((8, QB, HD), bf16),
            pltpu.VMEM((16, 128, D), bf16),
            pltpu.VMEM((8, 128, D), bf16),
            pltpu.VMEM((8, 128, D), bf16),
            dma((3, 16)),
            dma((3, 16)),
            dma((1, 16)),
            dma((1, 16)),
            dma,
            dma,
            dma,
            dma((3,)),
            dma((4,)),
            dma((8,)),
            dma((8,)),
            dma((3, 8)),
            dma((3, 8)),
        ],
        compiler_params=pltpu.CompilerParams(
            collective_id=collective_id, has_side_effects=True, vmem_limit_bytes=LIMIT
        ),
        name="attend",
    )(x, kv, wq, wkv, wo, bq, bkv, lo)


class Home:
    def __init__(self, home, c_count, c, e, rc, re, sems):
        self.home, self.c_count, self.c, self.e, self.rc, self.re = home, c_count, c, e, rc, re
        self.send, self.c_recv, self.e_recv, self.own_sem = sems
        self.sec, self.shd = lax.axis_index("section"), lax.axis_index("shard")
        self.half, self.low = self.shd // 8, lax.rem(self.shd, 8)
        self.me, self.place = half_group(self.sec, self.shd)
        self.here = self.sec == home

    def copies(self, n):
        if n < self.c_count:
            size = 256 // self.c_count
            src = self.c.at[pl.ds(size * n, size)]
            dst = self.rc.at[pl.ds(256 * self.sec + size * n, size)]
            return self.here, [(src, dst, (self.home, self.shd), self.send.at[n, 0], self.c_recv.at[n], self.own_sem.at[n, 0])]
        k = n - self.c_count
        return jnp.logical_and(self.here, self.low == k), [
            (
                self.e.at[pl.ds(128 * k, 128), pl.ds(256 * c, 256)],
                self.re.at[:, columns(2 * (8 * c + self.low) + self.sec, 256)],
                (self.home, 8 * self.half + k),
                self.send.at[n, c],
                self.e_recv.at[self.me, c],
                self.own_sem.at[n, c],
            )
            for c in range(2)
        ]

    def go(self, n, start):
        local, copies = self.copies(n)

        @pl.when(local)
        def _():
            for src, dst, _, _, _, sem in copies:
                one = pltpu.make_async_copy(src, dst, sem)
                one.start() if start else one.wait()

        @pl.when(jnp.logical_not(local))
        def _():
            for src, dst, there, send, recv, _ in copies:
                one = remote(src, dst, send, recv, there)
                one.start() if start else one.wait_send()

    def finish(self):
        for n in range(self.c_count + 8):
            self.go(n, False)

        @pl.when(self.here)
        def _():
            size = 256 // self.c_count
            for n in range(self.c_count):
                rows = pl.ds(size * n, size)
                remote(
                    self.c.at[rows], self.rc.at[rows], self.send.at[n, 0], self.c_recv.at[n], (1 - self.sec, self.shd)
                ).wait_recv()

            @pl.loop(1, 16)
            def _(d):
                n = lax.rem(self.me + d, 16)
                for c in range(2):
                    remote(
                        self.e.at[pl.ds(0, 128), pl.ds(0, 256)],
                        self.re.at[:, pl.ds(256 * c, 256)],
                        self.send.at[self.c_count, c],
                        self.e_recv.at[n, c],
                        self.place(n),
                    ).wait_recv()


def attend_back_kernel(plan, home, *refs):
    x_ref, n1_hbm, wq_hbm, wo_hbm, q_hbm, kv_hbm, mixed_hbm, lse_ref, lo_ref, gc, ge, cross = refs[:12]
    if home == 0:
        c_before, e_before = refs[12:14]
        refs = refs[:12] + refs[14:]
    o_ref, own_ref, far_ref, wo_ref, wq_ref, bq_ref, rc, re, crossed = refs[12:21]
    if home == 0:
        rc_before, re_before = refs[21:23]
        refs = refs[:21] + refs[23:]
    x_all, n1, wq, wo, q_all, kv_all, mixed, dq_all, dk, dv, part, came, buf = refs[21:34]
    kv_parts, kv_bufs, sent = refs[34:36], refs[36:38], refs[38]
    c_kept, c_came, e_kept, e_came = refs[39:43]
    g_send, g_recv, swap_send, swap_recv, own_sem, load_sem, bg_send, bg_recv = refs[43:51]
    pair_sems, kv_sems = refs[51:55], refs[55:59]
    home_sems, (kept_sem, x_send, x_recv) = refs[59:63], refs[63:66]
    deliver = home == 0
    if deliver:
        back_home = Home(home, 8, c_kept, e_kept, rc, re, home_sems)
        before = Home(1, 8, c_before, e_before, rc_before, re_before, refs[66:])
    h, trio = Hyper(CUBE), Hyper(TRIO)
    sec, shd = lax.axis_index("section"), lax.axis_index("shard")
    half, low = shd // 8, lax.rem(shd, 8)
    other = (sec, shd + 8 * (1 - 2 * half))
    me, place = half_group(sec, shd)
    barrier = pltpu.get_barrier_semaphore()

    @pl.loop(1, 16)
    def _(d):
        pl.semaphore_signal(
            barrier, inc=1, device_id=place(lax.rem(me + d, 16)), device_id_type=MESH
        )

    pl.semaphore_signal(barrier, inc=1, device_id=other, device_id_type=MESH)
    pl.semaphore_wait(barrier, 16)

    def beside(n):
        if n < 8:
            rows = pl.ds(32 * n, 32)
            src, dst = gc.at[1 - half, rows], c_came.at[rows]
        else:
            rows = pl.ds(128 * (n - 8), 128)
            src, dst = ge.at[1 - half, rows], e_came.at[rows]
        return remote(src, dst, bg_send.at[n], bg_recv.at[n], other)

    def land(n):
        beside(n).wait_recv()
        mine, theirs, first, count = (c_kept, c_came, 32 * n, 2) if n < 8 else (e_kept, e_came, 128 * (n - 8), 8)

        @pl.loop(0, count)
        def _(i):
            rows = pl.ds(pl.multiple_of(first + 16 * i, 16), 16)
            total = mine[rows, :].astype(jnp.float32) + theirs[rows, :].astype(jnp.float32)
            mine[rows, :] = total.astype(mine.dtype)

        if deliver:
            back_home.go(n, True)

    LAG = 7 if home == 0 else 16
    turns = []
    for n in range(16 + LAG):
        turn = []
        if n < 16:
            turn.append(beside(n).start)
            if deliver:
                turn.append(functools.partial(before.go, n, True))
        if n >= LAG:
            turn.append(functools.partial(land, n - LAG))
        turns.append(turn)

    def feed(steps, every):
        for n, step in enumerate(steps):
            step()
            if turns and n % every == every - 1:
                for one in turns.pop(0):
                    one()

    kept = [
        pltpu.make_async_copy(gc.at[half], c_kept, kept_sem.at[0]),
        pltpu.make_async_copy(ge.at[half], e_kept, kept_sem.at[1]),
    ]
    for one in kept:
        one.start()
    swap_rows = remote(cross, crossed, x_send, x_recv, (1 - sec, shd))

    def swap_step(step, sending):
        if home == 1:
            step()
        else:
            pl.when(sec == (0 if sending else 1))(step)

    own = pltpu.make_async_copy(x_ref, x_all.at[h.pos], own_sem)
    own.start()
    g = Gather(h, plan, x_ref, x_all, g_send, g_recv)
    g.start(range(len(plan)))
    pairs = ((wq_hbm, wq), (wo_hbm, wo), (q_hbm, q_all), (kv_hbm, kv_all), (mixed_hbm, mixed), (n1_hbm, n1))
    loads = [pltpu.make_async_copy(src, dst, load_sem.at[n]) for n, (src, dst) in enumerate(pairs)]
    for one in loads:
        one.start()
    own.wait()
    for one in loads[:5] + kept:
        one.wait()
    sums = PairSum(h, trio, plan, part, came, buf, pair_sems)

    bq_ref[...] = jnp.zeros_like(bq_ref)
    dk[...] = jnp.zeros_like(dk)
    dv[...] = jnp.zeros_like(dv)

    def compute(o):
        n = sums.pair(o)
        m, a = n // 4, pl.multiple_of(QB * lax.rem(n, 4), QB)
        keys = pl.ds(a, KB)
        q, k = q_all[n], kv_all[m, keys, :HD]
        gm = dot_nt(x_all[pl.ds(2 * n, 2)].reshape(QB, D), wo[...]).astype(jnp.bfloat16)
        s = dot_nt(k, q) * SCALE
        probs = jnp.where(kept_pairs(lo_ref[n], a), jnp.exp(s - lse_ref[n]), 0.0)
        gp = dot_nt(kv_all[m, keys, HD:], gm)
        row = jnp.sum(probs * gp, axis=0, keepdims=True)
        gs = (probs * (gp - row)).astype(jnp.bfloat16)
        dq = (dot_tn(gs, k) * SCALE).astype(jnp.bfloat16)
        dq_all[n] = dq
        bq_ref[...] += jnp.sum(dq.astype(jnp.float32), axis=0, keepdims=True)
        for c in range(4):
            rows = pl.ds(512 * c, 512)
            part[pl.ds(2 * n, 2), :, rows] = (
                dot_nt(dq, wq[rows, :]).astype(jnp.bfloat16).reshape(2, 128, 512)
            )
        sums.core_copy(o).start()
        dk[m, keys] += dot32(gs, q) * SCALE
        dv[m, keys] += dot32(probs.astype(jnp.bfloat16), gm)

    step, last_add = sums.following(compute)
    feed(pair_gather_steps(g, step), 2)
    last_add()
    swap_step(swap_rows.start, True)
    for one, first in zip(kv_parts, (WINDOW, 0)):
        rows = pl.ds(first, WINDOW)
        one[:, :, :HD] = dk[:, rows].astype(jnp.bfloat16).reshape(16, 128, HD)
        one[:, :, HD:] = dv[:, rows].astype(jnp.bfloat16).reshape(16, 128, HD)
    rest = chunk_reduce_steps(sums.sums, o_ref)
    kv_sums = [
        Reduce(h, BESIDE[n], kv_parts[n], kv_bufs[n], kv_sems[2 * n], kv_sems[2 * n + 1]) for n in range(2)
    ]
    for n in reversed(range(8)):
        for r in kv_sums:
            r.copy(0, 3, n).start()

    def product(left, right, c):
        cols = pl.ds(512 * c, 512)
        tile = dot_tn(left[...].reshape(D, HD), right[:, :, cols].reshape(D, 512))
        if right is x_all:
            wo_ref[:, cols] = tile.astype(wo_ref.dtype)
        else:
            wq_ref[cols, :] = tile.T.astype(wq_ref.dtype)

    products = [functools.partial(product, mixed, x_all, c) for c in range(4)]
    products += [loads[5].wait] + [functools.partial(product, dq_all, n1, c) for c in range(4)]
    kv_steps = [
        step
        for pair in zip(chunk_reduce_steps(kv_sums[0], own_ref), chunk_reduce_steps(kv_sums[1], far_ref))
        for step in pair
    ]
    feed(spaced(spaced(rest, kv_steps), products), 3)
    sent[0] = far_ref[...].astype(sent.dtype)
    swap = remote(sent.at[0], sent.at[1], swap_send, swap_recv, other)
    swap.start()
    while turns:
        for one in turns.pop(0):
            one()
    g.finish()
    sums.finish()
    for r in kv_sums:
        r.finish()
    swap.wait()
    far_ref[...] = sent[1].astype(jnp.float32)
    swap_step(swap_rows.wait_send, True)
    swap_step(swap_rows.wait_recv, False)
    for n in range(16):
        beside(n).wait_send()
    if deliver:
        back_home.finish()
        before.finish()
    else:
        summed = [
            pltpu.make_async_copy(c_kept, rc, kept_sem.at[0]),
            pltpu.make_async_copy(e_kept, re, kept_sem.at[1]),
        ]
        for one in summed:
            one.start()
        for one in summed:
            one.wait()


def attend_back_layer(x, n1, wq, wo, q, kv, mixed, lse, lo, gc, ge, cross, before, home, plan, collective_id):
    bf16, f32 = jnp.bfloat16, jnp.float32
    dma = pltpu.SemaphoreType.DMA
    hbm, vmem = pl.BlockSpec(memory_space=pl.ANY), pl.BlockSpec(memory_space=pltpu.VMEM)
    pair = pltpu.VMEM((16, 128, 2 * HD), bf16)
    homes = [jax.ShapeDtypeStruct((512, D), bf16), jax.ShapeDtypeStruct((128, 8192), bf16)]
    sums = [jax.ShapeDtypeStruct((256, D), bf16), jax.ShapeDtypeStruct((1024, 512), bf16)]
    home_sems = [dma((16, 2)), dma((8,)), dma((16, 2)), dma((16, 2))]
    return pl.pallas_call(
        functools.partial(attend_back_kernel, plan, home),
        out_shape=[
            jax.ShapeDtypeStruct((128, D), f32),
            jax.ShapeDtypeStruct((128, 2 * HD), f32),
            jax.ShapeDtypeStruct((128, 2 * HD), f32),
            jax.ShapeDtypeStruct((HD, D), bf16),
            jax.ShapeDtypeStruct((D, HD), bf16),
            jax.ShapeDtypeStruct((1, HD), f32),
        ]
        + (homes if home == 0 else sums)
        + [jax.ShapeDtypeStruct((128, D), bf16)]
        + (homes if home == 0 else []),
        in_specs=[hbm] * 7 + [vmem] * 2 + [hbm] * (3 + len(before)),
        out_specs=[vmem] * 6 + [hbm] * (3 + len(before)),
        scratch_shapes=[
            pltpu.VMEM((16, 128, D), bf16),
            pltpu.VMEM((16, 128, D), bf16),
            pltpu.VMEM((D, HD), bf16),
            pltpu.VMEM((HD, D), bf16),
            pltpu.VMEM((8, QB, HD), bf16),
            pltpu.VMEM((2, 2 * WINDOW, 2 * HD), bf16),
            pltpu.VMEM((8, QB, HD), bf16),
            pltpu.VMEM((8, QB, HD), bf16),
            pltpu.VMEM((2, 2 * WINDOW, HD), f32),
            pltpu.VMEM((2, 2 * WINDOW, HD), f32),
            pltpu.VMEM((16, 128, D), bf16),
            pltpu.VMEM((8, 128, D), bf16),
            pltpu.VMEM((8, 128, D), bf16),
            pair,
            pair,
            pair,
            pair,
            pltpu.VMEM((2, 128, 2 * HD), bf16),
            pltpu.VMEM((256, D), bf16),
            pltpu.VMEM((256, D), bf16),
            pltpu.VMEM((1024, 512), bf16),
            pltpu.VMEM((1024, 512), bf16),
            dma((3, 16)),
            dma((3, 16)),
            dma,
            dma,
            dma,
            dma((6,)),
            dma((16,)),
            dma((16,)),
            dma((8,)),
            dma((8,)),
            dma((3, 8)),
            dma((3, 8)),
            dma((1, 16)),
            dma((1, 16)),
            dma((1, 16)),
            dma((1, 16)),
            *home_sems,
            dma((2,)),
            dma,
            dma,
        ]
        + (home_sems if home == 0 else []),
        compiler_params=pltpu.CompilerParams(
            collective_id=collective_id, has_side_effects=True, vmem_limit_bytes=LIMIT
        ),
        name="attend_back",
    )(x, n1, wq, wo, q, kv, mixed, lse, lo, gc, ge, cross, *before)


BESIDE = ((0, 128, 0, 256, (4, 2, "x", 1)),), ((0, 128, 0, 256, (2, "x", 4, 1)),)
SMALL = tuple(
    (48 * n, 48, 0, 256, order)
    for n, order in enumerate(((8, "x", 4, 2, 1), (8, 4, 2, "x", 1), (8, 2, "x", 4, 1)))
)
BIAS = D + HD


def on_device_fast(
    embedded,
    cotangent,
    segments,
    first_gain,
    first_shift,
    mixer_weight,
    mixer_bias,
    output_weight,
    output_bias,
    second_gain,
    second_shift,
    expand_weight,
    expand_bias,
    contract_weight,
    contract_bias,
):
    bf16, f32 = jnp.bfloat16, jnp.float32
    sec, shd = lax.axis_index("section"), lax.axis_index("shard")
    half = shd // 8
    f = block_of(sec, shd)

    small = jnp.concatenate(
        [
            first_gain[0],
            first_shift[0],
            second_gain[0],
            second_shift[0],
            output_bias[0],
            contract_bias[0],
            expand_bias[0],
            mixer_bias[0],
        ]
    )
    small = jnp.concatenate([small, jnp.zeros((16 * 256 - small.shape[0],), bf16)]).reshape(16, 256)
    shared, wq, wo, we, wc = fetch_weights(
        jnp.concatenate([mixer_weight[0][:, D:], small], axis=0),
        mixer_weight[0],
        output_weight[0],
        expand_weight[0],
        contract_weight[0],
    )
    we = [we[s].reshape(8 * 128, 512) for s in range(2)]
    for s in range(2):
        we[s] = from_halves(we[s])
    wc = [from_halves(wc[s]) for s in range(2)]
    wq = wq.reshape(2, D, HD)
    shared = shared.reshape(2, 16, 144, 256)
    wkv = shared[:, :, :128].reshape(2, D, 256)
    vectors = shared[:, :, 128:].reshape(2, 16, 4096)

    def vector(n):
        return vectors[:, :, 128 * n : 128 * (n + 1)].reshape(2, D).astype(f32)

    gain_one, shift_one, gain_two, shift_two, bias_out, bias_con = [vector(n) for n in range(6)]
    bias_exp = vectors[:, :, 768:1280].reshape(2, 8192).astype(f32)
    hidden_units = [512 * (8 * h + lax.rem(shd, 8)) + 256 * sec for h in range(2)]
    bias_exp = jnp.concatenate(
        [lax.dynamic_slice_in_dim(bias_exp, first, 256, 1) for first in hidden_units], axis=1
    )
    bias_mix = vectors[:, :, 1280 : 1280 + 136].reshape(2, BIAS).astype(f32)
    bias_q = lax.dynamic_slice_in_dim(bias_mix, f * HD, HD, 1)
    bias_kv = jnp.concatenate([jnp.zeros((2, HD), f32), bias_mix[:, D:]], axis=1)

    starts = jnp.sum(
        (segments[:, None, :] < lax.dynamic_slice_in_dim(segments, half * WINDOW, WINDOW, 1)[:, :, None]),
        axis=2,
        dtype=jnp.int32,
    )
    lo = jnp.maximum(jnp.arange(1, WINDOW + 1)[None], starts - half * WINDOW + WINDOW)
    lo = lo.reshape(8, 1, QB)

    hidden = lax.dynamic_index_in_dim(embedded, sec, 0, keepdims=False).astype(f32)
    results, kept = [], []
    for s in range(2):
        n1 = layer_norm(hidden, gain_one[s], shift_one[s]).astype(bf16)
        kv_rows = (dot32(n1, wkv[s]) + bias_kv[s]).astype(bf16)
        rows, all_n1, q, kv, mixed, lse = attend_layer(
            n1,
            kv_rows,
            wq[s],
            wkv[s],
            wo[s],
            bias_q[s][None],
            bias_kv[s][None],
            lo,
            LIGHT if s == 0 else EVEN,
            3 + s,
        )
        middle = hidden + rows + bias_out[s]
        n2 = layer_norm(middle, gain_two[s], shift_two[s]).astype(bf16)
        rows, all_n2, act, slope = hidden_layer(False, n2, we[s], wc[s], (bias_exp[s][None],), LIGHT if s == 0 else EVEN, 9 + 2 * s, "hidden")
        result = middle + rows + bias_con[s]
        results.append(result.astype(bf16))
        kept.append((hidden, n1, all_n1, q, kv, lse, mixed, middle, all_n2, act, slope))
        hidden = results[-1].astype(f32)

    grad = lax.dynamic_index_in_dim(cotangent, sec, 0, keepdims=False).astype(f32)
    cross = jnp.where(sec == 0, results[1], results[0])
    came = [None, None]
    input_grads = [None, None]
    weight_grads = [None, None]
    small_grads = [None, None]
    for s in (1, 0):
        hidden, n1, all_n1, q, kv, lse, mixed, middle, all_n2, act, slope = kept[s]
        go = grad.astype(bf16)
        g_n2, d_wc, d_we, d_be = hidden_layer(
            True, go, we[s], wc[s], (slope, act, all_n2), EVEN, 10, "hidden_back"
        )
        d_wc, d_we, d_be = d_wc.reshape(2, 256, D), d_we.reshape(2, 1024, 512), d_be[0]
        _, back = jax.vjp(layer_norm, middle, gain_two[s], shift_two[s])
        g_mid, d_gain_two, d_shift_two = back(g_n2)
        g_mid = grad + g_mid
        ga = g_mid.astype(bf16)
        rows, kv_own, kv_far, d_wo, d_wq, d_bq, d_wc, d_we, crossed, *before = attend_back_layer(
            ga,
            all_n1,
            wq[s],
            wo[s],
            q,
            kv,
            mixed,
            lse,
            lo,
            d_wc,
            d_we,
            cross,
            () if s == 1 else weight_grads[1][2:],
            s,
            LIGHT,
            5 + s,
        )
        dkv_rows = (kv_own + jnp.where(half == 0, kv_far, 0.0)).astype(bf16)
        g_n1 = rows + dot_nt(dkv_rows, wkv[s])
        _, back = jax.vjp(layer_norm, hidden, gain_one[s], shift_one[s])
        g_in, d_gain_one, d_shift_one = back(g_n1)
        g_in = g_mid + g_in
        input_grads[s] = g_in
        d_wkv = dot_tn(n1, dkv_rows)
        d_bq = d_bq[0]
        d_bv = jnp.sum(dkv_rows[:, HD:].astype(f32), axis=0)
        weight_grads[s] = (d_wq.reshape(16, 128, HD), d_wo, d_wc, d_we)
        came[s] = crossed
        cross = g_in.astype(bf16)
        spread = [
            d_gain_one,
            d_shift_one,
            d_gain_two,
            d_shift_two,
            jnp.sum(ga.astype(f32), axis=0),
            jnp.sum(go.astype(f32), axis=0),
        ]
        placed = jnp.zeros((8192,), f32)
        for h, first in enumerate(hidden_units):
            placed = lax.dynamic_update_slice_in_dim(placed, d_be[256 * h : 256 * (h + 1)], first, 0)
        d_bm = lax.dynamic_update_slice_in_dim(jnp.zeros((D,), f32), d_bq, f * HD, 0)
        vec = jnp.concatenate(
            [one.reshape(16, 128) for one in spread]
            + [placed.reshape(16, 512), jnp.concatenate([d_bm, d_bv]).reshape(16, 136)],
            axis=1,
        )
        vec = jnp.pad(vec, ((0, 0), (0, 4096 - vec.shape[1]))).reshape(16, 16, 256)
        small_grads[s] = jnp.concatenate([d_wkv.reshape(16, 128, 256), vec], axis=1)
        grad = cross.astype(f32)

    mine, rq, ro, last_came = return_last(
        jnp.concatenate(small_grads, axis=0).astype(bf16),
        (weight_grads[0][0], weight_grads[1][0]),
        (weight_grads[0][1], weight_grads[1][1]),
        cross,
    )
    vec = mine[128:].reshape(4096)

    def both(r):
        return r[0].astype(f32) + r[1].astype(f32)

    def here(pair):
        return jnp.where(sec == 0, pair[0], pair[1])

    def by_micro(own, theirs):
        return jnp.stack([jnp.where(sec == 0, own, theirs), jnp.where(sec == 0, theirs, own)])[None]

    grad_rows = here((last_came, came[0])).astype(f32)
    return (
        by_micro(here(results), came[1]),
        by_micro(here(input_grads), grad_rows),
        vec[0:128][None],
        vec[128:256][None],
        jnp.concatenate([both(rq), mine[:128]], axis=1)[None],
        vec[1280 : 1280 + 136][None],
        both(ro)[None],
        vec[512:640][None],
        vec[256:384][None],
        vec[384:512][None],
        here((weight_grads[0][3], before[1])).astype(f32)[None],
        vec[768:1280][None],
        here((weight_grads[0][2], before[0])).astype(f32)[None],
        vec[640:768][None],
    )


def solution(mesh):
    in_specs = (
        P(None, "shard", None),
        P(None, "shard", None),
        P(),
        P("section", "shard"),
        P("section", "shard"),
        P("section", "shard", None),
        P("section", "shard"),
        P("section", "shard", None),
        P("section", "shard"),
        P("section", "shard"),
        P("section", "shard"),
        P("section", "shard", None),
        P("section", "shard"),
        P("section", "shard", None),
        P("section", "shard"),
    )
    out_specs = (
        P("section", None, "shard", None),
        P("section", None, "shard", None),
        P("section", "shard"),
        P("section", "shard"),
        P("section", "shard", None),
        P("section", "shard"),
        P("section", "shard", None),
        P("section", "shard"),
        P("section", "shard"),
        P("section", "shard"),
        P("section", "shard", None),
        P("section", "shard"),
        P("section", "shard", None),
        P("section", "shard"),
    )
    fits = mesh.shape["section"] == 2 and mesh.shape["shard"] == HEADS
    on_device = on_device_fast if fits else on_device_general
    return jax.shard_map(
        on_device, mesh=mesh, in_specs=in_specs, out_specs=out_specs, check_vma=False
    )
```

```python
import functools

import jax
import jax.numpy as jnp
from jax import lax
from jax.experimental import pallas as pl
from jax.experimental.pallas import tpu as pltpu
from jax.sharding import PartitionSpec as P

D = 2048
HEADS = 16
HD = 128
WINDOW = 1024


epsilon = 1e-05


def passed_along(block, axis, distance):
    devices = range(lax.axis_size(axis))
    route = [(i - distance, i) for i in devices if i - distance in devices]
    return lax.ppermute(block, axis, route)


def layer_norm(values, gain_row, shift_row):
    center = values - jnp.mean(values, axis=-1, keepdims=True)
    spread = jnp.mean(center * center, axis=-1, keepdims=True)
    return center * lax.rsqrt(spread + epsilon) * gain_row + shift_row


def gelu_tanh(values):
    return jax.nn.gelu(values, approximate=True)


def window_mask(segments, micro_index, device, row_count, reach_blocks):
    seg_row = lax.dynamic_index_in_dim(segments, micro_index, 0, keepdims=False)
    padded = jnp.concatenate([jnp.full((reach_blocks * row_count,), -1, jnp.int32), seg_row])
    key_segments = lax.dynamic_slice_in_dim(
        padded, device * row_count, (reach_blocks + 1) * row_count
    )
    query_segments = lax.dynamic_slice_in_dim(seg_row, device * row_count, row_count)
    distance = (
        jnp.arange(row_count)[:, None]
        + reach_blocks * row_count
        - jnp.arange((reach_blocks + 1) * row_count)[None, :]
    )
    return (
        (distance >= 0) & (distance < WINDOW) & (query_segments[:, None] == key_segments[None, :])
    )


def fetch_window(key_value, reach_blocks):
    earlier = [passed_along(key_value, "shard", offset) for offset in range(reach_blocks, 0, -1)]
    return jnp.concatenate(earlier + [key_value], axis=0)


def return_window(window_grad, reach_blocks, row_count):
    own_rows = window_grad[reach_blocks * row_count :]
    for offset in range(1, reach_blocks + 1):
        start_row = (reach_blocks - offset) * row_count
        own_rows = own_rows + passed_along(
            window_grad[start_row : start_row + row_count].astype(jnp.bfloat16), "shard", -offset
        ).astype(jnp.float32)
    return own_rows


def forward_layer(hidden, weights, key_mask, reach_blocks):
    (
        first_gain,
        first_shift,
        mixer_weight,
        mixer_bias,
        output_weight,
        output_bias,
        second_gain,
        second_shift,
        expand_weight,
        expand_bias,
        contract_weight,
        contract_bias,
    ) = weights
    row_count = hidden.shape[0]
    score_scale = HD ** (-0.5)
    normed_one = layer_norm(
        hidden, first_gain.astype(jnp.float32), first_shift.astype(jnp.float32)
    ).astype(jnp.bfloat16)
    full_bias = jnp.concatenate(
        [mixer_bias[:D], jnp.zeros((HD,), mixer_bias.dtype), mixer_bias[D:]]
    ).astype(jnp.float32)
    projected = (
        jnp.dot(normed_one, mixer_weight, preferred_element_type=jnp.float32) + full_bias
    ).astype(jnp.bfloat16)
    queries = projected[:, :D].reshape(row_count, HEADS, HD)
    window_pairs = fetch_window(projected[:, D:], reach_blocks)
    scores = (
        jnp.einsum("thd,kd->htk", queries, window_pairs[:, :HD], preferred_element_type=jnp.float32)
        * score_scale
    )
    masked = jnp.where(key_mask[None], scores, -1e30)
    top_score = jnp.max(masked, axis=2, keepdims=True)
    exponent = jnp.exp(masked - top_score)
    totals = jnp.sum(exponent, axis=2, keepdims=True)
    prob_low = (exponent / totals).astype(jnp.bfloat16)
    log_total = top_score + jnp.log(totals)
    mixed_rows = (
        jnp.einsum(
            "htk,kd->thd", prob_low, window_pairs[:, HD:], preferred_element_type=jnp.float32
        )
        .reshape(row_count, D)
        .astype(jnp.bfloat16)
    )
    middle = (
        hidden
        + jnp.dot(mixed_rows, output_weight, preferred_element_type=jnp.float32)
        + output_bias.astype(jnp.float32)
    )
    normed_two = layer_norm(
        middle, second_gain.astype(jnp.float32), second_shift.astype(jnp.float32)
    ).astype(jnp.bfloat16)
    pre_gelu = jnp.dot(
        normed_two, expand_weight, preferred_element_type=jnp.float32
    ) + expand_bias.astype(jnp.float32)
    activated = gelu_tanh(pre_gelu).astype(jnp.bfloat16)
    result = (
        middle
        + jnp.dot(activated, contract_weight, preferred_element_type=jnp.float32)
        + contract_bias.astype(jnp.float32)
    )
    return (
        result,
        (
            hidden,
            normed_one,
            projected,
            window_pairs,
            log_total,
            mixed_rows,
            middle,
            normed_two,
            pre_gelu,
            activated,
        ),
    )


def backward_layer(grad_result, weights, saved_state, key_mask, reach_blocks):
    (
        first_gain,
        first_shift,
        mixer_weight,
        mixer_bias,
        output_weight,
        output_bias,
        second_gain,
        second_shift,
        expand_weight,
        expand_bias,
        contract_weight,
        contract_bias,
    ) = weights
    (
        hidden,
        normed_one,
        projected,
        window_pairs,
        log_total,
        mixed_rows,
        middle,
        normed_two,
        pre_gelu,
        activated,
    ) = saved_state
    row_count = hidden.shape[0]
    score_scale = HD ** (-0.5)
    grad_out_low = grad_result.astype(jnp.bfloat16)
    grad_act = jnp.einsum(
        "rd,fd->rf", grad_out_low, contract_weight, preferred_element_type=jnp.float32
    )
    gelu_value, gelu_back = jax.vjp(gelu_tanh, pre_gelu)
    grad_pre = gelu_back(grad_act)[0].astype(jnp.bfloat16)
    grad_normed_two = jnp.einsum(
        "rf,df->rd", grad_pre, expand_weight, preferred_element_type=jnp.float32
    )
    norm_value_two, norm_back_two = jax.vjp(
        layer_norm, middle, second_gain.astype(jnp.float32), second_shift.astype(jnp.float32)
    )
    grad_middle_part, grad_gain_two, grad_shift_two = norm_back_two(grad_normed_two)
    grad_middle = grad_result + grad_middle_part
    grad_attended = grad_middle.astype(jnp.bfloat16)
    grad_mixed = (
        jnp.einsum("re,de->rd", grad_attended, output_weight, preferred_element_type=jnp.float32)
        .astype(jnp.bfloat16)
        .reshape(row_count, HEADS, HD)
    )
    queries = projected[:, :D].reshape(row_count, HEADS, HD)
    key_part = window_pairs[:, :HD]
    value_part = window_pairs[:, HD:]
    scores = (
        jnp.einsum("thd,kd->htk", queries, key_part, preferred_element_type=jnp.float32)
        * score_scale
    )
    prob_full = jnp.where(key_mask[None], jnp.exp(scores - log_total), 0.0)
    prob_low = prob_full.astype(jnp.bfloat16)
    grad_probs = jnp.einsum(
        "thd,kd->htk", grad_mixed, value_part, preferred_element_type=jnp.float32
    )
    row_dot = jnp.sum(prob_full * grad_probs, axis=2, keepdims=True)
    grad_scores = (prob_full * (grad_probs - row_dot)).astype(jnp.bfloat16)
    grad_queries = (
        jnp.einsum("htk,kd->thd", grad_scores, key_part, preferred_element_type=jnp.float32)
        * score_scale
    ).reshape(row_count, D)
    grad_keys = (
        jnp.einsum("htk,thd->kd", grad_scores, queries, preferred_element_type=jnp.float32)
        * score_scale
    )
    grad_values = jnp.einsum(
        "htk,thd->kd", prob_low, grad_mixed, preferred_element_type=jnp.float32
    )
    grad_window = jnp.concatenate([grad_keys, grad_values], axis=1)
    grad_own_pairs = return_window(grad_window, reach_blocks, row_count)
    grad_projected = jnp.concatenate([grad_queries, grad_own_pairs], axis=1).astype(jnp.bfloat16)
    grad_normed_one = jnp.einsum(
        "rq,dq->rd", grad_projected, mixer_weight, preferred_element_type=jnp.float32
    )
    norm_value_one, norm_back_one = jax.vjp(
        layer_norm, hidden, first_gain.astype(jnp.float32), first_shift.astype(jnp.float32)
    )
    grad_hidden_part, grad_gain_one, grad_shift_one = norm_back_one(grad_normed_one)
    grad_hidden = grad_middle + grad_hidden_part
    return (
        grad_hidden,
        (
            grad_projected,
            grad_attended,
            grad_pre,
            grad_out_low,
            grad_gain_one,
            grad_shift_one,
            grad_gain_two,
            grad_shift_two,
            normed_one,
            mixed_rows,
            normed_two,
            activated,
        ),
    )


def flatten_rows(stacked):
    return stacked.reshape((-1, stacked.shape[-1]))


def weight_terms(row_items, norm_items):
    (
        grad_projected_rows,
        grad_attended_rows,
        grad_pre_rows,
        grad_out_rows,
        normed_one_rows,
        mixed_all,
        normed_two_rows,
        activated_rows,
    ) = row_items
    first_gain_term, first_shift_term, second_gain_term, second_shift_term = norm_items
    mixer_weight_term = jnp.einsum(
        "rd,rq->dq", normed_one_rows, grad_projected_rows, preferred_element_type=jnp.float32
    )
    column_totals = jnp.sum(grad_projected_rows.astype(jnp.float32), axis=0)
    mixer_bias_term = jnp.concatenate([column_totals[:D], column_totals[D + HD :]])
    output_weight_term = jnp.einsum(
        "rd,re->de", mixed_all, grad_attended_rows, preferred_element_type=jnp.float32
    )
    output_bias_term = jnp.sum(grad_attended_rows.astype(jnp.float32), axis=0)
    expand_weight_term = jnp.einsum(
        "rd,rf->df", normed_two_rows, grad_pre_rows, preferred_element_type=jnp.float32
    )
    expand_bias_term = jnp.sum(grad_pre_rows.astype(jnp.float32), axis=0)
    contract_weight_term = jnp.einsum(
        "rf,rd->fd", activated_rows, grad_out_rows, preferred_element_type=jnp.float32
    )
    contract_bias_term = jnp.sum(grad_out_rows.astype(jnp.float32), axis=0)
    return (
        first_gain_term[None],
        first_shift_term[None],
        mixer_weight_term[None],
        mixer_bias_term[None],
        output_weight_term[None],
        output_bias_term[None],
        second_gain_term[None],
        second_shift_term[None],
        expand_weight_term[None],
        expand_bias_term[None],
        contract_weight_term[None],
        contract_bias_term[None],
    )


def on_device_general(
    embedded,
    cotangent,
    segments,
    first_gain,
    first_shift,
    mixer_weight,
    mixer_bias,
    output_weight,
    output_bias,
    second_gain,
    second_shift,
    expand_weight,
    expand_bias,
    contract_weight,
    contract_bias,
):
    section_index = lax.axis_index("section")
    device = lax.axis_index("shard")
    micro_count = embedded.shape[0]
    row_count = embedded.shape[1]
    reach_blocks = WINDOW // row_count
    own_params = (
        first_gain[0],
        first_shift[0],
        mixer_weight[0],
        mixer_bias[0],
        output_weight[0],
        output_bias[0],
        second_gain[0],
        second_shift[0],
        expand_weight[0],
        expand_bias[0],
        contract_weight[0],
        contract_bias[0],
    )
    forward_weights = (
        lax.all_gather(own_params[0], "shard", axis=0, tiled=True),
        lax.all_gather(own_params[1], "shard", axis=0, tiled=True),
        lax.all_gather(own_params[2], "shard", axis=0, tiled=True),
        lax.all_gather(own_params[3], "shard", axis=0, tiled=True),
        lax.all_gather(own_params[4], "shard", axis=0, tiled=True),
        lax.all_gather(own_params[5], "shard", axis=0, tiled=True),
        lax.all_gather(own_params[6], "shard", axis=0, tiled=True),
        lax.all_gather(own_params[7], "shard", axis=0, tiled=True),
        lax.all_gather(own_params[8], "shard", axis=0, tiled=True),
        lax.all_gather(own_params[9], "shard", axis=0, tiled=True),
        lax.all_gather(own_params[10], "shard", axis=0, tiled=True),
        lax.all_gather(own_params[11], "shard", axis=0, tiled=True),
    )
    zero_rows = jnp.zeros((row_count, D), jnp.float32)
    arrived = zero_rows
    sent_list = []
    kept_states = []
    for step_index in range(micro_count + 1):
        own_input = (
            embedded[step_index].astype(jnp.float32) if step_index < micro_count else zero_rows
        )
        hidden = jnp.where(section_index == 0, own_input, arrived)
        micro_index = jnp.clip(step_index - section_index, 0, micro_count - 1)
        key_mask = window_mask(segments, micro_index, device, row_count, reach_blocks)
        result, saved_state = forward_layer(hidden, forward_weights, key_mask, reach_blocks)
        result_low = result.astype(jnp.bfloat16)
        sent_list.append(result_low)
        kept_states.append(saved_state)
        if step_index < micro_count:
            arrived = passed_along(result_low, "section", 1).astype(jnp.float32)
    section_outputs = lax.dynamic_slice_in_dim(jnp.stack(sent_list), section_index, micro_count, 0)[
        None
    ]
    stacked_states = [
        jnp.stack([state_item[item_index] for state_item in kept_states])
        for item_index in range(10)
    ]
    valid_start = 1 - section_index
    arrived_grad = zero_rows
    grad_records = []
    hidden_grads = []
    for step_index in range(micro_count + 1):
        own_grad = (
            cotangent[step_index].astype(jnp.float32) if step_index < micro_count else zero_rows
        )
        grad_result = jnp.where(section_index == 1, own_grad, arrived_grad)
        forward_index = jnp.clip(step_index - 1 + 2 * section_index, 0, micro_count)
        micro_index = jnp.clip(step_index - 1 + section_index, 0, micro_count - 1)
        saved_state = [
            lax.dynamic_index_in_dim(stacked, forward_index, 0, keepdims=False)
            for stacked in stacked_states
        ]
        key_mask = window_mask(segments, micro_index, device, row_count, reach_blocks)
        grad_hidden, record = backward_layer(
            grad_result, forward_weights, saved_state, key_mask, reach_blocks
        )
        hidden_grads.append(grad_hidden)
        if step_index < micro_count:
            arrived_grad = passed_along(grad_hidden.astype(jnp.bfloat16), "section", -1).astype(
                jnp.float32
            )
        grad_records.append(record)
    input_grads = lax.dynamic_slice_in_dim(jnp.stack(hidden_grads), valid_start, micro_count, 0)[
        None
    ]
    chosen = [
        lax.dynamic_slice_in_dim(
            jnp.stack([record[item_index] for record in grad_records]), valid_start, micro_count, 0
        )
        for item_index in range(12)
    ]
    row_items = (
        flatten_rows(chosen[0]),
        flatten_rows(chosen[1]),
        flatten_rows(chosen[2]),
        flatten_rows(chosen[3]),
        flatten_rows(chosen[8]),
        flatten_rows(chosen[9]),
        flatten_rows(chosen[10]),
        flatten_rows(chosen[11]),
    )
    norm_items = (
        jnp.sum(chosen[4], axis=0),
        jnp.sum(chosen[5], axis=0),
        jnp.sum(chosen[6], axis=0),
        jnp.sum(chosen[7], axis=0),
    )
    all_terms = weight_terms(row_items, norm_items)
    summed = (
        lax.psum_scatter(all_terms[0], "shard", scatter_dimension=1, tiled=True),
        lax.psum_scatter(all_terms[1], "shard", scatter_dimension=1, tiled=True),
        lax.psum_scatter(all_terms[2], "shard", scatter_dimension=1, tiled=True),
        lax.psum_scatter(all_terms[3], "shard", scatter_dimension=1, tiled=True),
        lax.psum_scatter(all_terms[4], "shard", scatter_dimension=1, tiled=True),
        lax.psum_scatter(all_terms[5], "shard", scatter_dimension=1, tiled=True),
        lax.psum_scatter(all_terms[6], "shard", scatter_dimension=1, tiled=True),
        lax.psum_scatter(all_terms[7], "shard", scatter_dimension=1, tiled=True),
        lax.psum_scatter(all_terms[8], "shard", scatter_dimension=1, tiled=True),
        lax.psum_scatter(all_terms[9], "shard", scatter_dimension=1, tiled=True),
        lax.psum_scatter(all_terms[10], "shard", scatter_dimension=1, tiled=True),
        lax.psum_scatter(all_terms[11], "shard", scatter_dimension=1, tiled=True),
    )
    return (
        section_outputs,
        input_grads,
        summed[0],
        summed[1],
        summed[2],
        summed[3],
        summed[4],
        summed[5],
        summed[6],
        summed[7],
        summed[8],
        summed[9],
        summed[10],
        summed[11],
    )


MESH = pl.DeviceIdType.MESH
LIMIT = 60 << 20
CUBE = ("x", 4, 2, 1)
ALL = ("x", 8, 4, 2, 1)


def columns(n, wide):
    return pl.ds(pl.multiple_of(n * wide, wide), wide)


def remote(src, dst, send, recv, there):
    return pltpu.make_async_remote_copy(
        src_ref=src, dst_ref=dst, send_sem=send, recv_sem=recv, device_id=there, device_id_type=MESH
    )


class Hyper:
    def __init__(self, dims):
        sec = lax.axis_index("section")
        shd = lax.axis_index("shard")
        self.dims = dims
        self.partner, self.delta, self.pos = {}, {}, 0
        for n, d in enumerate(dims):
            weight = 1 << (len(dims) - 1 - n)
            if d == "x":
                bit = sec
                self.partner[d] = (1 - sec, shd)
            else:
                bit = lax.rem(shd // d, 2)
                self.partner[d] = (sec, shd + d * (1 - 2 * bit))
            self.pos = self.pos + bit * weight
            self.delta[d] = weight * (1 - 2 * bit)

    def at(self, order, offset):
        place = self.pos
        for j, d in enumerate(order):
            if offset >> j & 1:
                place = place + self.delta[d]
        return place

    def barrier(self, more=()):
        sem = pltpu.get_barrier_semaphore()
        partners = [self.partner[d] for d in self.dims] + list(more)
        for partner in partners:
            pl.semaphore_signal(sem, inc=1, device_id=partner, device_id_type=MESH)
        pl.semaphore_wait(sem, len(partners))


def cube_parts(rows, widths, col0=0):
    orders = (("x", 4, 2, 1), (4, 2, "x", 1), (2, "x", 4, 1))
    parts = []
    for width, order in zip(widths, orders):
        parts.append((0, rows, col0, width, order))
        col0 += width
    return tuple(parts)


class Gather:
    def __init__(self, h, parts, src, dst, send_sem, recv_sem):
        self.h, self.parts, self.src, self.dst = h, parts, src, dst
        self.send_sem, self.recv_sem = send_sem, recv_sem

    def copy(self, p, offset, j):
        r0, rn, c0, cn, order = self.parts[p]
        rows, cols = pl.ds(r0, rn), pl.ds(c0, cn)
        there = self.dst.at[self.h.at(order, offset), rows, cols]
        here = self.src.at[rows, cols] if offset == 0 else there
        n = offset | 1 << j
        return pltpu.make_async_remote_copy(
            src_ref=here,
            dst_ref=there,
            send_sem=self.send_sem.at[p, n],
            recv_sem=self.recv_sem.at[p, n],
            device_id=self.h.partner[order[j]],
            device_id_type=MESH,
        )

    def start(self, chosen):
        for j in range(len(self.h.dims)):
            for p in chosen:
                self.copy(p, 0, j).start()

    def forward(self, chosen):
        k = len(self.h.dims)
        for j in range(k):
            for low in range(1 << j):
                for p in chosen:
                    self.copy(p, low, j).wait_recv()
                    for later in range(j + 1, k):
                        self.copy(p, low | 1 << j, later).start()

    def finish(self):
        for p in range(len(self.parts)):
            for j in range(len(self.h.dims)):
                for low in range(1 << j):
                    self.copy(p, low, j).wait_send()


class Reduce:
    def __init__(self, h, parts, src, buf, send_sem, recv_sem):
        self.h, self.parts, self.src, self.buf = h, parts, src, buf
        self.send_sem, self.recv_sem = send_sem, recv_sem

    def window(self, p):
        r0, rn, c0, cn, order = self.parts[p]
        return pl.ds(r0, rn), pl.ds(c0, cn)

    def held(self, p, j, offset):
        if j == len(self.h.dims) - 1:
            return self.src.at[(self.h.at(self.parts[p][4], offset),) + self.window(p)]
        return self.buf.at[((1 << (j + 1)) | offset,) + self.window(p)]

    def copy(self, p, j, low):
        n = (1 << j) | low
        return remote(
            self.held(p, j, low | 1 << j),
            self.buf.at[(n,) + self.window(p)],
            self.send_sem.at[p, n],
            self.recv_sem.at[p, n],
            self.h.partner[self.parts[p][4][j]],
        )

    def add(self, p, j, low, out=None):
        self.copy(p, j, low).wait_recv()
        r0, rn, c0, cn, order = self.parts[p]
        mine = self.held(p, j, low)
        came = self.buf.at[((1 << j) | low,) + self.window(p)]
        step = 16

        @pl.loop(0, rn // step)
        def _(i):
            rows = pl.ds(pl.multiple_of(i * step, step), step)
            total = mine[rows, :].astype(jnp.float32) + came[rows, :].astype(jnp.float32)
            if j > 0:
                came[rows, :] = total.astype(came.dtype)
            else:
                out[pl.ds(pl.multiple_of(r0 + i * step, step), step), pl.ds(c0, cn)] = total

        if j > 0 and low >> (j - 1) & 1:
            self.copy(p, j - 1, low ^ (1 << (j - 1))).start()

    def finish(self):
        for p in range(len(self.parts)):
            for j in range(len(self.h.dims)):
                for low in range(1 << j):
                    self.copy(p, j, low).wait_send()


def block_of(sec, shd):
    return 8 * lax.rem(sec + lax.rem(shd, 2), 2) + lax.rem(shd, 8)


def half_group(sec, shd):
    first = 8 * (shd // 8)
    return 8 * sec + lax.rem(shd, 8), lambda n: (n // 8, first + lax.rem(n, 8))


class Spread:
    def __init__(self, pieces, own_sem, send, recv):
        self.sec, self.shd = lax.axis_index("section"), lax.axis_index("shard")
        self.me, self.place = half_group(self.sec, self.shd)
        self.pieces, self.own_sem, self.send, self.recv = pieces, own_sem, send, recv

    def copies(self, d):
        there = self.place(lax.rem(self.me + d, 16))
        return [
            remote(src, dst, self.send.at[n, d], self.recv.at[n, d], there)
            for n, (src, dst) in enumerate(self.pieces(*there))
        ]

    def own(self):
        return [
            pltpu.make_async_copy(src, dst, self.own_sem.at[n])
            for n, (src, dst) in enumerate(self.pieces(self.sec, self.shd))
        ]

    def start(self):
        @pl.loop(1, 16)
        def _(d):
            for one in self.copies(d):
                one.start()

        for one in self.own():
            one.start()


def everyone_barrier(me):
    sem = pltpu.get_barrier_semaphore()

    @pl.loop(1, 32)
    def _(d):
        there = lax.rem(me + d, 32)
        pl.semaphore_signal(
            sem, inc=1, device_id=(there // 16, lax.rem(there, 16)), device_id_type=MESH
        )

    pl.semaphore_wait(sem, 31)


def fetch_kernel(small, mix, out, exp, con, wkv, vec, wq, wo, we_0, we_1, wc_0, wc_1, *sems):
    q_send, q_recv, send, recv, con_send, con_recv, out_send, out_recv, own_sem = sems[:9]
    kv_send, kv_recv, v_send, v_recv = sems[9:]
    sec, shd = lax.axis_index("section"), lax.axis_index("shard")
    low, half = lax.rem(shd, 8), shd // 8
    me = 16 * sec + shd
    everyone_barrier(me)
    h = Hyper(ALL)
    mix_kv = mix.at[:, pl.ds(D, 2 * HD)]
    gathers = [Gather(h, ALL_KV, mix_kv, wkv, kv_send, kv_recv), Gather(h, ALL_SMALL, small, vec, v_send, v_recv)]
    for g in gathers:
        g.start(range(len(g.parts)))

    def spread_to(we):
        def pieces(ts, tj):
            for n in range(2):
                yield (
                    exp.at[:, columns(2 * (8 * n + lax.rem(tj, 8)) + ts, 256)],
                    we.at[low, :, pl.ds(256 * n, 256)],
                )

        return Spread(pieces, own_sem, send, recv)

    def to_section(step):
        for s, arrays in enumerate(((spread_to(we_0), wc_0), (spread_to(we_1), wc_1))):
            pl.when(sec == s)(functools.partial(step, *arrays))

    def query(d):
        there = lax.rem(me + d, 32)
        ts, tj = there // 16, lax.rem(there, 16)
        return remote(
            mix.at[:, columns(block_of(ts, tj), HD)], wq.at[sec, shd], q_send.at[d], q_recv.at[d], (ts, tj)
        )

    @pl.loop(1, 32)
    def _(d):
        query(d).start()

    to_section(lambda spread, wc: spread.start())

    to_x = lax.rem(half + lax.rem(shd, 2), 2)
    from_half = lax.rem(sec + lax.rem(shd, 2), 2)
    own_out = pltpu.make_async_copy(out, wo.at[sec], own_sem.at[6])
    for z in range(2):
        mine = jnp.logical_and(to_x == sec, half == z)
        there = remote(out, wo.at[sec], out_send.at[z], out_recv.at[sec], (to_x, 8 * z + low))

        @pl.when(mine)
        def _():
            own_out.start()

        @pl.when(jnp.logical_not(mine))
        def _():
            there.start()

    own = [
        pltpu.make_async_copy(mix_kv, wkv.at[h.pos], own_sem.at[2]),
        pltpu.make_async_copy(small, vec.at[h.pos], own_sem.at[3]),
        pltpu.make_async_copy(mix.at[:, columns(block_of(sec, shd), HD)], wq.at[sec, shd], own_sem.at[4]),
    ]
    for one in own:
        one.start()

    def own_rows(wc):
        return pltpu.make_async_copy(con.at[pl.ds(256 * sec, 256)], wc, own_sem.at[5])

    def rows(wc):
        return remote(con.at[pl.ds(256 * (1 - sec), 256)], wc, con_send, con_recv, (1 - sec, shd))

    def start_rows(spread, wc):
        own_rows(wc).start()
        rows(wc).start()

    to_section(start_rows)
    for j in range(len(ALL)):
        for n in range(1 << j):
            for g in gathers:
                for p in range(len(g.parts)):
                    g.copy(p, n, j).wait_recv()
                    for later in range(j + 1, len(ALL)):
                        g.copy(p, n | 1 << j, later).start()

    @pl.loop(1, 32)
    def _(d):
        query(d).wait_recv()

    for s in range(2):
        mine = jnp.logical_and(sec == s, from_half == half)

        @pl.when(jnp.logical_not(mine))
        def _():
            remote(out, wo.at[s], out_send.at[0], out_recv.at[s], (1 - sec, shd)).wait_recv()

    for s, wc in enumerate((wc_0, wc_1)):
        pl.when(sec != s)(rows(wc).wait_recv)

    @pl.loop(1, 16)
    def _(d):
        for n in range(2):
            some = pl.ds(256 * n, 256)
            remote(
                exp.at[:, some], we_0.at[0, :, some], send.at[n, d], recv.at[n, d], (1 - sec, shd)
            ).wait_recv()

    def sent(spread, wc):
        @pl.loop(1, 16)
        def _(d):
            for one in spread.copies(d):
                one.wait_send()

        for one in spread.own():
            one.wait()
        own_rows(wc).wait()
        rows(wc).wait_send()

    to_section(sent)

    @pl.loop(1, 32)
    def _(d):
        query(d).wait_send()

    for z in range(2):
        mine = jnp.logical_and(to_x == sec, half == z)
        there = remote(out, wo.at[sec], out_send.at[z], out_recv.at[sec], (to_x, 8 * z + low))

        @pl.when(mine)
        def _():
            own_out.wait()

        @pl.when(jnp.logical_not(mine))
        def _():
            there.wait_send()

    for g in gathers:
        g.finish()
    for one in own:
        one.wait()


def fetch_weights(small, mix, out, exp, con):
    bf16 = jnp.bfloat16
    dma = pltpu.SemaphoreType.DMA
    return pl.pallas_call(
        fetch_kernel,
        out_shape=(
            jax.ShapeDtypeStruct((32, 128, 2 * HD), bf16),
            jax.ShapeDtypeStruct((32,) + small.shape, bf16),
            jax.ShapeDtypeStruct((2, 16, 128, HD), bf16),
            jax.ShapeDtypeStruct((2, 128, D), bf16),
            jax.ShapeDtypeStruct((8, 128, 512), bf16),
            jax.ShapeDtypeStruct((8, 128, 512), bf16),
            jax.ShapeDtypeStruct((256, D), bf16),
            jax.ShapeDtypeStruct((256, D), bf16),
        ),
        in_specs=[pl.BlockSpec(memory_space=pl.ANY)] * 5,
        out_specs=[pl.BlockSpec(memory_space=pl.ANY)] * 8,
        scratch_shapes=[
            dma((32,)),
            dma((32,)),
            dma((2, 16)),
            dma((2, 16)),
            dma,
            dma,
            dma((2,)),
            dma((2,)),
            dma((7,)),
            dma((3, 32)),
            dma((3, 32)),
            dma((1, 32)),
            dma((1, 32)),
        ],
        compiler_params=pltpu.CompilerParams(
            collective_id=1, has_side_effects=True, vmem_limit_bytes=LIMIT
        ),
        name="fetch_weights",
    )(small, mix, out, exp, con)


def last_kernel(small, gq0, gq1, go0, go1, cross, total, rq, ro, crossed, *scratch):
    buf, s_send, s_recv, q_send, q_recv, out_send, out_recv, own_sem, x_send, x_recv = scratch
    sec, shd = lax.axis_index("section"), lax.axis_index("shard")
    half = shd // 8
    f = block_of(sec, shd)
    everyone_barrier(16 * sec + shd)
    h = Hyper(ALL)
    k = len(ALL)
    r = Reduce(h, SMALL, small, buf, s_send, s_recv)
    for low in reversed(range(1 << (k - 1))):
        for p in range(len(SMALL)):
            r.copy(p, k - 1, low).start()
    swap = remote(cross, crossed, x_send, x_recv, (1 - sec, shd))
    pl.when(sec == 1)(swap.start)

    def query(s, d):
        src = (gq0, gq1)[s].at[lax.rem(shd + d, 16)]
        dst = rq.at[half, :, columns(f, HD)]
        return src, dst, remote(src, dst, q_send.at[s, d], q_recv.at[sec, d], (s, lax.rem(shd + d, 16)))

    def rows(s):
        src, dst = (go0, go1)[s], ro.at[half]
        return src, dst, remote(src, dst, out_send.at[s], out_recv.at[half], (s, f))

    def either(local, n, copy, start):
        src, dst, there = copy
        here = pltpu.make_async_copy(src, dst, own_sem.at[n])

        @pl.when(local)
        def _():
            here.start() if start else here.wait()

        @pl.when(jnp.logical_not(local))
        def _():
            there.start() if start else there.wait_send()

    for s in range(2):
        either(sec == s, 0, query(s, 0), True)
        either(jnp.logical_and(sec == s, f == shd), 1, rows(s), True)

        @pl.loop(1, 16)
        def _(d):
            query(s, d)[2].start()

    for j in reversed(range(k)):
        for low in reversed(range(1 << j)):
            for p in range(len(SMALL)):
                r.add(p, j, low, total)
    pl.when(sec == 1)(swap.wait_send)
    pl.when(sec == 0)(swap.wait_recv)

    def arrival(s, d):
        return remote(gq0.at[0], rq.at[0, :, pl.ds(0, HD)], q_send.at[0, 0], q_recv.at[s, d], (1 - sec, shd))

    for s in range(2):

        @pl.when(sec != s)
        def _():
            arrival(s, 0).wait_recv()

        @pl.loop(1, 16)
        def _(d):
            arrival(s, d).wait_recv()

        @pl.when(jnp.logical_not(jnp.logical_and(f == shd, half == s)))
        def _():
            remote(go0, ro.at[s], out_send.at[0], out_recv.at[s], (1 - sec, shd)).wait_recv()

    for s in range(2):
        either(sec == s, 0, query(s, 0), False)
        either(jnp.logical_and(sec == s, f == shd), 1, rows(s), False)

        @pl.loop(1, 16)
        def _(d):
            query(s, d)[2].wait_send()

    r.finish()


def return_last(small, gq, go, cross):
    bf16, f32 = jnp.bfloat16, jnp.float32
    dma = pltpu.SemaphoreType.DMA
    hbm, vmem = pl.BlockSpec(memory_space=pl.ANY), pl.BlockSpec(memory_space=pltpu.VMEM)
    return pl.pallas_call(
        last_kernel,
        out_shape=(
            jax.ShapeDtypeStruct(small.shape[1:], f32),
            jax.ShapeDtypeStruct((2, 128, D), bf16),
            jax.ShapeDtypeStruct((2, 128, D), bf16),
            jax.ShapeDtypeStruct((128, D), bf16),
        ),
        in_specs=[vmem] + [hbm] * 5,
        out_specs=[vmem] + [hbm] * 3,
        scratch_shapes=[
            pltpu.VMEM(small.shape, bf16),
            dma((3, 32)),
            dma((3, 32)),
            dma((2, 16)),
            dma((2, 16)),
            dma((2,)),
            dma((2,)),
            dma((2,)),
            dma,
            dma,
        ],
        compiler_params=pltpu.CompilerParams(
            collective_id=2, has_side_effects=True, vmem_limit_bytes=LIMIT
        ),
        name="return_last",
    )(small, *gq, *go, cross)


HALVES = [[n, n + 8] for n in range(8)]


def from_halves(x):
    return lax.all_gather(x, "shard", axis=0, tiled=True, axis_index_groups=HALVES)


NT = (((1,), (1,)), ((), ()))
TN = (((0,), (0,)), ((), ()))


def dot32(a, b):
    return jnp.dot(a, b, preferred_element_type=jnp.float32)


def dot_nt(a, b):
    return lax.dot_general(a, b, NT, preferred_element_type=jnp.float32)


def dot_tn(a, b):
    return lax.dot_general(a, b, TN, preferred_element_type=jnp.float32)


EVEN = cube_parts(128, (768, 640, 640))
LIGHT = cube_parts(128, (896, 896, 256))
TRIO = ("x", 4, 2)
CHUNK = 64


def spaced(many, few):
    result = []
    for n, step in enumerate(many):
        result.append(step)
        done = len(few) * (n + 1) // len(many)
        result.extend(few[len(few) * n // len(many) : done])
    return result


def chunk_gather_steps(g, count):
    k = len(g.h.dims)

    def step(j, low):
        for p in range(count):
            g.copy(p, low, j).wait_recv()
            for later in range(j + 1, k):
                g.copy(p, low | 1 << j, later).start()

    return [functools.partial(step, j, low) for j in range(k) for low in range(1 << j)]


def chunk_reduce_steps(r, out):
    k = len(r.h.dims)
    return [
        functools.partial(r.add, p, j, low, out)
        for j in reversed(range(k))
        for low in reversed(range(1 << j))
        for p in range(len(r.parts))
    ]


GELU_K = (2.0 / 3.141592653589793) ** 0.5


def gelu_pair(u):
    square = u * u
    t = jnp.tanh(GELU_K * (u + 0.044715 * u * square))
    half = 0.5 * (1.0 + t)
    slope = half + 0.5 * u * (1.0 - t * t) * (GELU_K * (1.0 + 3 * 0.044715 * square))
    return u * half, slope


def hidden_kernel(back, plan, *refs):
    if back:
        x_ref, we_hbm, wc_hbm, slope_hbm, act_hbm, n2_hbm, o_ref, dc_out, de_out, be_ref = refs[:10]
        act_all, n2_all, d_tile = refs[10:13]
        scratch = refs[13:]
    else:
        x_ref, we_hbm, wc_hbm, be_ref, o_ref, x_out, h_out, slope_out = refs[:8]
        scratch = refs[8:]
    x_all, we, wc, h_all, slope, part, came, buf = scratch[:8]
    g_send, g_recv, c_send, c_recv, r_send, r_recv, own_sem, load_sem, out_sem = scratch[8:]
    h = Hyper(CUBE)
    trio = Hyper(TRIO)
    h.barrier()
    loads = [pltpu.make_async_copy(we_hbm, we, load_sem.at[0]), pltpu.make_async_copy(wc_hbm, wc, load_sem.at[1])]
    if back:
        loads.append(pltpu.make_async_copy(slope_hbm, slope, load_sem.at[2]))
        late = [
            pltpu.make_async_copy(act_hbm, act_all, load_sem.at[3]),
            pltpu.make_async_copy(n2_hbm, n2_all, load_sem.at[4]),
        ]
    parts = tuple((0, CHUNK, c0, cn, order) for _, _, c0, cn, order in plan)
    gathers, sums = [], []
    for n in range(2):
        mine = x_ref.at[pl.ds(CHUNK * n, CHUNK)]
        own = pltpu.make_async_copy(mine, x_all.at[n, h.pos], own_sem.at[n])
        own.start()
        loads.append(own)
        gathers.append(Gather(h, parts, mine, x_all.at[n], g_send.at[n], g_recv.at[n]))
        sums.append(
            Reduce(
                trio,
                tuple((0, CHUNK, c0, cn, order[:3]) for _, _, c0, cn, order in plan),
                came.at[n],
                buf.at[n],
                r_send.at[n],
                r_recv.at[n],
            )
        )
        gathers[n].start(range(len(plan)))
    for one in loads[:-2]:
        one.start()
    core = 1 - lax.rem(lax.axis_index("shard"), 2)

    def quad(r):
        return 4 * (h.pos // 4) + (h.delta["x"] if r & 2 else 0) + (h.delta[4] if r & 1 else 0)

    def pair(r, y):
        return quad(r) + 2 * (lax.rem(h.pos, 4) // 2) + (h.delta[2] if y else 0)

    def compute(n, r):
        four = pl.ds(quad(r), 4)
        x = x_all[n, four].reshape(4 * CHUNK, D)
        if back:
            inner = dot_nt(x, wc[...]).reshape(4, CHUNK, 512)
            mid = (inner * slope[n, four].astype(jnp.float32)).astype(jnp.bfloat16)
        else:
            inner = dot32(x, we[...]) + be_ref[...]
            act, grad = gelu_pair(inner)
            mid = act.astype(jnp.bfloat16).reshape(4, CHUNK, 512)
            slope[n, four] = grad.astype(jnp.bfloat16).reshape(4, CHUNK, 512)
        h_all[n, four] = mid
        mid = mid.reshape(4 * CHUNK, 512)
        if back:
            be_ref[...] += jnp.sum(mid.astype(jnp.float32), axis=0, keepdims=True)
        for c in range(4):
            cols = pl.ds(512 * c, 512)
            tile = dot_nt(mid, we[cols, :]) if back else dot32(mid, wc[:, cols])
            part[n, four, :, cols] = tile.astype(jnp.bfloat16).reshape(4, CHUNK, 512)
        for y in reversed(range(2)):
            core_copy(n, r, y).start()

    def core_copy(n, r, y):
        at = pair(r, y)
        return remote(
            part.at[n, at + core],
            came.at[n, at // 2],
            c_send.at[n, 2 * r + y],
            c_recv.at[n, 2 * r + y],
            h.partner[1],
        )

    def core_add(n, r):
        for y in reversed(range(2)):
            core_copy(n, r, y).wait_recv()
            at = pair(r, y)

            @pl.loop(0, CHUNK // 16)
            def _(i):
                rows = pl.ds(pl.multiple_of(i * 16, 16), 16)
                total = part[n, at + 1 - core, rows, :].astype(jnp.float32) + came[
                    n, at // 2, rows, :
                ].astype(jnp.float32)
                came[n, at // 2, rows, :] = total.astype(jnp.bfloat16)

            offset = ((r >> 1) & 1, r & 1, y)
            for p, (_, _, _, _, order) in enumerate(sums[n].parts):
                bits = [offset[TRIO.index(d)] for d in order]
                if bits[2]:
                    sums[n].copy(p, 2, bits[0] | bits[1] << 1).start()

    def compute_steps(n):
        steps = []
        for r in (3, 2, 1, 0):
            steps.append(functools.partial(compute, n, r))
            if r < 3:
                steps.append(functools.partial(core_add, n, r + 1))
        return steps + [functools.partial(core_add, n, 0)]

    for step in chunk_gather_steps(gathers[0], len(plan)):
        step()
    for one in loads:
        one.wait()
    if back:
        for one in late:
            one.start()
        be_ref[...] = jnp.zeros_like(be_ref)

    tiles = []

    def product(left, right, c, n, dst, slot):
        if len(tiles) >= 2:
            tiles[-2].wait()
        if left is act_all:
            x = right[:, :, :, pl.ds(512 * c, 512)].reshape(D, 512)
            d_tile[slot] = dot_tn(left[...].reshape(D, 512), x).astype(jnp.bfloat16)
        else:
            x = left[:, :, :, pl.ds(512 * c, 512)].reshape(D, 512)
            d_tile[slot] = dot_tn(x, right[...].reshape(D, 512)).astype(jnp.bfloat16)
        tiles.append(pltpu.make_async_copy(d_tile.at[slot], dst, out_sem.at[slot]))
        tiles[-1].start()

    for step in spaced(chunk_gather_steps(gathers[1], len(plan)), compute_steps(0)):
        step()
    out_rows = [o_ref.at[pl.ds(CHUNK * n, CHUNK)] for n in range(2)]
    first = chunk_reduce_steps(sums[0], out_rows[0])
    outs = []
    if back:
        wait_late = [one.wait for one in late]
        of_wc = [
            functools.partial(product, act_all, x_all, c, n, dc_out.at[:, pl.ds(512 * c, 512)], c % 2)
            for n, c in enumerate(range(4))
        ]
        of_we = [
            functools.partial(product, n2_all, h_all, c, n, de_out.at[pl.ds(512 * c, 512)], c % 2)
            for n, c in enumerate(range(4))
        ]
    else:
        outs = [pltpu.make_async_copy(x_all, x_out, out_sem.at[0])]
        outs[0].start()
    for step in spaced(first, compute_steps(1)):
        step()
    last_steps = chunk_reduce_steps(sums[1], out_rows[1])
    if back:
        last_steps = spaced(last_steps, wait_late + of_wc + of_we)
    else:
        outs.append(pltpu.make_async_copy(h_all, h_out, out_sem.at[1]))
        outs.append(pltpu.make_async_copy(slope, slope_out, out_sem.at[2]))
        for one in outs[1:]:
            one.start()
    for step in last_steps:
        step()
    outs += tiles[-2:]
    for n in range(2):
        gathers[n].finish()
        sums[n].finish()
        for r in range(4):
            for y in range(2):
                core_copy(n, r, y).wait_send()
    for one in outs:
        one.wait()


def hidden_layer(back, x, we, wc, rest, plan, collective_id, name):
    bf16, f32 = jnp.bfloat16, jnp.float32
    dma = pltpu.SemaphoreType.DMA
    hbm, vmem = pl.BlockSpec(memory_space=pl.ANY), pl.BlockSpec(memory_space=pltpu.VMEM)
    wide, narrow = (2, 16, CHUNK, D), (2, 16, CHUNK, 512)
    out = [jax.ShapeDtypeStruct((128, D), f32)]
    more = []
    if back:
        out += [
            jax.ShapeDtypeStruct((512, D), bf16),
            jax.ShapeDtypeStruct((D, 512), bf16),
            jax.ShapeDtypeStruct((1, 512), f32),
        ]
        out_specs = [vmem, hbm, hbm, vmem]
        more = [pltpu.VMEM(narrow, bf16), pltpu.VMEM(wide, bf16), pltpu.VMEM((2, 512, 512), bf16)]
    else:
        out += [
            jax.ShapeDtypeStruct(wide, bf16),
            jax.ShapeDtypeStruct(narrow, bf16),
            jax.ShapeDtypeStruct(narrow, bf16),
        ]
        out_specs = [vmem, hbm, hbm, hbm]
    return pl.pallas_call(
        functools.partial(hidden_kernel, back, plan),
        out_shape=out,
        in_specs=[hbm, hbm, hbm] + ([hbm] * 3 if back else [vmem]),
        out_specs=out_specs,
        scratch_shapes=more
        + [
            pltpu.VMEM(wide, bf16),
            pltpu.VMEM((D, 512), bf16),
            pltpu.VMEM((512, D), bf16),
            pltpu.VMEM(narrow, bf16),
            pltpu.VMEM(narrow, bf16),
            pltpu.VMEM(wide, bf16),
            pltpu.VMEM((2, 8, CHUNK, D), bf16),
            pltpu.VMEM((2, 8, CHUNK, D), bf16),
            dma((2, 3, 16)),
            dma((2, 3, 16)),
            dma((2, 8)),
            dma((2, 8)),
            dma((2, 3, 8)),
            dma((2, 3, 8)),
            dma((2,)),
            dma((5,)),
            dma((3,)),
        ],
        compiler_params=pltpu.CompilerParams(
            collective_id=collective_id, has_side_effects=True, vmem_limit_bytes=LIMIT
        ),
        name=name,
    )(x, we, wc, *rest)


QB = 256
KB = WINDOW + QB
SCALE = HD ** (-0.5)
NEAR = (2, 4, "x")


def kept_pairs(lo, a):
    key = a + lax.broadcasted_iota(jnp.int32, (KB, QB), 0)
    last = a + WINDOW + lax.broadcasted_iota(jnp.int32, (KB, QB), 1)
    return (key >= lo) & (key <= last)


class PairSum:
    def __init__(self, h, trio, plan, part, came, buf, sems):
        self.c_send, self.c_recv, r_send, r_recv = sems
        self.h, self.trio, self.part, self.came = h, trio, part, came
        parts = tuple((0, 128, c0, cn, order[:3]) for _, _, c0, cn, order in plan)
        self.sums = Reduce(trio, parts, came, buf, r_send, r_recv)
        self.core = lax.rem(lax.axis_index("shard"), 2)

    def pair(self, o):
        return self.trio.at(NEAR, o)

    def core_copy(self, o):
        n = self.pair(o)
        return remote(
            self.part.at[2 * n + 1 - self.core],
            self.came.at[n],
            self.c_send.at[o],
            self.c_recv.at[o],
            self.h.partner[1],
        )

    def core_add(self, o):
        self.core_copy(o).wait_recv()
        n = self.pair(o)

        @pl.loop(0, 8)
        def _(i):
            rows = pl.ds(pl.multiple_of(i * 16, 16), 16)
            total = self.part[2 * n + self.core, rows, :].astype(jnp.float32) + self.came[
                n, rows, :
            ].astype(jnp.float32)
            self.came[n, rows, :] = total.astype(jnp.bfloat16)

        for p, (_, _, _, _, order) in enumerate(self.sums.parts):
            bits = [o >> NEAR.index(d) & 1 for d in order]
            if bits[2]:
                self.sums.copy(p, 2, bits[0] | bits[1] << 1).start()

    def schedule(self, compute, out, lag=2):
        steps, waiting, made = [], [], []
        for n, o in enumerate(range(7, -1, -1)):
            steps.append(functools.partial(compute, o))
            if n:
                steps.append(functools.partial(self.core_add, o + 1))
                made.append(o + 1)
            for p, (_, _, _, _, order) in enumerate(self.sums.parts):
                for low in range(4):
                    own = sum((low >> b & 1) << NEAR.index(order[b]) for b in range(2))
                    if own in made and made.index(own) <= len(made) - 1 - lag and (p, low) not in waiting:
                        waiting.append((p, low))
                        steps.append(functools.partial(self.sums.add, p, 2, low, out))
        steps.append(functools.partial(self.core_add, 0))
        rest = [
            functools.partial(self.sums.add, p, j, low, out)
            for j in reversed(range(3))
            for low in reversed(range(1 << j))
            for p in range(len(self.sums.parts))
            if j < 2 or (p, low) not in waiting
        ]
        return steps, rest

    def following(self, compute):
        before = []

        def step(o):
            compute(o)
            if before:
                self.core_add(before.pop())
            before.append(o)

        return step, lambda: self.core_add(before.pop())

    def finish(self):
        self.sums.finish()
        for o in range(8):
            self.core_copy(o).wait_send()


def pair_gather_steps(g, used):
    def number(o, order):
        return sum((o >> NEAR.index(d) & 1) << n for n, d in enumerate(order[:3]))

    def link(j, low):
        for p in range(len(g.parts)):
            g.copy(p, low, j).wait_recv()
            for later in range(j + 1, 4):
                g.copy(p, low | 1 << j, later).start()

    def pair(o):
        for p, part in enumerate(g.parts):
            g.copy(p, number(o, part[4]), 3).wait_recv()
        used(o)

    steps = []
    for j in range(3):
        for low in range(1 << j):
            steps.append(functools.partial(link, j, low))
            for o in range(8):
                if max(1, *[number(o, part[4]) for part in g.parts]) == low | 1 << j:
                    steps.append(functools.partial(pair, o))
    return steps


def attend_kernel(plan, section, *refs):
    ins, refs = refs[:8], refs[8:]
    x_ref, kv_ref, wq_hbm, wkv_hbm, wo_hbm, bq_ref, bkv_ref, lo_ref = ins
    o_ref, x_out, q_out, kv_out, mixed_out, lse_ref = refs[:6]
    refs = refs[6:]
    x_all, wq, wkv, wo, far, far_all, q_all, kv_all, mixed, part, came, buf = refs[:12]
    g_send, g_recv, k_send, k_recv, swap_send, swap_recv, own_sem, load_sem, out_sem = refs[12:21]
    pair_sems = refs[21:]
    h, trio = Hyper(CUBE), Hyper(TRIO)
    sec, shd = lax.axis_index("section"), lax.axis_index("shard")
    other = (sec, shd + 8 * (1 - 2 * (shd // 8)))
    h.barrier((other,))
    swap = remote(kv_ref, far, swap_send, swap_recv, other)
    swap.start()
    loads = [
        pltpu.make_async_copy(x_ref, x_all.at[h.pos], own_sem),
        pltpu.make_async_copy(wq_hbm.at[section], wq, load_sem.at[0]),
        pltpu.make_async_copy(wkv_hbm.at[section], wkv, load_sem.at[1]),
        pltpu.make_async_copy(wo_hbm.at[section], wo, load_sem.at[2]),
    ]
    for one in loads:
        one.start()
    g = Gather(h, plan, x_ref, x_all, g_send, g_recv)
    g.start(range(len(plan)))
    swap.wait_recv()
    far_all[h.pos] = far[...]
    gkv = Gather(h, ((0, 128, 0, 2 * HD, CUBE),), far, far_all, k_send, k_recv)
    gkv.start(range(1))
    for one in loads:
        one.wait()
    sums = PairSum(h, trio, plan, part, came, buf, pair_sems)

    def project(o):
        n = sums.pair(o)
        x = x_all[pl.ds(2 * n, 2)].reshape(QB, D)
        q_all[n] = (dot32(x, wq[...]) + bq_ref[...]).astype(jnp.bfloat16)
        at = pl.ds(pl.multiple_of(WINDOW + QB * lax.rem(n, 4), QB), QB)
        kv_all[n // 4, at] = (dot32(x, wkv[...]) + bkv_ref[...]).astype(jnp.bfloat16)

    far_steps = chunk_gather_steps(gkv, 1)
    for step in spaced(pair_gather_steps(g, project), far_steps):
        step()
    kv_all[:, :WINDOW] = far_all[...].reshape(2, WINDOW, 2 * HD)

    def compute(o):
        n = sums.pair(o)
        m, a = n // 4, pl.multiple_of(QB * lax.rem(n, 4), QB)
        keys = pl.ds(a, KB)
        s = dot_nt(kv_all[m, keys, :HD], q_all[n]) * SCALE
        s = jnp.where(kept_pairs(lo_ref[n], a), s, -1e30)
        top = jnp.max(s, axis=0, keepdims=True)
        e = jnp.exp(s - top)
        total = jnp.sum(e, axis=0, keepdims=True)
        probs = (e * (1.0 / total)).astype(jnp.bfloat16)
        mix = dot_tn(probs, kv_all[m, keys, HD:]).astype(jnp.bfloat16)
        mixed[n] = mix
        lse_ref[n] = top + jnp.log(total)
        for c in range(4):
            cols = pl.ds(512 * c, 512)
            part[pl.ds(2 * n, 2), :, cols] = (
                dot32(mix, wo[:, cols]).astype(jnp.bfloat16).reshape(2, 128, 512)
            )
        sums.core_copy(o).start()

    outs = [
        pltpu.make_async_copy(x_all, x_out, out_sem.at[0]),
        pltpu.make_async_copy(q_all, q_out, out_sem.at[1]),
        pltpu.make_async_copy(kv_all, kv_out, out_sem.at[2]),
    ]
    for one in outs:
        one.start()
    steps, rest = sums.schedule(compute, o_ref)
    for step in steps:
        step()
    outs.append(pltpu.make_async_copy(mixed, mixed_out, out_sem.at[3]))
    outs[-1].start()
    for step in rest:
        step()
    g.finish()
    gkv.finish()
    swap.wait_send()
    sums.finish()
    for one in outs:
        one.wait()


def attend_layer(x, kv, wq, wkv, wo, bq, bkv, lo, plan, section):
    bf16, f32 = jnp.bfloat16, jnp.float32
    dma = pltpu.SemaphoreType.DMA
    hbm, vmem = pl.BlockSpec(memory_space=pl.ANY), pl.BlockSpec(memory_space=pltpu.VMEM)
    out = [
        jax.ShapeDtypeStruct((128, D), f32),
        jax.ShapeDtypeStruct((16, 128, D), bf16),
        jax.ShapeDtypeStruct((8, QB, HD), bf16),
        jax.ShapeDtypeStruct((2, 2 * WINDOW, 2 * HD), bf16),
        jax.ShapeDtypeStruct((8, QB, HD), bf16),
        jax.ShapeDtypeStruct((8, 1, QB), f32),
    ]
    out_specs = [vmem, hbm, hbm, hbm, hbm, vmem]
    return pl.pallas_call(
        functools.partial(attend_kernel, plan, section),
        out_shape=out,
        in_specs=[hbm] * 5 + [vmem] * 3,
        out_specs=out_specs,
        scratch_shapes=[
            pltpu.VMEM((16, 128, D), bf16),
            pltpu.VMEM((D, HD), bf16),
            pltpu.VMEM((D, 2 * HD), bf16),
            pltpu.VMEM((HD, D), bf16),
            pltpu.VMEM((128, 2 * HD), bf16),
            pltpu.VMEM((16, 128, 2 * HD), bf16),
            pltpu.VMEM((8, QB, HD), bf16),
            pltpu.VMEM((2, 2 * WINDOW, 2 * HD), bf16),
            pltpu.VMEM((8, QB, HD), bf16),
            pltpu.VMEM((16, 128, D), bf16),
            pltpu.VMEM((8, 128, D), bf16),
            pltpu.VMEM((8, 128, D), bf16),
            dma((3, 16)),
            dma((3, 16)),
            dma((1, 16)),
            dma((1, 16)),
            dma,
            dma,
            dma,
            dma((3,)),
            dma((4,)),
            dma((8,)),
            dma((8,)),
            dma((3, 8)),
            dma((3, 8)),
        ],
        compiler_params=pltpu.CompilerParams(
            collective_id=3 + section, has_side_effects=True, vmem_limit_bytes=LIMIT
        ),
        name="attend",
    )(x, kv, wq, wkv, wo, bq, bkv, lo)


class Home:
    def __init__(self, home, c_count, c, e, rc, re, sems):
        self.home, self.c_count, self.c, self.e, self.rc, self.re = home, c_count, c, e, rc, re
        self.send, self.c_recv, self.e_recv, self.own_sem = sems
        self.sec, self.shd = lax.axis_index("section"), lax.axis_index("shard")
        self.half, self.low = self.shd // 8, lax.rem(self.shd, 8)
        self.me, self.place = half_group(self.sec, self.shd)
        self.here = self.sec == home

    def copies(self, n):
        if n < self.c_count:
            size = 256 // self.c_count
            src = self.c.at[pl.ds(size * n, size)]
            dst = self.rc.at[pl.ds(256 * self.sec + size * n, size)]
            return self.here, [(src, dst, (self.home, self.shd), self.send.at[n, 0], self.c_recv.at[n], self.own_sem.at[n, 0])]
        k = n - self.c_count
        return jnp.logical_and(self.here, self.low == k), [
            (
                self.e.at[pl.ds(128 * k, 128), pl.ds(256 * c, 256)],
                self.re.at[:, columns(2 * (8 * c + self.low) + self.sec, 256)],
                (self.home, 8 * self.half + k),
                self.send.at[n, c],
                self.e_recv.at[self.me, c],
                self.own_sem.at[n, c],
            )
            for c in range(2)
        ]

    def go(self, n, start):
        local, copies = self.copies(n)

        @pl.when(local)
        def _():
            for src, dst, _, _, _, sem in copies:
                one = pltpu.make_async_copy(src, dst, sem)
                one.start() if start else one.wait()

        @pl.when(jnp.logical_not(local))
        def _():
            for src, dst, there, send, recv, _ in copies:
                one = remote(src, dst, send, recv, there)
                one.start() if start else one.wait_send()

    def finish(self):
        for n in range(self.c_count + 8):
            self.go(n, False)

        @pl.when(self.here)
        def _():
            size = 256 // self.c_count
            for n in range(self.c_count):
                rows = pl.ds(size * n, size)
                remote(
                    self.c.at[rows], self.rc.at[rows], self.send.at[n, 0], self.c_recv.at[n], (1 - self.sec, self.shd)
                ).wait_recv()

            @pl.loop(1, 16)
            def _(d):
                n = lax.rem(self.me + d, 16)
                for c in range(2):
                    remote(
                        self.e.at[pl.ds(0, 128), pl.ds(0, 256)],
                        self.re.at[:, pl.ds(256 * c, 256)],
                        self.send.at[self.c_count, c],
                        self.e_recv.at[n, c],
                        self.place(n),
                    ).wait_recv()


def attend_back_kernel(plan, home, *refs):
    x_ref, n1_hbm, wq_hbm, wo_hbm, q_hbm, kv_hbm, mixed_hbm, lse_ref, lo_ref, gc, ge, cross = refs[:12]
    if home == 0:
        c_before, e_before = refs[12:14]
        refs = refs[:12] + refs[14:]
    o_ref, own_ref, far_ref, wo_ref, wq_ref, bq_ref, rc, re, crossed = refs[12:21]
    if home == 0:
        rc_before, re_before = refs[21:23]
        refs = refs[:21] + refs[23:]
    x_all, n1, wq, wo, q_all, kv_all, mixed, dq_all, dk, dv, part, came, buf = refs[21:34]
    kv_parts, kv_bufs, sent = refs[34:36], refs[36:38], refs[38]
    c_kept, c_came, e_kept, e_came = refs[39:43]
    g_send, g_recv, swap_send, swap_recv, own_sem, load_sem, bg_send, bg_recv = refs[43:51]
    pair_sems, kv_sems = refs[51:55], refs[55:59]
    home_sems, (kept_sem, x_send, x_recv) = refs[59:63], refs[63:66]
    deliver = home == 0
    if deliver:
        back_home = Home(home, 8, c_kept, e_kept, rc, re, home_sems)
        before = Home(1, 8, c_before, e_before, rc_before, re_before, refs[66:])
    h, trio = Hyper(CUBE), Hyper(TRIO)
    sec, shd = lax.axis_index("section"), lax.axis_index("shard")
    half, low = shd // 8, lax.rem(shd, 8)
    other = (sec, shd + 8 * (1 - 2 * half))
    me, place = half_group(sec, shd)
    barrier = pltpu.get_barrier_semaphore()

    @pl.loop(1, 16)
    def _(d):
        pl.semaphore_signal(
            barrier, inc=1, device_id=place(lax.rem(me + d, 16)), device_id_type=MESH
        )

    pl.semaphore_signal(barrier, inc=1, device_id=other, device_id_type=MESH)
    pl.semaphore_wait(barrier, 16)

    def beside(n):
        if n < 8:
            rows = pl.ds(32 * n, 32)
            src, dst = gc.at[1 - half, rows], c_came.at[rows]
        else:
            rows = pl.ds(128 * (n - 8), 128)
            src, dst = ge.at[1 - half, rows], e_came.at[rows]
        return remote(src, dst, bg_send.at[n], bg_recv.at[n], other)

    def land(n):
        beside(n).wait_recv()
        mine, theirs, first, count = (c_kept, c_came, 32 * n, 2) if n < 8 else (e_kept, e_came, 128 * (n - 8), 8)

        @pl.loop(0, count)
        def _(i):
            rows = pl.ds(pl.multiple_of(first + 16 * i, 16), 16)
            total = mine[rows, :].astype(jnp.float32) + theirs[rows, :].astype(jnp.float32)
            mine[rows, :] = total.astype(mine.dtype)

        if deliver:
            back_home.go(n, True)

    LAG = 7 if home == 0 else 12
    turns = []
    for n in range(16 + LAG):
        turn = []
        if n < 16:
            turn.append(beside(n).start)
            if deliver:
                turn.append(functools.partial(before.go, n, True))
        if n >= LAG:
            turn.append(functools.partial(land, n - LAG))
        turns.append(turn)

    def feed(steps, every):
        for n, step in enumerate(steps):
            step()
            if turns and n % every == every - 1:
                for one in turns.pop(0):
                    one()

    kept = [
        pltpu.make_async_copy(gc.at[half], c_kept, kept_sem.at[0]),
        pltpu.make_async_copy(ge.at[half], e_kept, kept_sem.at[1]),
    ]
    for one in kept:
        one.start()
    swap_rows = remote(cross, crossed, x_send, x_recv, (1 - sec, shd))

    def swap_step(step, sending):
        if home == 1:
            step()
        else:
            pl.when(sec == (0 if sending else 1))(step)

    own = pltpu.make_async_copy(x_ref, x_all.at[h.pos], own_sem)
    own.start()
    g = Gather(h, plan, x_ref, x_all, g_send, g_recv)
    g.start(range(len(plan)))
    pairs = ((wq_hbm.at[home], wq), (wo_hbm.at[home], wo), (q_hbm, q_all), (kv_hbm, kv_all), (mixed_hbm, mixed), (n1_hbm, n1))
    loads = [pltpu.make_async_copy(src, dst, load_sem.at[n]) for n, (src, dst) in enumerate(pairs)]
    for one in loads:
        one.start()
    own.wait()
    for one in loads[:5] + kept:
        one.wait()
    sums = PairSum(h, trio, plan, part, came, buf, pair_sems)

    bq_ref[...] = jnp.zeros_like(bq_ref)
    dk[...] = jnp.zeros_like(dk)
    dv[...] = jnp.zeros_like(dv)

    def compute(o):
        n = sums.pair(o)
        m, a = n // 4, pl.multiple_of(QB * lax.rem(n, 4), QB)
        keys = pl.ds(a, KB)
        q, k = q_all[n], kv_all[m, keys, :HD]
        gm = dot_nt(x_all[pl.ds(2 * n, 2)].reshape(QB, D), wo[...]).astype(jnp.bfloat16)
        s = dot_nt(k, q) * SCALE
        probs = jnp.where(kept_pairs(lo_ref[n], a), jnp.exp(s - lse_ref[n]), 0.0)
        gp = dot_nt(kv_all[m, keys, HD:], gm)
        row = jnp.sum(probs * gp, axis=0, keepdims=True)
        gs = (probs * (gp - row)).astype(jnp.bfloat16)
        dq = (dot_tn(gs, k) * SCALE).astype(jnp.bfloat16)
        dq_all[n] = dq
        bq_ref[...] += jnp.sum(dq.astype(jnp.float32), axis=0, keepdims=True)
        for c in range(4):
            rows = pl.ds(512 * c, 512)
            part[pl.ds(2 * n, 2), :, rows] = (
                dot_nt(dq, wq[rows, :]).astype(jnp.bfloat16).reshape(2, 128, 512)
            )
        sums.core_copy(o).start()
        dk[m, keys] += dot32(gs, q) * SCALE
        dv[m, keys] += dot32(probs.astype(jnp.bfloat16), gm)

    step, last_add = sums.following(compute)
    feed(pair_gather_steps(g, step), 2)
    last_add()
    swap_step(swap_rows.start, True)
    for one, first in zip(kv_parts, (WINDOW, 0)):
        rows = pl.ds(first, WINDOW)
        one[:, :, :HD] = dk[:, rows].astype(jnp.bfloat16).reshape(16, 128, HD)
        one[:, :, HD:] = dv[:, rows].astype(jnp.bfloat16).reshape(16, 128, HD)
    rest = chunk_reduce_steps(sums.sums, o_ref)
    kv_sums = [
        Reduce(h, BESIDE[n], kv_parts[n], kv_bufs[n], kv_sems[2 * n], kv_sems[2 * n + 1]) for n in range(2)
    ]
    for n in reversed(range(8)):
        for r in kv_sums:
            r.copy(0, 3, n).start()

    def product(left, right, c):
        cols = pl.ds(512 * c, 512)
        tile = dot_tn(left[...].reshape(D, HD), right[:, :, cols].reshape(D, 512))
        if right is x_all:
            wo_ref[:, cols] = tile.astype(wo_ref.dtype)
        else:
            wq_ref[cols, :] = tile.T.astype(wq_ref.dtype)

    products = [functools.partial(product, mixed, x_all, c) for c in range(4)]
    products += [loads[5].wait] + [functools.partial(product, dq_all, n1, c) for c in range(4)]
    kv_steps = [
        step
        for pair in zip(chunk_reduce_steps(kv_sums[0], own_ref), chunk_reduce_steps(kv_sums[1], far_ref))
        for step in pair
    ]
    feed(spaced(spaced(rest, kv_steps), products), 3)
    sent[0] = far_ref[...].astype(sent.dtype)
    swap = remote(sent.at[0], sent.at[1], swap_send, swap_recv, other)
    swap.start()
    while turns:
        for one in turns.pop(0):
            one()
    g.finish()
    sums.finish()
    for r in kv_sums:
        r.finish()
    swap.wait()
    far_ref[...] = sent[1].astype(jnp.float32)
    swap_step(swap_rows.wait_send, True)
    swap_step(swap_rows.wait_recv, False)
    for n in range(16):
        beside(n).wait_send()
    if deliver:
        back_home.finish()
        before.finish()
    else:
        summed = [
            pltpu.make_async_copy(c_kept, rc, kept_sem.at[0]),
            pltpu.make_async_copy(e_kept, re, kept_sem.at[1]),
        ]
        for one in summed:
            one.start()
        for one in summed:
            one.wait()


def attend_back_layer(x, n1, wq, wo, q, kv, mixed, lse, lo, gc, ge, cross, before, home, plan, collective_id):
    bf16, f32 = jnp.bfloat16, jnp.float32
    dma = pltpu.SemaphoreType.DMA
    hbm, vmem = pl.BlockSpec(memory_space=pl.ANY), pl.BlockSpec(memory_space=pltpu.VMEM)
    pair = pltpu.VMEM((16, 128, 2 * HD), bf16)
    homes = [jax.ShapeDtypeStruct((512, D), bf16), jax.ShapeDtypeStruct((128, 8192), bf16)]
    sums = [jax.ShapeDtypeStruct((256, D), bf16), jax.ShapeDtypeStruct((1024, 512), bf16)]
    home_sems = [dma((16, 2)), dma((8,)), dma((16, 2)), dma((16, 2))]
    return pl.pallas_call(
        functools.partial(attend_back_kernel, plan, home),
        out_shape=[
            jax.ShapeDtypeStruct((128, D), f32),
            jax.ShapeDtypeStruct((128, 2 * HD), f32),
            jax.ShapeDtypeStruct((128, 2 * HD), f32),
            jax.ShapeDtypeStruct((HD, D), bf16),
            jax.ShapeDtypeStruct((D, HD), bf16),
            jax.ShapeDtypeStruct((1, HD), f32),
        ]
        + (homes if home == 0 else sums)
        + [jax.ShapeDtypeStruct((128, D), bf16)]
        + (homes if home == 0 else []),
        in_specs=[hbm] * 7 + [vmem] * 2 + [hbm] * (3 + len(before)),
        out_specs=[vmem] * 6 + [hbm] * (3 + len(before)),
        scratch_shapes=[
            pltpu.VMEM((16, 128, D), bf16),
            pltpu.VMEM((16, 128, D), bf16),
            pltpu.VMEM((D, HD), bf16),
            pltpu.VMEM((HD, D), bf16),
            pltpu.VMEM((8, QB, HD), bf16),
            pltpu.VMEM((2, 2 * WINDOW, 2 * HD), bf16),
            pltpu.VMEM((8, QB, HD), bf16),
            pltpu.VMEM((8, QB, HD), bf16),
            pltpu.VMEM((2, 2 * WINDOW, HD), f32),
            pltpu.VMEM((2, 2 * WINDOW, HD), f32),
            pltpu.VMEM((16, 128, D), bf16),
            pltpu.VMEM((8, 128, D), bf16),
            pltpu.VMEM((8, 128, D), bf16),
            pair,
            pair,
            pair,
            pair,
            pltpu.VMEM((2, 128, 2 * HD), bf16),
            pltpu.VMEM((256, D), bf16),
            pltpu.VMEM((256, D), bf16),
            pltpu.VMEM((1024, 512), bf16),
            pltpu.VMEM((1024, 512), bf16),
            dma((3, 16)),
            dma((3, 16)),
            dma,
            dma,
            dma,
            dma((6,)),
            dma((16,)),
            dma((16,)),
            dma((8,)),
            dma((8,)),
            dma((3, 8)),
            dma((3, 8)),
            dma((1, 16)),
            dma((1, 16)),
            dma((1, 16)),
            dma((1, 16)),
            *home_sems,
            dma((2,)),
            dma,
            dma,
        ]
        + (home_sems if home == 0 else []),
        compiler_params=pltpu.CompilerParams(
            collective_id=collective_id, has_side_effects=True, vmem_limit_bytes=LIMIT
        ),
        name="attend_back",
    )(x, n1, wq, wo, q, kv, mixed, lse, lo, gc, ge, cross, *before)


BESIDE = ((0, 128, 0, 256, (4, 2, "x", 1)),), ((0, 128, 0, 256, (2, "x", 4, 1)),)
SMALL = tuple(
    (48 * n, 48, 0, 256, order)
    for n, order in enumerate(((8, "x", 4, 2, 1), (8, 4, 2, "x", 1), (8, 2, "x", 4, 1)))
)
ALL_KV = tuple(
    (first, count, 0, 2 * HD, part[4]) for (first, count), part in zip(((0, 48), (48, 48), (96, 32)), SMALL)
)
ALL_SMALL = ((0, 16, 0, 128, SMALL[0][4]),)
BIAS = D + HD


def on_device_fast(
    embedded,
    cotangent,
    segments,
    first_gain,
    first_shift,
    mixer_weight,
    mixer_bias,
    output_weight,
    output_bias,
    second_gain,
    second_shift,
    expand_weight,
    expand_bias,
    contract_weight,
    contract_bias,
):
    bf16, f32 = jnp.bfloat16, jnp.float32
    sec, shd = lax.axis_index("section"), lax.axis_index("shard")
    half = shd // 8
    f = block_of(sec, shd)

    small = jnp.concatenate(
        [
            one[0].reshape(-1, 128)
            for one in (
                first_gain,
                first_shift,
                second_gain,
                second_shift,
                output_bias,
                contract_bias,
                expand_bias,
                jnp.pad(mixer_bias, ((0, 0), (0, 256 - mixer_bias.shape[1]))),
            )
        ],
        axis=0,
    )
    small = jnp.pad(small, ((0, 16 - small.shape[0]), (0, 0)))
    wkv, vectors, wq, wo, *halves = fetch_weights(
        small, mixer_weight[0], output_weight[0], expand_weight[0], contract_weight[0]
    )
    we = [from_halves(halves[s].reshape(8 * 128, 512)) for s in range(2)]
    wc = [from_halves(halves[2 + s]) for s in range(2)]
    wq = wq.reshape(2, D, HD)
    wkv = wkv.reshape(2, D, 2 * HD)
    vectors = vectors.reshape(2, 16, 16, 128)

    def vector(n):
        return vectors[:, :, n].reshape(2, D).astype(f32)

    gain_one, shift_one, gain_two, shift_two, bias_out, bias_con = [vector(n) for n in range(6)]
    bias_exp = vectors[:, :, 6:10].reshape(2, 8192).astype(f32)
    hidden_units = [512 * (8 * h + lax.rem(shd, 8)) + 256 * sec for h in range(2)]
    bias_exp = jnp.concatenate(
        [lax.dynamic_slice_in_dim(bias_exp, first, 256, 1) for first in hidden_units], axis=1
    )
    bias_mix = vectors[:, :, 10:12].reshape(2, 16, 256)[:, :, :136].reshape(2, BIAS).astype(f32)
    bias_q = lax.dynamic_slice_in_dim(bias_mix, f * HD, HD, 1)
    bias_kv = jnp.concatenate([jnp.zeros((2, HD), f32), bias_mix[:, D:]], axis=1)

    starts = jnp.sum(
        (segments[:, None, :] < lax.dynamic_slice_in_dim(segments, half * WINDOW, WINDOW, 1)[:, :, None]),
        axis=2,
        dtype=jnp.int32,
    )
    lo = jnp.maximum(jnp.arange(1, WINDOW + 1)[None], starts - half * WINDOW + WINDOW)
    lo = lo.reshape(8, 1, QB)

    hidden = lax.dynamic_index_in_dim(embedded, sec, 0, keepdims=False).astype(f32)
    results, kept = [], []
    for s in range(2):
        n1 = layer_norm(hidden, gain_one[s], shift_one[s]).astype(bf16)
        kv_rows = (dot32(n1, wkv[s]) + bias_kv[s]).astype(bf16)
        rows, all_n1, q, kv, mixed, lse = attend_layer(
            n1,
            kv_rows,
            wq,
            wkv,
            wo,
            bias_q[s][None],
            bias_kv[s][None],
            lo,
            LIGHT if s == 0 else EVEN,
            s,
        )
        middle = hidden + rows + bias_out[s]
        n2 = layer_norm(middle, gain_two[s], shift_two[s]).astype(bf16)
        rows, all_n2, act, slope = hidden_layer(False, n2, we[s], wc[s], (bias_exp[s][None],), LIGHT if s == 0 else EVEN, 9 + 2 * s, "hidden")
        result = middle + rows + bias_con[s]
        results.append(result.astype(bf16))
        kept.append((hidden, n1, all_n1, q, kv, lse, mixed, middle, all_n2, act, slope))
        hidden = results[-1].astype(f32)

    grad = lax.dynamic_index_in_dim(cotangent, sec, 0, keepdims=False).astype(f32)
    cross = jnp.where(sec == 0, results[1], results[0])
    came = [None, None]
    input_grads = [None, None]
    weight_grads = [None, None]
    small_grads = [None, None]
    for s in (1, 0):
        hidden, n1, all_n1, q, kv, lse, mixed, middle, all_n2, act, slope = kept[s]
        go = grad.astype(bf16)
        g_n2, d_wc, d_we, d_be = hidden_layer(
            True, go, we[s], wc[s], (slope, act, all_n2), EVEN, 10, "hidden_back"
        )
        d_wc, d_we, d_be = d_wc.reshape(2, 256, D), d_we.reshape(2, 1024, 512), d_be[0]
        _, back = jax.vjp(layer_norm, middle, gain_two[s], shift_two[s])
        g_mid, d_gain_two, d_shift_two = back(g_n2)
        g_mid = grad + g_mid
        ga = g_mid.astype(bf16)
        rows, kv_own, kv_far, d_wo, d_wq, d_bq, d_wc, d_we, crossed, *before = attend_back_layer(
            ga,
            all_n1,
            wq,
            wo,
            q,
            kv,
            mixed,
            lse,
            lo,
            d_wc,
            d_we,
            cross,
            () if s == 1 else weight_grads[1][2:],
            s,
            LIGHT,
            5 + s,
        )
        dkv_rows = (kv_own + jnp.where(half == 0, kv_far, 0.0)).astype(bf16)
        g_n1 = rows + dot_nt(dkv_rows, wkv[s])
        _, back = jax.vjp(layer_norm, hidden, gain_one[s], shift_one[s])
        g_in, d_gain_one, d_shift_one = back(g_n1)
        g_in = g_mid + g_in
        input_grads[s] = g_in
        d_wkv = dot_tn(n1, dkv_rows)
        d_bq = d_bq[0]
        d_bv = jnp.sum(dkv_rows[:, HD:].astype(f32), axis=0)
        weight_grads[s] = (d_wq.reshape(16, 128, HD), d_wo, d_wc, d_we)
        came[s] = crossed
        cross = g_in.astype(bf16)
        spread = [
            d_gain_one,
            d_shift_one,
            d_gain_two,
            d_shift_two,
            jnp.sum(ga.astype(f32), axis=0),
            jnp.sum(go.astype(f32), axis=0),
        ]
        placed = jnp.zeros((8192,), f32)
        for h, first in enumerate(hidden_units):
            placed = lax.dynamic_update_slice_in_dim(placed, d_be[256 * h : 256 * (h + 1)], first, 0)
        d_bm = lax.dynamic_update_slice_in_dim(jnp.zeros((D,), f32), d_bq, f * HD, 0)
        vec = jnp.concatenate(
            [one.reshape(16, 128) for one in spread]
            + [placed.reshape(16, 512), jnp.concatenate([d_bm, d_bv]).reshape(16, 136)],
            axis=1,
        )
        vec = jnp.pad(vec, ((0, 0), (0, 4096 - vec.shape[1]))).reshape(16, 16, 256)
        small_grads[s] = jnp.concatenate([d_wkv.reshape(16, 128, 256), vec], axis=1)
        grad = cross.astype(f32)

    mine, rq, ro, last_came = return_last(
        jnp.concatenate(small_grads, axis=0).astype(bf16),
        (weight_grads[0][0], weight_grads[1][0]),
        (weight_grads[0][1], weight_grads[1][1]),
        cross,
    )
    vec = mine[128:].reshape(4096)

    def both(r):
        return r[0].astype(f32) + r[1].astype(f32)

    def here(pair):
        return jnp.where(sec == 0, pair[0], pair[1])

    def by_micro(own, theirs):
        return jnp.stack([jnp.where(sec == 0, own, theirs), jnp.where(sec == 0, theirs, own)])[None]

    grad_rows = here((last_came, came[0])).astype(f32)
    return (
        by_micro(here(results), came[1]),
        by_micro(here(input_grads), grad_rows),
        vec[0:128][None],
        vec[128:256][None],
        jnp.concatenate([both(rq), mine[:128]], axis=1)[None],
        vec[1280 : 1280 + 136][None],
        both(ro)[None],
        vec[512:640][None],
        vec[256:384][None],
        vec[384:512][None],
        here((weight_grads[0][3], before[1])).astype(f32)[None],
        vec[768:1280][None],
        here((weight_grads[0][2], before[0])).astype(f32)[None],
        vec[640:768][None],
    )


def solution(mesh):
    in_specs = (
        P(None, "shard", None),
        P(None, "shard", None),
        P(),
        P("section", "shard"),
        P("section", "shard"),
        P("section", "shard", None),
        P("section", "shard"),
        P("section", "shard", None),
        P("section", "shard"),
        P("section", "shard"),
        P("section", "shard"),
        P("section", "shard", None),
        P("section", "shard"),
        P("section", "shard", None),
        P("section", "shard"),
    )
    out_specs = (
        P("section", None, "shard", None),
        P("section", None, "shard", None),
        P("section", "shard"),
        P("section", "shard"),
        P("section", "shard", None),
        P("section", "shard"),
        P("section", "shard", None),
        P("section", "shard"),
        P("section", "shard"),
        P("section", "shard"),
        P("section", "shard", None),
        P("section", "shard"),
        P("section", "shard", None),
        P("section", "shard"),
    )
    fits = mesh.shape["section"] == 2 and mesh.shape["shard"] == HEADS
    on_device = on_device_fast if fits else on_device_general
    return jax.shard_map(
        on_device, mesh=mesh, in_specs=in_specs, out_specs=out_specs, check_vma=False
    )
```

```python
import functools

import jax
import jax.numpy as jnp
from jax import lax
from jax.experimental import pallas as pl
from jax.experimental.pallas import tpu as pltpu
from jax.sharding import PartitionSpec as P

D = 2048
HEADS = 16
HD = 128
WINDOW = 1024


epsilon = 1e-05


def passed_along(block, axis, distance):
    devices = range(lax.axis_size(axis))
    route = [(i - distance, i) for i in devices if i - distance in devices]
    return lax.ppermute(block, axis, route)


def layer_norm(values, gain_row, shift_row):
    center = values - jnp.mean(values, axis=-1, keepdims=True)
    spread = jnp.mean(center * center, axis=-1, keepdims=True)
    return center * lax.rsqrt(spread + epsilon) * gain_row + shift_row


def gelu_tanh(values):
    return jax.nn.gelu(values, approximate=True)


def window_mask(segments, micro_index, device, row_count, reach_blocks):
    seg_row = lax.dynamic_index_in_dim(segments, micro_index, 0, keepdims=False)
    padded = jnp.concatenate([jnp.full((reach_blocks * row_count,), -1, jnp.int32), seg_row])
    key_segments = lax.dynamic_slice_in_dim(
        padded, device * row_count, (reach_blocks + 1) * row_count
    )
    query_segments = lax.dynamic_slice_in_dim(seg_row, device * row_count, row_count)
    distance = (
        jnp.arange(row_count)[:, None]
        + reach_blocks * row_count
        - jnp.arange((reach_blocks + 1) * row_count)[None, :]
    )
    return (
        (distance >= 0) & (distance < WINDOW) & (query_segments[:, None] == key_segments[None, :])
    )


def fetch_window(key_value, reach_blocks):
    earlier = [passed_along(key_value, "shard", offset) for offset in range(reach_blocks, 0, -1)]
    return jnp.concatenate(earlier + [key_value], axis=0)


def return_window(window_grad, reach_blocks, row_count):
    own_rows = window_grad[reach_blocks * row_count :]
    for offset in range(1, reach_blocks + 1):
        start_row = (reach_blocks - offset) * row_count
        own_rows = own_rows + passed_along(
            window_grad[start_row : start_row + row_count].astype(jnp.bfloat16), "shard", -offset
        ).astype(jnp.float32)
    return own_rows


def forward_layer(hidden, weights, key_mask, reach_blocks):
    (
        first_gain,
        first_shift,
        mixer_weight,
        mixer_bias,
        output_weight,
        output_bias,
        second_gain,
        second_shift,
        expand_weight,
        expand_bias,
        contract_weight,
        contract_bias,
    ) = weights
    row_count = hidden.shape[0]
    score_scale = HD ** (-0.5)
    normed_one = layer_norm(
        hidden, first_gain.astype(jnp.float32), first_shift.astype(jnp.float32)
    ).astype(jnp.bfloat16)
    full_bias = jnp.concatenate(
        [mixer_bias[:D], jnp.zeros((HD,), mixer_bias.dtype), mixer_bias[D:]]
    ).astype(jnp.float32)
    projected = (
        jnp.dot(normed_one, mixer_weight, preferred_element_type=jnp.float32) + full_bias
    ).astype(jnp.bfloat16)
    queries = projected[:, :D].reshape(row_count, HEADS, HD)
    window_pairs = fetch_window(projected[:, D:], reach_blocks)
    scores = (
        jnp.einsum("thd,kd->htk", queries, window_pairs[:, :HD], preferred_element_type=jnp.float32)
        * score_scale
    )
    masked = jnp.where(key_mask[None], scores, -1e30)
    top_score = jnp.max(masked, axis=2, keepdims=True)
    exponent = jnp.exp(masked - top_score)
    totals = jnp.sum(exponent, axis=2, keepdims=True)
    prob_low = (exponent / totals).astype(jnp.bfloat16)
    log_total = top_score + jnp.log(totals)
    mixed_rows = (
        jnp.einsum(
            "htk,kd->thd", prob_low, window_pairs[:, HD:], preferred_element_type=jnp.float32
        )
        .reshape(row_count, D)
        .astype(jnp.bfloat16)
    )
    middle = (
        hidden
        + jnp.dot(mixed_rows, output_weight, preferred_element_type=jnp.float32)
        + output_bias.astype(jnp.float32)
    )
    normed_two = layer_norm(
        middle, second_gain.astype(jnp.float32), second_shift.astype(jnp.float32)
    ).astype(jnp.bfloat16)
    pre_gelu = jnp.dot(
        normed_two, expand_weight, preferred_element_type=jnp.float32
    ) + expand_bias.astype(jnp.float32)
    activated = gelu_tanh(pre_gelu).astype(jnp.bfloat16)
    result = (
        middle
        + jnp.dot(activated, contract_weight, preferred_element_type=jnp.float32)
        + contract_bias.astype(jnp.float32)
    )
    return (
        result,
        (
            hidden,
            normed_one,
            projected,
            window_pairs,
            log_total,
            mixed_rows,
            middle,
            normed_two,
            pre_gelu,
            activated,
        ),
    )


def backward_layer(grad_result, weights, saved_state, key_mask, reach_blocks):
    (
        first_gain,
        first_shift,
        mixer_weight,
        mixer_bias,
        output_weight,
        output_bias,
        second_gain,
        second_shift,
        expand_weight,
        expand_bias,
        contract_weight,
        contract_bias,
    ) = weights
    (
        hidden,
        normed_one,
        projected,
        window_pairs,
        log_total,
        mixed_rows,
        middle,
        normed_two,
        pre_gelu,
        activated,
    ) = saved_state
    row_count = hidden.shape[0]
    score_scale = HD ** (-0.5)
    grad_out_low = grad_result.astype(jnp.bfloat16)
    grad_act = jnp.einsum(
        "rd,fd->rf", grad_out_low, contract_weight, preferred_element_type=jnp.float32
    )
    gelu_value, gelu_back = jax.vjp(gelu_tanh, pre_gelu)
    grad_pre = gelu_back(grad_act)[0].astype(jnp.bfloat16)
    grad_normed_two = jnp.einsum(
        "rf,df->rd", grad_pre, expand_weight, preferred_element_type=jnp.float32
    )
    norm_value_two, norm_back_two = jax.vjp(
        layer_norm, middle, second_gain.astype(jnp.float32), second_shift.astype(jnp.float32)
    )
    grad_middle_part, grad_gain_two, grad_shift_two = norm_back_two(grad_normed_two)
    grad_middle = grad_result + grad_middle_part
    grad_attended = grad_middle.astype(jnp.bfloat16)
    grad_mixed = (
        jnp.einsum("re,de->rd", grad_attended, output_weight, preferred_element_type=jnp.float32)
        .astype(jnp.bfloat16)
        .reshape(row_count, HEADS, HD)
    )
    queries = projected[:, :D].reshape(row_count, HEADS, HD)
    key_part = window_pairs[:, :HD]
    value_part = window_pairs[:, HD:]
    scores = (
        jnp.einsum("thd,kd->htk", queries, key_part, preferred_element_type=jnp.float32)
        * score_scale
    )
    prob_full = jnp.where(key_mask[None], jnp.exp(scores - log_total), 0.0)
    prob_low = prob_full.astype(jnp.bfloat16)
    grad_probs = jnp.einsum(
        "thd,kd->htk", grad_mixed, value_part, preferred_element_type=jnp.float32
    )
    row_dot = jnp.sum(prob_full * grad_probs, axis=2, keepdims=True)
    grad_scores = (prob_full * (grad_probs - row_dot)).astype(jnp.bfloat16)
    grad_queries = (
        jnp.einsum("htk,kd->thd", grad_scores, key_part, preferred_element_type=jnp.float32)
        * score_scale
    ).reshape(row_count, D)
    grad_keys = (
        jnp.einsum("htk,thd->kd", grad_scores, queries, preferred_element_type=jnp.float32)
        * score_scale
    )
    grad_values = jnp.einsum(
        "htk,thd->kd", prob_low, grad_mixed, preferred_element_type=jnp.float32
    )
    grad_window = jnp.concatenate([grad_keys, grad_values], axis=1)
    grad_own_pairs = return_window(grad_window, reach_blocks, row_count)
    grad_projected = jnp.concatenate([grad_queries, grad_own_pairs], axis=1).astype(jnp.bfloat16)
    grad_normed_one = jnp.einsum(
        "rq,dq->rd", grad_projected, mixer_weight, preferred_element_type=jnp.float32
    )
    norm_value_one, norm_back_one = jax.vjp(
        layer_norm, hidden, first_gain.astype(jnp.float32), first_shift.astype(jnp.float32)
    )
    grad_hidden_part, grad_gain_one, grad_shift_one = norm_back_one(grad_normed_one)
    grad_hidden = grad_middle + grad_hidden_part
    return (
        grad_hidden,
        (
            grad_projected,
            grad_attended,
            grad_pre,
            grad_out_low,
            grad_gain_one,
            grad_shift_one,
            grad_gain_two,
            grad_shift_two,
            normed_one,
            mixed_rows,
            normed_two,
            activated,
        ),
    )


def flatten_rows(stacked):
    return stacked.reshape((-1, stacked.shape[-1]))


def weight_terms(row_items, norm_items):
    (
        grad_projected_rows,
        grad_attended_rows,
        grad_pre_rows,
        grad_out_rows,
        normed_one_rows,
        mixed_all,
        normed_two_rows,
        activated_rows,
    ) = row_items
    first_gain_term, first_shift_term, second_gain_term, second_shift_term = norm_items
    mixer_weight_term = jnp.einsum(
        "rd,rq->dq", normed_one_rows, grad_projected_rows, preferred_element_type=jnp.float32
    )
    column_totals = jnp.sum(grad_projected_rows.astype(jnp.float32), axis=0)
    mixer_bias_term = jnp.concatenate([column_totals[:D], column_totals[D + HD :]])
    output_weight_term = jnp.einsum(
        "rd,re->de", mixed_all, grad_attended_rows, preferred_element_type=jnp.float32
    )
    output_bias_term = jnp.sum(grad_attended_rows.astype(jnp.float32), axis=0)
    expand_weight_term = jnp.einsum(
        "rd,rf->df", normed_two_rows, grad_pre_rows, preferred_element_type=jnp.float32
    )
    expand_bias_term = jnp.sum(grad_pre_rows.astype(jnp.float32), axis=0)
    contract_weight_term = jnp.einsum(
        "rf,rd->fd", activated_rows, grad_out_rows, preferred_element_type=jnp.float32
    )
    contract_bias_term = jnp.sum(grad_out_rows.astype(jnp.float32), axis=0)
    return (
        first_gain_term[None],
        first_shift_term[None],
        mixer_weight_term[None],
        mixer_bias_term[None],
        output_weight_term[None],
        output_bias_term[None],
        second_gain_term[None],
        second_shift_term[None],
        expand_weight_term[None],
        expand_bias_term[None],
        contract_weight_term[None],
        contract_bias_term[None],
    )


def on_device_general(
    embedded,
    cotangent,
    segments,
    first_gain,
    first_shift,
    mixer_weight,
    mixer_bias,
    output_weight,
    output_bias,
    second_gain,
    second_shift,
    expand_weight,
    expand_bias,
    contract_weight,
    contract_bias,
):
    section_index = lax.axis_index("section")
    device = lax.axis_index("shard")
    micro_count = embedded.shape[0]
    row_count = embedded.shape[1]
    reach_blocks = WINDOW // row_count
    own_params = (
        first_gain[0],
        first_shift[0],
        mixer_weight[0],
        mixer_bias[0],
        output_weight[0],
        output_bias[0],
        second_gain[0],
        second_shift[0],
        expand_weight[0],
        expand_bias[0],
        contract_weight[0],
        contract_bias[0],
    )
    forward_weights = (
        lax.all_gather(own_params[0], "shard", axis=0, tiled=True),
        lax.all_gather(own_params[1], "shard", axis=0, tiled=True),
        lax.all_gather(own_params[2], "shard", axis=0, tiled=True),
        lax.all_gather(own_params[3], "shard", axis=0, tiled=True),
        lax.all_gather(own_params[4], "shard", axis=0, tiled=True),
        lax.all_gather(own_params[5], "shard", axis=0, tiled=True),
        lax.all_gather(own_params[6], "shard", axis=0, tiled=True),
        lax.all_gather(own_params[7], "shard", axis=0, tiled=True),
        lax.all_gather(own_params[8], "shard", axis=0, tiled=True),
        lax.all_gather(own_params[9], "shard", axis=0, tiled=True),
        lax.all_gather(own_params[10], "shard", axis=0, tiled=True),
        lax.all_gather(own_params[11], "shard", axis=0, tiled=True),
    )
    zero_rows = jnp.zeros((row_count, D), jnp.float32)
    arrived = zero_rows
    sent_list = []
    kept_states = []
    for step_index in range(micro_count + 1):
        own_input = (
            embedded[step_index].astype(jnp.float32) if step_index < micro_count else zero_rows
        )
        hidden = jnp.where(section_index == 0, own_input, arrived)
        micro_index = jnp.clip(step_index - section_index, 0, micro_count - 1)
        key_mask = window_mask(segments, micro_index, device, row_count, reach_blocks)
        result, saved_state = forward_layer(hidden, forward_weights, key_mask, reach_blocks)
        result_low = result.astype(jnp.bfloat16)
        sent_list.append(result_low)
        kept_states.append(saved_state)
        if step_index < micro_count:
            arrived = passed_along(result_low, "section", 1).astype(jnp.float32)
    section_outputs = lax.dynamic_slice_in_dim(jnp.stack(sent_list), section_index, micro_count, 0)[
        None
    ]
    stacked_states = [
        jnp.stack([state_item[item_index] for state_item in kept_states])
        for item_index in range(10)
    ]
    valid_start = 1 - section_index
    arrived_grad = zero_rows
    grad_records = []
    hidden_grads = []
    for step_index in range(micro_count + 1):
        own_grad = (
            cotangent[step_index].astype(jnp.float32) if step_index < micro_count else zero_rows
        )
        grad_result = jnp.where(section_index == 1, own_grad, arrived_grad)
        forward_index = jnp.clip(step_index - 1 + 2 * section_index, 0, micro_count)
        micro_index = jnp.clip(step_index - 1 + section_index, 0, micro_count - 1)
        saved_state = [
            lax.dynamic_index_in_dim(stacked, forward_index, 0, keepdims=False)
            for stacked in stacked_states
        ]
        key_mask = window_mask(segments, micro_index, device, row_count, reach_blocks)
        grad_hidden, record = backward_layer(
            grad_result, forward_weights, saved_state, key_mask, reach_blocks
        )
        hidden_grads.append(grad_hidden)
        if step_index < micro_count:
            arrived_grad = passed_along(grad_hidden.astype(jnp.bfloat16), "section", -1).astype(
                jnp.float32
            )
        grad_records.append(record)
    input_grads = lax.dynamic_slice_in_dim(jnp.stack(hidden_grads), valid_start, micro_count, 0)[
        None
    ]
    chosen = [
        lax.dynamic_slice_in_dim(
            jnp.stack([record[item_index] for record in grad_records]), valid_start, micro_count, 0
        )
        for item_index in range(12)
    ]
    row_items = (
        flatten_rows(chosen[0]),
        flatten_rows(chosen[1]),
        flatten_rows(chosen[2]),
        flatten_rows(chosen[3]),
        flatten_rows(chosen[8]),
        flatten_rows(chosen[9]),
        flatten_rows(chosen[10]),
        flatten_rows(chosen[11]),
    )
    norm_items = (
        jnp.sum(chosen[4], axis=0),
        jnp.sum(chosen[5], axis=0),
        jnp.sum(chosen[6], axis=0),
        jnp.sum(chosen[7], axis=0),
    )
    all_terms = weight_terms(row_items, norm_items)
    summed = (
        lax.psum_scatter(all_terms[0], "shard", scatter_dimension=1, tiled=True),
        lax.psum_scatter(all_terms[1], "shard", scatter_dimension=1, tiled=True),
        lax.psum_scatter(all_terms[2], "shard", scatter_dimension=1, tiled=True),
        lax.psum_scatter(all_terms[3], "shard", scatter_dimension=1, tiled=True),
        lax.psum_scatter(all_terms[4], "shard", scatter_dimension=1, tiled=True),
        lax.psum_scatter(all_terms[5], "shard", scatter_dimension=1, tiled=True),
        lax.psum_scatter(all_terms[6], "shard", scatter_dimension=1, tiled=True),
        lax.psum_scatter(all_terms[7], "shard", scatter_dimension=1, tiled=True),
        lax.psum_scatter(all_terms[8], "shard", scatter_dimension=1, tiled=True),
        lax.psum_scatter(all_terms[9], "shard", scatter_dimension=1, tiled=True),
        lax.psum_scatter(all_terms[10], "shard", scatter_dimension=1, tiled=True),
        lax.psum_scatter(all_terms[11], "shard", scatter_dimension=1, tiled=True),
    )
    return (
        section_outputs,
        input_grads,
        summed[0],
        summed[1],
        summed[2],
        summed[3],
        summed[4],
        summed[5],
        summed[6],
        summed[7],
        summed[8],
        summed[9],
        summed[10],
        summed[11],
    )


MESH = pl.DeviceIdType.MESH
LIMIT = 60 << 20
CUBE = ("x", 4, 2, 1)
ALL = ("x", 8, 4, 2, 1)


def columns(n, wide):
    return pl.ds(pl.multiple_of(n * wide, wide), wide)


def remote(src, dst, send, recv, there):
    return pltpu.make_async_remote_copy(
        src_ref=src, dst_ref=dst, send_sem=send, recv_sem=recv, device_id=there, device_id_type=MESH
    )


class Hyper:
    def __init__(self, dims):
        sec = lax.axis_index("section")
        shd = lax.axis_index("shard")
        self.dims = dims
        self.partner, self.delta, self.pos = {}, {}, 0
        for n, d in enumerate(dims):
            weight = 1 << (len(dims) - 1 - n)
            if d == "x":
                bit = sec
                self.partner[d] = (1 - sec, shd)
            else:
                bit = lax.rem(shd // d, 2)
                self.partner[d] = (sec, shd + d * (1 - 2 * bit))
            self.pos = self.pos + bit * weight
            self.delta[d] = weight * (1 - 2 * bit)

    def at(self, order, offset):
        place = self.pos
        for j, d in enumerate(order):
            if offset >> j & 1:
                place = place + self.delta[d]
        return place

    def barrier(self, more=()):
        sem = pltpu.get_barrier_semaphore()
        partners = [self.partner[d] for d in self.dims] + list(more)
        for partner in partners:
            pl.semaphore_signal(sem, inc=1, device_id=partner, device_id_type=MESH)
        pl.semaphore_wait(sem, len(partners))


def cube_parts(rows, widths, col0=0):
    orders = (("x", 4, 2, 1), (4, 2, "x", 1), (2, "x", 4, 1))
    parts = []
    for width, order in zip(widths, orders):
        parts.append((0, rows, col0, width, order))
        col0 += width
    return tuple(parts)


class Gather:
    def __init__(self, h, parts, src, dst, send_sem, recv_sem):
        self.h, self.parts, self.src, self.dst = h, parts, src, dst
        self.send_sem, self.recv_sem = send_sem, recv_sem

    def copy(self, p, offset, j):
        r0, rn, c0, cn, order = self.parts[p]
        rows, cols = pl.ds(r0, rn), pl.ds(c0, cn)
        there = self.dst.at[self.h.at(order, offset), rows, cols]
        here = self.src.at[rows, cols] if offset == 0 else there
        n = offset | 1 << j
        return pltpu.make_async_remote_copy(
            src_ref=here,
            dst_ref=there,
            send_sem=self.send_sem.at[p, n],
            recv_sem=self.recv_sem.at[p, n],
            device_id=self.h.partner[order[j]],
            device_id_type=MESH,
        )

    def start(self, chosen):
        for j in range(len(self.h.dims)):
            for p in chosen:
                self.copy(p, 0, j).start()

    def forward(self, chosen):
        k = len(self.h.dims)
        for j in range(k):
            for low in range(1 << j):
                for p in chosen:
                    self.copy(p, low, j).wait_recv()
                    for later in range(j + 1, k):
                        self.copy(p, low | 1 << j, later).start()

    def finish(self):
        for p in range(len(self.parts)):
            for j in range(len(self.h.dims)):
                for low in range(1 << j):
                    self.copy(p, low, j).wait_send()


class Reduce:
    def __init__(self, h, parts, src, buf, send_sem, recv_sem):
        self.h, self.parts, self.src, self.buf = h, parts, src, buf
        self.send_sem, self.recv_sem = send_sem, recv_sem

    def window(self, p):
        r0, rn, c0, cn, order = self.parts[p]
        return pl.ds(r0, rn), pl.ds(c0, cn)

    def held(self, p, j, offset):
        if j == len(self.h.dims) - 1:
            return self.src.at[(self.h.at(self.parts[p][4], offset),) + self.window(p)]
        return self.buf.at[((1 << (j + 1)) | offset,) + self.window(p)]

    def copy(self, p, j, low):
        n = (1 << j) | low
        return remote(
            self.held(p, j, low | 1 << j),
            self.buf.at[(n,) + self.window(p)],
            self.send_sem.at[p, n],
            self.recv_sem.at[p, n],
            self.h.partner[self.parts[p][4][j]],
        )

    def add(self, p, j, low, out=None):
        self.copy(p, j, low).wait_recv()
        r0, rn, c0, cn, order = self.parts[p]
        mine = self.held(p, j, low)
        came = self.buf.at[((1 << j) | low,) + self.window(p)]
        step = 16

        @pl.loop(0, rn // step)
        def _(i):
            rows = pl.ds(pl.multiple_of(i * step, step), step)
            total = mine[rows, :].astype(jnp.float32) + came[rows, :].astype(jnp.float32)
            if j > 0:
                came[rows, :] = total.astype(came.dtype)
            else:
                out[pl.ds(pl.multiple_of(r0 + i * step, step), step), pl.ds(c0, cn)] = total

        if j > 0 and low >> (j - 1) & 1:
            self.copy(p, j - 1, low ^ (1 << (j - 1))).start()

    def finish(self):
        for p in range(len(self.parts)):
            for j in range(len(self.h.dims)):
                for low in range(1 << j):
                    self.copy(p, j, low).wait_send()


def block_of(sec, shd):
    return 8 * lax.rem(sec + lax.rem(shd, 2), 2) + lax.rem(shd, 8)


def half_group(sec, shd):
    first = 8 * (shd // 8)
    return 8 * sec + lax.rem(shd, 8), lambda n: (n // 8, first + lax.rem(n, 8))


class Spread:
    def __init__(self, pieces, own_sem, send, recv):
        self.sec, self.shd = lax.axis_index("section"), lax.axis_index("shard")
        self.me, self.place = half_group(self.sec, self.shd)
        self.pieces, self.own_sem, self.send, self.recv = pieces, own_sem, send, recv

    def copies(self, d):
        there = self.place(lax.rem(self.me + d, 16))
        return [
            remote(src, dst, self.send.at[n, d], self.recv.at[n, d], there)
            for n, (src, dst) in enumerate(self.pieces(*there))
        ]

    def own(self):
        return [
            pltpu.make_async_copy(src, dst, self.own_sem.at[n])
            for n, (src, dst) in enumerate(self.pieces(self.sec, self.shd))
        ]

    def start(self):
        @pl.loop(1, 16)
        def _(d):
            for one in self.copies(d):
                one.start()

        for one in self.own():
            one.start()


def everyone_barrier(me):
    sem = pltpu.get_barrier_semaphore()

    @pl.loop(1, 32)
    def _(d):
        there = lax.rem(me + d, 32)
        pl.semaphore_signal(
            sem, inc=1, device_id=(there // 16, lax.rem(there, 16)), device_id_type=MESH
        )

    pl.semaphore_wait(sem, 31)


def fetch_kernel(small, mix, out, exp, con, wkv, vec, wq, wo, we_0, we_1, wc_0, wc_1, *sems):
    q_send, q_recv, send, recv, con_send, con_recv, out_send, out_recv, own_sem = sems[:9]
    kv_send, kv_recv, v_send, v_recv = sems[9:]
    sec, shd = lax.axis_index("section"), lax.axis_index("shard")
    low, half = lax.rem(shd, 8), shd // 8
    me = 16 * sec + shd
    everyone_barrier(me)
    h = Hyper(ALL)
    mix_kv = mix.at[:, pl.ds(D, 2 * HD)]
    gathers = [Gather(h, ALL_KV, mix_kv, wkv, kv_send, kv_recv), Gather(h, ALL_SMALL, small, vec, v_send, v_recv)]
    for g in gathers:
        g.start(range(len(g.parts)))

    def spread_to(we):
        def pieces(ts, tj):
            for n in range(2):
                yield (
                    exp.at[:, columns(2 * (8 * n + lax.rem(tj, 8)) + ts, 256)],
                    we.at[low, :, pl.ds(256 * n, 256)],
                )

        return Spread(pieces, own_sem, send, recv)

    def to_section(step):
        for s, arrays in enumerate(((spread_to(we_0), wc_0), (spread_to(we_1), wc_1))):
            pl.when(sec == s)(functools.partial(step, *arrays))

    def query(d):
        there = lax.rem(me + d, 32)
        ts, tj = there // 16, lax.rem(there, 16)
        return remote(
            mix.at[:, columns(block_of(ts, tj), HD)], wq.at[sec, shd], q_send.at[d], q_recv.at[d], (ts, tj)
        )

    @pl.loop(1, 32)
    def _(d):
        query(d).start()

    to_section(lambda spread, wc: spread.start())

    to_x = lax.rem(half + lax.rem(shd, 2), 2)
    from_half = lax.rem(sec + lax.rem(shd, 2), 2)
    own_out = pltpu.make_async_copy(out, wo.at[sec], own_sem.at[6])
    for z in range(2):
        mine = jnp.logical_and(to_x == sec, half == z)
        there = remote(out, wo.at[sec], out_send.at[z], out_recv.at[sec], (to_x, 8 * z + low))

        @pl.when(mine)
        def _():
            own_out.start()

        @pl.when(jnp.logical_not(mine))
        def _():
            there.start()

    own = [
        pltpu.make_async_copy(mix_kv, wkv.at[h.pos], own_sem.at[2]),
        pltpu.make_async_copy(small, vec.at[h.pos], own_sem.at[3]),
        pltpu.make_async_copy(mix.at[:, columns(block_of(sec, shd), HD)], wq.at[sec, shd], own_sem.at[4]),
    ]
    for one in own:
        one.start()

    def own_rows(wc):
        return pltpu.make_async_copy(con.at[pl.ds(256 * sec, 256)], wc, own_sem.at[5])

    def rows(wc):
        return remote(con.at[pl.ds(256 * (1 - sec), 256)], wc, con_send, con_recv, (1 - sec, shd))

    def start_rows(spread, wc):
        own_rows(wc).start()
        rows(wc).start()

    to_section(start_rows)
    for j in range(len(ALL)):
        for n in range(1 << j):
            for g in gathers:
                for p in range(len(g.parts)):
                    g.copy(p, n, j).wait_recv()
                    for later in range(j + 1, len(ALL)):
                        g.copy(p, n | 1 << j, later).start()

    @pl.loop(1, 32)
    def _(d):
        query(d).wait_recv()

    for s in range(2):
        mine = jnp.logical_and(sec == s, from_half == half)

        @pl.when(jnp.logical_not(mine))
        def _():
            remote(out, wo.at[s], out_send.at[0], out_recv.at[s], (1 - sec, shd)).wait_recv()

    for s, wc in enumerate((wc_0, wc_1)):
        pl.when(sec != s)(rows(wc).wait_recv)

    @pl.loop(1, 16)
    def _(d):
        for n in range(2):
            some = pl.ds(256 * n, 256)
            remote(
                exp.at[:, some], we_0.at[0, :, some], send.at[n, d], recv.at[n, d], (1 - sec, shd)
            ).wait_recv()

    def sent(spread, wc):
        @pl.loop(1, 16)
        def _(d):
            for one in spread.copies(d):
                one.wait_send()

        for one in spread.own():
            one.wait()
        own_rows(wc).wait()
        rows(wc).wait_send()

    to_section(sent)

    @pl.loop(1, 32)
    def _(d):
        query(d).wait_send()

    for z in range(2):
        mine = jnp.logical_and(to_x == sec, half == z)
        there = remote(out, wo.at[sec], out_send.at[z], out_recv.at[sec], (to_x, 8 * z + low))

        @pl.when(mine)
        def _():
            own_out.wait()

        @pl.when(jnp.logical_not(mine))
        def _():
            there.wait_send()

    for g in gathers:
        g.finish()
    for one in own:
        one.wait()


def fetch_weights(small, mix, out, exp, con):
    bf16 = jnp.bfloat16
    dma = pltpu.SemaphoreType.DMA
    return pl.pallas_call(
        fetch_kernel,
        out_shape=(
            jax.ShapeDtypeStruct((32, 128, 2 * HD), bf16),
            jax.ShapeDtypeStruct((32,) + small.shape, bf16),
            jax.ShapeDtypeStruct((2, 16, 128, HD), bf16),
            jax.ShapeDtypeStruct((2, 128, D), bf16),
            jax.ShapeDtypeStruct((8, 128, 512), bf16),
            jax.ShapeDtypeStruct((8, 128, 512), bf16),
            jax.ShapeDtypeStruct((256, D), bf16),
            jax.ShapeDtypeStruct((256, D), bf16),
        ),
        in_specs=[pl.BlockSpec(memory_space=pl.ANY)] * 5,
        out_specs=[pl.BlockSpec(memory_space=pl.ANY)] * 8,
        scratch_shapes=[
            dma((32,)),
            dma((32,)),
            dma((2, 16)),
            dma((2, 16)),
            dma,
            dma,
            dma((2,)),
            dma((2,)),
            dma((7,)),
            dma((3, 32)),
            dma((3, 32)),
            dma((1, 32)),
            dma((1, 32)),
        ],
        compiler_params=pltpu.CompilerParams(
            collective_id=1, has_side_effects=True, vmem_limit_bytes=LIMIT
        ),
        name="fetch_weights",
    )(small, mix, out, exp, con)


def last_kernel(small, gq0, gq1, go0, go1, cross, total, rq, ro, crossed, *scratch):
    buf, s_send, s_recv, q_send, q_recv, out_send, out_recv, own_sem, x_send, x_recv = scratch
    sec, shd = lax.axis_index("section"), lax.axis_index("shard")
    half = shd // 8
    f = block_of(sec, shd)
    everyone_barrier(16 * sec + shd)
    h = Hyper(ALL)
    k = len(ALL)
    r = Reduce(h, SMALL, small, buf, s_send, s_recv)
    for low in reversed(range(1 << (k - 1))):
        for p in range(len(SMALL)):
            r.copy(p, k - 1, low).start()
    swap = remote(cross, crossed, x_send, x_recv, (1 - sec, shd))
    pl.when(sec == 1)(swap.start)

    def query(s, d):
        src = (gq0, gq1)[s].at[lax.rem(shd + d, 16)]
        dst = rq.at[half, :, columns(f, HD)]
        return src, dst, remote(src, dst, q_send.at[s, d], q_recv.at[sec, d], (s, lax.rem(shd + d, 16)))

    def rows(s):
        src, dst = (go0, go1)[s], ro.at[half]
        return src, dst, remote(src, dst, out_send.at[s], out_recv.at[half], (s, f))

    def either(local, n, copy, start):
        src, dst, there = copy
        here = pltpu.make_async_copy(src, dst, own_sem.at[n])

        @pl.when(local)
        def _():
            here.start() if start else here.wait()

        @pl.when(jnp.logical_not(local))
        def _():
            there.start() if start else there.wait_send()

    for s in range(2):
        either(sec == s, 0, query(s, 0), True)
        either(jnp.logical_and(sec == s, f == shd), 1, rows(s), True)

        @pl.loop(1, 16)
        def _(d):
            query(s, d)[2].start()

    for j in reversed(range(k)):
        for low in reversed(range(1 << j)):
            for p in range(len(SMALL)):
                r.add(p, j, low, total)
    pl.when(sec == 1)(swap.wait_send)
    pl.when(sec == 0)(swap.wait_recv)

    def arrival(s, d):
        return remote(gq0.at[0], rq.at[0, :, pl.ds(0, HD)], q_send.at[0, 0], q_recv.at[s, d], (1 - sec, shd))

    for s in range(2):

        @pl.when(sec != s)
        def _():
            arrival(s, 0).wait_recv()

        @pl.loop(1, 16)
        def _(d):
            arrival(s, d).wait_recv()

        @pl.when(jnp.logical_not(jnp.logical_and(f == shd, half == s)))
        def _():
            remote(go0, ro.at[s], out_send.at[0], out_recv.at[s], (1 - sec, shd)).wait_recv()

    for s in range(2):
        either(sec == s, 0, query(s, 0), False)
        either(jnp.logical_and(sec == s, f == shd), 1, rows(s), False)

        @pl.loop(1, 16)
        def _(d):
            query(s, d)[2].wait_send()

    r.finish()


def return_last(small, gq, go, cross):
    bf16, f32 = jnp.bfloat16, jnp.float32
    dma = pltpu.SemaphoreType.DMA
    hbm, vmem = pl.BlockSpec(memory_space=pl.ANY), pl.BlockSpec(memory_space=pltpu.VMEM)
    return pl.pallas_call(
        last_kernel,
        out_shape=(
            jax.ShapeDtypeStruct(small.shape[1:], f32),
            jax.ShapeDtypeStruct((2, 128, D), bf16),
            jax.ShapeDtypeStruct((2, 128, D), bf16),
            jax.ShapeDtypeStruct((128, D), bf16),
        ),
        in_specs=[vmem] + [hbm] * 5,
        out_specs=[vmem] + [hbm] * 3,
        scratch_shapes=[
            pltpu.VMEM(small.shape, bf16),
            dma((3, 32)),
            dma((3, 32)),
            dma((2, 16)),
            dma((2, 16)),
            dma((2,)),
            dma((2,)),
            dma((2,)),
            dma,
            dma,
        ],
        compiler_params=pltpu.CompilerParams(
            collective_id=2, has_side_effects=True, vmem_limit_bytes=LIMIT
        ),
        name="return_last",
    )(small, *gq, *go, cross)


HALVES = [[n, n + 8] for n in range(8)]


def from_halves(x):
    return lax.all_gather(x, "shard", axis=0, tiled=True, axis_index_groups=HALVES)


NT = (((1,), (1,)), ((), ()))
TN = (((0,), (0,)), ((), ()))


def dot32(a, b):
    return jnp.dot(a, b, preferred_element_type=jnp.float32)


def dot_nt(a, b):
    return lax.dot_general(a, b, NT, preferred_element_type=jnp.float32)


def dot_tn(a, b):
    return lax.dot_general(a, b, TN, preferred_element_type=jnp.float32)


EVEN = cube_parts(128, (768, 640, 640))
LIGHT = cube_parts(128, (896, 896, 256))
TRIO = ("x", 4, 2)
CHUNK = 64


def spaced(many, few):
    result = []
    for n, step in enumerate(many):
        result.append(step)
        done = len(few) * (n + 1) // len(many)
        result.extend(few[len(few) * n // len(many) : done])
    return result


def chunk_gather_steps(g, count):
    k = len(g.h.dims)

    def step(j, low):
        for p in range(count):
            g.copy(p, low, j).wait_recv()
            for later in range(j + 1, k):
                g.copy(p, low | 1 << j, later).start()

    return [functools.partial(step, j, low) for j in range(k) for low in range(1 << j)]


def chunk_reduce_steps(r, out):
    k = len(r.h.dims)
    return [
        functools.partial(r.add, p, j, low, out)
        for j in reversed(range(k))
        for low in reversed(range(1 << j))
        for p in range(len(r.parts))
    ]


GELU_K = (2.0 / 3.141592653589793) ** 0.5


def gelu_pair(u):
    square = u * u
    t = jnp.tanh(GELU_K * (u + 0.044715 * u * square))
    half = 0.5 * (1.0 + t)
    slope = half + 0.5 * u * (1.0 - t * t) * (GELU_K * (1.0 + 3 * 0.044715 * square))
    return u * half, slope


def hidden_kernel(back, plan, *refs):
    if back:
        x_ref, we_hbm, wc_hbm, slope_hbm, act_hbm, n2_hbm, o_ref, dc_out, de_out, be_ref = refs[:10]
        act_all, n2_all, d_tile = refs[10:13]
        scratch = refs[13:]
    else:
        x_ref, we_hbm, wc_hbm, be_ref, o_ref, x_out, h_out, slope_out = refs[:8]
        scratch = refs[8:]
    x_all, we, wc, h_all, slope, part, came, buf = scratch[:8]
    g_send, g_recv, c_send, c_recv, r_send, r_recv, own_sem, load_sem, out_sem = scratch[8:]
    h = Hyper(CUBE)
    trio = Hyper(TRIO)
    h.barrier()
    loads = [pltpu.make_async_copy(we_hbm, we, load_sem.at[0]), pltpu.make_async_copy(wc_hbm, wc, load_sem.at[1])]
    if back:
        loads.append(pltpu.make_async_copy(slope_hbm, slope, load_sem.at[2]))
        late = [
            pltpu.make_async_copy(act_hbm, act_all, load_sem.at[3]),
            pltpu.make_async_copy(n2_hbm, n2_all, load_sem.at[4]),
        ]
    parts = tuple((0, CHUNK, c0, cn, order) for _, _, c0, cn, order in plan)
    gathers, sums = [], []
    for n in range(2):
        mine = x_ref.at[pl.ds(CHUNK * n, CHUNK)]
        own = pltpu.make_async_copy(mine, x_all.at[n, h.pos], own_sem.at[n])
        own.start()
        loads.append(own)
        gathers.append(Gather(h, parts, mine, x_all.at[n], g_send.at[n], g_recv.at[n]))
        sums.append(
            Reduce(
                trio,
                tuple((0, CHUNK, c0, cn, order[:3]) for _, _, c0, cn, order in plan),
                came.at[n],
                buf.at[n],
                r_send.at[n],
                r_recv.at[n],
            )
        )
        gathers[n].start(range(len(plan)))
    for one in loads[:-2]:
        one.start()
    core = 1 - lax.rem(lax.axis_index("shard"), 2)

    def quad(r):
        return 4 * (h.pos // 4) + (h.delta["x"] if r & 2 else 0) + (h.delta[4] if r & 1 else 0)

    def pair(r, y):
        return quad(r) + 2 * (lax.rem(h.pos, 4) // 2) + (h.delta[2] if y else 0)

    def compute(n, r):
        four = pl.ds(quad(r), 4)
        x = x_all[n, four].reshape(4 * CHUNK, D)
        if back:
            inner = dot_nt(x, wc[...]).reshape(4, CHUNK, 512)
            mid = (inner * slope[n, four].astype(jnp.float32)).astype(jnp.bfloat16)
        else:
            inner = dot32(x, we[...]) + be_ref[...]
            act, grad = gelu_pair(inner)
            mid = act.astype(jnp.bfloat16).reshape(4, CHUNK, 512)
            slope[n, four] = grad.astype(jnp.bfloat16).reshape(4, CHUNK, 512)
        h_all[n, four] = mid
        mid = mid.reshape(4 * CHUNK, 512)
        if back:
            be_ref[...] += jnp.sum(mid.astype(jnp.float32), axis=0, keepdims=True)
        for c in range(4):
            cols = pl.ds(512 * c, 512)
            tile = dot_nt(mid, we[cols, :]) if back else dot32(mid, wc[:, cols])
            part[n, four, :, cols] = tile.astype(jnp.bfloat16).reshape(4, CHUNK, 512)
        for y in reversed(range(2)):
            core_copy(n, r, y).start()

    def core_copy(n, r, y):
        at = pair(r, y)
        return remote(
            part.at[n, at + core],
            came.at[n, at // 2],
            c_send.at[n, 2 * r + y],
            c_recv.at[n, 2 * r + y],
            h.partner[1],
        )

    def core_add(n, r):
        for y in reversed(range(2)):
            core_copy(n, r, y).wait_recv()
            at = pair(r, y)

            @pl.loop(0, CHUNK // 16)
            def _(i):
                rows = pl.ds(pl.multiple_of(i * 16, 16), 16)
                total = part[n, at + 1 - core, rows, :].astype(jnp.float32) + came[
                    n, at // 2, rows, :
                ].astype(jnp.float32)
                came[n, at // 2, rows, :] = total.astype(jnp.bfloat16)

            offset = ((r >> 1) & 1, r & 1, y)
            for p, (_, _, _, _, order) in enumerate(sums[n].parts):
                bits = [offset[TRIO.index(d)] for d in order]
                if bits[2]:
                    sums[n].copy(p, 2, bits[0] | bits[1] << 1).start()

    def compute_steps(n):
        steps = []
        for r in (3, 2, 1, 0):
            steps.append(functools.partial(compute, n, r))
            if r < 3:
                steps.append(functools.partial(core_add, n, r + 1))
        return steps + [functools.partial(core_add, n, 0)]

    for step in chunk_gather_steps(gathers[0], len(plan)):
        step()
    for one in loads:
        one.wait()
    if back:
        for one in late:
            one.start()
        be_ref[...] = jnp.zeros_like(be_ref)

    tiles = []

    def product(left, right, c, n, dst, slot):
        if len(tiles) >= 2:
            tiles[-2].wait()
        if left is act_all:
            x = right[:, :, :, pl.ds(512 * c, 512)].reshape(D, 512)
            d_tile[slot] = dot_tn(left[...].reshape(D, 512), x).astype(jnp.bfloat16)
        else:
            x = left[:, :, :, pl.ds(512 * c, 512)].reshape(D, 512)
            d_tile[slot] = dot_tn(x, right[...].reshape(D, 512)).astype(jnp.bfloat16)
        tiles.append(pltpu.make_async_copy(d_tile.at[slot], dst, out_sem.at[slot]))
        tiles[-1].start()

    for step in spaced(chunk_gather_steps(gathers[1], len(plan)), compute_steps(0)):
        step()
    out_rows = [o_ref.at[pl.ds(CHUNK * n, CHUNK)] for n in range(2)]
    first = chunk_reduce_steps(sums[0], out_rows[0])
    outs = []
    if back:
        wait_late = [one.wait for one in late]
        of_wc = [
            functools.partial(product, act_all, x_all, c, n, dc_out.at[:, pl.ds(512 * c, 512)], c % 2)
            for n, c in enumerate(range(4))
        ]
        of_we = [
            functools.partial(product, n2_all, h_all, c, n, de_out.at[pl.ds(512 * c, 512)], c % 2)
            for n, c in enumerate(range(4))
        ]
    else:
        outs = [pltpu.make_async_copy(x_all, x_out, out_sem.at[0])]
        outs[0].start()
    for step in spaced(first, compute_steps(1)):
        step()
    last_steps = chunk_reduce_steps(sums[1], out_rows[1])
    if back:
        last_steps = spaced(last_steps, wait_late + of_wc + of_we)
    else:
        outs.append(pltpu.make_async_copy(h_all, h_out, out_sem.at[1]))
        outs.append(pltpu.make_async_copy(slope, slope_out, out_sem.at[2]))
        for one in outs[1:]:
            one.start()
    for step in last_steps:
        step()
    outs += tiles[-2:]
    for n in range(2):
        gathers[n].finish()
        sums[n].finish()
        for r in range(4):
            for y in range(2):
                core_copy(n, r, y).wait_send()
    for one in outs:
        one.wait()


def hidden_layer(back, x, we, wc, rest, plan, collective_id, name):
    bf16, f32 = jnp.bfloat16, jnp.float32
    dma = pltpu.SemaphoreType.DMA
    hbm, vmem = pl.BlockSpec(memory_space=pl.ANY), pl.BlockSpec(memory_space=pltpu.VMEM)
    wide, narrow = (2, 16, CHUNK, D), (2, 16, CHUNK, 512)
    out = [jax.ShapeDtypeStruct((128, D), f32)]
    more = []
    if back:
        out += [
            jax.ShapeDtypeStruct((512, D), bf16),
            jax.ShapeDtypeStruct((D, 512), bf16),
            jax.ShapeDtypeStruct((1, 512), f32),
        ]
        out_specs = [vmem, hbm, hbm, vmem]
        more = [pltpu.VMEM(narrow, bf16), pltpu.VMEM(wide, bf16), pltpu.VMEM((2, 512, 512), bf16)]
    else:
        out += [
            jax.ShapeDtypeStruct(wide, bf16),
            jax.ShapeDtypeStruct(narrow, bf16),
            jax.ShapeDtypeStruct(narrow, bf16),
        ]
        out_specs = [vmem, hbm, hbm, hbm]
    return pl.pallas_call(
        functools.partial(hidden_kernel, back, plan),
        out_shape=out,
        in_specs=[hbm, hbm, hbm] + ([hbm] * 3 if back else [vmem]),
        out_specs=out_specs,
        scratch_shapes=more
        + [
            pltpu.VMEM(wide, bf16),
            pltpu.VMEM((D, 512), bf16),
            pltpu.VMEM((512, D), bf16),
            pltpu.VMEM(narrow, bf16),
            pltpu.VMEM(narrow, bf16),
            pltpu.VMEM(wide, bf16),
            pltpu.VMEM((2, 8, CHUNK, D), bf16),
            pltpu.VMEM((2, 8, CHUNK, D), bf16),
            dma((2, 3, 16)),
            dma((2, 3, 16)),
            dma((2, 8)),
            dma((2, 8)),
            dma((2, 3, 8)),
            dma((2, 3, 8)),
            dma((2,)),
            dma((5,)),
            dma((3,)),
        ],
        compiler_params=pltpu.CompilerParams(
            collective_id=collective_id, has_side_effects=True, vmem_limit_bytes=LIMIT
        ),
        name=name,
    )(x, we, wc, *rest)


QB = 256
KB = WINDOW + QB
SCALE = HD ** (-0.5)
NEAR = (2, 4, "x")


def kept_pairs(lo, a):
    key = a + lax.broadcasted_iota(jnp.int32, (KB, QB), 0)
    last = a + WINDOW + lax.broadcasted_iota(jnp.int32, (KB, QB), 1)
    return (key >= lo) & (key <= last)


class PairSum:
    def __init__(self, h, trio, plan, part, came, buf, sems):
        self.c_send, self.c_recv, r_send, r_recv = sems
        self.h, self.trio, self.part, self.came = h, trio, part, came
        parts = tuple((0, 128, c0, cn, order[:3]) for _, _, c0, cn, order in plan)
        self.sums = Reduce(trio, parts, came, buf, r_send, r_recv)
        self.core = lax.rem(lax.axis_index("shard"), 2)

    def pair(self, o):
        return self.trio.at(NEAR, o)

    def core_copy(self, o):
        n = self.pair(o)
        return remote(
            self.part.at[2 * n + 1 - self.core],
            self.came.at[n],
            self.c_send.at[o],
            self.c_recv.at[o],
            self.h.partner[1],
        )

    def core_add(self, o):
        self.core_copy(o).wait_recv()
        n = self.pair(o)

        @pl.loop(0, 8)
        def _(i):
            rows = pl.ds(pl.multiple_of(i * 16, 16), 16)
            total = self.part[2 * n + self.core, rows, :].astype(jnp.float32) + self.came[
                n, rows, :
            ].astype(jnp.float32)
            self.came[n, rows, :] = total.astype(jnp.bfloat16)

        for p, (_, _, _, _, order) in enumerate(self.sums.parts):
            bits = [o >> NEAR.index(d) & 1 for d in order]
            if bits[2]:
                self.sums.copy(p, 2, bits[0] | bits[1] << 1).start()

    def schedule(self, compute, out, lag=2):
        steps, waiting, made = [], [], []
        for n, o in enumerate(range(7, -1, -1)):
            steps.append(functools.partial(compute, o))
            if n:
                steps.append(functools.partial(self.core_add, o + 1))
                made.append(o + 1)
            for p, (_, _, _, _, order) in enumerate(self.sums.parts):
                for low in range(4):
                    own = sum((low >> b & 1) << NEAR.index(order[b]) for b in range(2))
                    if own in made and made.index(own) <= len(made) - 1 - lag and (p, low) not in waiting:
                        waiting.append((p, low))
                        steps.append(functools.partial(self.sums.add, p, 2, low, out))
        steps.append(functools.partial(self.core_add, 0))
        rest = [
            functools.partial(self.sums.add, p, j, low, out)
            for j in reversed(range(3))
            for low in reversed(range(1 << j))
            for p in range(len(self.sums.parts))
            if j < 2 or (p, low) not in waiting
        ]
        return steps, rest

    def following(self, compute):
        before = []

        def step(o):
            compute(o)
            if before:
                self.core_add(before.pop())
            before.append(o)

        return step, lambda: self.core_add(before.pop())

    def finish(self):
        self.sums.finish()
        for o in range(8):
            self.core_copy(o).wait_send()


def pair_gather_steps(g, used):
    def number(o, order):
        return sum((o >> NEAR.index(d) & 1) << n for n, d in enumerate(order[:3]))

    def link(j, low):
        for p in range(len(g.parts)):
            g.copy(p, low, j).wait_recv()
            for later in range(j + 1, 4):
                g.copy(p, low | 1 << j, later).start()

    def pair(o):
        for p, part in enumerate(g.parts):
            g.copy(p, number(o, part[4]), 3).wait_recv()
        used(o)

    steps = []
    for j in range(3):
        for low in range(1 << j):
            steps.append(functools.partial(link, j, low))
            for o in range(8):
                if max(1, *[number(o, part[4]) for part in g.parts]) == low | 1 << j:
                    steps.append(functools.partial(pair, o))
    return steps


def attend_kernel(plan, section, *refs):
    ins, refs = refs[:8], refs[8:]
    x_ref, kv_ref, wq_hbm, wkv_hbm, wo_hbm, bq_ref, bkv_ref, lo_ref = ins
    o_ref, x_out, q_out, kv_out, mixed_out, lse_ref = refs[:6]
    refs = refs[6:]
    x_all, wq, wkv, wo, far, far_all, q_all, kv_all, mixed, part, came, buf = refs[:12]
    g_send, g_recv, k_send, k_recv, swap_send, swap_recv, own_sem, load_sem, out_sem = refs[12:21]
    pair_sems = refs[21:]
    h, trio = Hyper(CUBE), Hyper(TRIO)
    sec, shd = lax.axis_index("section"), lax.axis_index("shard")
    other = (sec, shd + 8 * (1 - 2 * (shd // 8)))
    h.barrier((other,))
    swap = remote(kv_ref, far, swap_send, swap_recv, other)
    swap.start()
    loads = [
        pltpu.make_async_copy(x_ref, x_all.at[h.pos], own_sem),
        pltpu.make_async_copy(wq_hbm.at[section], wq, load_sem.at[0]),
        pltpu.make_async_copy(wkv_hbm.at[section], wkv, load_sem.at[1]),
        pltpu.make_async_copy(wo_hbm.at[section], wo, load_sem.at[2]),
    ]
    for one in loads:
        one.start()
    g = Gather(h, plan, x_ref, x_all, g_send, g_recv)
    g.start(range(len(plan)))
    swap.wait_recv()
    far_all[h.pos] = far[...]
    gkv = Gather(h, ((0, 128, 0, 2 * HD, CUBE),), far, far_all, k_send, k_recv)
    gkv.start(range(1))
    for one in loads:
        one.wait()
    sums = PairSum(h, trio, plan, part, came, buf, pair_sems)

    def project(o):
        n = sums.pair(o)
        x = x_all[pl.ds(2 * n, 2)].reshape(QB, D)
        q_all[n] = (dot32(x, wq[...]) + bq_ref[...]).astype(jnp.bfloat16)
        at = pl.ds(pl.multiple_of(WINDOW + QB * lax.rem(n, 4), QB), QB)
        kv_all[n // 4, at] = (dot32(x, wkv[...]) + bkv_ref[...]).astype(jnp.bfloat16)

    far_steps = chunk_gather_steps(gkv, 1)
    for step in spaced(pair_gather_steps(g, project), far_steps):
        step()
    kv_all[:, :WINDOW] = far_all[...].reshape(2, WINDOW, 2 * HD)

    def compute(o):
        n = sums.pair(o)
        m, a = n // 4, pl.multiple_of(QB * lax.rem(n, 4), QB)
        keys = pl.ds(a, KB)
        s = dot_nt(kv_all[m, keys, :HD], q_all[n]) * SCALE
        s = jnp.where(kept_pairs(lo_ref[n], a), s, -1e30)
        top = jnp.max(s, axis=0, keepdims=True)
        e = jnp.exp(s - top)
        total = jnp.sum(e, axis=0, keepdims=True)
        probs = (e * (1.0 / total)).astype(jnp.bfloat16)
        mix = dot_tn(probs, kv_all[m, keys, HD:]).astype(jnp.bfloat16)
        mixed[n] = mix
        lse_ref[n] = top + jnp.log(total)
        for c in range(4):
            cols = pl.ds(512 * c, 512)
            part[pl.ds(2 * n, 2), :, cols] = (
                dot32(mix, wo[:, cols]).astype(jnp.bfloat16).reshape(2, 128, 512)
            )
        sums.core_copy(o).start()

    outs = [
        pltpu.make_async_copy(x_all, x_out, out_sem.at[0]),
        pltpu.make_async_copy(q_all, q_out, out_sem.at[1]),
        pltpu.make_async_copy(kv_all, kv_out, out_sem.at[2]),
    ]
    for one in outs:
        one.start()
    steps, rest = sums.schedule(compute, o_ref)
    for step in steps:
        step()
    outs.append(pltpu.make_async_copy(mixed, mixed_out, out_sem.at[3]))
    outs[-1].start()
    for step in rest:
        step()
    g.finish()
    gkv.finish()
    swap.wait_send()
    sums.finish()
    for one in outs:
        one.wait()


def attend_layer(x, kv, wq, wkv, wo, bq, bkv, lo, plan, section):
    bf16, f32 = jnp.bfloat16, jnp.float32
    dma = pltpu.SemaphoreType.DMA
    hbm, vmem = pl.BlockSpec(memory_space=pl.ANY), pl.BlockSpec(memory_space=pltpu.VMEM)
    out = [
        jax.ShapeDtypeStruct((128, D), f32),
        jax.ShapeDtypeStruct((16, 128, D), bf16),
        jax.ShapeDtypeStruct((8, QB, HD), bf16),
        jax.ShapeDtypeStruct((2, 2 * WINDOW, 2 * HD), bf16),
        jax.ShapeDtypeStruct((8, QB, HD), bf16),
        jax.ShapeDtypeStruct((8, 1, QB), f32),
    ]
    out_specs = [vmem, hbm, hbm, hbm, hbm, vmem]
    return pl.pallas_call(
        functools.partial(attend_kernel, plan, section),
        out_shape=out,
        in_specs=[hbm] * 5 + [vmem] * 3,
        out_specs=out_specs,
        scratch_shapes=[
            pltpu.VMEM((16, 128, D), bf16),
            pltpu.VMEM((D, HD), bf16),
            pltpu.VMEM((D, 2 * HD), bf16),
            pltpu.VMEM((HD, D), bf16),
            pltpu.VMEM((128, 2 * HD), bf16),
            pltpu.VMEM((16, 128, 2 * HD), bf16),
            pltpu.VMEM((8, QB, HD), bf16),
            pltpu.VMEM((2, 2 * WINDOW, 2 * HD), bf16),
            pltpu.VMEM((8, QB, HD), bf16),
            pltpu.VMEM((16, 128, D), bf16),
            pltpu.VMEM((8, 128, D), bf16),
            pltpu.VMEM((8, 128, D), bf16),
            dma((3, 16)),
            dma((3, 16)),
            dma((1, 16)),
            dma((1, 16)),
            dma,
            dma,
            dma,
            dma((3,)),
            dma((4,)),
            dma((8,)),
            dma((8,)),
            dma((3, 8)),
            dma((3, 8)),
        ],
        compiler_params=pltpu.CompilerParams(
            collective_id=3 + section, has_side_effects=True, vmem_limit_bytes=LIMIT
        ),
        name="attend",
    )(x, kv, wq, wkv, wo, bq, bkv, lo)


class Home:
    def __init__(self, home, c_count, c, e, rc, re, sems):
        self.home, self.c_count, self.c, self.e, self.rc, self.re = home, c_count, c, e, rc, re
        self.send, self.c_recv, self.e_recv, self.own_sem = sems
        self.sec, self.shd = lax.axis_index("section"), lax.axis_index("shard")
        self.half, self.low = self.shd // 8, lax.rem(self.shd, 8)
        self.me, self.place = half_group(self.sec, self.shd)
        self.here = self.sec == home

    def copies(self, n):
        if n < self.c_count:
            size = 256 // self.c_count
            src = self.c.at[pl.ds(size * n, size)]
            dst = self.rc.at[pl.ds(256 * self.sec + size * n, size)]
            return self.here, [(src, dst, (self.home, self.shd), self.send.at[n, 0], self.c_recv.at[n], self.own_sem.at[n, 0])]
        k = n - self.c_count
        return jnp.logical_and(self.here, self.low == k), [
            (
                self.e.at[pl.ds(128 * k, 128), pl.ds(256 * c, 256)],
                self.re.at[:, columns(2 * (8 * c + self.low) + self.sec, 256)],
                (self.home, 8 * self.half + k),
                self.send.at[n, c],
                self.e_recv.at[self.me, c],
                self.own_sem.at[n, c],
            )
            for c in range(2)
        ]

    def go(self, n, start):
        local, copies = self.copies(n)

        @pl.when(local)
        def _():
            for src, dst, _, _, _, sem in copies:
                one = pltpu.make_async_copy(src, dst, sem)
                one.start() if start else one.wait()

        @pl.when(jnp.logical_not(local))
        def _():
            for src, dst, there, send, recv, _ in copies:
                one = remote(src, dst, send, recv, there)
                one.start() if start else one.wait_send()

    def finish(self):
        for n in range(self.c_count + 8):
            self.go(n, False)

        @pl.when(self.here)
        def _():
            size = 256 // self.c_count
            for n in range(self.c_count):
                rows = pl.ds(size * n, size)
                remote(
                    self.c.at[rows], self.rc.at[rows], self.send.at[n, 0], self.c_recv.at[n], (1 - self.sec, self.shd)
                ).wait_recv()

            @pl.loop(1, 16)
            def _(d):
                n = lax.rem(self.me + d, 16)
                for c in range(2):
                    remote(
                        self.e.at[pl.ds(0, 128), pl.ds(0, 256)],
                        self.re.at[:, pl.ds(256 * c, 256)],
                        self.send.at[self.c_count, c],
                        self.e_recv.at[n, c],
                        self.place(n),
                    ).wait_recv()


def attend_back_kernel(plan, home, *refs):
    x_ref, n1_hbm, wq_hbm, wo_hbm, q_hbm, kv_hbm, mixed_hbm, lse_ref, lo_ref, gc, ge, cross = refs[:12]
    if home == 0:
        c_before, e_before = refs[12:14]
        refs = refs[:12] + refs[14:]
    o_ref, own_ref, far_ref, wo_ref, wq_ref, bq_ref, rc, re, crossed = refs[12:21]
    x_all, n1, wq, wo, q_all, kv_all, mixed, dq_all, dk, dv, part, came, buf = refs[21:34]
    kv_parts, kv_bufs, sent = refs[34:36], refs[36:38], refs[38]
    c_kept, c_came, e_kept, e_came = refs[39:43]
    g_send, g_recv, swap_send, swap_recv, own_sem, load_sem, bg_send, bg_recv = refs[43:51]
    pair_sems, kv_sems = refs[51:55], refs[55:59]
    home_sems, (kept_sem, x_send, x_recv) = refs[59:63], refs[63:66]
    deliver = home == 0
    if deliver:
        back_home = Home(home, 8, c_kept, e_kept, rc, re, home_sems)
        before = Home(1, 8, c_before, e_before, rc, re, refs[66:])
    h, trio = Hyper(CUBE), Hyper(TRIO)
    sec, shd = lax.axis_index("section"), lax.axis_index("shard")
    half, low = shd // 8, lax.rem(shd, 8)
    other = (sec, shd + 8 * (1 - 2 * half))
    me, place = half_group(sec, shd)
    barrier = pltpu.get_barrier_semaphore()

    @pl.loop(1, 16)
    def _(d):
        pl.semaphore_signal(
            barrier, inc=1, device_id=place(lax.rem(me + d, 16)), device_id_type=MESH
        )

    pl.semaphore_signal(barrier, inc=1, device_id=other, device_id_type=MESH)
    pl.semaphore_wait(barrier, 16)

    def beside(n):
        if n < 8:
            rows = pl.ds(32 * n, 32)
            src, dst = gc.at[1 - half, rows], c_came.at[rows]
        else:
            rows = pl.ds(128 * (n - 8), 128)
            src, dst = ge.at[1 - half, rows], e_came.at[rows]
        return remote(src, dst, bg_send.at[n], bg_recv.at[n], other)

    def land(n):
        beside(n).wait_recv()
        mine, theirs, first, count = (c_kept, c_came, 32 * n, 2) if n < 8 else (e_kept, e_came, 128 * (n - 8), 8)

        @pl.loop(0, count)
        def _(i):
            rows = pl.ds(pl.multiple_of(first + 16 * i, 16), 16)
            total = mine[rows, :].astype(jnp.float32) + theirs[rows, :].astype(jnp.float32)
            mine[rows, :] = total.astype(mine.dtype)

        if deliver:
            back_home.go(n, True)

    LAG = 7 if home == 0 else 12
    turns = []
    for n in range(16 + LAG):
        turn = []
        if n < 16:
            turn.append(beside(n).start)
            if deliver:
                turn.append(functools.partial(before.go, n, True))
        if n >= LAG:
            turn.append(functools.partial(land, n - LAG))
        turns.append(turn)

    def feed(steps, every):
        for n, step in enumerate(steps):
            step()
            if turns and n % every == every - 1:
                for one in turns.pop(0):
                    one()

    kept = [
        pltpu.make_async_copy(gc.at[half], c_kept, kept_sem.at[0]),
        pltpu.make_async_copy(ge.at[half], e_kept, kept_sem.at[1]),
    ]
    for one in kept:
        one.start()
    swap_rows = remote(cross, crossed, x_send, x_recv, (1 - sec, shd))

    def swap_step(step, sending):
        if home == 1:
            step()
        else:
            pl.when(sec == (0 if sending else 1))(step)

    own = pltpu.make_async_copy(x_ref, x_all.at[h.pos], own_sem)
    own.start()
    g = Gather(h, plan, x_ref, x_all, g_send, g_recv)
    g.start(range(len(plan)))
    pairs = ((wq_hbm.at[home], wq), (wo_hbm.at[home], wo), (q_hbm, q_all), (kv_hbm, kv_all), (mixed_hbm, mixed), (n1_hbm, n1))
    loads = [pltpu.make_async_copy(src, dst, load_sem.at[n]) for n, (src, dst) in enumerate(pairs)]
    for one in loads:
        one.start()
    own.wait()
    for one in loads[:5] + kept:
        one.wait()
    sums = PairSum(h, trio, plan, part, came, buf, pair_sems)

    bq_ref[...] = jnp.zeros_like(bq_ref)
    dk[...] = jnp.zeros_like(dk)
    dv[...] = jnp.zeros_like(dv)

    def compute(o):
        n = sums.pair(o)
        m, a = n // 4, pl.multiple_of(QB * lax.rem(n, 4), QB)
        keys = pl.ds(a, KB)
        q, k = q_all[n], kv_all[m, keys, :HD]
        gm = dot_nt(x_all[pl.ds(2 * n, 2)].reshape(QB, D), wo[...]).astype(jnp.bfloat16)
        s = dot_nt(k, q) * SCALE
        probs = jnp.where(kept_pairs(lo_ref[n], a), jnp.exp(s - lse_ref[n]), 0.0)
        gp = dot_nt(kv_all[m, keys, HD:], gm)
        row = jnp.sum(probs * gp, axis=0, keepdims=True)
        gs = (probs * (gp - row)).astype(jnp.bfloat16)
        dq = (dot_tn(gs, k) * SCALE).astype(jnp.bfloat16)
        dq_all[n] = dq
        bq_ref[...] += jnp.sum(dq.astype(jnp.float32), axis=0, keepdims=True)
        for c in range(4):
            rows = pl.ds(512 * c, 512)
            part[pl.ds(2 * n, 2), :, rows] = (
                dot_nt(dq, wq[rows, :]).astype(jnp.bfloat16).reshape(2, 128, 512)
            )
        sums.core_copy(o).start()
        dk[m, keys] += dot32(gs, q) * SCALE
        dv[m, keys] += dot32(probs.astype(jnp.bfloat16), gm)

    step, last_add = sums.following(compute)
    for _ in range(2):
        for one in turns.pop(0):
            one()
    feed(pair_gather_steps(g, step), 2)
    last_add()
    swap_step(swap_rows.start, True)
    for one, first in zip(kv_parts, (WINDOW, 0)):
        rows = pl.ds(first, WINDOW)
        one[:, :, :HD] = dk[:, rows].astype(jnp.bfloat16).reshape(16, 128, HD)
        one[:, :, HD:] = dv[:, rows].astype(jnp.bfloat16).reshape(16, 128, HD)
    rest = chunk_reduce_steps(sums.sums, o_ref)
    kv_sums = [
        Reduce(h, BESIDE[n], kv_parts[n], kv_bufs[n], kv_sems[2 * n], kv_sems[2 * n + 1]) for n in range(2)
    ]
    for n in reversed(range(8)):
        for r in kv_sums:
            r.copy(0, 3, n).start()

    def product(left, right, c):
        cols = pl.ds(512 * c, 512)
        tile = dot_tn(left[...].reshape(D, HD), right[:, :, cols].reshape(D, 512))
        if right is x_all:
            wo_ref[:, cols] = tile.astype(wo_ref.dtype)
        else:
            wq_ref[cols, :] = tile.T.astype(wq_ref.dtype)

    products = [functools.partial(product, mixed, x_all, c) for c in range(4)]
    products += [loads[5].wait] + [functools.partial(product, dq_all, n1, c) for c in range(4)]
    kv_steps = [
        step
        for pair in zip(chunk_reduce_steps(kv_sums[0], own_ref), chunk_reduce_steps(kv_sums[1], far_ref))
        for step in pair
    ]
    feed(spaced(spaced(rest, kv_steps), products), 3)
    sent[0] = far_ref[...].astype(sent.dtype)
    swap = remote(sent.at[0], sent.at[1], swap_send, swap_recv, other)
    swap.start()
    while turns:
        for one in turns.pop(0):
            one()
    g.finish()
    sums.finish()
    for r in kv_sums:
        r.finish()
    swap.wait()
    far_ref[...] = sent[1].astype(jnp.float32)
    swap_step(swap_rows.wait_send, True)
    swap_step(swap_rows.wait_recv, False)
    for n in range(16):
        beside(n).wait_send()
    if deliver:
        back_home.finish()
        before.finish()
    else:
        summed = [
            pltpu.make_async_copy(c_kept, rc, kept_sem.at[0]),
            pltpu.make_async_copy(e_kept, re, kept_sem.at[1]),
        ]
        for one in summed:
            one.start()
        for one in summed:
            one.wait()


def attend_back_layer(x, n1, wq, wo, q, kv, mixed, lse, lo, gc, ge, cross, before, home, plan, collective_id):
    bf16, f32 = jnp.bfloat16, jnp.float32
    dma = pltpu.SemaphoreType.DMA
    hbm, vmem = pl.BlockSpec(memory_space=pl.ANY), pl.BlockSpec(memory_space=pltpu.VMEM)
    pair = pltpu.VMEM((16, 128, 2 * HD), bf16)
    homes = [jax.ShapeDtypeStruct((512, D), bf16), jax.ShapeDtypeStruct((128, 8192), bf16)]
    sums = [jax.ShapeDtypeStruct((256, D), bf16), jax.ShapeDtypeStruct((1024, 512), bf16)]
    home_sems = [dma((16, 2)), dma((8,)), dma((16, 2)), dma((16, 2))]
    return pl.pallas_call(
        functools.partial(attend_back_kernel, plan, home),
        out_shape=[
            jax.ShapeDtypeStruct((128, D), f32),
            jax.ShapeDtypeStruct((128, 2 * HD), f32),
            jax.ShapeDtypeStruct((128, 2 * HD), f32),
            jax.ShapeDtypeStruct((HD, D), bf16),
            jax.ShapeDtypeStruct((D, HD), bf16),
            jax.ShapeDtypeStruct((1, HD), f32),
        ]
        + (homes if home == 0 else sums)
        + [jax.ShapeDtypeStruct((128, D), bf16)],
        in_specs=[hbm] * 7 + [vmem] * 2 + [hbm] * (3 + len(before)),
        out_specs=[vmem] * 6 + [hbm] * 3,
        scratch_shapes=[
            pltpu.VMEM((16, 128, D), bf16),
            pltpu.VMEM((16, 128, D), bf16),
            pltpu.VMEM((D, HD), bf16),
            pltpu.VMEM((HD, D), bf16),
            pltpu.VMEM((8, QB, HD), bf16),
            pltpu.VMEM((2, 2 * WINDOW, 2 * HD), bf16),
            pltpu.VMEM((8, QB, HD), bf16),
            pltpu.VMEM((8, QB, HD), bf16),
            pltpu.VMEM((2, 2 * WINDOW, HD), f32),
            pltpu.VMEM((2, 2 * WINDOW, HD), f32),
            pltpu.VMEM((16, 128, D), bf16),
            pltpu.VMEM((8, 128, D), bf16),
            pltpu.VMEM((8, 128, D), bf16),
            pair,
            pair,
            pair,
            pair,
            pltpu.VMEM((2, 128, 2 * HD), bf16),
            pltpu.VMEM((256, D), bf16),
            pltpu.VMEM((256, D), bf16),
            pltpu.VMEM((1024, 512), bf16),
            pltpu.VMEM((1024, 512), bf16),
            dma((3, 16)),
            dma((3, 16)),
            dma,
            dma,
            dma,
            dma((6,)),
            dma((16,)),
            dma((16,)),
            dma((8,)),
            dma((8,)),
            dma((3, 8)),
            dma((3, 8)),
            dma((1, 16)),
            dma((1, 16)),
            dma((1, 16)),
            dma((1, 16)),
            *home_sems,
            dma((2,)),
            dma,
            dma,
        ]
        + (home_sems if home == 0 else []),
        compiler_params=pltpu.CompilerParams(
            collective_id=collective_id, has_side_effects=True, vmem_limit_bytes=LIMIT
        ),
        name="attend_back",
    )(x, n1, wq, wo, q, kv, mixed, lse, lo, gc, ge, cross, *before)


BESIDE = ((0, 128, 0, 256, (4, 2, "x", 1)),), ((0, 128, 0, 256, (2, "x", 4, 1)),)
SMALL = tuple(
    (48 * n, 48, 0, 256, order)
    for n, order in enumerate(((8, "x", 4, 2, 1), (8, 4, 2, "x", 1), (8, 2, "x", 4, 1)))
)
ALL_KV = tuple(
    (first, count, 0, 2 * HD, part[4]) for (first, count), part in zip(((0, 48), (48, 48), (96, 32)), SMALL)
)
ALL_SMALL = ((0, 16, 0, 128, SMALL[0][4]),)
BIAS = D + HD


def on_device_fast(
    embedded,
    cotangent,
    segments,
    first_gain,
    first_shift,
    mixer_weight,
    mixer_bias,
    output_weight,
    output_bias,
    second_gain,
    second_shift,
    expand_weight,
    expand_bias,
    contract_weight,
    contract_bias,
):
    bf16, f32 = jnp.bfloat16, jnp.float32
    sec, shd = lax.axis_index("section"), lax.axis_index("shard")
    half = shd // 8
    f = block_of(sec, shd)

    small = jnp.concatenate(
        [
            one[0].reshape(-1, 128)
            for one in (
                first_gain,
                first_shift,
                second_gain,
                second_shift,
                output_bias,
                contract_bias,
                expand_bias,
                jnp.pad(mixer_bias, ((0, 0), (0, 256 - mixer_bias.shape[1]))),
            )
        ],
        axis=0,
    )
    small = jnp.pad(small, ((0, 16 - small.shape[0]), (0, 0)))
    wkv, vectors, wq, wo, *halves = fetch_weights(
        small, mixer_weight[0], output_weight[0], expand_weight[0], contract_weight[0]
    )
    we = [from_halves(halves[s].reshape(8 * 128, 512)) for s in range(2)]
    wc = [from_halves(halves[2 + s]) for s in range(2)]
    wq = wq.reshape(2, D, HD)
    wkv = wkv.reshape(2, D, 2 * HD)
    vectors = vectors.reshape(2, 16, 16, 128)

    def vector(n):
        return vectors[:, :, n].reshape(2, D).astype(f32)

    gain_one, shift_one, gain_two, shift_two, bias_out, bias_con = [vector(n) for n in range(6)]
    bias_exp = vectors[:, :, 6:10].reshape(2, 8192).astype(f32)
    hidden_units = [512 * (8 * h + lax.rem(shd, 8)) + 256 * sec for h in range(2)]
    bias_exp = jnp.concatenate(
        [lax.dynamic_slice_in_dim(bias_exp, first, 256, 1) for first in hidden_units], axis=1
    )
    bias_mix = vectors[:, :, 10:12].reshape(2, 16, 256)[:, :, :136].reshape(2, BIAS).astype(f32)
    bias_q = lax.dynamic_slice_in_dim(bias_mix, f * HD, HD, 1)
    bias_kv = jnp.concatenate([jnp.zeros((2, HD), f32), bias_mix[:, D:]], axis=1)

    starts = jnp.sum(
        (segments[:, None, :] < lax.dynamic_slice_in_dim(segments, half * WINDOW, WINDOW, 1)[:, :, None]),
        axis=2,
        dtype=jnp.int32,
    )
    lo = jnp.maximum(jnp.arange(1, WINDOW + 1)[None], starts - half * WINDOW + WINDOW)
    lo = lo.reshape(8, 1, QB)

    hidden = lax.dynamic_index_in_dim(embedded, sec, 0, keepdims=False).astype(f32)
    results, kept = [], []
    for s in range(2):
        n1 = layer_norm(hidden, gain_one[s], shift_one[s]).astype(bf16)
        kv_rows = (dot32(n1, wkv[s]) + bias_kv[s]).astype(bf16)
        rows, all_n1, q, kv, mixed, lse = attend_layer(
            n1,
            kv_rows,
            wq,
            wkv,
            wo,
            bias_q[s][None],
            bias_kv[s][None],
            lo,
            LIGHT if s == 0 else EVEN,
            s,
        )
        middle = hidden + rows + bias_out[s]
        n2 = layer_norm(middle, gain_two[s], shift_two[s]).astype(bf16)
        rows, all_n2, act, slope = hidden_layer(False, n2, we[s], wc[s], (bias_exp[s][None],), LIGHT if s == 0 else EVEN, 9 + 2 * s, "hidden")
        result = middle + rows + bias_con[s]
        results.append(result.astype(bf16))
        kept.append((hidden, n1, all_n1, q, kv, lse, mixed, middle, all_n2, act, slope))
        hidden = results[-1].astype(f32)

    grad = lax.dynamic_index_in_dim(cotangent, sec, 0, keepdims=False).astype(f32)
    cross = jnp.where(sec == 0, results[1], results[0])
    came = [None, None]
    input_grads = [None, None]
    weight_grads = [None, None]
    small_grads = [None, None]
    for s in (1, 0):
        hidden, n1, all_n1, q, kv, lse, mixed, middle, all_n2, act, slope = kept[s]
        go = grad.astype(bf16)
        g_n2, d_wc, d_we, d_be = hidden_layer(
            True, go, we[s], wc[s], (slope, act, all_n2), EVEN, 10, "hidden_back"
        )
        d_wc, d_we, d_be = d_wc.reshape(2, 256, D), d_we.reshape(2, 1024, 512), d_be[0]
        _, back = jax.vjp(layer_norm, middle, gain_two[s], shift_two[s])
        g_mid, d_gain_two, d_shift_two = back(g_n2)
        g_mid = grad + g_mid
        ga = g_mid.astype(bf16)
        rows, kv_own, kv_far, d_wo, d_wq, d_bq, d_wc, d_we, crossed = attend_back_layer(
            ga,
            all_n1,
            wq,
            wo,
            q,
            kv,
            mixed,
            lse,
            lo,
            d_wc,
            d_we,
            cross,
            () if s == 1 else weight_grads[1][2:],
            s,
            LIGHT,
            5 + s,
        )
        dkv_rows = (kv_own + jnp.where(half == 0, kv_far, 0.0)).astype(bf16)
        g_n1 = rows + dot_nt(dkv_rows, wkv[s])
        _, back = jax.vjp(layer_norm, hidden, gain_one[s], shift_one[s])
        g_in, d_gain_one, d_shift_one = back(g_n1)
        g_in = g_mid + g_in
        input_grads[s] = g_in
        d_wkv = dot_tn(n1, dkv_rows)
        d_bq = d_bq[0]
        d_bv = jnp.sum(dkv_rows[:, HD:].astype(f32), axis=0)
        weight_grads[s] = (d_wq.reshape(16, 128, HD), d_wo, d_wc, d_we)
        came[s] = crossed
        cross = g_in.astype(bf16)
        spread = [
            d_gain_one,
            d_shift_one,
            d_gain_two,
            d_shift_two,
            jnp.sum(ga.astype(f32), axis=0),
            jnp.sum(go.astype(f32), axis=0),
        ]
        placed = jnp.zeros((8192,), f32)
        for h, first in enumerate(hidden_units):
            placed = lax.dynamic_update_slice_in_dim(placed, d_be[256 * h : 256 * (h + 1)], first, 0)
        d_bm = lax.dynamic_update_slice_in_dim(jnp.zeros((D,), f32), d_bq, f * HD, 0)
        vec = jnp.concatenate(
            [one.reshape(16, 128) for one in spread]
            + [placed.reshape(16, 512), jnp.concatenate([d_bm, d_bv]).reshape(16, 136)],
            axis=1,
        )
        vec = jnp.pad(vec, ((0, 0), (0, 4096 - vec.shape[1]))).reshape(16, 16, 256)
        small_grads[s] = jnp.concatenate([d_wkv.reshape(16, 128, 256), vec], axis=1)
        grad = cross.astype(f32)

    mine, rq, ro, last_came = return_last(
        jnp.concatenate(small_grads, axis=0).astype(bf16),
        (weight_grads[0][0], weight_grads[1][0]),
        (weight_grads[0][1], weight_grads[1][1]),
        cross,
    )
    vec = mine[128:].reshape(4096)

    def both(r):
        return r[0].astype(f32) + r[1].astype(f32)

    def here(pair):
        return jnp.where(sec == 0, pair[0], pair[1])

    def by_micro(own, theirs):
        return jnp.stack([jnp.where(sec == 0, own, theirs), jnp.where(sec == 0, theirs, own)])[None]

    grad_rows = here((last_came, came[0])).astype(f32)
    return (
        by_micro(here(results), came[1]),
        by_micro(here(input_grads), grad_rows),
        vec[0:128][None],
        vec[128:256][None],
        jnp.concatenate([both(rq), mine[:128]], axis=1)[None],
        vec[1280 : 1280 + 136][None],
        both(ro)[None],
        vec[512:640][None],
        vec[256:384][None],
        vec[384:512][None],
        weight_grads[0][3].astype(f32)[None],
        vec[768:1280][None],
        weight_grads[0][2].astype(f32)[None],
        vec[640:768][None],
    )


def solution(mesh):
    in_specs = (
        P(None, "shard", None),
        P(None, "shard", None),
        P(),
        P("section", "shard"),
        P("section", "shard"),
        P("section", "shard", None),
        P("section", "shard"),
        P("section", "shard", None),
        P("section", "shard"),
        P("section", "shard"),
        P("section", "shard"),
        P("section", "shard", None),
        P("section", "shard"),
        P("section", "shard", None),
        P("section", "shard"),
    )
    out_specs = (
        P("section", None, "shard", None),
        P("section", None, "shard", None),
        P("section", "shard"),
        P("section", "shard"),
        P("section", "shard", None),
        P("section", "shard"),
        P("section", "shard", None),
        P("section", "shard"),
        P("section", "shard"),
        P("section", "shard"),
        P("section", "shard", None),
        P("section", "shard"),
        P("section", "shard", None),
        P("section", "shard"),
    )
    fits = mesh.shape["section"] == 2 and mesh.shape["shard"] == HEADS
    on_device = on_device_fast if fits else on_device_general
    return jax.shard_map(
        on_device, mesh=mesh, in_specs=in_specs, out_specs=out_specs, check_vma=False
    )
```
